256 devices in a mesh: rep: 16 (over x, y_hi, core), tp: 16 (over z, y_lo).
Axes of the slice: x: 4, y: 4 (y_hi: 2, y_lo: 2; y = y_hi * 2 + y_lo), z: 8, core: 2. Of those that a mesh axis runs over, the one named last changes fastest.
Arguments:
- queries: bfloat16 [64, 8192], P('rep', 'tp'), may hold values from -160 to 160
- assignment: int32 [64], replicated, may hold values from 0 to 63, each once
- prefix_keys: bfloat16 [131072, 1024], P(('rep', 'tp')), may hold values from -6 to 6
- prefix_values: bfloat16 [131072, 1024], P(('rep', 'tp')), may hold values from -6 to 6
- suffix_keys: bfloat16 [64, 2048, 1024], P('rep', 'tp'), may hold values from -10 to 10
- suffix_values: bfloat16 [64, 2048, 1024], P('rep', 'tp'), may hold values from -6 to 6
- lengths: int32 [64], P('rep'), may hold values from 1 to 2048, 65536 in all
Outputs:
- attended: bfloat16 [64, 8192], P('rep', 'tp')
The draws below stay inside these ranges and needn't reach their ends.
Inputs may be any that keep to these rules, and one draw needn't show every extreme that they name: `assignment`: each request row names its own slot. `lengths`: some slot holds exactly 2048 live positions.
All inputs are finite; a program needn't handle non-finite values. No bound on the sum of `lengths` on one device may be relied on, other than what follows from the above.
Results may differ from the reference program's by a relative error of at most 0.0045.
Values may be sent and summed in bfloat16 or wider, within the bound.
A program may use at most 64 MiB of HBM per device.

```python
import math
import jax
import jax.numpy as jnp
import numpy as np
from jax import lax

HEADS = 64
KVH = 8
HD = 128
SUF = 2048
ROWS = 64
PRE = 131072


def draw_queries(key, part):
    key = jax.random.fold_in(key, 11)
    first = jax.random.fold_in(key, 0)
    values = 3.0 * jax.random.normal(first, (ROWS, HEADS * HD), jnp.float32)
    values = jnp.clip(values, -15.0, 15.0)
    return values.astype(jnp.bfloat16)


def block_scale(stream_key, shape, cuts, low, top_value):
    factor_of, own = 1.0, jax.random.fold_in(stream_key, 6)
    for axis_at, parts in cuts:
        draws = jnp.exp(jax.random.uniform(jax.random.fold_in(own, axis_at), (parts,), jnp.float32, low / len(cuts), top_value / len(cuts)))
        factor_of = factor_of * jnp.repeat(draws, shape[axis_at] // parts).reshape([-1 if axis == axis_at else 1 for axis in range(len(shape))])
    return factor_of


def length_profile(count, total, reach, skew):
    loads = [(1 << 20) // math.isqrt(rank ** skew) + 1 for rank in range(2, count + 1)]
    surplus, holding = total - reach - (count - 1), [1] * (count - 1)
    while surplus > 0:
        free = [i for i in range(count - 1) if holding[i] < reach]
        mass, left = sum([loads[i] for i in free]), surplus
        for i in free:
            extra = min(reach - holding[i], max(1, left * loads[i] // mass), surplus)
            holding[i] = holding[i] + extra
            surplus = surplus - extra
    return np.array([reach] + holding)


def uneven(own_key, amount, total, limit, skew):
    if amount == 2:
        one = jax.random.randint(own_key, (), max(1, total - limit), min(limit, total - 1) + 1)
        return jnp.stack([one, total - one])
    sizes = jnp.asarray(length_profile(amount, total, limit, skew), jnp.int32)
    couples = (amount - 1) // 2
    source_of, sink = sizes[1:1 + 2 * couples:2], sizes[2:2 + 2 * couples:2]
    margin = jnp.minimum(source_of - 1, limit - sink)
    passed = jax.random.randint(jax.random.fold_in(own_key, 1), (couples,), 0, 1 << 20) % (margin + 1)
    sizes = sizes.at[1:1 + 2 * couples:2].set(source_of - passed).at[2:2 + 2 * couples:2].set(sink + passed)
    return sizes[jax.random.permutation(jax.random.fold_in(own_key, 2), amount)]


def bell_draw(own_key, extent, spread, bound, cuts=(), kind=jnp.bfloat16):
    loudness = block_scale(own_key, extent, cuts, -0.22, 0.18) if cuts else 1.0
    result = jax.random.normal(own_key, extent, jnp.float32) * spread * loudness
    return jnp.minimum(jnp.maximum(result, -bound), bound).astype(kind)


def setup_inputs(seed: int = 0) -> dict:
    seeds = jax.random.split(jax.random.key(seed), 8)
    return {
        "queries": draw_queries(jax.random.fold_in(seeds[7], 71), 0),
        "assignment": jax.random.permutation(seeds[1], ROWS).astype(jnp.int32),
        "prefix_keys": bell_draw(seeds[2], (PRE, KVH * HD), 1.0, 6.0, ((0, 256),)),
        "prefix_values": bell_draw(seeds[3], (PRE, KVH * HD), 1.0, 6.0, ((0, 256),)),
        "suffix_keys": bell_draw(seeds[4], (ROWS, SUF, KVH * HD), 1.6, 10.0, ((0, 16), (1, 16))),
        "suffix_values": bell_draw(seeds[5], (ROWS, SUF, KVH * HD), 1.0, 6.0, ((0, 16), (1, 16))),
        "lengths": uneven(seeds[6], ROWS, ROWS * SUF // 2, SUF, 2).astype(jnp.int32),
    }


def reference(queries, assignment, prefix_keys, prefix_values, suffix_keys, suffix_values, lengths):
    group = HEADS // KVH
    scale = HD ** -0.5
    slot_queries = jnp.zeros_like(queries).at[assignment].set(queries)
    keys_all = prefix_keys.astype(jnp.float32).reshape(-1, KVH, HD)
    values_all = prefix_values.astype(jnp.float32).reshape(-1, KVH, HD)
    positions = jnp.arange(SUF, dtype=jnp.int32)

    def one_slot(items):
        query, own_keys, own_values, length = items
        query3 = query.astype(jnp.float32).reshape(KVH, group, HD)
        prefix_scores = jnp.einsum("kgd,pkd->kgp", query3, keys_all) * scale
        own_k = own_keys.astype(jnp.float32).reshape(SUF, KVH, HD)
        own_v = own_values.astype(jnp.float32).reshape(SUF, KVH, HD)
        suffix_scores = jnp.einsum("kgd,jkd->kgj", query3, own_k) * scale
        live = (positions < length)[None, None, :]
        suffix_scores = jnp.where(live, suffix_scores, -jnp.inf)
        top = jnp.maximum(jnp.max(prefix_scores, axis=-1), jnp.max(suffix_scores, axis=-1))
        prefix_weights = jnp.exp(prefix_scores - top[..., None]).astype(jnp.bfloat16)
        suffix_weights = jnp.where(live, jnp.exp(suffix_scores - top[..., None]), 0.0).astype(jnp.bfloat16)
        prefix_weights = lax.optimization_barrier(prefix_weights).astype(jnp.float32)
        suffix_weights = lax.optimization_barrier(suffix_weights).astype(jnp.float32)
        total = jnp.sum(prefix_weights, axis=-1) + jnp.sum(suffix_weights, axis=-1)
        numer = jnp.einsum("kgp,pkd->kgd", prefix_weights, values_all)
        numer = numer + jnp.einsum("kgj,jkd->kgd", suffix_weights, own_v)
        return (numer / total[..., None]).reshape(HEADS * HD).astype(jnp.bfloat16)

    return lax.map(one_slot, (slot_queries, suffix_keys, suffix_values, lengths))
```

```python
import functools
import math

import jax
import jax.numpy as jnp
from jax import lax
from jax.experimental import pallas as pl
from jax.experimental.pallas import tpu as pltpu
from jax.sharding import PartitionSpec as P

MESH = pl.DeviceIdType.MESH
HD = 128
HEADS_CORE = 4
C2 = math.log2(math.e) * HD ** (-0.5)
NEG = -(2.0**100)
BF = jnp.bfloat16
F32 = jnp.float32
NT = (((1,), (1,)), ((), ()))
NN = (((1,), (0,)), ((), ()))


def dot(a, b, dims):
    return lax.dot_general(a, b, dims, preferred_element_type=F32)


def kernel(
    q_ref, asg_ref, len_ref, pk, pv, sk, sv, out_ref,
    kbuf, vbuf, skbuf, svbuf, vt, svt, qf, q0, q1, q2, qs, perm, lens, lensall, nsuf, sbuf, r1, s2, r2,
    ldsem, xsend, xrecv, zsend, zrecv, gsend, grecv, rsend, rrecv, tsend, trecv,
):
    rep, tp = lax.axis_index("rep"), lax.axis_index("tp")
    x, yh, c = rep // 4, (rep // 2) % 2, rep % 2
    z, yl = tp // 2, tp % 2
    y = yh * 2 + yl
    hz = z // 4

    def dev(x_, y_, z_, c_):
        return (x_ * 4 + (y_ // 2) * 2 + c_, z_ * 2 + y_ % 2)

    mine = pl.multiple_of(c * 512, 512)
    theirs = pl.multiple_of((1 - c) * 512, 512)
    rows2 = pl.multiple_of(c * 512, 512)
    pairs = ((pk, kbuf), (sk, skbuf), (pv, vbuf), (sv, svbuf))

    def local_dst(i):
        buf = pairs[i][1]
        return buf.at[pl.ds(rows2, 512)] if i % 2 == 0 else buf.at[pl.ds(c * 4, 4)]

    def src_of(i, cols):
        ref = pairs[i][0]
        return ref.at[:, pl.ds(cols, 512)] if i % 2 == 0 else ref.at[:, :, pl.ds(cols, 512)]

    loads = [pltpu.make_async_copy(src_of(i, mine), local_dst(i), ldsem.at[i]) for i in range(4)]
    for copy in loads:
        copy.start()

    barrier = pltpu.get_barrier_semaphore()

    def greet(x_, y_, z_, c_):
        pl.semaphore_signal(barrier, inc=1, device_id=dev(x_, y_, z_, c_), device_id_type=MESH)

    partner = dev(x, y, z, 1 - c)
    greet(x, y, z, 1 - c)
    for o in range(1, 16):
        greet((x + o // 4) % 4, (y + o % 4) % 4, z, c)
    for k in range(4):
        for cs in range(2):
            zs = 4 * c + k

            @pl.when(jnp.logical_or(zs != z, cs != c))
            def _(zs=zs, cs=cs):
                greet(x, y, zs, cs)

    for zs in range(8):

        @pl.when(jnp.logical_or(jnp.logical_or(zs != z, z % 4 != y), hz != c))
        def _(zs=zs):
            greet(x, z % 4, zs, hz)

    q = q_ref[...].astype(F32)
    for g in range(4):
        qf[g * 4 : g * 4 + 4, :] = q[:, g * 128 : (g + 1) * 128]
    q0[...] = qf[...].astype(BF)

    lane = lax.broadcasted_iota(jnp.int32, (1, 128), 1)
    lane_row = ((lane // 64) * 2 + (lane // 16) % 2) * 4 + lane % 4
    lane_g = ((lane // 32) % 2) * 4 + (lane // 4) % 4
    sub = lax.broadcasted_iota(jnp.int32, (512, 128), 0)
    sub_row = (sub // 128) * 16 + ((sub // 64) % 2) * 8 + ((sub // 16) % 2) * 4 + sub % 4
    sub_g = ((sub // 32) % 2) * 4 + (sub // 4) % 4
    sub_code = sub_row * 8 + sub_g
    for xs in range(4):
        held = jnp.zeros((1, 128), jnp.int32)
        for r in range(16):
            held = jnp.where(lane_row == r, asg_ref[xs * 16 + r], held)
        code = held * 8 + lane_g
        perm[:, xs * 128 : (xs + 1) * 128] = jnp.where(sub_code == code, 1.0, 0.0).astype(BF)

    own_len = jnp.zeros((8, 128), jnp.int32)
    lane8 = lax.broadcasted_iota(jnp.int32, (8, 128), 1)
    for s in range(4):
        own_len = jnp.where(lane8 % 4 == s, len_ref[s], own_len)
    lens[...] = own_len

    n_z = jnp.where(hz == c, 7, 8)
    n_t = jnp.where(4 * c + y == z, 7, 8)
    pl.semaphore_wait(barrier, 16 + n_z + n_t)

    def ztile(ref_z):
        return q1.at[ref_z % 4, pl.ds(pl.multiple_of(c * 16, 16), 16)]

    for o in (4, 3, 5, 2, 6, 1, 7):
        z_ = (z + o) % 8
        pltpu.make_async_remote_copy(
            src_ref=q0, dst_ref=ztile(z), send_sem=zsend.at[0], recv_sem=zrecv.at[z % 4],
            device_id=dev(x, y, z_, hz), device_id_type=MESH,
        ).start()

    @pl.when(hz == c)
    def _():
        pltpu.make_async_copy(q0, ztile(z), zrecv.at[z % 4]).start()

    @pl.when(hz != c)
    def _():
        pltpu.make_async_remote_copy(
            src_ref=q0, dst_ref=ztile(z), send_sem=zsend.at[1], recv_sem=zrecv.at[z % 4],
            device_id=partner, device_id_type=MESH,
        ).start()

    exchanges = [
        pltpu.make_async_remote_copy(
            src_ref=src_of(i, theirs), dst_ref=local_dst(i), send_sem=xsend.at[i], recv_sem=xrecv.at[i],
            device_id=partner, device_id_type=MESH,
        )
        for i in range(4)
    ]
    exchanges.append(
        pltpu.make_async_remote_copy(
            src_ref=lens, dst_ref=lensall, send_sem=xsend.at[4], recv_sem=xrecv.at[4],
            device_id=partner, device_id_type=MESH,
        )
    )
    exchanges[4].start()
    for i in range(4):
        exchanges[i].start()

    me_rows = pl.ds(pl.multiple_of((x * 4 + y) * 32, 32), 32)
    for k in range(4):
        pltpu.make_async_copy(q1.at[k], q1.at[k], zrecv.at[k]).wait()
        pltpu.make_async_copy(q1.at[k], q2.at[k, me_rows], grecv.at[k]).start()
        for o in range(1, 16):
            pltpu.make_async_remote_copy(
                src_ref=q1.at[k], dst_ref=q2.at[k, me_rows], send_sem=gsend, recv_sem=grecv.at[k],
                device_id=dev((x + o // 4) % 4, (y + o % 4) % 4, z, c), device_id_type=MESH,
            ).start()

    ones = jnp.ones((16, 1024), BF)
    for i in range(4):
        loads[i].wait()
    for i in range(5):
        exchanges[i].wait_recv()

    def transpose_values(k, _):
        cols = pl.ds(pl.multiple_of(k * 128, 128), 128)
        vt[k, :128, :] = vbuf[:, cols].T
        vt[k, 128:, :] = ones
        svt[k, :128, :] = svbuf[:, :, cols].reshape(1024, 128).T
        svt[k, 128:, :] = ones
        return 0

    lax.fori_loop(0, 4, transpose_values, 0)

    lane_c = (lane // 16) % 2
    live = jnp.where(lane_c == c, lens[0:1, :], lensall[0:1, :]) - tp * 128
    live = jnp.where(lane // 64 == yh, live, 0)
    depth = lax.broadcasted_iota(jnp.int32, (128, 128), 0)

    def head(k, _):
        cols = pl.ds(pl.multiple_of(k * 128, 128), 128)
        pltpu.make_async_copy(q2.at[k], q2.at[k], grecv.at[k]).wait()
        qs[...] = dot(perm[...], q2[k], NN).astype(BF)

        own = qs[pl.ds(pl.multiple_of(x * 128, 128), 128), :]
        ss = dot(skbuf[:, :, cols].reshape(1024, 128), own, NT) * C2
        parts = []
        for s in range(8):
            limit = jnp.where(jnp.logical_and(lane_c == s // 4, lane % 4 == s % 4), live, 0)
            parts.append(jnp.where(depth < limit, ss[s * 128 : (s + 1) * 128], NEG))
        ss = jnp.concatenate(parts, axis=0)
        ms = jnp.max(ss, axis=0, keepdims=True).astype(BF).astype(F32)
        nsuf[...] = dot(svt[k], jnp.exp2(ss - ms).astype(BF), NN)

        keys = kbuf[:, cols]
        for half in range(2):
            sc = dot(keys, qs[half * 256 : half * 256 + 256, :], NT) * C2
            mp = jnp.max(sc, axis=0, keepdims=True)
            msj = [jnp.where(x == half * 2 + a, ms, NEG) for a in range(2)]
            m = jnp.maximum(mp, jnp.concatenate(msj, axis=1)).astype(BF).astype(F32)
            num = dot(vt[k], jnp.exp2(sc - m).astype(BF), NN)
            for a in range(2):
                j = half * 2 + a
                ma = m[:, a * 128 : a * 128 + 128]
                na = num[:, a * 128 : a * 128 + 128] + jnp.exp2(msj[a] - ma) * nsuf[...]
                slot = k * 4 + j
                sbuf[slot, :128, :] = na[:128].astype(BF)
                total = na[128:144]
                hi = total.astype(BF).astype(F32)
                row = lax.broadcasted_iota(jnp.int32, (16, 128), 0)
                stats = jnp.where(row == 0, ma, jnp.where(row == 1, hi, total - hi))
                sbuf[slot, 128:, :] = stats.astype(BF)
                here = jnp.logical_and(x == j, y == k)

                @pl.when(here)
                def _(slot=slot):
                    pltpu.make_async_copy(sbuf.at[slot], r1.at[x * 4 + y], rrecv).start()

                @pl.when(jnp.logical_not(here))
                def _(slot=slot, j=j):
                    pltpu.make_async_remote_copy(
                        src_ref=sbuf.at[slot], dst_ref=r1.at[x * 4 + y], send_sem=rsend, recv_sem=rrecv,
                        device_id=dev(j, k, z, c), device_id_type=MESH,
                    ).start()

        return 0

    lax.fori_loop(0, 4, head, 0)

    pltpu.make_async_copy(r1, r1, rrecv).wait()
    stats = [r1[i, 128:, :].astype(F32) for i in range(16)]
    m1 = functools.reduce(jnp.maximum, [s[0:1] for s in stats])
    total = jnp.zeros((1, 128), F32)
    numer = jnp.zeros((128, 128), F32)
    for i in range(16):
        w = jnp.exp2(stats[i][0:1] - m1)
        total = total + w * (stats[i][1:2] + stats[i][2:3])
        numer = numer + w * r1[i, :128, :].astype(F32)
    hi = total.astype(BF).astype(F32)
    row = lax.broadcasted_iota(jnp.int32, (16, 128), 0)
    stat = jnp.where(row == 0, m1, jnp.where(row == 1, hi, total - hi)).astype(BF)
    flat = numer.T.astype(BF)
    for d in range(8):
        s2[d, :16, :] = flat[d * 16 : d * 16 + 16, :]
        s2[d, 16:, :] = stat

    zt = 4 * c + y
    for o in range(1, 8):
        y_, c_ = (y + o // 2) % 4, (c + o % 2) % 2
        pltpu.make_async_remote_copy(
            src_ref=s2.at[y_ * 2 + c_], dst_ref=r2.at[z], send_sem=tsend.at[0], recv_sem=trecv,
            device_id=dev(x, y_, zt, c_), device_id_type=MESH,
        ).start()

    @pl.when(zt == z)
    def _():
        pltpu.make_async_copy(s2.at[y * 2 + c], r2.at[z], trecv).start()

    @pl.when(zt != z)
    def _():
        pltpu.make_async_remote_copy(
            src_ref=s2.at[y * 2 + c], dst_ref=r2.at[z], send_sem=tsend.at[1], recv_sem=trecv,
            device_id=dev(x, y, zt, c), device_id_type=MESH,
        ).start()

    pltpu.make_async_copy(r2, r2, trecv).wait()

    offset = y * 32 + c * 16
    pick = lax.broadcasted_iota(jnp.int32, (16, 128), 1) == lax.broadcasted_iota(jnp.int32, (16, 128), 0) + offset
    stats = [r2[i, 16:, :].astype(F32) for i in range(8)]
    m2 = functools.reduce(jnp.maximum, [s[0:1] for s in stats])
    ws = [jnp.exp2(s[0:1] - m2) for s in stats]
    total = functools.reduce(jnp.add, [w * (s[1:2] + s[2:3]) for w, s in zip(ws, stats)])
    acc = jnp.zeros((16, 128), F32)
    for i in range(8):
        column = jnp.sum(jnp.where(pick, ws[i], 0.0), axis=1, keepdims=True)
        acc = acc + column * r2[i, :16, :].astype(F32)
    column = jnp.sum(jnp.where(pick, total, 0.0), axis=1, keepdims=True)
    acc = acc / column
    for g in range(4):
        out_ref[:, g * 128 : (g + 1) * 128] = acc[g * 4 : g * 4 + 4, :].astype(BF)

    for i in range(5):
        exchanges[i].wait_send()
    pltpu.make_async_copy(s2.at[pl.ds(0, 7), pl.ds(0, 16)], s2.at[pl.ds(0, 7), pl.ds(0, 16)], zsend.at[0]).wait()

    @pl.when(hz != c)
    def _():
        pltpu.make_async_copy(q0, q0, zsend.at[1]).wait()

    most = q2.at[:, pl.ds(0, 480)]
    pltpu.make_async_copy(most, most, gsend).wait()
    most = sbuf.at[pl.ds(0, 15)]
    pltpu.make_async_copy(most, most, rsend).wait()
    most = s2.at[pl.ds(0, 7)]
    pltpu.make_async_copy(most, most, tsend.at[0]).wait()

    @pl.when(zt != z)
    def _():
        pltpu.make_async_copy(s2.at[0], s2.at[0], tsend.at[1]).wait()


def shards(queries, assignment, prefix_keys, prefix_values, suffix_keys, suffix_values, lengths):
    vmem, smem, far = (
        pl.BlockSpec(memory_space=pltpu.VMEM),
        pl.BlockSpec(memory_space=pltpu.SMEM),
        pl.BlockSpec(memory_space=pl.ANY),
    )
    dma = pltpu.SemaphoreType.DMA
    return pl.pallas_call(
        kernel,
        out_shape=jax.ShapeDtypeStruct(queries.shape, BF),
        in_specs=[vmem, smem, smem, far, far, far, far],
        out_specs=vmem,
        scratch_shapes=[
            pltpu.VMEM((1024, 512), BF),
            pltpu.VMEM((1024, 512), BF),
            pltpu.VMEM((8, 128, 512), BF),
            pltpu.VMEM((8, 128, 512), BF),
            pltpu.VMEM((4, 144, 1024), BF),
            pltpu.VMEM((4, 144, 1024), BF),
            pltpu.VMEM((16, 128), F32),
            pltpu.VMEM((16, 128), BF),
            pltpu.VMEM((4, 32, 128), BF),
            pltpu.VMEM((4, 512, 128), BF),
            pltpu.VMEM((512, 128), BF),
            pltpu.VMEM((512, 512), BF),
            pltpu.VMEM((8, 128), jnp.int32),
            pltpu.VMEM((8, 128), jnp.int32),
            pltpu.VMEM((144, 128), F32),
            pltpu.VMEM((16, 144, 128), BF),
            pltpu.VMEM((16, 144, 128), BF),
            pltpu.VMEM((8, 32, 128), BF),
            pltpu.VMEM((8, 32, 128), BF),
            dma((4,)),
            dma((5,)),
            dma((5,)),
            dma((2,)),
            dma((4,)),
            dma(()),
            dma((4,)),
            dma(()),
            dma(()),
            dma((2,)),
            dma(()),
        ],
        compiler_params=pltpu.CompilerParams(
            collective_id=0, has_side_effects=True, vmem_limit_bytes=48 * 1024 * 1024
        ),
        cost_estimate=pl.CostEstimate(flops=1_300_000_000, bytes_accessed=4_300_000, transcendentals=2_600_000),
    )(queries, assignment, lengths, prefix_keys, prefix_values, suffix_keys, suffix_values)


def solution(mesh):
    in_specs = (
        P("rep", "tp"),
        P(),
        P(("rep", "tp"), None),
        P(("rep", "tp"), None),
        P("rep", "tp", None),
        P("rep", "tp", None),
        P("rep"),
    )
    out_specs = P("rep", "tp")
    return jax.shard_map(shards, mesh=mesh, in_specs=in_specs, out_specs=out_specs, check_vma=False)
```

```python
import functools
import math

import jax
import jax.numpy as jnp
from jax import lax
from jax.experimental import pallas as pl
from jax.experimental.pallas import tpu as pltpu
from jax.sharding import PartitionSpec as P

MESH = pl.DeviceIdType.MESH
HD = 128
HEADS_CORE = 4
C2 = math.log2(math.e) * HD ** (-0.5)
NEG = -(2.0**100)
BF = jnp.bfloat16
F32 = jnp.float32
NT = (((1,), (1,)), ((), ()))
NN = (((1,), (0,)), ((), ()))


def dot(a, b, dims):
    return lax.dot_general(a, b, dims, preferred_element_type=F32)


def kernel(
    q_hbm, asg_hbm, len_hbm, pk, pv, sk, sv, out_ref,
    kbuf, vbuf, skbuf, svbuf, vt, svt, qf, q0, q1, q2, qs, perm, lens, lensall, nsuf, sbuf, r1, s2, r2,
    q_ref, asg_ref, len_ref, smallsem, ldsem, xsend, xrecv, zsend, zrecv, gsend, grecv, rsend, rrecv, tsend, trecv,
):
    rep, tp = lax.axis_index("rep"), lax.axis_index("tp")
    x, yh, c = rep // 4, (rep // 2) % 2, rep % 2
    z, yl = tp // 2, tp % 2
    y = yh * 2 + yl
    hz = z // 4

    def dev(x_, y_, z_, c_):
        return (x_ * 4 + (y_ // 2) * 2 + c_, z_ * 2 + y_ % 2)

    small = [
        pltpu.make_async_copy(src, dst, smallsem.at[i])
        for i, (src, dst) in enumerate(((q_hbm, q_ref), (asg_hbm, asg_ref), (len_hbm, len_ref)))
    ]
    for copy in small:
        copy.start()

    mine = pl.multiple_of(c * 512, 512)
    theirs = pl.multiple_of((1 - c) * 512, 512)
    rows2 = pl.multiple_of(c * 512, 512)
    pairs = ((pk, kbuf), (sk, skbuf), (pv, vbuf), (sv, svbuf))

    def local_dst(i):
        buf = pairs[i][1]
        return buf.at[pl.ds(rows2, 512)] if i % 2 == 0 else buf.at[pl.ds(c * 4, 4)]

    def src_of(i, cols):
        ref = pairs[i][0]
        return ref.at[:, pl.ds(cols, 512)] if i % 2 == 0 else ref.at[:, :, pl.ds(cols, 512)]

    loads = [pltpu.make_async_copy(src_of(i, mine), local_dst(i), ldsem.at[i]) for i in range(4)]
    barrier = pltpu.get_barrier_semaphore()

    def greet(x_, y_, z_, c_):
        pl.semaphore_signal(barrier, inc=1, device_id=dev(x_, y_, z_, c_), device_id_type=MESH)

    partner = dev(x, y, z, 1 - c)
    greet(x, y, z, 1 - c)
    for o in range(1, 16):
        greet((x + o // 4) % 4, (y + o % 4) % 4, z, c)
    for k in range(4):
        for cs in range(2):
            zs = 4 * c + k

            @pl.when(jnp.logical_or(zs != z, cs != c))
            def _(zs=zs, cs=cs):
                greet(x, y, zs, cs)

    for zs in range(8):

        @pl.when(jnp.logical_or(jnp.logical_or(zs != z, z % 4 != y), hz != c))
        def _(zs=zs):
            greet(x, z % 4, zs, hz)

    for copy in loads:
        copy.start()

    for copy in small:
        copy.wait()
    q = q_ref[...].astype(F32)
    for g in range(4):
        qf[g * 4 : g * 4 + 4, :] = q[:, g * 128 : (g + 1) * 128]
    q0[...] = qf[...].astype(BF)

    lane = lax.broadcasted_iota(jnp.int32, (1, 128), 1)
    lane_row = ((lane // 64) * 2 + (lane // 16) % 2) * 4 + lane % 4
    lane_g = ((lane // 32) % 2) * 4 + (lane // 4) % 4
    sub = lax.broadcasted_iota(jnp.int32, (512, 128), 0)
    sub_row = (sub // 128) * 16 + ((sub // 64) % 2) * 8 + ((sub // 16) % 2) * 4 + sub % 4
    sub_g = ((sub // 32) % 2) * 4 + (sub // 4) % 4
    sub_code = sub_row * 8 + sub_g
    for xs in range(4):
        held = jnp.zeros((1, 128), jnp.int32)
        for r in range(16):
            held = jnp.where(lane_row == r, asg_ref[xs * 16 + r], held)
        code = held * 8 + lane_g
        perm[:, xs * 128 : (xs + 1) * 128] = jnp.where(sub_code == code, 1.0, 0.0).astype(BF)

    own_len = jnp.zeros((8, 128), jnp.int32)
    lane8 = lax.broadcasted_iota(jnp.int32, (8, 128), 1)
    for s in range(4):
        own_len = jnp.where(lane8 % 4 == s, len_ref[s], own_len)
    lens[...] = own_len

    n_z = jnp.where(hz == c, 7, 8)
    n_t = jnp.where(4 * c + y == z, 7, 8)
    pl.semaphore_wait(barrier, 16 + n_z + n_t)

    def ztile(ref_z):
        return q1.at[ref_z % 4, pl.ds(pl.multiple_of(c * 16, 16), 16)]

    for o in (4, 3, 5, 2, 6, 1, 7):
        z_ = (z + o) % 8
        pltpu.make_async_remote_copy(
            src_ref=q0, dst_ref=ztile(z), send_sem=zsend.at[0], recv_sem=zrecv.at[z % 4],
            device_id=dev(x, y, z_, hz), device_id_type=MESH,
        ).start()

    @pl.when(hz == c)
    def _():
        pltpu.make_async_copy(q0, ztile(z), zrecv.at[z % 4]).start()

    @pl.when(hz != c)
    def _():
        pltpu.make_async_remote_copy(
            src_ref=q0, dst_ref=ztile(z), send_sem=zsend.at[1], recv_sem=zrecv.at[z % 4],
            device_id=partner, device_id_type=MESH,
        ).start()

    exchanges = [
        pltpu.make_async_remote_copy(
            src_ref=src_of(i, theirs), dst_ref=local_dst(i), send_sem=xsend.at[i], recv_sem=xrecv.at[i],
            device_id=partner, device_id_type=MESH,
        )
        for i in range(4)
    ]
    exchanges.append(
        pltpu.make_async_remote_copy(
            src_ref=lens, dst_ref=lensall, send_sem=xsend.at[4], recv_sem=xrecv.at[4],
            device_id=partner, device_id_type=MESH,
        )
    )
    exchanges[4].start()
    for i in range(4):
        exchanges[i].start()

    me_rows = pl.ds(pl.multiple_of((x * 4 + y) * 32, 32), 32)
    for k in range(4):
        pltpu.make_async_copy(q1.at[k], q1.at[k], zrecv.at[k]).wait()
        pltpu.make_async_copy(q1.at[k], q2.at[k, me_rows], grecv.at[k]).start()
        for o in range(1, 16):
            pltpu.make_async_remote_copy(
                src_ref=q1.at[k], dst_ref=q2.at[k, me_rows], send_sem=gsend, recv_sem=grecv.at[k],
                device_id=dev((x + o // 4) % 4, (y + o % 4) % 4, z, c), device_id_type=MESH,
            ).start()

    ones = jnp.ones((16, 1024), BF)
    for i in range(4):
        loads[i].wait()
    for i in range(5):
        exchanges[i].wait_recv()

    def transpose_values(k, _):
        cols = pl.ds(pl.multiple_of(k * 128, 128), 128)
        vt[k, :128, :] = vbuf[:, cols].T
        vt[k, 128:, :] = ones
        svt[k, :128, :] = svbuf[:, :, cols].reshape(1024, 128).T
        svt[k, 128:, :] = ones
        return 0

    lax.fori_loop(0, 4, transpose_values, 0)

    lane_c = (lane // 16) % 2
    live = jnp.where(lane_c == c, lens[0:1, :], lensall[0:1, :]) - tp * 128
    live = jnp.where(lane // 64 == yh, live, 0)
    depth = lax.broadcasted_iota(jnp.int32, (128, 128), 0)

    def head(k, _):
        cols = pl.ds(pl.multiple_of(k * 128, 128), 128)
        pltpu.make_async_copy(q2.at[k], q2.at[k], grecv.at[k]).wait()
        qs[...] = dot(perm[...], q2[k], NN).astype(BF)

        own = qs[pl.ds(pl.multiple_of(x * 128, 128), 128), :]
        ss = dot(skbuf[:, :, cols].reshape(1024, 128), own, NT) * C2
        parts = []
        for s in range(8):
            limit = jnp.where(jnp.logical_and(lane_c == s // 4, lane % 4 == s % 4), live, 0)
            parts.append(jnp.where(depth < limit, ss[s * 128 : (s + 1) * 128], NEG))
        ss = jnp.concatenate(parts, axis=0)
        ms = jnp.max(ss, axis=0, keepdims=True).astype(BF).astype(F32)
        nsuf[...] = dot(svt[k], jnp.exp2(ss - ms).astype(BF), NN)

        keys = kbuf[:, cols]
        for half in range(2):
            sc = dot(keys, qs[half * 256 : half * 256 + 256, :], NT) * C2
            mp = jnp.max(sc, axis=0, keepdims=True)
            msj = [jnp.where(x == half * 2 + a, ms, NEG) for a in range(2)]
            m = jnp.maximum(mp, jnp.concatenate(msj, axis=1)).astype(BF).astype(F32)
            num = dot(vt[k], jnp.exp2(sc - m).astype(BF), NN)
            for a in range(2):
                j = half * 2 + a
                ma = m[:, a * 128 : a * 128 + 128]
                na = num[:, a * 128 : a * 128 + 128] + jnp.exp2(msj[a] - ma) * nsuf[...]
                slot = k * 4 + j
                sbuf[slot, :128, :] = na[:128].astype(BF)
                total = na[128:144]
                hi = total.astype(BF).astype(F32)
                row = lax.broadcasted_iota(jnp.int32, (16, 128), 0)
                stats = jnp.where(row == 0, ma, jnp.where(row == 1, hi, total - hi))
                sbuf[slot, 128:, :] = stats.astype(BF)
                here = jnp.logical_and(x == j, y == k)

                @pl.when(here)
                def _(slot=slot):
                    pltpu.make_async_copy(sbuf.at[slot], r1.at[x * 4 + y], rrecv).start()

                @pl.when(jnp.logical_not(here))
                def _(slot=slot, j=j):
                    pltpu.make_async_remote_copy(
                        src_ref=sbuf.at[slot], dst_ref=r1.at[x * 4 + y], send_sem=rsend, recv_sem=rrecv,
                        device_id=dev(j, k, z, c), device_id_type=MESH,
                    ).start()

        return 0

    lax.fori_loop(0, 4, head, 0)

    pltpu.make_async_copy(r1, r1, rrecv).wait()
    stats = [r1[i, 128:, :].astype(F32) for i in range(16)]
    m1 = functools.reduce(jnp.maximum, [s[0:1] for s in stats])
    total = jnp.zeros((1, 128), F32)
    numer = jnp.zeros((128, 128), F32)
    for i in range(16):
        w = jnp.exp2(stats[i][0:1] - m1)
        total = total + w * (stats[i][1:2] + stats[i][2:3])
        numer = numer + w * r1[i, :128, :].astype(F32)
    hi = total.astype(BF).astype(F32)
    row = lax.broadcasted_iota(jnp.int32, (16, 128), 0)
    stat = jnp.where(row == 0, m1, jnp.where(row == 1, hi, total - hi)).astype(BF)
    flat = numer.T.astype(BF)
    for d in range(8):
        s2[d, :16, :] = flat[d * 16 : d * 16 + 16, :]
        s2[d, 16:, :] = stat

    zt = 4 * c + y
    for o in range(1, 8):
        y_, c_ = (y + o // 2) % 4, (c + o % 2) % 2
        pltpu.make_async_remote_copy(
            src_ref=s2.at[y_ * 2 + c_], dst_ref=r2.at[z], send_sem=tsend.at[0], recv_sem=trecv,
            device_id=dev(x, y_, zt, c_), device_id_type=MESH,
        ).start()

    @pl.when(zt == z)
    def _():
        pltpu.make_async_copy(s2.at[y * 2 + c], r2.at[z], trecv).start()

    @pl.when(zt != z)
    def _():
        pltpu.make_async_remote_copy(
            src_ref=s2.at[y * 2 + c], dst_ref=r2.at[z], send_sem=tsend.at[1], recv_sem=trecv,
            device_id=dev(x, y, zt, c), device_id_type=MESH,
        ).start()

    pltpu.make_async_copy(r2, r2, trecv).wait()

    offset = y * 32 + c * 16
    pick = lax.broadcasted_iota(jnp.int32, (16, 128), 1) == lax.broadcasted_iota(jnp.int32, (16, 128), 0) + offset
    stats = [r2[i, 16:, :].astype(F32) for i in range(8)]
    m2 = functools.reduce(jnp.maximum, [s[0:1] for s in stats])
    ws = [jnp.exp2(s[0:1] - m2) for s in stats]
    total = functools.reduce(jnp.add, [w * (s[1:2] + s[2:3]) for w, s in zip(ws, stats)])
    acc = jnp.zeros((16, 128), F32)
    for i in range(8):
        column = jnp.sum(jnp.where(pick, ws[i], 0.0), axis=1, keepdims=True)
        acc = acc + column * r2[i, :16, :].astype(F32)
    column = jnp.sum(jnp.where(pick, total, 0.0), axis=1, keepdims=True)
    acc = acc / column
    for g in range(4):
        out_ref[:, g * 128 : (g + 1) * 128] = acc[g * 4 : g * 4 + 4, :].astype(BF)

    for i in range(5):
        exchanges[i].wait_send()
    pltpu.make_async_copy(s2.at[pl.ds(0, 7), pl.ds(0, 16)], s2.at[pl.ds(0, 7), pl.ds(0, 16)], zsend.at[0]).wait()

    @pl.when(hz != c)
    def _():
        pltpu.make_async_copy(q0, q0, zsend.at[1]).wait()

    most = q2.at[:, pl.ds(0, 480)]
    pltpu.make_async_copy(most, most, gsend).wait()
    most = sbuf.at[pl.ds(0, 15)]
    pltpu.make_async_copy(most, most, rsend).wait()
    most = s2.at[pl.ds(0, 7)]
    pltpu.make_async_copy(most, most, tsend.at[0]).wait()

    @pl.when(zt != z)
    def _():
        pltpu.make_async_copy(s2.at[0], s2.at[0], tsend.at[1]).wait()


def shards(queries, assignment, prefix_keys, prefix_values, suffix_keys, suffix_values, lengths):
    vmem, far = pl.BlockSpec(memory_space=pltpu.VMEM), pl.BlockSpec(memory_space=pl.ANY)
    dma = pltpu.SemaphoreType.DMA
    return pl.pallas_call(
        kernel,
        out_shape=jax.ShapeDtypeStruct(queries.shape, BF),
        in_specs=[far, far, far, far, far, far, far],
        out_specs=vmem,
        scratch_shapes=[
            pltpu.VMEM((1024, 512), BF),
            pltpu.VMEM((1024, 512), BF),
            pltpu.VMEM((8, 128, 512), BF),
            pltpu.VMEM((8, 128, 512), BF),
            pltpu.VMEM((4, 144, 1024), BF),
            pltpu.VMEM((4, 144, 1024), BF),
            pltpu.VMEM((16, 128), F32),
            pltpu.VMEM((16, 128), BF),
            pltpu.VMEM((4, 32, 128), BF),
            pltpu.VMEM((4, 512, 128), BF),
            pltpu.VMEM((512, 128), BF),
            pltpu.VMEM((512, 512), BF),
            pltpu.VMEM((8, 128), jnp.int32),
            pltpu.VMEM((8, 128), jnp.int32),
            pltpu.VMEM((144, 128), F32),
            pltpu.VMEM((16, 144, 128), BF),
            pltpu.VMEM((16, 144, 128), BF),
            pltpu.VMEM((8, 32, 128), BF),
            pltpu.VMEM((8, 32, 128), BF),
            pltpu.VMEM((4, 512), BF),
            pltpu.SMEM((64,), jnp.int32),
            pltpu.SMEM((4,), jnp.int32),
            dma((3,)),
            dma((4,)),
            dma((5,)),
            dma((5,)),
            dma((2,)),
            dma((4,)),
            dma(()),
            dma((4,)),
            dma(()),
            dma(()),
            dma((2,)),
            dma(()),
        ],
        compiler_params=pltpu.CompilerParams(
            collective_id=0, has_side_effects=True, vmem_limit_bytes=60 * 1024 * 1024
        ),
        cost_estimate=pl.CostEstimate(flops=1_300_000_000, bytes_accessed=4_300_000, transcendentals=2_600_000),
    )(queries, assignment, lengths, prefix_keys, prefix_values, suffix_keys, suffix_values)


def solution(mesh):
    in_specs = (
        P("rep", "tp"),
        P(),
        P(("rep", "tp"), None),
        P(("rep", "tp"), None),
        P("rep", "tp", None),
        P("rep", "tp", None),
        P("rep"),
    )
    out_specs = P("rep", "tp")
    return jax.shard_map(shards, mesh=mesh, in_specs=in_specs, out_specs=out_specs, check_vma=False)
```

```python
import functools
import math

import jax
import jax.numpy as jnp
from jax import lax
from jax.experimental import pallas as pl
from jax.experimental.pallas import tpu as pltpu
from jax.sharding import PartitionSpec as P

MESH = pl.DeviceIdType.MESH
HD = 128
HEADS_CORE = 4
C2 = math.log2(math.e) * HD ** (-0.5)
NEG = -(2.0**100)
BF = jnp.bfloat16
F32 = jnp.float32
NT = (((1,), (1,)), ((), ()))
NN = (((1,), (0,)), ((), ()))


def dot(a, b, dims):
    return lax.dot_general(a, b, dims, preferred_element_type=F32)


def kernel(
    q_hbm, asg_hbm, len_hbm, pk, pv, sk, sv, out_ref,
    kbuf, vbuf, skbuf, svbuf, qf, q0, q1, q2, qs, perm, lens, lensall, bias, sbuf, r1, s2, r2,
    q_ref, asg_ref, len_ref, smallsem, ldsem, xsend, xrecv, zsend, zrecv, gsend, grecv, rsend, rrecv, tsend, trecv,
):
    rep, tp = lax.axis_index("rep"), lax.axis_index("tp")
    x, yh, c = rep // 4, (rep // 2) % 2, rep % 2
    z, yl = tp // 2, tp % 2
    y = yh * 2 + yl
    hz = z // 4

    def dev(x_, y_, z_, c_):
        return (x_ * 4 + (y_ // 2) * 2 + c_, z_ * 2 + y_ % 2)

    small = [
        pltpu.make_async_copy(src, dst, smallsem.at[i])
        for i, (src, dst) in enumerate(((q_hbm, q_ref), (asg_hbm, asg_ref), (len_hbm, len_ref)))
    ]
    for copy in small:
        copy.start()

    mine = pl.multiple_of(c * 512, 512)
    theirs = pl.multiple_of((1 - c) * 512, 512)
    rows2 = pl.multiple_of(c * 512, 512)
    pairs = ((pk, kbuf), (sk, skbuf), (pv, vbuf), (sv, svbuf))

    def local_dst(i):
        buf = pairs[i][1]
        return buf.at[pl.ds(rows2, 512)] if i % 2 == 0 else buf.at[pl.ds(c * 4, 4)]

    def src_of(i, cols):
        ref = pairs[i][0]
        return ref.at[:, pl.ds(cols, 512)] if i % 2 == 0 else ref.at[:, :, pl.ds(cols, 512)]

    loads = [pltpu.make_async_copy(src_of(i, mine), local_dst(i), ldsem.at[i]) for i in range(4)]
    barrier = pltpu.get_barrier_semaphore()

    def greet(x_, y_, z_, c_):
        pl.semaphore_signal(barrier, inc=1, device_id=dev(x_, y_, z_, c_), device_id_type=MESH)

    partner = dev(x, y, z, 1 - c)
    greet(x, y, z, 1 - c)
    for o in range(1, 16):
        greet((x + o // 4) % 4, (y + o % 4) % 4, z, c)
    for k in range(4):
        for cs in range(2):
            zs = 4 * c + k

            @pl.when(jnp.logical_or(zs != z, cs != c))
            def _(zs=zs, cs=cs):
                greet(x, y, zs, cs)

    for zs in range(8):

        @pl.when(jnp.logical_or(jnp.logical_or(zs != z, z % 4 != y), hz != c))
        def _(zs=zs):
            greet(x, z % 4, zs, hz)

    for copy in loads:
        copy.start()

    for copy in small:
        copy.wait()
    q = q_ref[...].astype(F32)
    for g in range(4):
        qf[g * 4 : g * 4 + 4, :] = q[:, g * 128 : (g + 1) * 128]
    q0[...] = qf[...].astype(BF)

    lane = lax.broadcasted_iota(jnp.int32, (1, 128), 1)
    lane_row = ((lane // 64) * 2 + (lane // 16) % 2) * 4 + lane % 4
    lane_g = ((lane // 32) % 2) * 4 + (lane // 4) % 4
    sub = lax.broadcasted_iota(jnp.int32, (512, 128), 0)
    sub_row = (sub // 128) * 16 + ((sub // 64) % 2) * 8 + ((sub // 16) % 2) * 4 + sub % 4
    sub_g = ((sub // 32) % 2) * 4 + (sub // 4) % 4
    sub_code = sub_row * 8 + sub_g
    for xs in range(4):
        held = jnp.zeros((1, 128), jnp.int32)
        for r in range(16):
            held = jnp.where(lane_row == r, asg_ref[xs * 16 + r], held)
        code = held * 8 + lane_g
        perm[:, xs * 128 : (xs + 1) * 128] = jnp.where(sub_code == code, 1.0, 0.0).astype(BF)

    own_len = jnp.zeros((8, 128), jnp.int32)
    sub8 = lax.broadcasted_iota(jnp.int32, (8, 128), 0)
    for s in range(4):
        own_len = jnp.where(sub8 % 4 == s, len_ref[s], own_len)
    lens[...] = own_len

    n_z = jnp.where(hz == c, 7, 8)
    n_t = jnp.where(4 * c + y == z, 7, 8)
    pl.semaphore_wait(barrier, 16 + n_z + n_t)

    def ztile(ref_z):
        return q1.at[ref_z % 4, pl.ds(pl.multiple_of(c * 16, 16), 16)]

    for o in (4, 3, 5, 2, 6, 1, 7):
        z_ = (z + o) % 8
        pltpu.make_async_remote_copy(
            src_ref=q0, dst_ref=ztile(z), send_sem=zsend.at[0], recv_sem=zrecv.at[z % 4],
            device_id=dev(x, y, z_, hz), device_id_type=MESH,
        ).start()

    @pl.when(hz == c)
    def _():
        pltpu.make_async_copy(q0, ztile(z), zrecv.at[z % 4]).start()

    @pl.when(hz != c)
    def _():
        pltpu.make_async_remote_copy(
            src_ref=q0, dst_ref=ztile(z), send_sem=zsend.at[1], recv_sem=zrecv.at[z % 4],
            device_id=partner, device_id_type=MESH,
        ).start()

    exchanges = [
        pltpu.make_async_remote_copy(
            src_ref=src_of(i, theirs), dst_ref=local_dst(i), send_sem=xsend.at[i], recv_sem=xrecv.at[i],
            device_id=partner, device_id_type=MESH,
        )
        for i in range(4)
    ]
    exchanges.append(
        pltpu.make_async_remote_copy(
            src_ref=lens, dst_ref=lensall, send_sem=xsend.at[4], recv_sem=xrecv.at[4],
            device_id=partner, device_id_type=MESH,
        )
    )
    exchanges[4].start()
    for i in range(4):
        exchanges[i].start()

    me_rows = pl.ds(pl.multiple_of((x * 4 + y) * 32, 32), 32)
    for k in range(4):
        pltpu.make_async_copy(q1.at[k], q1.at[k], zrecv.at[k]).wait()
    for i in range(4):
        k = (y + 1 + i) % 4
        pltpu.make_async_copy(q1.at[k], q2.at[k, me_rows], grecv.at[k]).start()
        for o in range(1, 16):
            y_ = (y + o % 4) % 4
            k = (y_ + 1 + i) % 4
            pltpu.make_async_remote_copy(
                src_ref=q1.at[k], dst_ref=q2.at[k, me_rows], send_sem=gsend, recv_sem=grecv.at[k],
                device_id=dev((x + o // 4) % 4, y_, z, c), device_id_type=MESH,
            ).start()

    exchanges[4].wait_recv()
    rows = lax.broadcasted_iota(jnp.int32, (128, 128), 0)
    lanes = lax.broadcasted_iota(jnp.int32, (128, 128), 1)
    lens_own = jnp.concatenate([lens[...]] * 16, axis=0)
    lens_other = jnp.concatenate([lensall[...]] * 16, axis=0)
    row_c = (rows // 16) % 2
    live = jnp.where(row_c == c, lens_own, lens_other) - tp * 128
    live = jnp.where(rows // 64 == yh, live, 0)
    row_slot = row_c * 4 + rows % 4
    for s in range(8):
        limit = jnp.where(row_slot == s, live, 0)
        bias[:, s * 128 : s * 128 + 128] = jnp.where(lanes < limit, 0.0, NEG)

    for i in range(4):
        loads[i].wait()
        exchanges[i].wait_recv()

    eye = rows == lanes
    ones = jnp.ones((1024, 128), BF)
    stat_row = lax.broadcasted_iota(jnp.int32, (16, 128), 0)

    def as_row(column):
        return jnp.sum(jnp.where(eye, column, 0.0), axis=0, keepdims=True)

    def stat_tile(top, total):
        hi = total.astype(BF).astype(F32)
        return jnp.where(stat_row == 0, top, jnp.where(stat_row == 1, hi, total - hi)).astype(BF)

    def weights(scores, top):
        return jnp.exp2(scores - top).astype(BF)

    def largest(scores):
        return jnp.max(scores, axis=1, keepdims=True)

    def head(i, _):
        k = (y + 1 + i) % 4
        cols = pl.ds(pl.multiple_of(k * 128, 128), 128)
        pltpu.make_async_copy(q2.at[k], q2.at[k], grecv.at[k]).wait()
        qs[...] = dot(perm[...], q2[k], NN).astype(BF)
        chunks = [(x + 1 + a) % 4 for a in range(4)]
        parts = [qs[pl.ds(pl.multiple_of(j * 128, 128), 128), :] for j in chunks]
        keys = kbuf[:, cols]
        values = jnp.concatenate([vbuf[:, cols], ones], axis=1)
        suffix_keys = skbuf[:, :, cols].reshape(1024, 128)
        suffix_values = jnp.concatenate([svbuf[:, :, cols].reshape(1024, 128), ones], axis=1)

        s0 = dot(jnp.concatenate(parts[:2], axis=0), keys, NT) * C2
        s1 = dot(jnp.concatenate(parts[2:], axis=0), keys, NT) * C2
        ss = dot(parts[3], suffix_keys, NT) * C2 + bias[...]
        m0 = largest(s0).astype(BF).astype(F32)
        n0 = dot(weights(s0, m0), values, NN)
        m1 = largest(s1)
        m1 = jnp.concatenate([m1[:128], jnp.maximum(m1[128:], largest(ss))], axis=0).astype(BF).astype(F32)
        n1 = dot(weights(s1, m1), values, NN)
        ns = dot(weights(ss, m1[128:]), suffix_values, NN)

        pieces = [
            (m0[:128], n0[:128]),
            (m0[128:], n0[128:]),
            (m1[:128], n1[:128]),
            (m1[128:], n1[128:] + ns),
        ]
        for a in range(4):
            m, n = pieces[a]
            slot = i * 4 + a
            sbuf[slot, :128, :] = n[:, :128].astype(BF)
            sbuf[slot, 128:, :] = stat_tile(as_row(m), as_row(n[:, 128:]))

            def send(slot=slot, j=chunks[a]):
                pltpu.make_async_remote_copy(
                    src_ref=sbuf.at[slot], dst_ref=r1.at[x * 4 + y], send_sem=rsend, recv_sem=rrecv,
                    device_id=dev(j, k, z, c), device_id_type=MESH,
                ).start()

            if a < 3:
                send()
            else:
                pl.when(i < 3)(send)
        return 0

    lax.fori_loop(0, 4, head, 0)
    pltpu.make_async_copy(sbuf.at[15], r1.at[x * 4 + y], rrecv).start()

    pltpu.make_async_copy(r1, r1, rrecv).wait()
    stats = [r1[i, 128:, :].astype(F32) for i in range(16)]
    top = functools.reduce(jnp.maximum, [s[0:1] for s in stats])
    ws = [jnp.exp2(s[0:1] - top) for s in stats]
    total = functools.reduce(jnp.add, [w * (s[1:2] + s[2:3]) for w, s in zip(ws, stats)])
    his = [w.astype(BF).astype(F32) for w in ws]
    spread = [
        jnp.concatenate([jnp.where(eye, w, 0.0).astype(BF) for w in part], axis=1)
        for part in (his, [w - h for w, h in zip(ws, his)])
    ]
    both = dot(jnp.concatenate(spread, axis=0), jnp.concatenate([r1[i, :128, :] for i in range(16)], axis=0), NN)
    flat = (both[:128] + both[128:]).astype(BF)
    stat = stat_tile(top, total)
    for d in range(8):
        s2[d, :16, :] = flat[d * 16 : d * 16 + 16, :]
        s2[d, 16:, :] = stat

    zt = 4 * c + y
    for o in range(1, 8):
        y_, c_ = (y + o // 2) % 4, (c + o % 2) % 2
        pltpu.make_async_remote_copy(
            src_ref=s2.at[y_ * 2 + c_], dst_ref=r2.at[z], send_sem=tsend.at[0], recv_sem=trecv,
            device_id=dev(x, y_, zt, c_), device_id_type=MESH,
        ).start()

    @pl.when(zt == z)
    def _():
        pltpu.make_async_copy(s2.at[y * 2 + c], r2.at[z], trecv).start()

    @pl.when(zt != z)
    def _():
        pltpu.make_async_remote_copy(
            src_ref=s2.at[y * 2 + c], dst_ref=r2.at[z], send_sem=tsend.at[1], recv_sem=trecv,
            device_id=dev(x, y, zt, c), device_id_type=MESH,
        ).start()

    pltpu.make_async_copy(r2, r2, trecv).wait()

    offset = y * 32 + c * 16
    pick = lax.broadcasted_iota(jnp.int32, (16, 128), 1) == lax.broadcasted_iota(jnp.int32, (16, 128), 0) + offset
    stats = [r2[i, 16:, :].astype(F32) for i in range(8)]
    m2 = functools.reduce(jnp.maximum, [s[0:1] for s in stats])
    ws = [jnp.exp2(s[0:1] - m2) for s in stats]
    total = functools.reduce(jnp.add, [w * (s[1:2] + s[2:3]) for w, s in zip(ws, stats)])
    acc = jnp.zeros((16, 128), F32)
    for i in range(8):
        column = jnp.sum(jnp.where(pick, ws[i], 0.0), axis=1, keepdims=True)
        acc = acc + column * r2[i, :16, :].astype(F32)
    column = jnp.sum(jnp.where(pick, total, 0.0), axis=1, keepdims=True)
    acc = acc / column
    for g in range(4):
        out_ref[:, g * 128 : (g + 1) * 128] = acc[g * 4 : g * 4 + 4, :].astype(BF)

    for i in range(5):
        exchanges[i].wait_send()
    pltpu.make_async_copy(s2.at[pl.ds(0, 7), pl.ds(0, 16)], s2.at[pl.ds(0, 7), pl.ds(0, 16)], zsend.at[0]).wait()

    @pl.when(hz != c)
    def _():
        pltpu.make_async_copy(q0, q0, zsend.at[1]).wait()

    most = q2.at[:, pl.ds(0, 480)]
    pltpu.make_async_copy(most, most, gsend).wait()
    most = sbuf.at[pl.ds(0, 15)]
    pltpu.make_async_copy(most, most, rsend).wait()
    most = s2.at[pl.ds(0, 7)]
    pltpu.make_async_copy(most, most, tsend.at[0]).wait()

    @pl.when(zt != z)
    def _():
        pltpu.make_async_copy(s2.at[0], s2.at[0], tsend.at[1]).wait()


def shards(queries, assignment, prefix_keys, prefix_values, suffix_keys, suffix_values, lengths):
    vmem, far = pl.BlockSpec(memory_space=pltpu.VMEM), pl.BlockSpec(memory_space=pl.ANY)
    dma = pltpu.SemaphoreType.DMA
    return pl.pallas_call(
        kernel,
        out_shape=jax.ShapeDtypeStruct(queries.shape, BF),
        in_specs=[far, far, far, far, far, far, far],
        out_specs=vmem,
        scratch_shapes=[
            pltpu.VMEM((1024, 512), BF),
            pltpu.VMEM((1024, 512), BF),
            pltpu.VMEM((8, 128, 512), BF),
            pltpu.VMEM((8, 128, 512), BF),
            pltpu.VMEM((16, 128), F32),
            pltpu.VMEM((16, 128), BF),
            pltpu.VMEM((4, 32, 128), BF),
            pltpu.VMEM((4, 512, 128), BF),
            pltpu.VMEM((512, 128), BF),
            pltpu.VMEM((512, 512), BF),
            pltpu.VMEM((8, 128), jnp.int32),
            pltpu.VMEM((8, 128), jnp.int32),
            pltpu.VMEM((128, 1024), F32),
            pltpu.VMEM((16, 144, 128), BF),
            pltpu.VMEM((16, 144, 128), BF),
            pltpu.VMEM((8, 32, 128), BF),
            pltpu.VMEM((8, 32, 128), BF),
            pltpu.VMEM((4, 512), BF),
            pltpu.SMEM((64,), jnp.int32),
            pltpu.SMEM((4,), jnp.int32),
            dma((3,)),
            dma((4,)),
            dma((5,)),
            dma((5,)),
            dma((2,)),
            dma((4,)),
            dma(()),
            dma((4,)),
            dma(()),
            dma(()),
            dma((2,)),
            dma(()),
        ],
        compiler_params=pltpu.CompilerParams(
            collective_id=0, has_side_effects=True, vmem_limit_bytes=60 * 1024 * 1024
        ),
        cost_estimate=pl.CostEstimate(flops=1_300_000_000, bytes_accessed=4_300_000, transcendentals=2_600_000),
    )(queries, assignment, lengths, prefix_keys, prefix_values, suffix_keys, suffix_values)


def solution(mesh):
    in_specs = (
        P("rep", "tp"),
        P(),
        P(("rep", "tp"), None),
        P(("rep", "tp"), None),
        P("rep", "tp", None),
        P("rep", "tp", None),
        P("rep"),
    )
    out_specs = P("rep", "tp")
    return jax.shard_map(shards, mesh=mesh, in_specs=in_specs, out_specs=out_specs, check_vma=False)
```

```python
import functools
import math

import jax
import jax.numpy as jnp
from jax import lax
from jax.experimental import pallas as pl
from jax.experimental.pallas import tpu as pltpu
from jax.sharding import PartitionSpec as P

MESH = pl.DeviceIdType.MESH
HD = 128
HEADS_CORE = 4
C2 = math.log2(math.e) * HD ** (-0.5)
NEG = -(2.0**100)
BF = jnp.bfloat16
F32 = jnp.float32
NT = (((1,), (1,)), ((), ()))
NN = (((1,), (0,)), ((), ()))


def dot(a, b, dims):
    return lax.dot_general(a, b, dims, preferred_element_type=F32)


def kernel(
    q_hbm, asg_hbm, len_hbm, pk, pv, sk, sv, out_ref,
    kbuf, vbuf, skbuf, svbuf, qf, q0, q1, q2, qs, perm, lens, lensall, bias, sbuf, r1, s2, r2,
    q_ref, asg_ref, len_ref, smallsem, ldsem, xsend, xrecv, zsend, zrecv, hsend, hrecv, gsend, grecv, rsend, rrecv, tsend, trecv,
):
    rep, tp = lax.axis_index("rep"), lax.axis_index("tp")
    x, yh, c = rep // 4, (rep // 2) % 2, rep % 2
    z, yl = tp // 2, tp % 2
    y = yh * 2 + yl
    hz = z // 4

    def dev(x_, y_, z_, c_):
        return (x_ * 4 + (y_ // 2) * 2 + c_, z_ * 2 + y_ % 2)

    small = [
        pltpu.make_async_copy(src, dst, smallsem.at[i])
        for i, (src, dst) in enumerate(((q_hbm, q_ref), (asg_hbm, asg_ref), (len_hbm, len_ref)))
    ]
    for copy in small:
        copy.start()

    mine = pl.multiple_of(c * 512, 512)
    theirs = pl.multiple_of((1 - c) * 512, 512)
    rows2 = pl.multiple_of(c * 512, 512)
    pairs = ((pk, kbuf), (sk, skbuf), (pv, vbuf), (sv, svbuf))

    def local_dst(i):
        buf = pairs[i][1]
        return buf.at[pl.ds(rows2, 512)] if i % 2 == 0 else buf.at[pl.ds(c * 4, 4)]

    def src_of(i, cols):
        ref = pairs[i][0]
        return ref.at[:, pl.ds(cols, 512)] if i % 2 == 0 else ref.at[:, :, pl.ds(cols, 512)]

    loads = [pltpu.make_async_copy(src_of(i, mine), local_dst(i), ldsem.at[i]) for i in range(4)]
    barrier = pltpu.get_barrier_semaphore()

    def greet(x_, y_, z_, c_):
        pl.semaphore_signal(barrier, inc=1, device_id=dev(x_, y_, z_, c_), device_id_type=MESH)

    partner = dev(x, y, z, 1 - c)
    greet(x, y, z, 1 - c)
    for o in range(1, 16):
        greet((x + o // 4) % 4, (y + o % 4) % 4, z, c)
    for k in range(4):
        for cs in range(2):
            zs = 4 * c + k

            @pl.when(jnp.logical_or(zs != z, cs != c))
            def _(zs=zs, cs=cs):
                greet(x, y, zs, cs)

    for zs in range(8):

        @pl.when(jnp.logical_or(jnp.logical_or(zs != z, z % 4 != y), hz != c))
        def _(zs=zs):
            greet(x, z % 4, zs, hz)

    for copy in loads:
        copy.start()

    for copy in small:
        copy.wait()
    q = q_ref[...].astype(F32)
    for g in range(4):
        qf[g * 4 : g * 4 + 4, :] = q[:, g * 128 : (g + 1) * 128]
    q0[...] = qf[...].astype(BF)

    lane = lax.broadcasted_iota(jnp.int32, (1, 128), 1)
    lane_row = ((lane // 64) * 2 + (lane // 16) % 2) * 4 + lane % 4
    lane_g = ((lane // 32) % 2) * 4 + (lane // 4) % 4
    sub = lax.broadcasted_iota(jnp.int32, (512, 128), 0)
    sub_row = (sub // 128) * 16 + ((sub // 64) % 2) * 8 + ((sub // 16) % 2) * 4 + sub % 4
    sub_g = ((sub // 32) % 2) * 4 + (sub // 4) % 4
    sub_code = sub_row * 8 + sub_g
    for xs in range(4):
        held = jnp.zeros((1, 128), jnp.int32)
        for r in range(16):
            held = jnp.where(lane_row == r, asg_ref[xs * 16 + r], held)
        code = held * 8 + lane_g
        perm[:, xs * 128 : (xs + 1) * 128] = jnp.where(sub_code == code, 1.0, 0.0).astype(BF)

    own_len = jnp.zeros((8, 128), jnp.int32)
    sub8 = lax.broadcasted_iota(jnp.int32, (8, 128), 0)
    for s in range(4):
        own_len = jnp.where(sub8 % 4 == s, len_ref[s], own_len)
    lens[...] = own_len

    n_z = jnp.where(hz == c, 7, 8)
    n_t = jnp.where(4 * c + y == z, 7, 8)
    pl.semaphore_wait(barrier, 16 + n_z + n_t)

    def ztile(ref_z):
        return q1.at[ref_z % 4, pl.ds(pl.multiple_of(c * 16, 16), 16)]

    for o in (4, 3, 5, 2, 6, 1, 7):
        z_ = (z + o) % 8
        pltpu.make_async_remote_copy(
            src_ref=q0, dst_ref=ztile(z), send_sem=zsend.at[0], recv_sem=zrecv.at[z % 4],
            device_id=dev(x, y, z_, hz), device_id_type=MESH,
        ).start()

    @pl.when(hz == c)
    def _():
        pltpu.make_async_copy(q0, ztile(z), zrecv.at[z % 4]).start()

    @pl.when(hz != c)
    def _():
        pltpu.make_async_remote_copy(
            src_ref=q0, dst_ref=ztile(z), send_sem=zsend.at[1], recv_sem=zrecv.at[z % 4],
            device_id=partner, device_id_type=MESH,
        ).start()

    exchanges = [
        pltpu.make_async_remote_copy(
            src_ref=src_of(i, theirs), dst_ref=local_dst(i), send_sem=xsend.at[i], recv_sem=xrecv.at[i],
            device_id=partner, device_id_type=MESH,
        )
        for i in range(4)
    ]
    exchanges.append(
        pltpu.make_async_remote_copy(
            src_ref=lens, dst_ref=lensall, send_sem=xsend.at[4], recv_sem=xrecv.at[4],
            device_id=partner, device_id_type=MESH,
        )
    )
    exchanges[4].start()
    for i in range(4):
        exchanges[i].start()

    for k in range(4):
        pltpu.make_async_copy(q1.at[k], q1.at[k], zrecv.at[k]).wait()
        pltpu.make_async_copy(q1.at[k], q2.at[k, x, y], hrecv.at[k]).start()
        for o in (1, 3, 2):
            to = dev(x, (y + o) % 4, z, c) if k % 2 == 0 else dev((x + o) % 4, y, z, c)
            pltpu.make_async_remote_copy(
                src_ref=q1.at[k], dst_ref=q2.at[k, x, y], send_sem=hsend, recv_sem=hrecv.at[k],
                device_id=to, device_id_type=MESH,
            ).start()
    for i in range(4):
        k = (y + 1 + i) % 4
        pltpu.make_async_copy(q2.at[k, 0], q2.at[k, 0], hrecv.at[k]).wait()

        @pl.when(k % 2 == 0)
        def _(k=k):
            for o in (1, 3, 2):
                pltpu.make_async_remote_copy(
                    src_ref=q2.at[k, x], dst_ref=q2.at[k, x], send_sem=gsend, recv_sem=grecv.at[k],
                    device_id=dev((x + o) % 4, y, z, c), device_id_type=MESH,
                ).start()

        @pl.when(k % 2 == 1)
        def _(k=k):
            for o in (1, 3, 2):
                pltpu.make_async_remote_copy(
                    src_ref=q2.at[k, :, y], dst_ref=q2.at[k, :, y], send_sem=gsend, recv_sem=grecv.at[k],
                    device_id=dev(x, (y + o) % 4, z, c), device_id_type=MESH,
                ).start()

    exchanges[4].wait_recv()
    rows = lax.broadcasted_iota(jnp.int32, (128, 128), 0)
    lanes = lax.broadcasted_iota(jnp.int32, (128, 128), 1)
    lens_own = jnp.concatenate([lens[...]] * 16, axis=0)
    lens_other = jnp.concatenate([lensall[...]] * 16, axis=0)
    row_c = (rows // 16) % 2
    live = jnp.where(row_c == c, lens_own, lens_other) - tp * 128
    live = jnp.where(rows // 64 == yh, live, 0)
    row_slot = row_c * 4 + rows % 4
    for s in range(8):
        limit = jnp.where(row_slot == s, live, 0)
        bias[:, s * 128 : s * 128 + 128] = jnp.where(lanes < limit, 0.0, NEG)

    for i in range(4):
        loads[i].wait()
        exchanges[i].wait_recv()

    eye = rows == lanes
    ones = jnp.ones((1024, 128), BF)
    stat_row = lax.broadcasted_iota(jnp.int32, (16, 128), 0)

    def as_row(column):
        return jnp.sum(jnp.where(eye, column, 0.0), axis=0, keepdims=True)

    def stat_tile(top, total):
        hi = total.astype(BF).astype(F32)
        return jnp.where(stat_row == 0, top, jnp.where(stat_row == 1, hi, total - hi)).astype(BF)

    def weights(scores, top):
        return jnp.exp2(scores - top).astype(BF)

    def largest(scores):
        return jnp.max(scores, axis=1, keepdims=True)

    def head(i, _):
        k = (y + 1 + i) % 4
        cols = pl.ds(pl.multiple_of(k * 128, 128), 128)
        arrived = q2.at[k, pl.ds(0, 3)]
        pltpu.make_async_copy(arrived, arrived, grecv.at[k]).wait()
        qs[...] = dot(perm[...], q2[k].reshape(512, 128), NN).astype(BF)
        chunks = [(x + 1 + a) % 4 for a in range(4)]
        parts = [qs[pl.ds(pl.multiple_of(j * 128, 128), 128), :] for j in chunks]
        keys = kbuf[:, cols]
        values = jnp.concatenate([vbuf[:, cols], ones], axis=1)
        suffix_keys = skbuf[:, :, cols].reshape(1024, 128)
        suffix_values = jnp.concatenate([svbuf[:, :, cols].reshape(1024, 128), ones], axis=1)

        s0 = dot(jnp.concatenate(parts[:2], axis=0), keys, NT) * C2
        s1 = dot(jnp.concatenate(parts[2:], axis=0), keys, NT) * C2
        ss = dot(parts[3], suffix_keys, NT) * C2 + bias[...]
        m0 = largest(s0).astype(BF).astype(F32)
        n0 = dot(weights(s0, m0), values, NN)
        m1 = largest(s1)
        m1 = jnp.concatenate([m1[:128], jnp.maximum(m1[128:], largest(ss))], axis=0).astype(BF).astype(F32)
        n1 = dot(weights(s1, m1), values, NN)
        ns = dot(weights(ss, m1[128:]), suffix_values, NN)

        pieces = [
            (m0[:128], n0[:128]),
            (m0[128:], n0[128:]),
            (m1[:128], n1[:128]),
            (m1[128:], n1[128:] + ns),
        ]
        for a in range(4):
            m, n = pieces[a]
            slot = i * 4 + a
            sbuf[slot, :128, :] = n[:, :128].astype(BF)
            sbuf[slot, 128:, :] = stat_tile(as_row(m), as_row(n[:, 128:]))

            def send(slot=slot, j=chunks[a]):
                pltpu.make_async_remote_copy(
                    src_ref=sbuf.at[slot], dst_ref=r1.at[x * 4 + y], send_sem=rsend, recv_sem=rrecv,
                    device_id=dev(j, k, z, c), device_id_type=MESH,
                ).start()

            if a < 3:
                send()
            else:
                pl.when(i < 3)(send)
        return 0

    lax.fori_loop(0, 4, head, 0)
    pltpu.make_async_copy(sbuf.at[15], r1.at[x * 4 + y], rrecv).start()

    pltpu.make_async_copy(r1, r1, rrecv).wait()
    stats = [r1[i, 128:, :].astype(F32) for i in range(16)]
    top = functools.reduce(jnp.maximum, [s[0:1] for s in stats])
    ws = [jnp.exp2(s[0:1] - top) for s in stats]
    total = functools.reduce(jnp.add, [w * (s[1:2] + s[2:3]) for w, s in zip(ws, stats)])
    his = [w.astype(BF).astype(F32) for w in ws]
    spread = [
        jnp.concatenate([jnp.where(eye, w, 0.0).astype(BF) for w in part], axis=1)
        for part in (his, [w - h for w, h in zip(ws, his)])
    ]
    both = dot(jnp.concatenate(spread, axis=0), jnp.concatenate([r1[i, :128, :] for i in range(16)], axis=0), NN)
    flat = (both[:128] + both[128:]).astype(BF)
    stat = stat_tile(top, total)
    for d in range(8):
        s2[d, :16, :] = flat[d * 16 : d * 16 + 16, :]
        s2[d, 16:, :] = stat

    zt = 4 * c + y
    for o in range(1, 8):
        y_, c_ = (y + o // 2) % 4, (c + o % 2) % 2
        pltpu.make_async_remote_copy(
            src_ref=s2.at[y_ * 2 + c_], dst_ref=r2.at[z], send_sem=tsend.at[0], recv_sem=trecv,
            device_id=dev(x, y_, zt, c_), device_id_type=MESH,
        ).start()

    @pl.when(zt == z)
    def _():
        pltpu.make_async_copy(s2.at[y * 2 + c], r2.at[z], trecv).start()

    @pl.when(zt != z)
    def _():
        pltpu.make_async_remote_copy(
            src_ref=s2.at[y * 2 + c], dst_ref=r2.at[z], send_sem=tsend.at[1], recv_sem=trecv,
            device_id=dev(x, y, zt, c), device_id_type=MESH,
        ).start()

    pltpu.make_async_copy(r2, r2, trecv).wait()

    offset = y * 32 + c * 16
    pick = lax.broadcasted_iota(jnp.int32, (16, 128), 1) == lax.broadcasted_iota(jnp.int32, (16, 128), 0) + offset
    stats = [r2[i, 16:, :].astype(F32) for i in range(8)]
    m2 = functools.reduce(jnp.maximum, [s[0:1] for s in stats])
    ws = [jnp.exp2(s[0:1] - m2) for s in stats]
    total = functools.reduce(jnp.add, [w * (s[1:2] + s[2:3]) for w, s in zip(ws, stats)])
    acc = jnp.zeros((16, 128), F32)
    for i in range(8):
        column = jnp.sum(jnp.where(pick, ws[i], 0.0), axis=1, keepdims=True)
        acc = acc + column * r2[i, :16, :].astype(F32)
    column = jnp.sum(jnp.where(pick, total, 0.0), axis=1, keepdims=True)
    acc = acc / column
    for g in range(4):
        out_ref[:, g * 128 : (g + 1) * 128] = acc[g * 4 : g * 4 + 4, :].astype(BF)

    for i in range(5):
        exchanges[i].wait_send()
    pltpu.make_async_copy(s2.at[pl.ds(0, 7), pl.ds(0, 16)], s2.at[pl.ds(0, 7), pl.ds(0, 16)], zsend.at[0]).wait()

    @pl.when(hz != c)
    def _():
        pltpu.make_async_copy(q0, q0, zsend.at[1]).wait()

    most = q2.at[pl.ds(0, 3), 0]
    pltpu.make_async_copy(most, most, hsend).wait()
    most = q2.at[pl.ds(0, 3)]
    pltpu.make_async_copy(most, most, gsend).wait()
    most = sbuf.at[pl.ds(0, 15)]
    pltpu.make_async_copy(most, most, rsend).wait()
    most = s2.at[pl.ds(0, 7)]
    pltpu.make_async_copy(most, most, tsend.at[0]).wait()

    @pl.when(zt != z)
    def _():
        pltpu.make_async_copy(s2.at[0], s2.at[0], tsend.at[1]).wait()


def shards(queries, assignment, prefix_keys, prefix_values, suffix_keys, suffix_values, lengths):
    vmem, far = pl.BlockSpec(memory_space=pltpu.VMEM), pl.BlockSpec(memory_space=pl.ANY)
    dma = pltpu.SemaphoreType.DMA
    return pl.pallas_call(
        kernel,
        out_shape=jax.ShapeDtypeStruct(queries.shape, BF),
        in_specs=[far, far, far, far, far, far, far],
        out_specs=vmem,
        scratch_shapes=[
            pltpu.VMEM((1024, 512), BF),
            pltpu.VMEM((1024, 512), BF),
            pltpu.VMEM((8, 128, 512), BF),
            pltpu.VMEM((8, 128, 512), BF),
            pltpu.VMEM((16, 128), F32),
            pltpu.VMEM((16, 128), BF),
            pltpu.VMEM((4, 32, 128), BF),
            pltpu.VMEM((4, 4, 4, 32, 128), BF),
            pltpu.VMEM((512, 128), BF),
            pltpu.VMEM((512, 512), BF),
            pltpu.VMEM((8, 128), jnp.int32),
            pltpu.VMEM((8, 128), jnp.int32),
            pltpu.VMEM((128, 1024), F32),
            pltpu.VMEM((16, 144, 128), BF),
            pltpu.VMEM((16, 144, 128), BF),
            pltpu.VMEM((8, 32, 128), BF),
            pltpu.VMEM((8, 32, 128), BF),
            pltpu.VMEM((4, 512), BF),
            pltpu.SMEM((64,), jnp.int32),
            pltpu.SMEM((4,), jnp.int32),
            dma((3,)),
            dma((4,)),
            dma((5,)),
            dma((5,)),
            dma((2,)),
            dma((4,)),
            dma(()),
            dma((4,)),
            dma(()),
            dma((4,)),
            dma(()),
            dma(()),
            dma((2,)),
            dma(()),
        ],
        compiler_params=pltpu.CompilerParams(
            collective_id=0, has_side_effects=True, vmem_limit_bytes=60 * 1024 * 1024
        ),
        cost_estimate=pl.CostEstimate(flops=1_300_000_000, bytes_accessed=4_300_000, transcendentals=2_600_000),
    )(queries, assignment, lengths, prefix_keys, prefix_values, suffix_keys, suffix_values)


def solution(mesh):
    in_specs = (
        P("rep", "tp"),
        P(),
        P(("rep", "tp"), None),
        P(("rep", "tp"), None),
        P("rep", "tp", None),
        P("rep", "tp", None),
        P("rep"),
    )
    out_specs = P("rep", "tp")
    return jax.shard_map(shards, mesh=mesh, in_specs=in_specs, out_specs=out_specs, check_vma=False)
```

```python
import functools
import math

import jax
import jax.numpy as jnp
from jax import lax
from jax.experimental import pallas as pl
from jax.experimental.pallas import tpu as pltpu
from jax.sharding import PartitionSpec as P

MESH = pl.DeviceIdType.MESH
HD = 128
HEADS_CORE = 4
C2 = math.log2(math.e) * HD ** (-0.5)
NEG = -(2.0**100)
BF = jnp.bfloat16
F32 = jnp.float32
NT = (((1,), (1,)), ((), ()))
NN = (((1,), (0,)), ((), ()))


def dot(a, b, dims):
    return lax.dot_general(a, b, dims, preferred_element_type=F32)


def kernel(
    q_hbm, asg_hbm, len_hbm, pk, pv, sk, sv, out_ref,
    kbuf, vbuf, skbuf, svbuf, qf, q0, q1, q2, qs, perm, lens, lensall, bias, sbuf, r1, s2, r2,
    q_ref, asg_ref, len_ref, smallsem, ldsem, xsend, xrecv, zsend, zrecv, gsend, grecv, rsend, rrecv, tsend, trecv,
):
    rep, tp = lax.axis_index("rep"), lax.axis_index("tp")
    x, yh, c = rep // 4, (rep // 2) % 2, rep % 2
    z, yl = tp // 2, tp % 2
    y = yh * 2 + yl
    hz = z // 4

    def dev(x_, y_, z_, c_):
        return (x_ * 4 + (y_ // 2) * 2 + c_, z_ * 2 + y_ % 2)

    small = [
        pltpu.make_async_copy(src, dst, smallsem.at[i])
        for i, (src, dst) in enumerate(((q_hbm, q_ref), (asg_hbm, asg_ref), (len_hbm, len_ref)))
    ]
    for copy in small:
        copy.start()

    mine = pl.multiple_of(c * 512, 512)
    theirs = pl.multiple_of((1 - c) * 512, 512)
    rows2 = pl.multiple_of(c * 512, 512)
    pairs = ((pk, kbuf), (sk, skbuf), (pv, vbuf), (sv, svbuf))

    def local_dst(i):
        buf = pairs[i][1]
        return buf.at[pl.ds(rows2, 512)] if i % 2 == 0 else buf.at[pl.ds(c * 4, 4)]

    def src_of(i, cols):
        ref = pairs[i][0]
        return ref.at[:, pl.ds(cols, 512)] if i % 2 == 0 else ref.at[:, :, pl.ds(cols, 512)]

    loads = [pltpu.make_async_copy(src_of(i, mine), local_dst(i), ldsem.at[i]) for i in range(4)]
    barrier = pltpu.get_barrier_semaphore()

    def greet(x_, y_, z_, c_):
        pl.semaphore_signal(barrier, inc=1, device_id=dev(x_, y_, z_, c_), device_id_type=MESH)

    partner = dev(x, y, z, 1 - c)
    greet(x, y, z, 1 - c)
    for o in range(1, 16):
        greet((x + o // 4) % 4, (y + o % 4) % 4, z, c)
    for k in range(4):
        for cs in range(2):
            zs = 4 * c + k

            @pl.when(jnp.logical_or(zs != z, cs != c))
            def _(zs=zs, cs=cs):
                greet(x, y, zs, cs)

    for zs in range(8):

        @pl.when(jnp.logical_or(jnp.logical_or(zs != z, z % 4 != y), hz != c))
        def _(zs=zs):
            greet(x, z % 4, zs, hz)

    for copy in loads:
        copy.start()

    for copy in small:
        copy.wait()
    q = q_ref[...].astype(F32)
    for g in range(4):
        qf[g * 4 : g * 4 + 4, :] = q[:, g * 128 : (g + 1) * 128]
    q0[...] = qf[...].astype(BF)

    lane = lax.broadcasted_iota(jnp.int32, (1, 128), 1)
    lane_row = ((lane // 64) * 2 + (lane // 16) % 2) * 4 + lane % 4
    lane_g = ((lane // 32) % 2) * 4 + (lane // 4) % 4
    sub = lax.broadcasted_iota(jnp.int32, (512, 128), 0)
    sub_row = (sub // 128) * 16 + ((sub // 64) % 2) * 8 + ((sub // 16) % 2) * 4 + sub % 4
    sub_g = ((sub // 32) % 2) * 4 + (sub // 4) % 4
    sub_code = sub_row * 8 + sub_g
    for xs in range(4):
        held = jnp.zeros((1, 128), jnp.int32)
        for r in range(16):
            held = jnp.where(lane_row == r, asg_ref[xs * 16 + r], held)
        code = held * 8 + lane_g
        perm[:, xs * 128 : (xs + 1) * 128] = jnp.where(sub_code == code, 1.0, 0.0).astype(BF)

    own_len = jnp.zeros((8, 128), jnp.int32)
    sub8 = lax.broadcasted_iota(jnp.int32, (8, 128), 0)
    for s in range(4):
        own_len = jnp.where(sub8 % 4 == s, len_ref[s], own_len)
    lens[...] = own_len

    n_z = jnp.where(hz == c, 7, 8)
    n_t = jnp.where(4 * c + y == z, 7, 8)
    pl.semaphore_wait(barrier, 16 + n_z + n_t)

    def ztile(ref_z):
        return q1.at[ref_z % 4, pl.ds(pl.multiple_of(c * 16, 16), 16)]

    for o in (4, 3, 5, 2, 6, 1, 7):
        z_ = (z + o) % 8
        pltpu.make_async_remote_copy(
            src_ref=q0, dst_ref=ztile(z), send_sem=zsend.at[0], recv_sem=zrecv.at[z % 4],
            device_id=dev(x, y, z_, hz), device_id_type=MESH,
        ).start()

    @pl.when(hz == c)
    def _():
        pltpu.make_async_copy(q0, ztile(z), zrecv.at[z % 4]).start()

    @pl.when(hz != c)
    def _():
        pltpu.make_async_remote_copy(
            src_ref=q0, dst_ref=ztile(z), send_sem=zsend.at[1], recv_sem=zrecv.at[z % 4],
            device_id=partner, device_id_type=MESH,
        ).start()

    exchanges = [
        pltpu.make_async_remote_copy(
            src_ref=src_of(i, theirs), dst_ref=local_dst(i), send_sem=xsend.at[i], recv_sem=xrecv.at[i],
            device_id=partner, device_id_type=MESH,
        )
        for i in range(4)
    ]
    exchanges.append(
        pltpu.make_async_remote_copy(
            src_ref=lens, dst_ref=lensall, send_sem=xsend.at[4], recv_sem=xrecv.at[4],
            device_id=partner, device_id_type=MESH,
        )
    )
    exchanges[4].start()

    me_rows = pl.ds(pl.multiple_of((x * 4 + y) * 32, 32), 32)
    for k in range(4):
        pltpu.make_async_copy(q1.at[k], q1.at[k], zrecv.at[k]).wait()
    for i in range(4):
        k = (y + 1 + i) % 4
        pltpu.make_async_copy(q1.at[k], q2.at[k, me_rows], grecv.at[k]).start()
        for o in range(1, 16):
            y_ = (y + o % 4) % 4
            k = (y_ + 1 + i) % 4
            pltpu.make_async_remote_copy(
                src_ref=q1.at[k], dst_ref=q2.at[k, me_rows], send_sem=gsend, recv_sem=grecv.at[k],
                device_id=dev((x + o // 4) % 4, y_, z, c), device_id_type=MESH,
            ).start()

    for i in (0, 2, 1, 3):
        exchanges[i].start()

    exchanges[4].wait_recv()
    rows = lax.broadcasted_iota(jnp.int32, (128, 128), 0)
    lanes = lax.broadcasted_iota(jnp.int32, (128, 128), 1)
    lens_own = jnp.concatenate([lens[...]] * 16, axis=0)
    lens_other = jnp.concatenate([lensall[...]] * 16, axis=0)
    row_c = (rows // 16) % 2
    live = jnp.where(row_c == c, lens_own, lens_other) - tp * 128
    live = jnp.where(rows // 64 == yh, live, 0)
    row_slot = row_c * 4 + rows % 4
    for s in range(8):
        limit = jnp.where(row_slot == s, live, 0)
        bias[:, s * 128 : s * 128 + 128] = jnp.where(lanes < limit, 0.0, NEG)

    for i in range(4):
        loads[i].wait()
        exchanges[i].wait_recv()

    eye = rows == lanes
    ones = jnp.ones((1024, 128), BF)
    stat_row = lax.broadcasted_iota(jnp.int32, (16, 128), 0)

    def as_row(column):
        return jnp.sum(jnp.where(eye, column, 0.0), axis=0, keepdims=True)

    def stat_tile(top, total):
        hi = total.astype(BF).astype(F32)
        return jnp.where(stat_row == 0, top, jnp.where(stat_row == 1, hi, total - hi)).astype(BF)

    def weights(scores, top):
        return jnp.exp2(scores - top).astype(BF)

    def largest(scores):
        return jnp.max(scores, axis=1, keepdims=True)

    def head(i, _):
        k = (y + 1 + i) % 4
        cols = pl.ds(pl.multiple_of(k * 128, 128), 128)
        pltpu.make_async_copy(q2.at[k], q2.at[k], grecv.at[k]).wait()
        qs[...] = dot(perm[...], q2[k], NN).astype(BF)
        chunks = [(x + 1 + a) % 4 for a in range(4)]
        parts = [qs[pl.ds(pl.multiple_of(j * 128, 128), 128), :] for j in chunks]
        keys = kbuf[:, cols]
        values = jnp.concatenate([vbuf[:, cols], ones], axis=1)
        suffix_keys = skbuf[:, :, cols].reshape(1024, 128)
        suffix_values = jnp.concatenate([svbuf[:, :, cols].reshape(1024, 128), ones], axis=1)

        s0 = dot(jnp.concatenate(parts[:2], axis=0), keys, NT) * C2
        s1 = dot(jnp.concatenate(parts[2:], axis=0), keys, NT) * C2
        ss = dot(parts[3], suffix_keys, NT) * C2 + bias[...]
        m0 = largest(s0).astype(BF).astype(F32)
        n0 = dot(weights(s0, m0), values, NN)
        m1 = largest(s1)
        m1 = jnp.concatenate([m1[:128], jnp.maximum(m1[128:], largest(ss))], axis=0).astype(BF).astype(F32)
        n1 = dot(weights(s1, m1), values, NN)
        ns = dot(weights(ss, m1[128:]), suffix_values, NN)

        pieces = [
            (m0[:128], n0[:128]),
            (m0[128:], n0[128:]),
            (m1[:128], n1[:128]),
            (m1[128:], n1[128:] + ns),
        ]
        for a in range(4):
            m, n = pieces[a]
            slot = i * 4 + a
            sbuf[slot, :128, :] = n[:, :128].astype(BF)
            sbuf[slot, 128:, :] = stat_tile(as_row(m), as_row(n[:, 128:]))

            def send(slot=slot, j=chunks[a]):
                pltpu.make_async_remote_copy(
                    src_ref=sbuf.at[slot], dst_ref=r1.at[x * 4 + y], send_sem=rsend, recv_sem=rrecv,
                    device_id=dev(j, k, z, c), device_id_type=MESH,
                ).start()

            if a < 3:
                send()
            else:
                pl.when(i < 3)(send)
        return 0

    lax.fori_loop(0, 4, head, 0)
    pltpu.make_async_copy(sbuf.at[15], r1.at[x * 4 + y], rrecv).start()

    pltpu.make_async_copy(r1, r1, rrecv).wait()
    stats = [r1[i, 128:, :].astype(F32) for i in range(16)]
    top = functools.reduce(jnp.maximum, [s[0:1] for s in stats])
    ws = [jnp.exp2(s[0:1] - top) for s in stats]
    total = functools.reduce(jnp.add, [w * (s[1:2] + s[2:3]) for w, s in zip(ws, stats)])
    his = [w.astype(BF).astype(F32) for w in ws]
    spread = [
        jnp.concatenate([jnp.where(eye, w, 0.0).astype(BF) for w in part], axis=1)
        for part in (his, [w - h for w, h in zip(ws, his)])
    ]
    both = dot(jnp.concatenate(spread, axis=0), jnp.concatenate([r1[i, :128, :] for i in range(16)], axis=0), NN)
    flat = (both[:128] + both[128:]).astype(BF)
    stat = stat_tile(top, total)
    for d in range(8):
        s2[d, :16, :] = flat[d * 16 : d * 16 + 16, :]
        s2[d, 16:, :] = stat

    zt = 4 * c + y
    for o in range(1, 8):
        y_, c_ = (y + o // 2) % 4, (c + o % 2) % 2
        pltpu.make_async_remote_copy(
            src_ref=s2.at[y_ * 2 + c_], dst_ref=r2.at[z], send_sem=tsend.at[0], recv_sem=trecv,
            device_id=dev(x, y_, zt, c_), device_id_type=MESH,
        ).start()

    @pl.when(zt == z)
    def _():
        pltpu.make_async_copy(s2.at[y * 2 + c], r2.at[z], trecv).start()

    @pl.when(zt != z)
    def _():
        pltpu.make_async_remote_copy(
            src_ref=s2.at[y * 2 + c], dst_ref=r2.at[z], send_sem=tsend.at[1], recv_sem=trecv,
            device_id=dev(x, y, zt, c), device_id_type=MESH,
        ).start()

    pltpu.make_async_copy(r2, r2, trecv).wait()

    offset = y * 32 + c * 16
    pick = lax.broadcasted_iota(jnp.int32, (16, 128), 1) == lax.broadcasted_iota(jnp.int32, (16, 128), 0) + offset
    stats = [r2[i, 16:, :].astype(F32) for i in range(8)]
    m2 = functools.reduce(jnp.maximum, [s[0:1] for s in stats])
    ws = [jnp.exp2(s[0:1] - m2) for s in stats]
    total = functools.reduce(jnp.add, [w * (s[1:2] + s[2:3]) for w, s in zip(ws, stats)])
    acc = jnp.zeros((16, 128), F32)
    for i in range(8):
        column = jnp.sum(jnp.where(pick, ws[i], 0.0), axis=1, keepdims=True)
        acc = acc + column * r2[i, :16, :].astype(F32)
    column = jnp.sum(jnp.where(pick, total, 0.0), axis=1, keepdims=True)
    acc = acc / column
    for g in range(4):
        out_ref[:, g * 128 : (g + 1) * 128] = acc[g * 4 : g * 4 + 4, :].astype(BF)

    for i in range(5):
        exchanges[i].wait_send()
    pltpu.make_async_copy(s2.at[pl.ds(0, 7), pl.ds(0, 16)], s2.at[pl.ds(0, 7), pl.ds(0, 16)], zsend.at[0]).wait()

    @pl.when(hz != c)
    def _():
        pltpu.make_async_copy(q0, q0, zsend.at[1]).wait()

    most = q2.at[:, pl.ds(0, 480)]
    pltpu.make_async_copy(most, most, gsend).wait()
    most = sbuf.at[pl.ds(0, 15)]
    pltpu.make_async_copy(most, most, rsend).wait()
    most = s2.at[pl.ds(0, 7)]
    pltpu.make_async_copy(most, most, tsend.at[0]).wait()

    @pl.when(zt != z)
    def _():
        pltpu.make_async_copy(s2.at[0], s2.at[0], tsend.at[1]).wait()


def shards(queries, assignment, prefix_keys, prefix_values, suffix_keys, suffix_values, lengths):
    vmem, far = pl.BlockSpec(memory_space=pltpu.VMEM), pl.BlockSpec(memory_space=pl.ANY)
    dma = pltpu.SemaphoreType.DMA
    return pl.pallas_call(
        kernel,
        out_shape=jax.ShapeDtypeStruct(queries.shape, BF),
        in_specs=[far, far, far, far, far, far, far],
        out_specs=vmem,
        scratch_shapes=[
            pltpu.VMEM((1024, 512), BF),
            pltpu.VMEM((1024, 512), BF),
            pltpu.VMEM((8, 128, 512), BF),
            pltpu.VMEM((8, 128, 512), BF),
            pltpu.VMEM((16, 128), F32),
            pltpu.VMEM((16, 128), BF),
            pltpu.VMEM((4, 32, 128), BF),
            pltpu.VMEM((4, 512, 128), BF),
            pltpu.VMEM((512, 128), BF),
            pltpu.VMEM((512, 512), BF),
            pltpu.VMEM((8, 128), jnp.int32),
            pltpu.VMEM((8, 128), jnp.int32),
            pltpu.VMEM((128, 1024), F32),
            pltpu.VMEM((16, 144, 128), BF),
            pltpu.VMEM((16, 144, 128), BF),
            pltpu.VMEM((8, 32, 128), BF),
            pltpu.VMEM((8, 32, 128), BF),
            pltpu.VMEM((4, 512), BF),
            pltpu.SMEM((64,), jnp.int32),
            pltpu.SMEM((4,), jnp.int32),
            dma((3,)),
            dma((4,)),
            dma((5,)),
            dma((5,)),
            dma((2,)),
            dma((4,)),
            dma(()),
            dma((4,)),
            dma(()),
            dma(()),
            dma((2,)),
            dma(()),
        ],
        compiler_params=pltpu.CompilerParams(
            collective_id=0, has_side_effects=True, vmem_limit_bytes=60 * 1024 * 1024
        ),
        cost_estimate=pl.CostEstimate(flops=1_300_000_000, bytes_accessed=4_300_000, transcendentals=2_600_000),
    )(queries, assignment, lengths, prefix_keys, prefix_values, suffix_keys, suffix_values)


def solution(mesh):
    in_specs = (
        P("rep", "tp"),
        P(),
        P(("rep", "tp"), None),
        P(("rep", "tp"), None),
        P("rep", "tp", None),
        P("rep", "tp", None),
        P("rep"),
    )
    out_specs = P("rep", "tp")
    return jax.shard_map(shards, mesh=mesh, in_specs=in_specs, out_specs=out_specs, check_vma=False)
```

```python
import functools
import math

import jax
import jax.numpy as jnp
from jax import lax
from jax.experimental import pallas as pl
from jax.experimental.pallas import tpu as pltpu
from jax.sharding import PartitionSpec as P

MESH = pl.DeviceIdType.MESH
HD = 128
HEADS_CORE = 4
C2 = math.log2(math.e) * HD ** (-0.5)
NEG = -(2.0**100)
BF = jnp.bfloat16
F32 = jnp.float32
NT = (((1,), (1,)), ((), ()))
NN = (((1,), (0,)), ((), ()))


def dot(a, b, dims):
    return lax.dot_general(a, b, dims, preferred_element_type=F32)


def kernel(
    q_hbm, asg_hbm, len_hbm, pk, pv, sk, sv, out_ref,
    kbuf, vbuf, skbuf, svbuf, qf, q0, q1, q2, qs, perm, lens, lensall, bias, sbuf, r1, s2, r2,
    q_ref, asg_ref, len_ref, smallsem, ldsem, xsend, xrecv, zsend, zrecv, gsend, grecv, rsend, rrecv, tsend, trecv,
):
    rep, tp = lax.axis_index("rep"), lax.axis_index("tp")
    x, yh, c = rep // 4, (rep // 2) % 2, rep % 2
    z, yl = tp // 2, tp % 2
    y = yh * 2 + yl
    hz = z // 4

    def dev(x_, y_, z_, c_):
        return (x_ * 4 + (y_ // 2) * 2 + c_, z_ * 2 + y_ % 2)

    small = [
        pltpu.make_async_copy(src, dst, smallsem.at[i])
        for i, (src, dst) in enumerate(((q_hbm, q_ref), (asg_hbm, asg_ref), (len_hbm, len_ref)))
    ]
    for copy in small:
        copy.start()

    mine = pl.multiple_of(c * 512, 512)
    theirs = pl.multiple_of((1 - c) * 512, 512)
    rows2 = pl.multiple_of(c * 512, 512)
    pairs = ((pk, kbuf), (sk, skbuf), (pv, vbuf), (sv, svbuf))

    def local_dst(i):
        buf = pairs[i][1]
        return buf.at[pl.ds(rows2, 512)] if i % 2 == 0 else buf.at[pl.ds(c * 4, 4)]

    def src_of(i, cols):
        ref = pairs[i][0]
        return ref.at[:, pl.ds(cols, 512)] if i % 2 == 0 else ref.at[:, :, pl.ds(cols, 512)]

    loads = [pltpu.make_async_copy(src_of(i, mine), local_dst(i), ldsem.at[i]) for i in range(4)]
    barrier = pltpu.get_barrier_semaphore()

    def greet(x_, y_, z_, c_):
        pl.semaphore_signal(barrier, inc=1, device_id=dev(x_, y_, z_, c_), device_id_type=MESH)

    partner = dev(x, y, z, 1 - c)
    greet(x, y, z, 1 - c)
    for o in range(1, 16):
        greet((x + o // 4) % 4, (y + o % 4) % 4, z, c)
    for k in range(4):
        for cs in range(2):
            zs = 4 * c + k

            @pl.when(jnp.logical_or(zs != z, cs != c))
            def _(zs=zs, cs=cs):
                greet(x, y, zs, cs)

    for zs in range(8):

        @pl.when(jnp.logical_or(jnp.logical_or(zs != z, z % 4 != y), hz != c))
        def _(zs=zs):
            greet(x, z % 4, zs, hz)

    for copy in loads:
        copy.start()

    for copy in small:
        copy.wait()
    q = q_ref[...].astype(F32)
    for g in range(4):
        qf[g * 4 : g * 4 + 4, :] = q[:, g * 128 : (g + 1) * 128]
    q0[...] = qf[...].astype(BF)

    lane = lax.broadcasted_iota(jnp.int32, (1, 128), 1)
    lane_row = ((lane // 64) * 2 + (lane // 16) % 2) * 4 + lane % 4
    lane_g = ((lane // 32) % 2) * 4 + (lane // 4) % 4
    sub = lax.broadcasted_iota(jnp.int32, (512, 128), 0)
    sub_row = (sub // 128) * 16 + ((sub // 64) % 2) * 8 + ((sub // 16) % 2) * 4 + sub % 4
    sub_g = ((sub // 32) % 2) * 4 + (sub // 4) % 4
    sub_code = sub_row * 8 + sub_g
    for xs in range(4):
        held = jnp.zeros((1, 128), jnp.int32)
        for r in range(16):
            held = jnp.where(lane_row == r, asg_ref[xs * 16 + r], held)
        code = held * 8 + lane_g
        perm[:, xs * 128 : (xs + 1) * 128] = jnp.where(sub_code == code, 1.0, 0.0).astype(BF)

    own_len = jnp.zeros((8, 128), jnp.int32)
    sub8 = lax.broadcasted_iota(jnp.int32, (8, 128), 0)
    for s in range(4):
        own_len = jnp.where(sub8 % 4 == s, len_ref[s], own_len)
    lens[...] = own_len

    n_z = jnp.where(hz == c, 7, 8)
    n_t = jnp.where(4 * c + y == z, 7, 8)
    pl.semaphore_wait(barrier, 16 + n_z + n_t)

    def ztile(ref_z):
        return q1.at[ref_z % 4, pl.ds(pl.multiple_of(c * 16, 16), 16)]

    for o in (4, 3, 5, 2, 6, 1, 7):
        z_ = (z + o) % 8
        pltpu.make_async_remote_copy(
            src_ref=q0, dst_ref=ztile(z), send_sem=zsend.at[0], recv_sem=zrecv.at[z % 4],
            device_id=dev(x, y, z_, hz), device_id_type=MESH,
        ).start()

    @pl.when(hz == c)
    def _():
        pltpu.make_async_copy(q0, ztile(z), zrecv.at[z % 4]).start()

    @pl.when(hz != c)
    def _():
        pltpu.make_async_remote_copy(
            src_ref=q0, dst_ref=ztile(z), send_sem=zsend.at[1], recv_sem=zrecv.at[z % 4],
            device_id=partner, device_id_type=MESH,
        ).start()

    exchanges = [
        pltpu.make_async_remote_copy(
            src_ref=src_of(i, theirs), dst_ref=local_dst(i), send_sem=xsend.at[i], recv_sem=xrecv.at[i],
            device_id=partner, device_id_type=MESH,
        )
        for i in range(4)
    ]
    exchanges.append(
        pltpu.make_async_remote_copy(
            src_ref=lens, dst_ref=lensall, send_sem=xsend.at[4], recv_sem=xrecv.at[4],
            device_id=partner, device_id_type=MESH,
        )
    )
    exchanges[4].start()
    exchanges[0].start()

    me_rows = pl.ds(pl.multiple_of((x * 4 + y) * 32, 32), 32)
    for k in range(4):
        pltpu.make_async_copy(q1.at[k], q1.at[k], zrecv.at[k]).wait()
    for i in range(4):
        k = (y + 1 + i) % 4
        pltpu.make_async_copy(q1.at[k], q2.at[k, me_rows], grecv.at[k]).start()
        for o in range(1, 16):
            y_ = (y + o % 4) % 4
            k = (y_ + 1 + i) % 4
            pltpu.make_async_remote_copy(
                src_ref=q1.at[k], dst_ref=q2.at[k, me_rows], send_sem=gsend, recv_sem=grecv.at[k],
                device_id=dev((x + o // 4) % 4, y_, z, c), device_id_type=MESH,
            ).start()
        if i < 3:
            exchanges[(2, 1, 3)[i]].start()

    exchanges[4].wait_recv()
    rows = lax.broadcasted_iota(jnp.int32, (128, 128), 0)
    lanes = lax.broadcasted_iota(jnp.int32, (128, 128), 1)
    lens_own = jnp.concatenate([lens[...]] * 16, axis=0)
    lens_other = jnp.concatenate([lensall[...]] * 16, axis=0)
    row_c = (rows // 16) % 2
    live = jnp.where(row_c == c, lens_own, lens_other) - tp * 128
    live = jnp.where(rows // 64 == yh, live, 0)
    row_slot = row_c * 4 + rows % 4
    for s in range(8):
        limit = jnp.where(row_slot == s, live, 0)
        bias[:, s * 128 : s * 128 + 128] = jnp.where(lanes < limit, 0.0, NEG)

    for i in range(4):
        loads[i].wait()
        exchanges[i].wait_recv()

    eye = rows == lanes
    ones = jnp.ones((1024, 128), BF)
    stat_row = lax.broadcasted_iota(jnp.int32, (16, 128), 0)

    def as_row(column):
        return jnp.sum(jnp.where(eye, column, 0.0), axis=0, keepdims=True)

    def stat_tile(top, total):
        hi = total.astype(BF).astype(F32)
        return jnp.where(stat_row == 0, top, jnp.where(stat_row == 1, hi, total - hi)).astype(BF)

    def weights(scores, top):
        return jnp.exp2(scores - top).astype(BF)

    def largest(scores):
        return jnp.max(scores, axis=1, keepdims=True)

    def head(i, _):
        k = (y + 1 + i) % 4
        cols = pl.ds(pl.multiple_of(k * 128, 128), 128)
        pltpu.make_async_copy(q2.at[k], q2.at[k], grecv.at[k]).wait()
        qs[...] = dot(perm[...], q2[k], NN).astype(BF)
        chunks = [(x + 1 + a) % 4 for a in range(4)]
        parts = [qs[pl.ds(pl.multiple_of(j * 128, 128), 128), :] for j in chunks]
        keys = kbuf[:, cols]
        values = jnp.concatenate([vbuf[:, cols], ones], axis=1)
        suffix_keys = skbuf[:, :, cols].reshape(1024, 128)
        suffix_values = jnp.concatenate([svbuf[:, :, cols].reshape(1024, 128), ones], axis=1)

        s0 = dot(jnp.concatenate(parts[:2], axis=0), keys, NT) * C2
        s1 = dot(jnp.concatenate(parts[2:], axis=0), keys, NT) * C2
        ss = dot(parts[3], suffix_keys, NT) * C2 + bias[...]
        m0 = largest(s0).astype(BF).astype(F32)
        n0 = dot(weights(s0, m0), values, NN)
        m1 = largest(s1)
        m1 = jnp.concatenate([m1[:128], jnp.maximum(m1[128:], largest(ss))], axis=0).astype(BF).astype(F32)
        n1 = dot(weights(s1, m1), values, NN)
        ns = dot(weights(ss, m1[128:]), suffix_values, NN)

        pieces = [
            (m0[:128], n0[:128]),
            (m0[128:], n0[128:]),
            (m1[:128], n1[:128]),
            (m1[128:], n1[128:] + ns),
        ]
        for a in range(4):
            m, n = pieces[a]
            slot = i * 4 + a
            sbuf[slot, :128, :] = n[:, :128].astype(BF)
            sbuf[slot, 128:, :] = stat_tile(as_row(m), as_row(n[:, 128:]))

            def send(slot=slot, j=chunks[a]):
                pltpu.make_async_remote_copy(
                    src_ref=sbuf.at[slot], dst_ref=r1.at[x * 4 + y], send_sem=rsend, recv_sem=rrecv,
                    device_id=dev(j, k, z, c), device_id_type=MESH,
                ).start()

            if a < 3:
                send()
            else:
                pl.when(i < 3)(send)
        return 0

    lax.fori_loop(0, 4, head, 0)
    pltpu.make_async_copy(sbuf.at[15], r1.at[x * 4 + y], rrecv).start()

    pltpu.make_async_copy(r1, r1, rrecv).wait()
    stats = [r1[i, 128:, :].astype(F32) for i in range(16)]
    top = functools.reduce(jnp.maximum, [s[0:1] for s in stats])
    ws = [jnp.exp2(s[0:1] - top) for s in stats]
    total = functools.reduce(jnp.add, [w * (s[1:2] + s[2:3]) for w, s in zip(ws, stats)])
    his = [w.astype(BF).astype(F32) for w in ws]
    spread = [
        jnp.concatenate([jnp.where(eye, w, 0.0).astype(BF) for w in part], axis=1)
        for part in (his, [w - h for w, h in zip(ws, his)])
    ]
    both = dot(jnp.concatenate(spread, axis=0), jnp.concatenate([r1[i, :128, :] for i in range(16)], axis=0), NN)
    flat = (both[:128] + both[128:]).astype(BF)
    stat = stat_tile(top, total)
    for d in range(8):
        s2[d, :16, :] = flat[d * 16 : d * 16 + 16, :]
        s2[d, 16:, :] = stat

    zt = 4 * c + y
    for o in range(1, 8):
        y_, c_ = (y + o // 2) % 4, (c + o % 2) % 2
        pltpu.make_async_remote_copy(
            src_ref=s2.at[y_ * 2 + c_], dst_ref=r2.at[z], send_sem=tsend.at[0], recv_sem=trecv,
            device_id=dev(x, y_, zt, c_), device_id_type=MESH,
        ).start()

    @pl.when(zt == z)
    def _():
        pltpu.make_async_copy(s2.at[y * 2 + c], r2.at[z], trecv).start()

    @pl.when(zt != z)
    def _():
        pltpu.make_async_remote_copy(
            src_ref=s2.at[y * 2 + c], dst_ref=r2.at[z], send_sem=tsend.at[1], recv_sem=trecv,
            device_id=dev(x, y, zt, c), device_id_type=MESH,
        ).start()

    pltpu.make_async_copy(r2, r2, trecv).wait()

    offset = y * 32 + c * 16
    pick = lax.broadcasted_iota(jnp.int32, (16, 128), 1) == lax.broadcasted_iota(jnp.int32, (16, 128), 0) + offset
    stats = [r2[i, 16:, :].astype(F32) for i in range(8)]
    m2 = functools.reduce(jnp.maximum, [s[0:1] for s in stats])
    ws = [jnp.exp2(s[0:1] - m2) for s in stats]
    total = functools.reduce(jnp.add, [w * (s[1:2] + s[2:3]) for w, s in zip(ws, stats)])
    acc = jnp.zeros((16, 128), F32)
    for i in range(8):
        column = jnp.sum(jnp.where(pick, ws[i], 0.0), axis=1, keepdims=True)
        acc = acc + column * r2[i, :16, :].astype(F32)
    column = jnp.sum(jnp.where(pick, total, 0.0), axis=1, keepdims=True)
    acc = acc / column
    for g in range(4):
        out_ref[:, g * 128 : (g + 1) * 128] = acc[g * 4 : g * 4 + 4, :].astype(BF)

    for i in range(5):
        exchanges[i].wait_send()
    pltpu.make_async_copy(s2.at[pl.ds(0, 7), pl.ds(0, 16)], s2.at[pl.ds(0, 7), pl.ds(0, 16)], zsend.at[0]).wait()

    @pl.when(hz != c)
    def _():
        pltpu.make_async_copy(q0, q0, zsend.at[1]).wait()

    most = q2.at[:, pl.ds(0, 480)]
    pltpu.make_async_copy(most, most, gsend).wait()
    most = sbuf.at[pl.ds(0, 15)]
    pltpu.make_async_copy(most, most, rsend).wait()
    most = s2.at[pl.ds(0, 7)]
    pltpu.make_async_copy(most, most, tsend.at[0]).wait()

    @pl.when(zt != z)
    def _():
        pltpu.make_async_copy(s2.at[0], s2.at[0], tsend.at[1]).wait()


def shards(queries, assignment, prefix_keys, prefix_values, suffix_keys, suffix_values, lengths):
    vmem, far = pl.BlockSpec(memory_space=pltpu.VMEM), pl.BlockSpec(memory_space=pl.ANY)
    dma = pltpu.SemaphoreType.DMA
    return pl.pallas_call(
        kernel,
        out_shape=jax.ShapeDtypeStruct(queries.shape, BF),
        in_specs=[far, far, far, far, far, far, far],
        out_specs=vmem,
        scratch_shapes=[
            pltpu.VMEM((1024, 512), BF),
            pltpu.VMEM((1024, 512), BF),
            pltpu.VMEM((8, 128, 512), BF),
            pltpu.VMEM((8, 128, 512), BF),
            pltpu.VMEM((16, 128), F32),
            pltpu.VMEM((16, 128), BF),
            pltpu.VMEM((4, 32, 128), BF),
            pltpu.VMEM((4, 512, 128), BF),
            pltpu.VMEM((512, 128), BF),
            pltpu.VMEM((512, 512), BF),
            pltpu.VMEM((8, 128), jnp.int32),
            pltpu.VMEM((8, 128), jnp.int32),
            pltpu.VMEM((128, 1024), F32),
            pltpu.VMEM((16, 144, 128), BF),
            pltpu.VMEM((16, 144, 128), BF),
            pltpu.VMEM((8, 32, 128), BF),
            pltpu.VMEM((8, 32, 128), BF),
            pltpu.VMEM((4, 512), BF),
            pltpu.SMEM((64,), jnp.int32),
            pltpu.SMEM((4,), jnp.int32),
            dma((3,)),
            dma((4,)),
            dma((5,)),
            dma((5,)),
            dma((2,)),
            dma((4,)),
            dma(()),
            dma((4,)),
            dma(()),
            dma(()),
            dma((2,)),
            dma(()),
        ],
        compiler_params=pltpu.CompilerParams(
            collective_id=0, has_side_effects=True, vmem_limit_bytes=60 * 1024 * 1024
        ),
        cost_estimate=pl.CostEstimate(flops=1_300_000_000, bytes_accessed=4_300_000, transcendentals=2_600_000),
    )(queries, assignment, lengths, prefix_keys, prefix_values, suffix_keys, suffix_values)


def solution(mesh):
    in_specs = (
        P("rep", "tp"),
        P(),
        P(("rep", "tp"), None),
        P(("rep", "tp"), None),
        P("rep", "tp", None),
        P("rep", "tp", None),
        P("rep"),
    )
    out_specs = P("rep", "tp")
    return jax.shard_map(shards, mesh=mesh, in_specs=in_specs, out_specs=out_specs, check_vma=False)
```

```python
import functools
import math

import jax
import jax.numpy as jnp
from jax import lax
from jax.experimental import pallas as pl
from jax.experimental.pallas import tpu as pltpu
from jax.sharding import PartitionSpec as P

MESH = pl.DeviceIdType.MESH
HD = 128
HEADS_CORE = 4
C2 = math.log2(math.e) * HD ** (-0.5)
NEG = -(2.0**100)
BF = jnp.bfloat16
F32 = jnp.float32
NN = (((1,), (0,)), ((), ()))


def dot(a, b, dims):
    return lax.dot_general(a, b, dims, preferred_element_type=F32)


def kernel(
    q_hbm, asg_hbm, len_hbm, pk, pv, sk, sv, out_ref,
    kbuf, vbuf, skbuf, svbuf, kt, skt, qf, q0, q1, q2, qs, perm, lens, lensall, bias, sbuf, r1, s2, r2,
    q_ref, asg_ref, len_ref, smallsem, ldsem, xsend, xrecv, zsend, zrecv, gsend, grecv, rsend, rrecv, tsend, trecv,
):
    rep, tp = lax.axis_index("rep"), lax.axis_index("tp")
    x, yh, c = rep // 4, (rep // 2) % 2, rep % 2
    z, yl = tp // 2, tp % 2
    y = yh * 2 + yl
    hz = z // 4

    def dev(x_, y_, z_, c_):
        return (x_ * 4 + (y_ // 2) * 2 + c_, z_ * 2 + y_ % 2)

    small = [
        pltpu.make_async_copy(src, dst, smallsem.at[i])
        for i, (src, dst) in enumerate(((q_hbm, q_ref), (asg_hbm, asg_ref), (len_hbm, len_ref)))
    ]
    for copy in small:
        copy.start()

    mine = pl.multiple_of(c * 512, 512)
    theirs = pl.multiple_of((1 - c) * 512, 512)
    rows2 = pl.multiple_of(c * 512, 512)
    pairs = ((pk, kbuf), (sk, skbuf), (pv, vbuf), (sv, svbuf))

    def local_dst(i):
        buf = pairs[i][1]
        return buf.at[pl.ds(rows2, 512)] if i % 2 == 0 else buf.at[pl.ds(c * 4, 4)]

    def src_of(i, cols):
        ref = pairs[i][0]
        return ref.at[:, pl.ds(cols, 512)] if i % 2 == 0 else ref.at[:, :, pl.ds(cols, 512)]

    loads = [pltpu.make_async_copy(src_of(i, mine), local_dst(i), ldsem.at[i]) for i in range(4)]
    barrier = pltpu.get_barrier_semaphore()

    def greet(x_, y_, z_, c_):
        pl.semaphore_signal(barrier, inc=1, device_id=dev(x_, y_, z_, c_), device_id_type=MESH)

    partner = dev(x, y, z, 1 - c)
    greet(x, y, z, 1 - c)
    for o in range(1, 16):
        greet((x + o // 4) % 4, (y + o % 4) % 4, z, c)
    for k in range(4):
        for cs in range(2):
            zs = 4 * c + k

            @pl.when(jnp.logical_or(zs != z, cs != c))
            def _(zs=zs, cs=cs):
                greet(x, y, zs, cs)

    for zs in range(8):

        @pl.when(jnp.logical_or(jnp.logical_or(zs != z, z % 4 != y), hz != c))
        def _(zs=zs):
            greet(x, z % 4, zs, hz)

    for copy in loads:
        copy.start()

    for copy in small:
        copy.wait()
    q = q_ref[...].astype(F32)
    for g in range(4):
        qf[g * 4 : g * 4 + 4, :] = q[:, g * 128 : (g + 1) * 128]
    q0[...] = qf[...].astype(BF)

    lane = lax.broadcasted_iota(jnp.int32, (1, 128), 1)
    lane_row = ((lane // 64) * 2 + (lane // 16) % 2) * 4 + lane % 4
    lane_g = ((lane // 32) % 2) * 4 + (lane // 4) % 4
    sub = lax.broadcasted_iota(jnp.int32, (512, 128), 0)
    sub_row = (sub // 128) * 16 + ((sub // 64) % 2) * 8 + ((sub // 16) % 2) * 4 + sub % 4
    sub_g = ((sub // 32) % 2) * 4 + (sub // 4) % 4
    sub_code = sub_row * 8 + sub_g
    for xs in range(4):
        held = jnp.zeros((1, 128), jnp.int32)
        for r in range(16):
            held = jnp.where(lane_row == r, asg_ref[xs * 16 + r], held)
        code = held * 8 + lane_g
        perm[:, xs * 128 : (xs + 1) * 128] = jnp.where(sub_code == code, 1.0, 0.0).astype(BF)

    own_len = jnp.zeros((8, 128), jnp.int32)
    sub8 = lax.broadcasted_iota(jnp.int32, (8, 128), 0)
    for s in range(4):
        own_len = jnp.where(sub8 % 4 == s, len_ref[s], own_len)
    lens[...] = own_len

    n_z = jnp.where(hz == c, 7, 8)
    n_t = jnp.where(4 * c + y == z, 7, 8)
    pl.semaphore_wait(barrier, 16 + n_z + n_t)

    def ztile(ref_z):
        return q1.at[ref_z % 4, pl.ds(pl.multiple_of(c * 16, 16), 16)]

    for o in (4, 3, 5, 2, 6, 1, 7):
        z_ = (z + o) % 8
        pltpu.make_async_remote_copy(
            src_ref=q0, dst_ref=ztile(z), send_sem=zsend.at[0], recv_sem=zrecv.at[z % 4],
            device_id=dev(x, y, z_, hz), device_id_type=MESH,
        ).start()

    @pl.when(hz == c)
    def _():
        pltpu.make_async_copy(q0, ztile(z), zrecv.at[z % 4]).start()

    @pl.when(hz != c)
    def _():
        pltpu.make_async_remote_copy(
            src_ref=q0, dst_ref=ztile(z), send_sem=zsend.at[1], recv_sem=zrecv.at[z % 4],
            device_id=partner, device_id_type=MESH,
        ).start()

    exchanges = [
        pltpu.make_async_remote_copy(
            src_ref=src_of(i, theirs), dst_ref=local_dst(i), send_sem=xsend.at[i], recv_sem=xrecv.at[i],
            device_id=partner, device_id_type=MESH,
        )
        for i in range(4)
    ]
    exchanges.append(
        pltpu.make_async_remote_copy(
            src_ref=lens, dst_ref=lensall, send_sem=xsend.at[4], recv_sem=xrecv.at[4],
            device_id=partner, device_id_type=MESH,
        )
    )
    exchanges[4].start()
    exchanges[0].start()

    me_rows = pl.ds(pl.multiple_of((x * 4 + y) * 32, 32), 32)
    for k in range(4):
        pltpu.make_async_copy(q1.at[k], q1.at[k], zrecv.at[k]).wait()
    for i in range(4):
        k = (y + 1 + i) % 4
        pltpu.make_async_copy(q1.at[k], q2.at[k, me_rows], grecv.at[k]).start()
        for o in range(1, 16):
            y_ = (y + o % 4) % 4
            k = (y_ + 1 + i) % 4
            pltpu.make_async_remote_copy(
                src_ref=q1.at[k], dst_ref=q2.at[k, me_rows], send_sem=gsend, recv_sem=grecv.at[k],
                device_id=dev((x + o // 4) % 4, y_, z, c), device_id_type=MESH,
            ).start()
        if i < 3:
            exchanges[(2, 1, 3)[i]].start()

    exchanges[4].wait_recv()
    rows = lax.broadcasted_iota(jnp.int32, (128, 128), 0)
    lanes = lax.broadcasted_iota(jnp.int32, (128, 128), 1)
    lens_own = jnp.concatenate([lens[...]] * 16, axis=0)
    lens_other = jnp.concatenate([lensall[...]] * 16, axis=0)
    row_c = (rows // 16) % 2
    live = jnp.where(row_c == c, lens_own, lens_other) - tp * 128
    live = jnp.where(rows // 64 == yh, live, 0)
    row_slot = row_c * 4 + rows % 4
    for s in range(8):
        limit = jnp.where(row_slot == s, live, 0)
        bias[:, s * 128 : s * 128 + 128] = jnp.where(lanes < limit, 0.0, NEG)

    def across(buffer, flipped, rows):
        def one(k, _):
            cols = pl.ds(pl.multiple_of(k * 128, 128), 128)
            flipped[k] = rows(buffer, cols).T
            return 0

        lax.fori_loop(0, 4, one, 0)

    for i in range(4):
        loads[i].wait()
    exchanges[0].wait_recv()
    across(kbuf, kt, lambda ref, cols: ref[:, cols])
    exchanges[1].wait_recv()
    across(skbuf, skt, lambda ref, cols: ref[:, :, cols].reshape(1024, 128))
    exchanges[2].wait_recv()
    exchanges[3].wait_recv()

    eye = rows == lanes
    ones = jnp.ones((1024, 128), BF)
    stat_row = lax.broadcasted_iota(jnp.int32, (16, 128), 0)

    def as_row(column):
        return jnp.sum(jnp.where(eye, column, 0.0), axis=0, keepdims=True)

    def stat_tile(top, total):
        hi = total.astype(BF).astype(F32)
        return jnp.where(stat_row == 0, top, jnp.where(stat_row == 1, hi, total - hi)).astype(BF)

    def weights(scores, top):
        return jnp.exp2(scores - top).astype(BF)

    def largest(scores):
        return jnp.max(scores, axis=1, keepdims=True)

    def head(i, _):
        k = (y + 1 + i) % 4
        cols = pl.ds(pl.multiple_of(k * 128, 128), 128)
        pltpu.make_async_copy(q2.at[k], q2.at[k], grecv.at[k]).wait()
        qs[...] = dot(perm[...], q2[k], NN).astype(BF)
        chunks = [(x + 1 + a) % 4 for a in range(4)]
        parts = [qs[pl.ds(pl.multiple_of(j * 128, 128), 128), :] for j in chunks]
        keys = kt[k]
        values = jnp.concatenate([vbuf[:, cols], ones], axis=1)
        suffix_values = jnp.concatenate([svbuf[:, :, cols].reshape(1024, 128), ones], axis=1)

        s0 = dot(jnp.concatenate(parts[:2], axis=0), keys, NN) * C2
        s1 = dot(jnp.concatenate(parts[2:], axis=0), keys, NN) * C2
        ss = dot(parts[3], skt[k], NN) * C2 + bias[...]
        m0 = largest(s0).astype(BF).astype(F32)
        n0 = dot(weights(s0, m0), values, NN)
        m1 = largest(s1)
        m1 = jnp.concatenate([m1[:128], jnp.maximum(m1[128:], largest(ss))], axis=0).astype(BF).astype(F32)
        n1 = dot(weights(s1, m1), values, NN)
        ns = dot(weights(ss, m1[128:]), suffix_values, NN)

        pieces = [
            (m0[:128], n0[:128]),
            (m0[128:], n0[128:]),
            (m1[:128], n1[:128]),
            (m1[128:], n1[128:] + ns),
        ]
        for a in range(4):
            m, n = pieces[a]
            slot = i * 4 + a
            sbuf[slot, :128, :] = n[:, :128].astype(BF)
            sbuf[slot, 128:, :] = stat_tile(as_row(m), as_row(n[:, 128:]))

            def send(slot=slot, j=chunks[a]):
                pltpu.make_async_remote_copy(
                    src_ref=sbuf.at[slot], dst_ref=r1.at[x * 4 + y], send_sem=rsend, recv_sem=rrecv,
                    device_id=dev(j, k, z, c), device_id_type=MESH,
                ).start()

            if a < 3:
                send()
            else:
                pl.when(i < 3)(send)
        return 0

    lax.fori_loop(0, 4, head, 0)
    pltpu.make_async_copy(sbuf.at[15], r1.at[x * 4 + y], rrecv).start()

    pltpu.make_async_copy(r1, r1, rrecv).wait()
    stats = [r1[i, 128:, :].astype(F32) for i in range(16)]
    top = functools.reduce(jnp.maximum, [s[0:1] for s in stats])
    ws = [jnp.exp2(s[0:1] - top) for s in stats]
    total = functools.reduce(jnp.add, [w * (s[1:2] + s[2:3]) for w, s in zip(ws, stats)])
    his = [w.astype(BF).astype(F32) for w in ws]
    spread = [
        jnp.concatenate([jnp.where(eye, w, 0.0).astype(BF) for w in part], axis=1)
        for part in (his, [w - h for w, h in zip(ws, his)])
    ]
    both = dot(jnp.concatenate(spread, axis=0), jnp.concatenate([r1[i, :128, :] for i in range(16)], axis=0), NN)
    flat = (both[:128] + both[128:]).astype(BF)
    stat = stat_tile(top, total)
    for d in range(8):
        s2[d, :16, :] = flat[d * 16 : d * 16 + 16, :]
        s2[d, 16:, :] = stat

    zt = 4 * c + y
    for o in range(1, 8):
        y_, c_ = (y + o // 2) % 4, (c + o % 2) % 2
        pltpu.make_async_remote_copy(
            src_ref=s2.at[y_ * 2 + c_], dst_ref=r2.at[z], send_sem=tsend.at[0], recv_sem=trecv,
            device_id=dev(x, y_, zt, c_), device_id_type=MESH,
        ).start()

    @pl.when(zt == z)
    def _():
        pltpu.make_async_copy(s2.at[y * 2 + c], r2.at[z], trecv).start()

    @pl.when(zt != z)
    def _():
        pltpu.make_async_remote_copy(
            src_ref=s2.at[y * 2 + c], dst_ref=r2.at[z], send_sem=tsend.at[1], recv_sem=trecv,
            device_id=dev(x, y, zt, c), device_id_type=MESH,
        ).start()

    pltpu.make_async_copy(r2, r2, trecv).wait()

    offset = y * 32 + c * 16
    pick = lax.broadcasted_iota(jnp.int32, (16, 128), 1) == lax.broadcasted_iota(jnp.int32, (16, 128), 0) + offset
    stats = [r2[i, 16:, :].astype(F32) for i in range(8)]
    m2 = functools.reduce(jnp.maximum, [s[0:1] for s in stats])
    ws = [jnp.exp2(s[0:1] - m2) for s in stats]
    total = functools.reduce(jnp.add, [w * (s[1:2] + s[2:3]) for w, s in zip(ws, stats)])
    acc = jnp.zeros((16, 128), F32)
    for i in range(8):
        column = jnp.sum(jnp.where(pick, ws[i], 0.0), axis=1, keepdims=True)
        acc = acc + column * r2[i, :16, :].astype(F32)
    column = jnp.sum(jnp.where(pick, total, 0.0), axis=1, keepdims=True)
    acc = acc / column
    for g in range(4):
        out_ref[:, g * 128 : (g + 1) * 128] = acc[g * 4 : g * 4 + 4, :].astype(BF)

    for i in range(5):
        exchanges[i].wait_send()
    pltpu.make_async_copy(s2.at[pl.ds(0, 7), pl.ds(0, 16)], s2.at[pl.ds(0, 7), pl.ds(0, 16)], zsend.at[0]).wait()

    @pl.when(hz != c)
    def _():
        pltpu.make_async_copy(q0, q0, zsend.at[1]).wait()

    most = q2.at[:, pl.ds(0, 480)]
    pltpu.make_async_copy(most, most, gsend).wait()
    most = sbuf.at[pl.ds(0, 15)]
    pltpu.make_async_copy(most, most, rsend).wait()
    most = s2.at[pl.ds(0, 7)]
    pltpu.make_async_copy(most, most, tsend.at[0]).wait()

    @pl.when(zt != z)
    def _():
        pltpu.make_async_copy(s2.at[0], s2.at[0], tsend.at[1]).wait()


def shards(queries, assignment, prefix_keys, prefix_values, suffix_keys, suffix_values, lengths):
    vmem, far = pl.BlockSpec(memory_space=pltpu.VMEM), pl.BlockSpec(memory_space=pl.ANY)
    dma = pltpu.SemaphoreType.DMA
    return pl.pallas_call(
        kernel,
        out_shape=jax.ShapeDtypeStruct(queries.shape, BF),
        in_specs=[far, far, far, far, far, far, far],
        out_specs=vmem,
        scratch_shapes=[
            pltpu.VMEM((1024, 512), BF),
            pltpu.VMEM((1024, 512), BF),
            pltpu.VMEM((8, 128, 512), BF),
            pltpu.VMEM((8, 128, 512), BF),
            pltpu.VMEM((4, 128, 1024), BF),
            pltpu.VMEM((4, 128, 1024), BF),
            pltpu.VMEM((16, 128), F32),
            pltpu.VMEM((16, 128), BF),
            pltpu.VMEM((4, 32, 128), BF),
            pltpu.VMEM((4, 512, 128), BF),
            pltpu.VMEM((512, 128), BF),
            pltpu.VMEM((512, 512), BF),
            pltpu.VMEM((8, 128), jnp.int32),
            pltpu.VMEM((8, 128), jnp.int32),
            pltpu.VMEM((128, 1024), F32),
            pltpu.VMEM((16, 144, 128), BF),
            pltpu.VMEM((16, 144, 128), BF),
            pltpu.VMEM((8, 32, 128), BF),
            pltpu.VMEM((8, 32, 128), BF),
            pltpu.VMEM((4, 512), BF),
            pltpu.SMEM((64,), jnp.int32),
            pltpu.SMEM((4,), jnp.int32),
            dma((3,)),
            dma((4,)),
            dma((5,)),
            dma((5,)),
            dma((2,)),
            dma((4,)),
            dma(()),
            dma((4,)),
            dma(()),
            dma(()),
            dma((2,)),
            dma(()),
        ],
        compiler_params=pltpu.CompilerParams(
            collective_id=0, has_side_effects=True, vmem_limit_bytes=60 * 1024 * 1024
        ),
        cost_estimate=pl.CostEstimate(flops=1_300_000_000, bytes_accessed=4_300_000, transcendentals=2_600_000),
    )(queries, assignment, lengths, prefix_keys, prefix_values, suffix_keys, suffix_values)


def solution(mesh):
    in_specs = (
        P("rep", "tp"),
        P(),
        P(("rep", "tp"), None),
        P(("rep", "tp"), None),
        P("rep", "tp", None),
        P("rep", "tp", None),
        P("rep"),
    )
    out_specs = P("rep", "tp")
    return jax.shard_map(shards, mesh=mesh, in_specs=in_specs, out_specs=out_specs, check_vma=False)
```

```python
import functools
import math

import jax
import jax.numpy as jnp
from jax import lax
from jax.experimental import pallas as pl
from jax.experimental.pallas import tpu as pltpu
from jax.sharding import PartitionSpec as P

MESH = pl.DeviceIdType.MESH
HD = 128
HEADS_CORE = 4
C2 = math.log2(math.e) * HD ** (-0.5)
NEG = -(2.0**100)
BF = jnp.bfloat16
F32 = jnp.float32
NT = (((1,), (1,)), ((), ()))
NN = (((1,), (0,)), ((), ()))


def dot(a, b, dims):
    return lax.dot_general(a, b, dims, preferred_element_type=F32)


def kernel(
    q_hbm, asg_hbm, len_hbm, pk, pv, sk, sv, out_ref,
    kbuf, vbuf, skbuf, svbuf, qf, q0, q1, q2, qs, perm, lens, lensall, bias, sbuf, r1, s2, r2,
    q_ref, asg_ref, len_ref, smallsem, ldsem, xsend, xrecv, zsend, zrecv, gsend, grecv, rsend, rrecv, tsend, trecv,
):
    rep, tp = lax.axis_index("rep"), lax.axis_index("tp")
    x, yh, c = rep // 4, (rep // 2) % 2, rep % 2
    z, yl = tp // 2, tp % 2
    y = yh * 2 + yl
    hz = z // 4

    def dev(x_, y_, z_, c_):
        return (x_ * 4 + (y_ // 2) * 2 + c_, z_ * 2 + y_ % 2)

    small = [
        pltpu.make_async_copy(src, dst, smallsem.at[i])
        for i, (src, dst) in enumerate(((q_hbm, q_ref), (asg_hbm, asg_ref), (len_hbm, len_ref)))
    ]
    for copy in small:
        copy.start()

    mine = pl.multiple_of(c * 512, 512)
    theirs = pl.multiple_of((1 - c) * 512, 512)
    pairs = ((pk, kbuf), (pv, vbuf), (sk, skbuf), (sv, svbuf))

    def share(t, k, first, slot):
        src, dst = pairs[t]
        cols = pl.ds(pl.multiple_of(first + k * 128, 128), 128)
        if t < 2:
            return src.at[:, cols], dst.at[k, pl.ds(pl.multiple_of(slot * 512, 512), 512)]
        return src.at[:, :, cols], dst.at[k, pl.ds(slot * 4, 4)]

    loads = []
    for i in range(4):
        for t in range(4):
            src, dst = share(t, (y + 1 + i) % 4, mine, c)
            loads.append(pltpu.make_async_copy(src, dst, ldsem.at[i * 4 + t]))

    barrier = pltpu.get_barrier_semaphore()

    def greet(x_, y_, z_, c_):
        pl.semaphore_signal(barrier, inc=1, device_id=dev(x_, y_, z_, c_), device_id_type=MESH)

    partner = dev(x, y, z, 1 - c)
    greet(x, y, z, 1 - c)
    for o in range(1, 16):
        greet((x + o // 4) % 4, (y + o % 4) % 4, z, c)
    for k in range(4):
        for cs in range(2):
            zs = 4 * c + k

            @pl.when(jnp.logical_or(zs != z, cs != c))
            def _(zs=zs, cs=cs):
                greet(x, y, zs, cs)

    for zs in range(8):

        @pl.when(jnp.logical_or(jnp.logical_or(zs != z, z % 4 != y), hz != c))
        def _(zs=zs):
            greet(x, z % 4, zs, hz)

    for copy in loads:
        copy.start()

    for copy in small:
        copy.wait()
    q = q_ref[...].astype(F32)
    for g in range(4):
        qf[g * 4 : g * 4 + 4, :] = q[:, g * 128 : (g + 1) * 128]
    q0[...] = qf[...].astype(BF)

    lane = lax.broadcasted_iota(jnp.int32, (1, 128), 1)
    lane_row = ((lane // 64) * 2 + (lane // 16) % 2) * 4 + lane % 4
    lane_g = ((lane // 32) % 2) * 4 + (lane // 4) % 4
    sub = lax.broadcasted_iota(jnp.int32, (512, 128), 0)
    sub_row = (sub // 128) * 16 + ((sub // 64) % 2) * 8 + ((sub // 16) % 2) * 4 + sub % 4
    sub_g = ((sub // 32) % 2) * 4 + (sub // 4) % 4
    sub_code = sub_row * 8 + sub_g
    for xs in range(4):
        held = jnp.zeros((1, 128), jnp.int32)
        for r in range(16):
            held = jnp.where(lane_row == r, asg_ref[xs * 16 + r], held)
        code = held * 8 + lane_g
        perm[:, xs * 128 : (xs + 1) * 128] = jnp.where(sub_code == code, 1.0, 0.0).astype(BF)

    own_len = jnp.zeros((8, 128), jnp.int32)
    sub8 = lax.broadcasted_iota(jnp.int32, (8, 128), 0)
    for s in range(4):
        own_len = jnp.where(sub8 % 4 == s, len_ref[s], own_len)
    lens[...] = own_len

    n_z = jnp.where(hz == c, 7, 8)
    n_t = jnp.where(4 * c + y == z, 7, 8)
    pl.semaphore_wait(barrier, 16 + n_z + n_t)

    def ztile(ref_z):
        return q1.at[ref_z % 4, pl.ds(pl.multiple_of(c * 16, 16), 16)]

    for o in (4, 3, 5, 2, 6, 1, 7):
        z_ = (z + o) % 8
        pltpu.make_async_remote_copy(
            src_ref=q0, dst_ref=ztile(z), send_sem=zsend.at[0], recv_sem=zrecv.at[z % 4],
            device_id=dev(x, y, z_, hz), device_id_type=MESH,
        ).start()

    @pl.when(hz == c)
    def _():
        pltpu.make_async_copy(q0, ztile(z), zrecv.at[z % 4]).start()

    @pl.when(hz != c)
    def _():
        pltpu.make_async_remote_copy(
            src_ref=q0, dst_ref=ztile(z), send_sem=zsend.at[1], recv_sem=zrecv.at[z % 4],
            device_id=partner, device_id_type=MESH,
        ).start()

    exchanges = []
    for i in range(4):
        for t in range(4):
            src, dst = share(t, (y + 1 + i) % 4, theirs, c)
            exchanges.append(
                pltpu.make_async_remote_copy(
                    src_ref=src, dst_ref=dst, send_sem=xsend.at[i * 4 + t], recv_sem=xrecv.at[i * 4 + t],
                    device_id=partner, device_id_type=MESH,
                )
            )
    exchanges.append(
        pltpu.make_async_remote_copy(
            src_ref=lens, dst_ref=lensall, send_sem=xsend.at[16], recv_sem=xrecv.at[16],
            device_id=partner, device_id_type=MESH,
        )
    )
    exchanges[16].start()
    for t in range(4):
        exchanges[t].start()

    me_rows = pl.ds(pl.multiple_of((x * 4 + y) * 32, 32), 32)
    for k in range(4):
        pltpu.make_async_copy(q1.at[k], q1.at[k], zrecv.at[k]).wait()
    for i in range(4):
        k = (y + 1 + i) % 4
        pltpu.make_async_copy(q1.at[k], q2.at[k, me_rows], grecv.at[k]).start()
        for o in range(1, 16):
            y_ = (y + o % 4) % 4
            k = (y_ + 1 + i) % 4
            pltpu.make_async_remote_copy(
                src_ref=q1.at[k], dst_ref=q2.at[k, me_rows], send_sem=gsend, recv_sem=grecv.at[k],
                device_id=dev((x + o // 4) % 4, y_, z, c), device_id_type=MESH,
            ).start()
        if i < 3:
            for t in range(4):
                exchanges[i * 4 + 4 + t].start()

    exchanges[16].wait_recv()
    rows = lax.broadcasted_iota(jnp.int32, (128, 128), 0)
    lanes = lax.broadcasted_iota(jnp.int32, (128, 128), 1)
    lens_own = jnp.concatenate([lens[...]] * 16, axis=0)
    lens_other = jnp.concatenate([lensall[...]] * 16, axis=0)
    row_c = (rows // 16) % 2
    live = jnp.where(row_c == c, lens_own, lens_other) - tp * 128
    live = jnp.where(rows // 64 == yh, live, 0)
    row_slot = row_c * 4 + rows % 4
    for s in range(8):
        limit = jnp.where(row_slot == s, live, 0)
        bias[:, s * 128 : s * 128 + 128] = jnp.where(lanes < limit, 0.0, NEG)

    eye = rows == lanes
    ones = jnp.ones((1024, 128), BF)
    stat_row = lax.broadcasted_iota(jnp.int32, (16, 128), 0)

    def as_row(column):
        return jnp.sum(jnp.where(eye, column, 0.0), axis=0, keepdims=True)

    def stat_tile(top, total):
        hi = total.astype(BF).astype(F32)
        return jnp.where(stat_row == 0, top, jnp.where(stat_row == 1, hi, total - hi)).astype(BF)

    def weights(scores, top):
        return jnp.exp2(scores - top).astype(BF)

    def largest(scores):
        return jnp.max(scores, axis=1, keepdims=True)

    def head(i, _):
        k = (y + 1 + i) % 4
        for t in range(4):
            src, dst = share(t, k, mine, c)
            pltpu.make_async_copy(src, dst, ldsem.at[i * 4 + t]).wait()
            pltpu.make_async_copy(dst, dst, xrecv.at[i * 4 + t]).wait()
        pltpu.make_async_copy(q2.at[k], q2.at[k], grecv.at[k]).wait()
        qs[...] = dot(perm[...], q2[k], NN).astype(BF)
        chunks = [(x + 1 + a) % 4 for a in range(4)]
        parts = [qs[pl.ds(pl.multiple_of(j * 128, 128), 128), :] for j in chunks]
        keys = kbuf[k]
        values = jnp.concatenate([vbuf[k], ones], axis=1)
        suffix_keys = skbuf[k].reshape(1024, 128)
        suffix_values = jnp.concatenate([svbuf[k].reshape(1024, 128), ones], axis=1)

        s0 = dot(jnp.concatenate(parts[:2], axis=0), keys, NT) * C2
        s1 = dot(jnp.concatenate(parts[2:], axis=0), keys, NT) * C2
        ss = dot(parts[3], suffix_keys, NT) * C2 + bias[...]
        m0 = largest(s0).astype(BF).astype(F32)
        n0 = dot(weights(s0, m0), values, NN)
        m1 = largest(s1)
        m1 = jnp.concatenate([m1[:128], jnp.maximum(m1[128:], largest(ss))], axis=0).astype(BF).astype(F32)
        n1 = dot(weights(s1, m1), values, NN)
        ns = dot(weights(ss, m1[128:]), suffix_values, NN)

        pieces = [
            (m0[:128], n0[:128]),
            (m0[128:], n0[128:]),
            (m1[:128], n1[:128]),
            (m1[128:], n1[128:] + ns),
        ]
        for a in range(4):
            m, n = pieces[a]
            slot = i * 4 + a
            sbuf[slot, :128, :] = n[:, :128].astype(BF)
            sbuf[slot, 128:, :] = stat_tile(as_row(m), as_row(n[:, 128:]))

            def send(slot=slot, j=chunks[a]):
                pltpu.make_async_remote_copy(
                    src_ref=sbuf.at[slot], dst_ref=r1.at[x * 4 + y], send_sem=rsend, recv_sem=rrecv,
                    device_id=dev(j, k, z, c), device_id_type=MESH,
                ).start()

            if a < 3:
                send()
            else:
                pl.when(i < 3)(send)
        return 0

    lax.fori_loop(0, 4, head, 0)
    pltpu.make_async_copy(sbuf.at[15], r1.at[x * 4 + y], rrecv).start()

    pltpu.make_async_copy(r1, r1, rrecv).wait()
    stats = [r1[i, 128:, :].astype(F32) for i in range(16)]
    top = functools.reduce(jnp.maximum, [s[0:1] for s in stats])
    ws = [jnp.exp2(s[0:1] - top) for s in stats]
    total = functools.reduce(jnp.add, [w * (s[1:2] + s[2:3]) for w, s in zip(ws, stats)])
    his = [w.astype(BF).astype(F32) for w in ws]
    spread = [
        jnp.concatenate([jnp.where(eye, w, 0.0).astype(BF) for w in part], axis=1)
        for part in (his, [w - h for w, h in zip(ws, his)])
    ]
    both = dot(jnp.concatenate(spread, axis=0), jnp.concatenate([r1[i, :128, :] for i in range(16)], axis=0), NN)
    flat = (both[:128] + both[128:]).astype(BF)
    stat = stat_tile(top, total)
    for d in range(8):
        s2[d, :16, :] = flat[d * 16 : d * 16 + 16, :]
        s2[d, 16:, :] = stat

    zt = 4 * c + y
    for o in range(1, 8):
        y_, c_ = (y + o // 2) % 4, (c + o % 2) % 2
        pltpu.make_async_remote_copy(
            src_ref=s2.at[y_ * 2 + c_], dst_ref=r2.at[z], send_sem=tsend.at[0], recv_sem=trecv,
            device_id=dev(x, y_, zt, c_), device_id_type=MESH,
        ).start()

    @pl.when(zt == z)
    def _():
        pltpu.make_async_copy(s2.at[y * 2 + c], r2.at[z], trecv).start()

    @pl.when(zt != z)
    def _():
        pltpu.make_async_remote_copy(
            src_ref=s2.at[y * 2 + c], dst_ref=r2.at[z], send_sem=tsend.at[1], recv_sem=trecv,
            device_id=dev(x, y, zt, c), device_id_type=MESH,
        ).start()

    pltpu.make_async_copy(r2, r2, trecv).wait()

    offset = y * 32 + c * 16
    pick = lax.broadcasted_iota(jnp.int32, (16, 128), 1) == lax.broadcasted_iota(jnp.int32, (16, 128), 0) + offset
    stats = [r2[i, 16:, :].astype(F32) for i in range(8)]
    m2 = functools.reduce(jnp.maximum, [s[0:1] for s in stats])
    ws = [jnp.exp2(s[0:1] - m2) for s in stats]
    total = functools.reduce(jnp.add, [w * (s[1:2] + s[2:3]) for w, s in zip(ws, stats)])
    acc = jnp.zeros((16, 128), F32)
    for i in range(8):
        column = jnp.sum(jnp.where(pick, ws[i], 0.0), axis=1, keepdims=True)
        acc = acc + column * r2[i, :16, :].astype(F32)
    column = jnp.sum(jnp.where(pick, total, 0.0), axis=1, keepdims=True)
    acc = acc / column
    for g in range(4):
        out_ref[:, g * 128 : (g + 1) * 128] = acc[g * 4 : g * 4 + 4, :].astype(BF)

    for copy in exchanges:
        copy.wait_send()
    pltpu.make_async_copy(s2.at[pl.ds(0, 7), pl.ds(0, 16)], s2.at[pl.ds(0, 7), pl.ds(0, 16)], zsend.at[0]).wait()

    @pl.when(hz != c)
    def _():
        pltpu.make_async_copy(q0, q0, zsend.at[1]).wait()

    most = q2.at[:, pl.ds(0, 480)]
    pltpu.make_async_copy(most, most, gsend).wait()
    most = sbuf.at[pl.ds(0, 15)]
    pltpu.make_async_copy(most, most, rsend).wait()
    most = s2.at[pl.ds(0, 7)]
    pltpu.make_async_copy(most, most, tsend.at[0]).wait()

    @pl.when(zt != z)
    def _():
        pltpu.make_async_copy(s2.at[0], s2.at[0], tsend.at[1]).wait()


def shards(queries, assignment, prefix_keys, prefix_values, suffix_keys, suffix_values, lengths):
    vmem, far = pl.BlockSpec(memory_space=pltpu.VMEM), pl.BlockSpec(memory_space=pl.ANY)
    dma = pltpu.SemaphoreType.DMA
    return pl.pallas_call(
        kernel,
        out_shape=jax.ShapeDtypeStruct(queries.shape, BF),
        in_specs=[far, far, far, far, far, far, far],
        out_specs=vmem,
        scratch_shapes=[
            pltpu.VMEM((4, 1024, 128), BF),
            pltpu.VMEM((4, 1024, 128), BF),
            pltpu.VMEM((4, 8, 128, 128), BF),
            pltpu.VMEM((4, 8, 128, 128), BF),
            pltpu.VMEM((16, 128), F32),
            pltpu.VMEM((16, 128), BF),
            pltpu.VMEM((4, 32, 128), BF),
            pltpu.VMEM((4, 512, 128), BF),
            pltpu.VMEM((512, 128), BF),
            pltpu.VMEM((512, 512), BF),
            pltpu.VMEM((8, 128), jnp.int32),
            pltpu.VMEM((8, 128), jnp.int32),
            pltpu.VMEM((128, 1024), F32),
            pltpu.VMEM((16, 144, 128), BF),
            pltpu.VMEM((16, 144, 128), BF),
            pltpu.VMEM((8, 32, 128), BF),
            pltpu.VMEM((8, 32, 128), BF),
            pltpu.VMEM((4, 512), BF),
            pltpu.SMEM((64,), jnp.int32),
            pltpu.SMEM((4,), jnp.int32),
            dma((3,)),
            dma((16,)),
            dma((17,)),
            dma((17,)),
            dma((2,)),
            dma((4,)),
            dma(()),
            dma((4,)),
            dma(()),
            dma(()),
            dma((2,)),
            dma(()),
        ],
        compiler_params=pltpu.CompilerParams(
            collective_id=0, has_side_effects=True, vmem_limit_bytes=60 * 1024 * 1024
        ),
        cost_estimate=pl.CostEstimate(flops=1_300_000_000, bytes_accessed=4_300_000, transcendentals=2_600_000),
    )(queries, assignment, lengths, prefix_keys, prefix_values, suffix_keys, suffix_values)


def solution(mesh):
    in_specs = (
        P("rep", "tp"),
        P(),
        P(("rep", "tp"), None),
        P(("rep", "tp"), None),
        P("rep", "tp", None),
        P("rep", "tp", None),
        P("rep"),
    )
    out_specs = P("rep", "tp")
    return jax.shard_map(shards, mesh=mesh, in_specs=in_specs, out_specs=out_specs, check_vma=False)
```

```python
import functools
import math

import jax
import jax.numpy as jnp
from jax import lax
from jax.experimental import pallas as pl
from jax.experimental.pallas import tpu as pltpu
from jax.sharding import PartitionSpec as P

MESH = pl.DeviceIdType.MESH
HD = 128
HEADS_CORE = 4
C2 = math.log2(math.e) * HD ** (-0.5)
NEG = -(2.0**100)
BF = jnp.bfloat16
F32 = jnp.float32
NT = (((1,), (1,)), ((), ()))
NN = (((1,), (0,)), ((), ()))


def dot(a, b, dims):
    return lax.dot_general(a, b, dims, preferred_element_type=F32)


def kernel(
    q_hbm, asg_hbm, len_hbm, pk, pv, sk, sv, out_ref,
    kbuf, vbuf, skbuf, svbuf, qf, q0, q1, q2, qs, perm, lens, lensall, bias, sbuf, r1, s2, r2,
    q_ref, asg_ref, len_ref, smallsem, ldsem, xsend, xrecv, zsend, zrecv, gsend, grecv, rsend, rrecv, tsend, trecv,
):
    rep, tp = lax.axis_index("rep"), lax.axis_index("tp")
    x, yh, c = rep // 4, (rep // 2) % 2, rep % 2
    z, yl = tp // 2, tp % 2
    y = yh * 2 + yl
    hz = z // 4

    def dev(x_, y_, z_, c_):
        return (x_ * 4 + (y_ // 2) * 2 + c_, z_ * 2 + y_ % 2)

    small = [
        pltpu.make_async_copy(src, dst, smallsem.at[i])
        for i, (src, dst) in enumerate(((q_hbm, q_ref), (asg_hbm, asg_ref), (len_hbm, len_ref)))
    ]
    for copy in small:
        copy.start()

    mine = pl.multiple_of(c * 512, 512)
    theirs = pl.multiple_of((1 - c) * 512, 512)
    rows2 = pl.multiple_of(c * 512, 512)
    pairs = ((pk, kbuf), (sk, skbuf), (pv, vbuf), (sv, svbuf))

    def local_dst(i):
        buf = pairs[i][1]
        return buf.at[pl.ds(rows2, 512)] if i % 2 == 0 else buf.at[pl.ds(c * 4, 4)]

    def src_of(i, cols):
        ref = pairs[i][0]
        return ref.at[:, pl.ds(cols, 512)] if i % 2 == 0 else ref.at[:, :, pl.ds(cols, 512)]

    loads = [pltpu.make_async_copy(src_of(i, mine), local_dst(i), ldsem.at[i]) for i in range(4)]
    barrier = pltpu.get_barrier_semaphore()

    def greet(x_, y_, z_, c_):
        pl.semaphore_signal(barrier, inc=1, device_id=dev(x_, y_, z_, c_), device_id_type=MESH)

    partner = dev(x, y, z, 1 - c)
    greet(x, y, z, 1 - c)
    for o in range(1, 16):
        greet((x + o // 4) % 4, (y + o % 4) % 4, z, c)
    for k in range(4):
        for cs in range(2):
            zs = 4 * c + k

            @pl.when(jnp.logical_or(zs != z, cs != c))
            def _(zs=zs, cs=cs):
                greet(x, y, zs, cs)

    for zs in range(8):

        @pl.when(jnp.logical_or(jnp.logical_or(zs != z, z % 4 != y), hz != c))
        def _(zs=zs):
            greet(x, z % 4, zs, hz)

    for copy in loads:
        copy.start()

    for copy in small:
        copy.wait()
    q = q_ref[...].astype(F32)
    for g in range(4):
        qf[g * 4 : g * 4 + 4, :] = q[:, g * 128 : (g + 1) * 128]
    q0[...] = qf[...].astype(BF)

    lane = lax.broadcasted_iota(jnp.int32, (1, 128), 1)
    lane_row = ((lane // 64) * 2 + (lane // 16) % 2) * 4 + lane % 4
    lane_g = ((lane // 32) % 2) * 4 + (lane // 4) % 4
    sub = lax.broadcasted_iota(jnp.int32, (512, 128), 0)
    sub_row = (sub // 128) * 16 + ((sub // 64) % 2) * 8 + ((sub // 16) % 2) * 4 + sub % 4
    sub_g = ((sub // 32) % 2) * 4 + (sub // 4) % 4
    sub_code = sub_row * 8 + sub_g
    for xs in range(4):
        held = jnp.zeros((1, 128), jnp.int32)
        for r in range(16):
            held = jnp.where(lane_row == r, asg_ref[xs * 16 + r], held)
        code = held * 8 + lane_g
        perm[:, xs * 128 : (xs + 1) * 128] = jnp.where(sub_code == code, 1.0, 0.0).astype(BF)

    own_len = jnp.zeros((8, 128), jnp.int32)
    sub8 = lax.broadcasted_iota(jnp.int32, (8, 128), 0)
    for s in range(4):
        own_len = jnp.where(sub8 % 4 == s, len_ref[s], own_len)
    lens[...] = own_len

    n_z = jnp.where(hz == c, 7, 8)
    n_t = jnp.where(4 * c + y == z, 7, 8)
    pl.semaphore_wait(barrier, 16 + n_z + n_t)

    def ztile(ref_z):
        return q1.at[ref_z % 4, pl.ds(pl.multiple_of(c * 16, 16), 16)]

    for o in (4, 3, 5, 2, 6, 1, 7):
        z_ = (z + o) % 8
        pltpu.make_async_remote_copy(
            src_ref=q0, dst_ref=ztile(z), send_sem=zsend.at[0], recv_sem=zrecv.at[z % 4],
            device_id=dev(x, y, z_, hz), device_id_type=MESH,
        ).start()

    @pl.when(hz == c)
    def _():
        pltpu.make_async_copy(q0, ztile(z), zrecv.at[z % 4]).start()

    @pl.when(hz != c)
    def _():
        pltpu.make_async_remote_copy(
            src_ref=q0, dst_ref=ztile(z), send_sem=zsend.at[1], recv_sem=zrecv.at[z % 4],
            device_id=partner, device_id_type=MESH,
        ).start()

    exchanges = [
        pltpu.make_async_remote_copy(
            src_ref=src_of(i, theirs), dst_ref=local_dst(i), send_sem=xsend.at[i], recv_sem=xrecv.at[i],
            device_id=partner, device_id_type=MESH,
        )
        for i in range(4)
    ]
    exchanges.append(
        pltpu.make_async_remote_copy(
            src_ref=lens, dst_ref=lensall, send_sem=xsend.at[4], recv_sem=xrecv.at[4],
            device_id=partner, device_id_type=MESH,
        )
    )
    exchanges[4].start()
    exchanges[0].start()

    me_rows = pl.ds(pl.multiple_of((x * 4 + y) * 32, 32), 32)
    for k in range(4):
        pltpu.make_async_copy(q1.at[k], q1.at[k], zrecv.at[k]).wait()
    for i in range(4):
        k = (y + 1 + i) % 4
        pltpu.make_async_copy(q1.at[k], q2.at[k, me_rows], grecv.at[k]).start()
        for o in range(1, 16):
            y_ = (y + o % 4) % 4
            k = (y_ + 1 + i) % 4
            pltpu.make_async_remote_copy(
                src_ref=q1.at[k], dst_ref=q2.at[k, me_rows], send_sem=gsend, recv_sem=grecv.at[k],
                device_id=dev((x + o // 4) % 4, y_, z, c), device_id_type=MESH,
            ).start()
        if i < 3:
            exchanges[(2, 1, 3)[i]].start()

    exchanges[4].wait_recv()
    rows = lax.broadcasted_iota(jnp.int32, (64, 128), 0)
    lanes = lax.broadcasted_iota(jnp.int32, (64, 128), 1)
    lens_own = jnp.concatenate([lens[...]] * 8, axis=0)
    lens_other = jnp.concatenate([lensall[...]] * 8, axis=0)
    row_c = (rows // 16) % 2
    live = jnp.where(row_c == c, lens_own, lens_other) - tp * 128
    row_slot = row_c * 4 + rows % 4
    for s in range(8):
        limit = jnp.where(row_slot == s, live, 0)
        bias[:, s * 128 : s * 128 + 128] = jnp.where(lanes < limit, 0.0, NEG)

    for i in range(4):
        loads[i].wait()
        exchanges[i].wait_recv()

    square = (128, 128)
    eye = lax.broadcasted_iota(jnp.int32, square, 0) == lax.broadcasted_iota(jnp.int32, square, 1)
    ones = jnp.ones((1024, 128), BF)
    stat_row = lax.broadcasted_iota(jnp.int32, (16, 128), 0)

    def as_row(column):
        return jnp.sum(jnp.where(eye, column, 0.0), axis=0, keepdims=True)

    def stat_tile(top, total):
        hi = total.astype(BF).astype(F32)
        return jnp.where(stat_row == 0, top, jnp.where(stat_row == 1, hi, total - hi)).astype(BF)

    def weights(scores, top):
        return jnp.exp2(scores - top).astype(BF)

    def largest(scores):
        return jnp.max(scores, axis=1, keepdims=True)

    def two_heads(i, _):
        ks = [(y + 1 + 2 * i + h) % 4 for h in range(2)]
        for k in ks:
            pltpu.make_async_copy(q2.at[k], q2.at[k], grecv.at[k]).wait()
        qs[...] = dot(perm[...], jnp.concatenate([q2[k] for k in ks], axis=1), NN).astype(BF)
        chunks = [(x + 1 + a) % 4 for a in range(4)]
        places = [pl.ds(pl.multiple_of(j * 128, 128), 128) for j in chunks]
        own = pl.ds(pl.multiple_of(x * 128 + yh * 64, 64), 64)

        scores = []
        for h, k in enumerate(ks):
            at = slice(h * 128, h * 128 + 128)
            cols = pl.ds(pl.multiple_of(k * 128, 128), 128)
            parts = [qs[place, at] for place in places]
            keys = kbuf[:, cols]
            s0 = dot(jnp.concatenate(parts[:2], axis=0), keys, NT) * C2
            s1 = dot(jnp.concatenate(parts[2:], axis=0), keys, NT) * C2
            ss = dot(qs[own, at], skbuf[:, :, cols].reshape(1024, 128), NT) * C2 + bias[...]
            scores.append((s0, s1, ss))

        for h, k in enumerate(ks):
            cols = pl.ds(pl.multiple_of(k * 128, 128), 128)
            values = jnp.concatenate([vbuf[:, cols], ones], axis=1)
            suffix_values = jnp.concatenate([svbuf[:, :, cols].reshape(1024, 128), ones], axis=1)
            s0, s1, ss = scores[h]
            m0 = largest(s0).astype(BF).astype(F32)
            n0 = dot(weights(s0, m0), values, NN)
            m1, ms = largest(s1), largest(ss)
            low = jnp.full((64, 1), NEG, F32)
            ms = jnp.concatenate([jnp.where(yh == 0, ms, low), jnp.where(yh == 0, low, ms)], axis=0)
            m1 = jnp.concatenate([m1[:128], jnp.maximum(m1[128:], ms)], axis=0).astype(BF).astype(F32)
            n1 = dot(weights(s1, m1), values, NN)
            ns = dot(weights(ss, jnp.where(yh == 0, m1[128:192], m1[192:])), suffix_values, NN)
            ns = jnp.concatenate([jnp.where(yh == 0, ns, 0.0), jnp.where(yh == 0, 0.0, ns)], axis=0)

            pieces = [
                (m0[:128], n0[:128]),
                (m0[128:], n0[128:]),
                (m1[:128], n1[:128]),
                (m1[128:], n1[128:] + ns),
            ]
            for a in range(4):
                m, n = pieces[a]
                slot = i * 8 + h * 4 + a
                sbuf[slot, :128, :] = n[:, :128].astype(BF)
                sbuf[slot, 128:, :] = stat_tile(as_row(m), as_row(n[:, 128:]))

                def send(slot=slot, j=chunks[a], k=k):
                    pltpu.make_async_remote_copy(
                        src_ref=sbuf.at[slot], dst_ref=r1.at[x * 4 + y], send_sem=rsend, recv_sem=rrecv,
                        device_id=dev(j, k, z, c), device_id_type=MESH,
                    ).start()

                if h < 1 or a < 3:
                    send()
                else:
                    pl.when(i < 1)(send)
        return 0

    lax.fori_loop(0, 2, two_heads, 0)
    pltpu.make_async_copy(sbuf.at[15], r1.at[x * 4 + y], rrecv).start()

    pltpu.make_async_copy(r1, r1, rrecv).wait()
    stats = [r1[i, 128:, :].astype(F32) for i in range(16)]
    top = functools.reduce(jnp.maximum, [s[0:1] for s in stats])
    ws = [jnp.exp2(s[0:1] - top) for s in stats]
    total = functools.reduce(jnp.add, [w * (s[1:2] + s[2:3]) for w, s in zip(ws, stats)])
    his = [w.astype(BF).astype(F32) for w in ws]
    spread = [
        jnp.concatenate([jnp.where(eye, w, 0.0).astype(BF) for w in part], axis=1)
        for part in (his, [w - h for w, h in zip(ws, his)])
    ]
    both = dot(jnp.concatenate(spread, axis=0), jnp.concatenate([r1[i, :128, :] for i in range(16)], axis=0), NN)
    flat = (both[:128] + both[128:]).astype(BF)
    stat = stat_tile(top, total)
    for d in range(8):
        s2[d, :16, :] = flat[d * 16 : d * 16 + 16, :]
        s2[d, 16:, :] = stat

    zt = 4 * c + y
    for o in range(1, 8):
        y_, c_ = (y + o // 2) % 4, (c + o % 2) % 2
        pltpu.make_async_remote_copy(
            src_ref=s2.at[y_ * 2 + c_], dst_ref=r2.at[z], send_sem=tsend.at[0], recv_sem=trecv,
            device_id=dev(x, y_, zt, c_), device_id_type=MESH,
        ).start()

    @pl.when(zt == z)
    def _():
        pltpu.make_async_copy(s2.at[y * 2 + c], r2.at[z], trecv).start()

    @pl.when(zt != z)
    def _():
        pltpu.make_async_remote_copy(
            src_ref=s2.at[y * 2 + c], dst_ref=r2.at[z], send_sem=tsend.at[1], recv_sem=trecv,
            device_id=dev(x, y, zt, c), device_id_type=MESH,
        ).start()

    pltpu.make_async_copy(r2, r2, trecv).wait()

    offset = y * 32 + c * 16
    pick = lax.broadcasted_iota(jnp.int32, (16, 128), 1) == lax.broadcasted_iota(jnp.int32, (16, 128), 0) + offset
    stats = [r2[i, 16:, :].astype(F32) for i in range(8)]
    m2 = functools.reduce(jnp.maximum, [s[0:1] for s in stats])
    ws = [jnp.exp2(s[0:1] - m2) for s in stats]
    total = functools.reduce(jnp.add, [w * (s[1:2] + s[2:3]) for w, s in zip(ws, stats)])
    acc = jnp.zeros((16, 128), F32)
    for i in range(8):
        column = jnp.sum(jnp.where(pick, ws[i], 0.0), axis=1, keepdims=True)
        acc = acc + column * r2[i, :16, :].astype(F32)
    column = jnp.sum(jnp.where(pick, total, 0.0), axis=1, keepdims=True)
    acc = acc / column
    for g in range(4):
        out_ref[:, g * 128 : (g + 1) * 128] = acc[g * 4 : g * 4 + 4, :].astype(BF)

    for i in range(5):
        exchanges[i].wait_send()
    pltpu.make_async_copy(s2.at[pl.ds(0, 7), pl.ds(0, 16)], s2.at[pl.ds(0, 7), pl.ds(0, 16)], zsend.at[0]).wait()

    @pl.when(hz != c)
    def _():
        pltpu.make_async_copy(q0, q0, zsend.at[1]).wait()

    most = q2.at[:, pl.ds(0, 480)]
    pltpu.make_async_copy(most, most, gsend).wait()
    most = sbuf.at[pl.ds(0, 15)]
    pltpu.make_async_copy(most, most, rsend).wait()
    most = s2.at[pl.ds(0, 7)]
    pltpu.make_async_copy(most, most, tsend.at[0]).wait()

    @pl.when(zt != z)
    def _():
        pltpu.make_async_copy(s2.at[0], s2.at[0], tsend.at[1]).wait()


def shards(queries, assignment, prefix_keys, prefix_values, suffix_keys, suffix_values, lengths):
    vmem, far = pl.BlockSpec(memory_space=pltpu.VMEM), pl.BlockSpec(memory_space=pl.ANY)
    dma = pltpu.SemaphoreType.DMA
    return pl.pallas_call(
        kernel,
        out_shape=jax.ShapeDtypeStruct(queries.shape, BF),
        in_specs=[far, far, far, far, far, far, far],
        out_specs=vmem,
        scratch_shapes=[
            pltpu.VMEM((1024, 512), BF),
            pltpu.VMEM((1024, 512), BF),
            pltpu.VMEM((8, 128, 512), BF),
            pltpu.VMEM((8, 128, 512), BF),
            pltpu.VMEM((16, 128), F32),
            pltpu.VMEM((16, 128), BF),
            pltpu.VMEM((4, 32, 128), BF),
            pltpu.VMEM((4, 512, 128), BF),
            pltpu.VMEM((512, 256), BF),
            pltpu.VMEM((512, 512), BF),
            pltpu.VMEM((8, 128), jnp.int32),
            pltpu.VMEM((8, 128), jnp.int32),
            pltpu.VMEM((64, 1024), F32),
            pltpu.VMEM((16, 144, 128), BF),
            pltpu.VMEM((16, 144, 128), BF),
            pltpu.VMEM((8, 32, 128), BF),
            pltpu.VMEM((8, 32, 128), BF),
            pltpu.VMEM((4, 512), BF),
            pltpu.SMEM((64,), jnp.int32),
            pltpu.SMEM((4,), jnp.int32),
            dma((3,)),
            dma((4,)),
            dma((5,)),
            dma((5,)),
            dma((2,)),
            dma((4,)),
            dma(()),
            dma((4,)),
            dma(()),
            dma(()),
            dma((2,)),
            dma(()),
        ],
        compiler_params=pltpu.CompilerParams(
            collective_id=0, has_side_effects=True, vmem_limit_bytes=60 * 1024 * 1024
        ),
        cost_estimate=pl.CostEstimate(flops=1_300_000_000, bytes_accessed=4_300_000, transcendentals=2_600_000),
    )(queries, assignment, lengths, prefix_keys, prefix_values, suffix_keys, suffix_values)


def solution(mesh):
    in_specs = (
        P("rep", "tp"),
        P(),
        P(("rep", "tp"), None),
        P(("rep", "tp"), None),
        P("rep", "tp", None),
        P("rep", "tp", None),
        P("rep"),
    )
    out_specs = P("rep", "tp")
    return jax.shard_map(shards, mesh=mesh, in_specs=in_specs, out_specs=out_specs, check_vma=False)
```

```python
import functools
import math

import jax
import jax.numpy as jnp
from jax import lax
from jax.experimental import pallas as pl
from jax.experimental.pallas import tpu as pltpu
from jax.sharding import PartitionSpec as P

MESH = pl.DeviceIdType.MESH
HD = 128
HEADS_CORE = 4
C2 = math.log2(math.e) * HD ** (-0.5)
NEG = -(2.0**100)
BF = jnp.bfloat16
F32 = jnp.float32
NT = (((1,), (1,)), ((), ()))
NN = (((1,), (0,)), ((), ()))


def dot(a, b, dims):
    return lax.dot_general(a, b, dims, preferred_element_type=F32)


def kernel(
    q_hbm, asg_hbm, len_hbm, pk, pv, sk, sv, out_ref,
    kbuf, vbuf, skbuf, svbuf, qf, q0, q1, q2, qs, qx, perm, bias, sbuf, cross, r1, s2, r2,
    q_ref, asg_ref, len_ref, smallsem, ldsem, xsend, xrecv, zsend, zrecv, gsend, grecv, rsend, rrecv, csend, qxsend, qxrecv, tsend, trecv,
):
    rep, tp = lax.axis_index("rep"), lax.axis_index("tp")
    x, yh, c = rep // 4, (rep // 2) % 2, rep % 2
    z, yl = tp // 2, tp % 2
    y = yh * 2 + yl
    hz = z // 4

    def dev(x_, y_, z_, c_):
        return (x_ * 4 + (y_ // 2) * 2 + c_, z_ * 2 + y_ % 2)

    small = [
        pltpu.make_async_copy(src, dst, smallsem.at[i])
        for i, (src, dst) in enumerate(((q_hbm, q_ref), (asg_hbm, asg_ref), (len_hbm, len_ref)))
    ]
    for copy in small:
        copy.start()

    mine = pl.multiple_of(c * 512, 512)
    theirs = pl.multiple_of((1 - c) * 512, 512)
    here = pl.ds(mine, 512)
    loads = [
        pltpu.make_async_copy(pk.at[:, here], kbuf.at[here], ldsem.at[0]),
        pltpu.make_async_copy(pv.at[:, here], vbuf.at[here], ldsem.at[1]),
        pltpu.make_async_copy(sk, skbuf, ldsem.at[2]),
        pltpu.make_async_copy(sv, svbuf, ldsem.at[3]),
    ]

    barrier = pltpu.get_barrier_semaphore()

    def greet(x_, y_, z_, c_):
        pl.semaphore_signal(barrier, inc=1, device_id=dev(x_, y_, z_, c_), device_id_type=MESH)

    partner = dev(x, y, z, 1 - c)
    greet(x, y, z, 1 - c)
    for o in range(1, 4):
        greet(x, (y + o) % 4, z, 1 - c)
    for o in range(1, 16):
        greet((x + o // 4) % 4, (y + o % 4) % 4, z, c)
    for k in range(4):
        for cs in range(2):
            zs = 4 * c + k

            @pl.when(jnp.logical_or(zs != z, cs != c))
            def _(zs=zs, cs=cs):
                greet(x, y, zs, cs)

    for zs in range(8):

        @pl.when(jnp.logical_or(jnp.logical_or(zs != z, z % 4 != y), hz != c))
        def _(zs=zs):
            greet(x, z % 4, zs, hz)

    for copy in loads:
        copy.start()

    for copy in small:
        copy.wait()
    q = q_ref[...].astype(F32)
    for g in range(4):
        qf[g * 4 : g * 4 + 4, :] = q[:, g * 128 : (g + 1) * 128]
    q0[...] = qf[...].astype(BF)

    lane = lax.broadcasted_iota(jnp.int32, (1, 128), 1)
    lane_row = ((lane // 64) * 2 + (lane // 16) % 2) * 4 + lane % 4
    lane_g = ((lane // 32) % 2) * 4 + (lane // 4) % 4
    sub = lax.broadcasted_iota(jnp.int32, (512, 128), 0)
    sub_row = (sub // 128) * 16 + ((sub // 64) % 2) * 8 + ((sub // 16) % 2) * 4 + sub % 4
    sub_g = ((sub // 32) % 2) * 4 + (sub // 4) % 4
    sub_code = sub_row * 8 + sub_g
    for xs in range(4):
        held = jnp.zeros((1, 128), jnp.int32)
        for r in range(16):
            held = jnp.where(lane_row == r, asg_ref[xs * 16 + r], held)
        code = held * 8 + lane_g
        perm[:, xs * 128 : (xs + 1) * 128] = jnp.where(sub_code == code, 1.0, 0.0).astype(BF)

    rows = lax.broadcasted_iota(jnp.int32, (64, 128), 0)
    lanes = lax.broadcasted_iota(jnp.int32, (64, 128), 1)
    for s in range(4):
        limit = jnp.where(jnp.logical_and((rows // 16) % 2 == c, rows % 4 == s), len_ref[s] - tp * 128, 0)
        bias[:, s * 128 : s * 128 + 128] = jnp.where(lanes < limit, 0.0, NEG)

    n_z = jnp.where(hz == c, 7, 8)
    n_t = jnp.where(4 * c + y == z, 7, 8)
    pl.semaphore_wait(barrier, 19 + n_z + n_t)

    def ztile(ref_z):
        return q1.at[ref_z % 4, pl.ds(pl.multiple_of(c * 16, 16), 16)]

    for o in (4, 3, 5, 2, 6, 1, 7):
        z_ = (z + o) % 8
        pltpu.make_async_remote_copy(
            src_ref=q0, dst_ref=ztile(z), send_sem=zsend.at[0], recv_sem=zrecv.at[z % 4],
            device_id=dev(x, y, z_, hz), device_id_type=MESH,
        ).start()

    @pl.when(hz == c)
    def _():
        pltpu.make_async_copy(q0, ztile(z), zrecv.at[z % 4]).start()

    @pl.when(hz != c)
    def _():
        pltpu.make_async_remote_copy(
            src_ref=q0, dst_ref=ztile(z), send_sem=zsend.at[1], recv_sem=zrecv.at[z % 4],
            device_id=partner, device_id_type=MESH,
        ).start()

    exchanges = [
        pltpu.make_async_remote_copy(
            src_ref=src.at[:, pl.ds(theirs, 512)], dst_ref=dst.at[here], send_sem=xsend.at[i], recv_sem=xrecv.at[i],
            device_id=partner, device_id_type=MESH,
        )
        for i, (src, dst) in enumerate(((pk, kbuf), (pv, vbuf)))
    ]
    exchanges[0].start()

    me_rows = pl.ds(pl.multiple_of((x * 4 + y) * 32, 32), 32)
    for k in range(4):
        pltpu.make_async_copy(q1.at[k], q1.at[k], zrecv.at[k]).wait()
    for i in range(4):
        k = (y + 1 + i) % 4
        pltpu.make_async_copy(q1.at[k], q2.at[k, me_rows], grecv.at[k]).start()
        for o in range(1, 16):
            y_ = (y + o % 4) % 4
            k = (y_ + 1 + i) % 4
            pltpu.make_async_remote_copy(
                src_ref=q1.at[k], dst_ref=q2.at[k, me_rows], send_sem=gsend, recv_sem=grecv.at[k],
                device_id=dev((x + o // 4) % 4, y_, z, c), device_id_type=MESH,
            ).start()
        if i == 0:
            exchanges[1].start()

    def clear(slot, _):
        cross[slot, :128, :] = jnp.zeros((128, 128), BF)
        return 0

    lax.fori_loop(0, 4, clear, 0)
    for i in range(4):
        loads[i].wait()
    for i in range(2):
        exchanges[i].wait_recv()

    square = (128, 128)
    eye = lax.broadcasted_iota(jnp.int32, square, 0) == lax.broadcasted_iota(jnp.int32, square, 1)
    ones = jnp.ones((1024, 128), BF)
    stat_row = lax.broadcasted_iota(jnp.int32, (16, 128), 0)

    def as_row(column):
        return jnp.sum(jnp.where(eye, column, 0.0), axis=0, keepdims=True)

    def stat_tile(top, total):
        hi = total.astype(BF).astype(F32)
        return jnp.where(stat_row == 0, top, jnp.where(stat_row == 1, hi, total - hi)).astype(BF)

    def weights(scores, top):
        return jnp.exp2(scores - top).astype(BF)

    def largest(scores):
        return jnp.max(scores, axis=1, keepdims=True)

    def suffix_scores(query, cols):
        return dot(query, skbuf[:, :, cols].reshape(512, 128), NT) * C2 + bias[...]

    def suffix_sums(scores, top, cols):
        values = jnp.concatenate([svbuf[:, :, cols].reshape(512, 128), ones[:512]], axis=1)
        return dot(weights(scores, top), values, NN)

    def placed(part, other):
        return jnp.concatenate([jnp.where(yh == 0, part, other), jnp.where(yh == 0, other, part)], axis=0)

    low = jnp.full((64, 1), NEG, F32)

    def other_head(i):
        k = (y + 1 + i) % 4
        cols = pl.ds(pl.multiple_of(theirs + k * 128, 128), 128)
        pltpu.make_async_copy(qx.at[i], qx.at[i], qxrecv.at[i]).wait()
        ss = suffix_scores(qx[i], cols)
        ms = largest(ss).astype(BF).astype(F32)
        ns = suffix_sums(ss, ms, cols)
        cross[i, pl.ds(pl.multiple_of(yh * 64, 64), 64), :] = ns[:, :128].astype(BF)
        cross[i, 128:, :] = stat_tile(as_row(placed(ms, low)), as_row(placed(ns[:, 128:], jnp.zeros((64, 128), F32))))
        pltpu.make_async_remote_copy(
            src_ref=cross.at[i], dst_ref=r1.at[16 + y], send_sem=csend, recv_sem=rrecv,
            device_id=dev(x, k, z, 1 - c), device_id_type=MESH,
        ).start()

    def head(i, _):
        k = (y + 1 + i) % 4
        cols = pl.ds(pl.multiple_of(k * 128, 128), 128)
        own_cols = pl.ds(pl.multiple_of(mine + k * 128, 128), 128)
        pltpu.make_async_copy(q2.at[k], q2.at[k], grecv.at[k]).wait()
        qs[i] = dot(perm[...], q2[k], NN).astype(BF)
        chunks = [(x + 1 + a) % 4 for a in range(4)]
        parts = [qs[i, pl.ds(pl.multiple_of(j * 128, 128), 128), :] for j in chunks]
        own = pl.ds(pl.multiple_of(x * 128 + yh * 64, 64), 64)
        pltpu.make_async_remote_copy(
            src_ref=qs.at[i, own], dst_ref=qx.at[i], send_sem=qxsend, recv_sem=qxrecv.at[i],
            device_id=partner, device_id_type=MESH,
        ).start()
        keys = kbuf[:, cols]
        values = jnp.concatenate([vbuf[:, cols], ones], axis=1)

        s0 = dot(jnp.concatenate(parts[:2], axis=0), keys, NT) * C2
        s1 = dot(jnp.concatenate(parts[2:], axis=0), keys, NT) * C2
        ss = suffix_scores(qs[i, own, :], own_cols)
        m0 = largest(s0).astype(BF).astype(F32)
        n0 = dot(weights(s0, m0), values, NN)
        m1 = largest(s1)
        m1 = jnp.concatenate([m1[:128], jnp.maximum(m1[128:], placed(largest(ss), low))], axis=0)
        m1 = m1.astype(BF).astype(F32)
        n1 = dot(weights(s1, m1), values, NN)
        ns = suffix_sums(ss, jnp.where(yh == 0, m1[128:192], m1[192:]), own_cols)

        pieces = [
            (m0[:128], n0[:128]),
            (m0[128:], n0[128:]),
            (m1[:128], n1[:128]),
            (m1[128:], n1[128:] + placed(ns, 0.0)),
        ]
        for a in range(4):
            m, n = pieces[a]
            slot = i * 4 + a
            sbuf[slot, :128, :] = n[:, :128].astype(BF)
            sbuf[slot, 128:, :] = stat_tile(as_row(m), as_row(n[:, 128:]))

            def send(slot=slot, j=chunks[a]):
                pltpu.make_async_remote_copy(
                    src_ref=sbuf.at[slot], dst_ref=r1.at[x * 4 + y], send_sem=rsend, recv_sem=rrecv,
                    device_id=dev(j, k, z, c), device_id_type=MESH,
                ).start()

            if a < 3:
                send()
            else:
                pl.when(i < 3)(send)

        @pl.when(i > 0)
        def _():
            other_head(i - 1)

        return 0

    lax.fori_loop(0, 4, head, 0)
    pltpu.make_async_copy(sbuf.at[15], r1.at[x * 4 + y], rrecv).start()
    other_head(3)

    pltpu.make_async_copy(r1, r1, rrecv).wait()
    stats = [r1[i, 128:, :].astype(F32) for i in range(20)]
    top = functools.reduce(jnp.maximum, [s[0:1] for s in stats])
    ws = [jnp.exp2(s[0:1] - top) for s in stats]
    total = functools.reduce(jnp.add, [w * (s[1:2] + s[2:3]) for w, s in zip(ws, stats)])
    his = [w.astype(BF).astype(F32) for w in ws]
    spread = [
        jnp.concatenate([jnp.where(eye, w, 0.0).astype(BF) for w in part], axis=1)
        for part in (his, [w - h for w, h in zip(ws, his)])
    ]
    both = dot(jnp.concatenate(spread, axis=0), jnp.concatenate([r1[i, :128, :] for i in range(20)], axis=0), NN)
    flat = (both[:128] + both[128:]).astype(BF)
    stat = stat_tile(top, total)
    for d in range(8):
        s2[d, :16, :] = flat[d * 16 : d * 16 + 16, :]
        s2[d, 16:, :] = stat

    zt = 4 * c + y
    for o in range(1, 8):
        y_, c_ = (y + o // 2) % 4, (c + o % 2) % 2
        pltpu.make_async_remote_copy(
            src_ref=s2.at[y_ * 2 + c_], dst_ref=r2.at[z], send_sem=tsend.at[0], recv_sem=trecv,
            device_id=dev(x, y_, zt, c_), device_id_type=MESH,
        ).start()

    @pl.when(zt == z)
    def _():
        pltpu.make_async_copy(s2.at[y * 2 + c], r2.at[z], trecv).start()

    @pl.when(zt != z)
    def _():
        pltpu.make_async_remote_copy(
            src_ref=s2.at[y * 2 + c], dst_ref=r2.at[z], send_sem=tsend.at[1], recv_sem=trecv,
            device_id=dev(x, y, zt, c), device_id_type=MESH,
        ).start()

    pltpu.make_async_copy(r2, r2, trecv).wait()

    offset = y * 32 + c * 16
    pick = lax.broadcasted_iota(jnp.int32, (16, 128), 1) == lax.broadcasted_iota(jnp.int32, (16, 128), 0) + offset
    stats = [r2[i, 16:, :].astype(F32) for i in range(8)]
    m2 = functools.reduce(jnp.maximum, [s[0:1] for s in stats])
    ws = [jnp.exp2(s[0:1] - m2) for s in stats]
    total = functools.reduce(jnp.add, [w * (s[1:2] + s[2:3]) for w, s in zip(ws, stats)])
    acc = jnp.zeros((16, 128), F32)
    for i in range(8):
        column = jnp.sum(jnp.where(pick, ws[i], 0.0), axis=1, keepdims=True)
        acc = acc + column * r2[i, :16, :].astype(F32)
    column = jnp.sum(jnp.where(pick, total, 0.0), axis=1, keepdims=True)
    acc = acc / column
    for g in range(4):
        out_ref[:, g * 128 : (g + 1) * 128] = acc[g * 4 : g * 4 + 4, :].astype(BF)

    for i in range(2):
        exchanges[i].wait_send()
    pltpu.make_async_copy(qx, qx, qxsend).wait()
    pltpu.make_async_copy(cross, cross, csend).wait()
    pltpu.make_async_copy(s2.at[pl.ds(0, 7), pl.ds(0, 16)], s2.at[pl.ds(0, 7), pl.ds(0, 16)], zsend.at[0]).wait()

    @pl.when(hz != c)
    def _():
        pltpu.make_async_copy(q0, q0, zsend.at[1]).wait()

    most = q2.at[:, pl.ds(0, 480)]
    pltpu.make_async_copy(most, most, gsend).wait()
    most = sbuf.at[pl.ds(0, 15)]
    pltpu.make_async_copy(most, most, rsend).wait()
    most = s2.at[pl.ds(0, 7)]
    pltpu.make_async_copy(most, most, tsend.at[0]).wait()

    @pl.when(zt != z)
    def _():
        pltpu.make_async_copy(s2.at[0], s2.at[0], tsend.at[1]).wait()


def shards(queries, assignment, prefix_keys, prefix_values, suffix_keys, suffix_values, lengths):
    vmem, far = pl.BlockSpec(memory_space=pltpu.VMEM), pl.BlockSpec(memory_space=pl.ANY)
    dma = pltpu.SemaphoreType.DMA
    return pl.pallas_call(
        kernel,
        out_shape=jax.ShapeDtypeStruct(queries.shape, BF),
        in_specs=[far, far, far, far, far, far, far],
        out_specs=vmem,
        scratch_shapes=[
            pltpu.VMEM((1024, 512), BF),
            pltpu.VMEM((1024, 512), BF),
            pltpu.VMEM((4, 128, 1024), BF),
            pltpu.VMEM((4, 128, 1024), BF),
            pltpu.VMEM((16, 128), F32),
            pltpu.VMEM((16, 128), BF),
            pltpu.VMEM((4, 32, 128), BF),
            pltpu.VMEM((4, 512, 128), BF),
            pltpu.VMEM((4, 512, 128), BF),
            pltpu.VMEM((4, 64, 128), BF),
            pltpu.VMEM((512, 512), BF),
            pltpu.VMEM((64, 512), F32),
            pltpu.VMEM((16, 144, 128), BF),
            pltpu.VMEM((4, 144, 128), BF),
            pltpu.VMEM((20, 144, 128), BF),
            pltpu.VMEM((8, 32, 128), BF),
            pltpu.VMEM((8, 32, 128), BF),
            pltpu.VMEM((4, 512), BF),
            pltpu.SMEM((64,), jnp.int32),
            pltpu.SMEM((4,), jnp.int32),
            dma((3,)),
            dma((4,)),
            dma((2,)),
            dma((2,)),
            dma((2,)),
            dma((4,)),
            dma(()),
            dma((4,)),
            dma(()),
            dma(()),
            dma(()),
            dma(()),
            dma((4,)),
            dma((2,)),
            dma(()),
        ],
        compiler_params=pltpu.CompilerParams(
            collective_id=0, has_side_effects=True, vmem_limit_bytes=60 * 1024 * 1024
        ),
        cost_estimate=pl.CostEstimate(flops=1_300_000_000, bytes_accessed=4_300_000, transcendentals=2_600_000),
    )(queries, assignment, lengths, prefix_keys, prefix_values, suffix_keys, suffix_values)


def solution(mesh):
    in_specs = (
        P("rep", "tp"),
        P(),
        P(("rep", "tp"), None),
        P(("rep", "tp"), None),
        P("rep", "tp", None),
        P("rep", "tp", None),
        P("rep"),
    )
    out_specs = P("rep", "tp")
    return jax.shard_map(shards, mesh=mesh, in_specs=in_specs, out_specs=out_specs, check_vma=False)
```

```python
import functools
import math

import jax
import jax.numpy as jnp
from jax import lax
from jax.experimental import pallas as pl
from jax.experimental.pallas import tpu as pltpu
from jax.sharding import PartitionSpec as P

MESH = pl.DeviceIdType.MESH
HD = 128
HEADS_CORE = 4
C2 = math.log2(math.e) * HD ** (-0.5)
NEG = -(2.0**100)
BF = jnp.bfloat16
F32 = jnp.float32
NT = (((1,), (1,)), ((), ()))
NN = (((1,), (0,)), ((), ()))


def dot(a, b, dims):
    return lax.dot_general(a, b, dims, preferred_element_type=F32)


def kernel(
    q_hbm, asg_hbm, len_hbm, pk, pv, sk, sv, out_ref,
    kbuf, vbuf, skbuf, svbuf, qf, q0, q1, q2, qs, perm, lens, lensall, bias, sbuf, r1, s2, r2,
    q_ref, asg_ref, len_ref, smallsem, ldsem, xsend, xrecv, zsend, zrecv, gsend, grecv, rsend, rrecv, tsend, trecv,
):
    rep, tp = lax.axis_index("rep"), lax.axis_index("tp")
    x, yh, c = rep // 4, (rep // 2) % 2, rep % 2
    z, yl = tp // 2, tp % 2
    y = yh * 2 + yl
    hz = z // 4

    def dev(x_, y_, z_, c_):
        return (x_ * 4 + (y_ // 2) * 2 + c_, z_ * 2 + y_ % 2)

    small = [
        pltpu.make_async_copy(src, dst, smallsem.at[i])
        for i, (src, dst) in enumerate(((q_hbm, q_ref), (asg_hbm, asg_ref), (len_hbm, len_ref)))
    ]
    for copy in small:
        copy.start()

    mine = pl.multiple_of(c * 512, 512)
    theirs = pl.multiple_of((1 - c) * 512, 512)
    rows2 = pl.multiple_of(c * 512, 512)
    pairs = ((pk, kbuf), (sk, skbuf), (pv, vbuf), (sv, svbuf))

    def local_dst(i):
        buf = pairs[i][1]
        return buf.at[pl.ds(rows2, 512)] if i % 2 == 0 else buf.at[pl.ds(c * 4, 4)]

    def src_of(i, cols):
        ref = pairs[i][0]
        return ref.at[:, pl.ds(cols, 512)] if i % 2 == 0 else ref.at[:, :, pl.ds(cols, 512)]

    loads = [pltpu.make_async_copy(src_of(i, mine), local_dst(i), ldsem.at[i]) for i in range(4)]
    barrier = pltpu.get_barrier_semaphore()

    def greet(x_, y_, z_, c_):
        pl.semaphore_signal(barrier, inc=1, device_id=dev(x_, y_, z_, c_), device_id_type=MESH)

    partner = dev(x, y, z, 1 - c)
    for k in range(4):
        for cs in range(2):
            zs = 4 * c + k

            @pl.when(jnp.logical_or(zs != z, cs != c))
            def _(zs=zs, cs=cs):
                greet(x, y, zs, cs)

    greet(x, y, z, 1 - c)
    for o in range(1, 16):
        greet((x + o // 4) % 4, (y + o % 4) % 4, z, c)
    for zs in range(8):

        @pl.when(jnp.logical_or(jnp.logical_or(zs != z, z % 4 != y), hz != c))
        def _(zs=zs):
            greet(x, z % 4, zs, hz)

    for copy in loads:
        copy.start()

    small[0].wait()
    q = q_ref[...].astype(F32)
    for g in range(4):
        qf[g * 4 : g * 4 + 4, :] = q[:, g * 128 : (g + 1) * 128]
    q0[...] = qf[...].astype(BF)

    n_z = jnp.where(hz == c, 7, 8)
    n_t = jnp.where(4 * c + y == z, 7, 8)
    pl.semaphore_wait(barrier, 16 + n_z + n_t)

    def ztile(ref_z):
        return q1.at[ref_z % 4, pl.ds(pl.multiple_of(c * 16, 16), 16)]

    for o in (4, 3, 5, 2, 6, 1, 7):
        z_ = (z + o) % 8
        pltpu.make_async_remote_copy(
            src_ref=q0, dst_ref=ztile(z), send_sem=zsend.at[0], recv_sem=zrecv.at[z % 4],
            device_id=dev(x, y, z_, hz), device_id_type=MESH,
        ).start()

    @pl.when(hz == c)
    def _():
        pltpu.make_async_copy(q0, ztile(z), zrecv.at[z % 4]).start()

    @pl.when(hz != c)
    def _():
        pltpu.make_async_remote_copy(
            src_ref=q0, dst_ref=ztile(z), send_sem=zsend.at[1], recv_sem=zrecv.at[z % 4],
            device_id=partner, device_id_type=MESH,
        ).start()

    exchanges = [
        pltpu.make_async_remote_copy(
            src_ref=src_of(i, theirs), dst_ref=local_dst(i), send_sem=xsend.at[i], recv_sem=xrecv.at[i],
            device_id=partner, device_id_type=MESH,
        )
        for i in range(4)
    ]
    exchanges.append(
        pltpu.make_async_remote_copy(
            src_ref=lens, dst_ref=lensall, send_sem=xsend.at[4], recv_sem=xrecv.at[4],
            device_id=partner, device_id_type=MESH,
        )
    )
    exchanges[0].start()

    small[1].wait()
    small[2].wait()
    own_len = jnp.zeros((8, 128), jnp.int32)
    sub8 = lax.broadcasted_iota(jnp.int32, (8, 128), 0)
    for s in range(4):
        own_len = jnp.where(sub8 % 4 == s, len_ref[s], own_len)
    lens[...] = own_len

    exchanges[4].start()

    lane = lax.broadcasted_iota(jnp.int32, (1, 128), 1)
    lane_row = ((lane // 64) * 2 + (lane // 16) % 2) * 4 + lane % 4
    lane_g = ((lane // 32) % 2) * 4 + (lane // 4) % 4
    sub = lax.broadcasted_iota(jnp.int32, (512, 128), 0)
    sub_row = (sub // 128) * 16 + ((sub // 64) % 2) * 8 + ((sub // 16) % 2) * 4 + sub % 4
    sub_g = ((sub // 32) % 2) * 4 + (sub // 4) % 4
    sub_code = sub_row * 8 + sub_g
    for xs in range(4):
        held = jnp.zeros((1, 128), jnp.int32)
        for r in range(16):
            held = jnp.where(lane_row == r, asg_ref[xs * 16 + r], held)
        code = held * 8 + lane_g
        perm[:, xs * 128 : (xs + 1) * 128] = jnp.where(sub_code == code, 1.0, 0.0).astype(BF)

    me_rows = pl.ds(pl.multiple_of((x * 4 + y) * 32, 32), 32)
    for k in range(4):
        pltpu.make_async_copy(q1.at[k], q1.at[k], zrecv.at[k]).wait()
    for i in range(4):
        k = (y + 1 + i) % 4
        pltpu.make_async_copy(q1.at[k], q2.at[k, me_rows], grecv.at[k]).start()
        for o in range(1, 16):
            y_ = (y + o % 4) % 4
            k = (y_ + 1 + i) % 4
            pltpu.make_async_remote_copy(
                src_ref=q1.at[k], dst_ref=q2.at[k, me_rows], send_sem=gsend, recv_sem=grecv.at[k],
                device_id=dev((x + o // 4) % 4, y_, z, c), device_id_type=MESH,
            ).start()
        if i < 3:
            exchanges[(2, 1, 3)[i]].start()

    exchanges[4].wait_recv()
    rows = lax.broadcasted_iota(jnp.int32, (128, 128), 0)
    lanes = lax.broadcasted_iota(jnp.int32, (128, 128), 1)
    lens_own = jnp.concatenate([lens[...]] * 16, axis=0)
    lens_other = jnp.concatenate([lensall[...]] * 16, axis=0)
    row_c = (rows // 16) % 2
    live = jnp.where(row_c == c, lens_own, lens_other) - tp * 128
    live = jnp.where(rows // 64 == yh, live, 0)
    row_slot = row_c * 4 + rows % 4
    for s in range(8):
        limit = jnp.where(row_slot == s, live, 0)
        bias[:, s * 128 : s * 128 + 128] = jnp.where(lanes < limit, 0.0, NEG)

    for i in range(4):
        loads[i].wait()
        exchanges[i].wait_recv()

    eye = rows == lanes
    ones = jnp.ones((1024, 128), BF)
    stat_row = lax.broadcasted_iota(jnp.int32, (16, 128), 0)

    def as_row(column):
        return jnp.sum(jnp.where(eye, column, 0.0), axis=0, keepdims=True)

    def stat_tile(top, total):
        hi = total.astype(BF).astype(F32)
        return jnp.where(stat_row == 0, top, jnp.where(stat_row == 1, hi, total - hi)).astype(BF)

    def weights(scores, top):
        return jnp.exp2(scores - top).astype(BF)

    def largest(scores):
        return jnp.max(scores, axis=1, keepdims=True)

    def head(i, _):
        k = (y + 1 + i) % 4
        cols = pl.ds(pl.multiple_of(k * 128, 128), 128)
        pltpu.make_async_copy(q2.at[k], q2.at[k], grecv.at[k]).wait()
        qs[...] = dot(perm[...], q2[k], NN).astype(BF)
        chunks = [(x + 1 + a) % 4 for a in range(4)]
        parts = [qs[pl.ds(pl.multiple_of(j * 128, 128), 128), :] for j in chunks]
        keys = kbuf[:, cols]
        values = jnp.concatenate([vbuf[:, cols], ones], axis=1)
        suffix_keys = skbuf[:, :, cols].reshape(1024, 128)
        suffix_values = jnp.concatenate([svbuf[:, :, cols].reshape(1024, 128), ones], axis=1)

        s0 = dot(jnp.concatenate(parts[:2], axis=0), keys, NT) * C2
        s1 = dot(jnp.concatenate(parts[2:], axis=0), keys, NT) * C2
        ss = dot(parts[3], suffix_keys, NT) * C2 + bias[...]
        m0 = largest(s0).astype(BF).astype(F32)
        n0 = dot(weights(s0, m0), values, NN)
        m1 = largest(s1)
        m1 = jnp.concatenate([m1[:128], jnp.maximum(m1[128:], largest(ss))], axis=0).astype(BF).astype(F32)
        n1 = dot(weights(s1, m1), values, NN)
        ns = dot(weights(ss, m1[128:]), suffix_values, NN)

        pieces = [
            (m0[:128], n0[:128]),
            (m0[128:], n0[128:]),
            (m1[:128], n1[:128]),
            (m1[128:], n1[128:] + ns),
        ]
        for a in range(4):
            m, n = pieces[a]
            slot = i * 4 + a
            sbuf[slot, :128, :] = n[:, :128].astype(BF)
            sbuf[slot, 128:, :] = stat_tile(as_row(m), as_row(n[:, 128:]))

            def send(slot=slot, j=chunks[a]):
                pltpu.make_async_remote_copy(
                    src_ref=sbuf.at[slot], dst_ref=r1.at[x * 4 + y], send_sem=rsend, recv_sem=rrecv,
                    device_id=dev(j, k, z, c), device_id_type=MESH,
                ).start()

            if a < 3:
                send()
            else:
                pl.when(i < 3)(send)
        return 0

    lax.fori_loop(0, 4, head, 0)
    pltpu.make_async_copy(sbuf.at[15], r1.at[x * 4 + y], rrecv).start()

    pltpu.make_async_copy(r1, r1, rrecv).wait()
    stats = [r1[i, 128:, :].astype(F32) for i in range(16)]
    top = functools.reduce(jnp.maximum, [s[0:1] for s in stats])
    ws = [jnp.exp2(s[0:1] - top) for s in stats]
    total = functools.reduce(jnp.add, [w * (s[1:2] + s[2:3]) for w, s in zip(ws, stats)])
    his = [w.astype(BF).astype(F32) for w in ws]
    spread = [
        jnp.concatenate([jnp.where(eye, w, 0.0).astype(BF) for w in part], axis=1)
        for part in (his, [w - h for w, h in zip(ws, his)])
    ]
    both = dot(jnp.concatenate(spread, axis=0), jnp.concatenate([r1[i, :128, :] for i in range(16)], axis=0), NN)
    flat = (both[:128] + both[128:]).astype(BF)
    stat = stat_tile(top, total)
    for d in range(8):
        s2[d, :16, :] = flat[d * 16 : d * 16 + 16, :]
        s2[d, 16:, :] = stat

    zt = 4 * c + y
    for o in range(1, 8):
        y_, c_ = (y + o // 2) % 4, (c + o % 2) % 2
        pltpu.make_async_remote_copy(
            src_ref=s2.at[y_ * 2 + c_], dst_ref=r2.at[z], send_sem=tsend.at[0], recv_sem=trecv,
            device_id=dev(x, y_, zt, c_), device_id_type=MESH,
        ).start()

    @pl.when(zt == z)
    def _():
        pltpu.make_async_copy(s2.at[y * 2 + c], r2.at[z], trecv).start()

    @pl.when(zt != z)
    def _():
        pltpu.make_async_remote_copy(
            src_ref=s2.at[y * 2 + c], dst_ref=r2.at[z], send_sem=tsend.at[1], recv_sem=trecv,
            device_id=dev(x, y, zt, c), device_id_type=MESH,
        ).start()

    pltpu.make_async_copy(r2, r2, trecv).wait()

    offset = y * 32 + c * 16
    pick = lax.broadcasted_iota(jnp.int32, (16, 128), 1) == lax.broadcasted_iota(jnp.int32, (16, 128), 0) + offset
    stats = [r2[i, 16:, :].astype(F32) for i in range(8)]
    m2 = functools.reduce(jnp.maximum, [s[0:1] for s in stats])
    ws = [jnp.exp2(s[0:1] - m2) for s in stats]
    total = functools.reduce(jnp.add, [w * (s[1:2] + s[2:3]) for w, s in zip(ws, stats)])
    acc = jnp.zeros((16, 128), F32)
    for i in range(8):
        column = jnp.sum(jnp.where(pick, ws[i], 0.0), axis=1, keepdims=True)
        acc = acc + column * r2[i, :16, :].astype(F32)
    column = jnp.sum(jnp.where(pick, total, 0.0), axis=1, keepdims=True)
    acc = acc / column
    for g in range(4):
        out_ref[:, g * 128 : (g + 1) * 128] = acc[g * 4 : g * 4 + 4, :].astype(BF)

    for i in range(5):
        exchanges[i].wait_send()
    pltpu.make_async_copy(s2.at[pl.ds(0, 7), pl.ds(0, 16)], s2.at[pl.ds(0, 7), pl.ds(0, 16)], zsend.at[0]).wait()

    @pl.when(hz != c)
    def _():
        pltpu.make_async_copy(q0, q0, zsend.at[1]).wait()

    most = q2.at[:, pl.ds(0, 480)]
    pltpu.make_async_copy(most, most, gsend).wait()
    most = sbuf.at[pl.ds(0, 15)]
    pltpu.make_async_copy(most, most, rsend).wait()
    most = s2.at[pl.ds(0, 7)]
    pltpu.make_async_copy(most, most, tsend.at[0]).wait()

    @pl.when(zt != z)
    def _():
        pltpu.make_async_copy(s2.at[0], s2.at[0], tsend.at[1]).wait()


def shards(queries, assignment, prefix_keys, prefix_values, suffix_keys, suffix_values, lengths):
    vmem, far = pl.BlockSpec(memory_space=pltpu.VMEM), pl.BlockSpec(memory_space=pl.ANY)
    dma = pltpu.SemaphoreType.DMA
    return pl.pallas_call(
        kernel,
        out_shape=jax.ShapeDtypeStruct(queries.shape, BF),
        in_specs=[far, far, far, far, far, far, far],
        out_specs=vmem,
        scratch_shapes=[
            pltpu.VMEM((1024, 512), BF),
            pltpu.VMEM((1024, 512), BF),
            pltpu.VMEM((8, 128, 512), BF),
            pltpu.VMEM((8, 128, 512), BF),
            pltpu.VMEM((16, 128), F32),
            pltpu.VMEM((16, 128), BF),
            pltpu.VMEM((4, 32, 128), BF),
            pltpu.VMEM((4, 512, 128), BF),
            pltpu.VMEM((512, 128), BF),
            pltpu.VMEM((512, 512), BF),
            pltpu.VMEM((8, 128), jnp.int32),
            pltpu.VMEM((8, 128), jnp.int32),
            pltpu.VMEM((128, 1024), F32),
            pltpu.VMEM((16, 144, 128), BF),
            pltpu.VMEM((16, 144, 128), BF),
            pltpu.VMEM((8, 32, 128), BF),
            pltpu.VMEM((8, 32, 128), BF),
            pltpu.VMEM((4, 512), BF),
            pltpu.SMEM((64,), jnp.int32),
            pltpu.SMEM((4,), jnp.int32),
            dma((3,)),
            dma((4,)),
            dma((5,)),
            dma((5,)),
            dma((2,)),
            dma((4,)),
            dma(()),
            dma((4,)),
            dma(()),
            dma(()),
            dma((2,)),
            dma(()),
        ],
        compiler_params=pltpu.CompilerParams(
            collective_id=0, has_side_effects=True, vmem_limit_bytes=48 * 1024 * 1024
        ),
        cost_estimate=pl.CostEstimate(flops=1_300_000_000, bytes_accessed=4_300_000, transcendentals=2_600_000),
    )(
        *(
            pltpu.with_memory_space_constraint(operand, pltpu.HBM)
            for operand in (
                queries, assignment, lengths, prefix_keys, prefix_values, suffix_keys, suffix_values
            )
        )
    )


def solution(mesh):
    in_specs = (
        P("rep", "tp"),
        P(),
        P(("rep", "tp"), None),
        P(("rep", "tp"), None),
        P("rep", "tp", None),
        P("rep", "tp", None),
        P("rep"),
    )
    out_specs = P("rep", "tp")
    return jax.shard_map(shards, mesh=mesh, in_specs=in_specs, out_specs=out_specs, check_vma=False)
```

```python
import functools
import math

import jax
import jax.numpy as jnp
from jax import lax
from jax.experimental import pallas as pl
from jax.experimental.pallas import tpu as pltpu
from jax.sharding import PartitionSpec as P

MESH = pl.DeviceIdType.MESH
HD = 128
HEADS_CORE = 4
C2 = math.log2(math.e) * HD ** (-0.5)
NEG = -(2.0**100)
BF = jnp.bfloat16
F32 = jnp.float32
NT = (((1,), (1,)), ((), ()))
NN = (((1,), (0,)), ((), ()))


def dot(a, b, dims):
    return lax.dot_general(a, b, dims, preferred_element_type=F32)


def kernel(
    q_hbm, asg_hbm, len_hbm, pk, pv, sk, sv, out_ref,
    kbuf, vbuf, skbuf, svbuf, qf, q0, q1, q2, qs, perm, lens, lensall, bias, sbuf, r1, s2, r2,
    q_ref, asg_ref, len_ref, smallsem, ldsem, xsend, xrecv, zsend, zrecv, gsend, grecv, rsend, rrecv, tsend, trecv,
):
    rep, tp = lax.axis_index("rep"), lax.axis_index("tp")
    x, yh, c = rep // 4, (rep // 2) % 2, rep % 2
    z, yl = tp // 2, tp % 2
    y = yh * 2 + yl
    hz = z // 4

    def dev(x_, y_, z_, c_):
        return (x_ * 4 + (y_ // 2) * 2 + c_, z_ * 2 + y_ % 2)

    small = [
        pltpu.make_async_copy(src, dst, smallsem.at[i])
        for i, (src, dst) in enumerate(((q_hbm, q_ref), (asg_hbm, asg_ref), (len_hbm, len_ref)))
    ]
    for copy in small:
        copy.start()

    mine = pl.multiple_of(c * 512, 512)
    theirs = pl.multiple_of((1 - c) * 512, 512)
    rows2 = pl.multiple_of(c * 512, 512)
    pairs = ((pk, kbuf), (sk, skbuf), (pv, vbuf), (sv, svbuf))

    def local_dst(i):
        buf = pairs[i][1]
        return buf.at[pl.ds(rows2, 512)] if i % 2 == 0 else buf.at[pl.ds(c * 4, 4)]

    def src_of(i, cols):
        ref = pairs[i][0]
        return ref.at[:, pl.ds(cols, 512)] if i % 2 == 0 else ref.at[:, :, pl.ds(cols, 512)]

    loads = [pltpu.make_async_copy(src_of(i, mine), local_dst(i), ldsem.at[i]) for i in range(4)]
    barrier = pltpu.get_barrier_semaphore()

    def greet(x_, y_, z_, c_):
        pl.semaphore_signal(barrier, inc=1, device_id=dev(x_, y_, z_, c_), device_id_type=MESH)

    partner = dev(x, y, z, 1 - c)
    for k in range(4):
        for cs in range(2):
            zs = 4 * c + k

            @pl.when(jnp.logical_or(zs != z, cs != c))
            def _(zs=zs, cs=cs):
                greet(x, y, zs, cs)

    greet(x, y, z, 1 - c)
    for o in range(1, 16):
        greet((x + o // 4) % 4, (y + o % 4) % 4, z, c)
    for zs in range(8):

        @pl.when(jnp.logical_or(jnp.logical_or(zs != z, z % 4 != y), hz != c))
        def _(zs=zs):
            greet(x, z % 4, zs, hz)

    for copy in loads:
        copy.start()

    small[0].wait()
    q = q_ref[...].astype(F32)
    for g in range(4):
        qf[g * 4 : g * 4 + 4, :] = q[:, g * 128 : (g + 1) * 128]
    q0[...] = qf[...].astype(BF)

    n_z = jnp.where(hz == c, 7, 8)
    n_t = jnp.where(4 * c + y == z, 7, 8)
    pl.semaphore_wait(barrier, 16 + n_z + n_t)

    def ztile(ref_z):
        return q1.at[ref_z % 4, pl.ds(pl.multiple_of(c * 16, 16), 16)]

    for o in (4, 3, 5, 2, 6, 1, 7):
        z_ = (z + o) % 8
        pltpu.make_async_remote_copy(
            src_ref=q0, dst_ref=ztile(z), send_sem=zsend.at[0], recv_sem=zrecv.at[z % 4],
            device_id=dev(x, y, z_, hz), device_id_type=MESH,
        ).start()

    @pl.when(hz == c)
    def _():
        pltpu.make_async_copy(q0, ztile(z), zrecv.at[z % 4]).start()

    @pl.when(hz != c)
    def _():
        pltpu.make_async_remote_copy(
            src_ref=q0, dst_ref=ztile(z), send_sem=zsend.at[1], recv_sem=zrecv.at[z % 4],
            device_id=partner, device_id_type=MESH,
        ).start()

    exchanges = [
        pltpu.make_async_remote_copy(
            src_ref=src_of(i, theirs), dst_ref=local_dst(i), send_sem=xsend.at[i], recv_sem=xrecv.at[i],
            device_id=partner, device_id_type=MESH,
        )
        for i in range(4)
    ]
    exchanges.append(
        pltpu.make_async_remote_copy(
            src_ref=lens, dst_ref=lensall, send_sem=xsend.at[4], recv_sem=xrecv.at[4],
            device_id=partner, device_id_type=MESH,
        )
    )
    exchanges[0].start()

    small[1].wait()
    small[2].wait()
    own_len = jnp.zeros((8, 128), jnp.int32)
    sub8 = lax.broadcasted_iota(jnp.int32, (8, 128), 0)
    for s in range(4):
        own_len = jnp.where(sub8 % 4 == s, len_ref[s], own_len)
    lens[...] = own_len

    exchanges[4].start()

    lane = lax.broadcasted_iota(jnp.int32, (1, 128), 1)
    lane_row = ((lane // 64) * 2 + (lane // 16) % 2) * 4 + lane % 4
    lane_g = ((lane // 32) % 2) * 4 + (lane // 4) % 4
    sub = lax.broadcasted_iota(jnp.int32, (512, 128), 0)
    sub_row = (sub // 128) * 16 + ((sub // 64) % 2) * 8 + ((sub // 16) % 2) * 4 + sub % 4
    sub_g = ((sub // 32) % 2) * 4 + (sub // 4) % 4
    sub_code = sub_row * 8 + sub_g
    for xs in range(4):
        held = jnp.zeros((1, 128), jnp.int32)
        for r in range(16):
            held = jnp.where(lane_row == r, asg_ref[xs * 16 + r], held)
        code = held * 8 + lane_g
        perm[:, xs * 128 : (xs + 1) * 128] = jnp.where(sub_code == code, 1.0, 0.0).astype(BF)

    me_rows = pl.ds(pl.multiple_of((x * 4 + y) * 32, 32), 32)
    for k in range(4):
        pltpu.make_async_copy(q1.at[k], q1.at[k], zrecv.at[k]).wait()
    for i in range(4):
        k = (y + 1 + i) % 4
        pltpu.make_async_copy(q1.at[k], q2.at[k, me_rows], grecv.at[k]).start()
        for o in range(1, 16):
            y_ = (y + o % 4) % 4
            k = (y_ + 1 + i) % 4
            pltpu.make_async_remote_copy(
                src_ref=q1.at[k], dst_ref=q2.at[k, me_rows], send_sem=gsend, recv_sem=grecv.at[k],
                device_id=dev((x + o // 4) % 4, y_, z, c), device_id_type=MESH,
            ).start()
        if i < 3:
            exchanges[(2, 1, 3)[i]].start()

    exchanges[4].wait_recv()
    rows = lax.broadcasted_iota(jnp.int32, (64, 128), 0)
    lanes = lax.broadcasted_iota(jnp.int32, (64, 128), 1)
    lens_own = jnp.concatenate([lens[...]] * 8, axis=0)
    lens_other = jnp.concatenate([lensall[...]] * 8, axis=0)
    row_c = (rows // 16) % 2
    live = jnp.where(row_c == c, lens_own, lens_other) - tp * 128
    row_slot = row_c * 4 + rows % 4
    for s in range(8):
        limit = jnp.where(row_slot == s, live, 0)
        bias[:, s * 128 : s * 128 + 128] = jnp.where(lanes < limit, 0.0, NEG)

    for i in range(4):
        loads[i].wait()
        exchanges[i].wait_recv()

    square = (128, 128)
    eye = lax.broadcasted_iota(jnp.int32, square, 0) == lax.broadcasted_iota(jnp.int32, square, 1)
    ones = jnp.ones((1024, 128), BF)
    stat_row = lax.broadcasted_iota(jnp.int32, (16, 128), 0)

    def as_row(column):
        return jnp.sum(jnp.where(eye, column, 0.0), axis=0, keepdims=True)

    def stat_tile(top, total):
        hi = total.astype(BF).astype(F32)
        return jnp.where(stat_row == 0, top, jnp.where(stat_row == 1, hi, total - hi)).astype(BF)

    def weights(scores, top):
        return jnp.exp2(scores - top).astype(BF)

    def largest(scores):
        return jnp.max(scores, axis=1, keepdims=True)

    def head(i, _):
        k = (y + 1 + i) % 4
        cols = pl.ds(pl.multiple_of(k * 128, 128), 128)
        pltpu.make_async_copy(q2.at[k], q2.at[k], grecv.at[k]).wait()
        qs[...] = dot(perm[...], q2[k], NN).astype(BF)
        chunks = [(x + 1 + a) % 4 for a in range(4)]
        parts = [qs[pl.ds(pl.multiple_of(j * 128, 128), 128), :] for j in chunks]
        keys = kbuf[:, cols]
        values = jnp.concatenate([vbuf[:, cols], ones], axis=1)
        suffix_keys = skbuf[:, :, cols].reshape(1024, 128)
        suffix_values = jnp.concatenate([svbuf[:, :, cols].reshape(1024, 128), ones], axis=1)

        s0 = dot(jnp.concatenate(parts[:2], axis=0), keys, NT) * C2
        s1 = dot(jnp.concatenate(parts[2:], axis=0), keys, NT) * C2
        own = pl.ds(pl.multiple_of(x * 128 + yh * 64, 64), 64)
        ss = dot(qs[own, :], suffix_keys, NT) * C2 + bias[...]

        def send(a):
            pltpu.make_async_remote_copy(
                src_ref=sbuf.at[i * 4 + a], dst_ref=r1.at[x * 4 + y], send_sem=rsend, recv_sem=rrecv,
                device_id=dev(chunks[a], k, z, c), device_id_type=MESH,
            ).start()

        def put(a, m, n):
            sbuf[i * 4 + a, :128, :] = n[:, :128].astype(BF)
            sbuf[i * 4 + a, 128:, :] = stat_tile(as_row(m), as_row(n[:, 128:]))

        m0 = largest(s0).astype(BF).astype(F32)
        n0 = dot(weights(s0, m0), values, NN)
        put(0, m0[:128], n0[:128])
        send(0)
        put(1, m0[128:], n0[128:])
        send(1)

        m1, ms = largest(s1), largest(ss)
        low = jnp.full((64, 1), NEG, F32)
        ms = jnp.concatenate([jnp.where(yh == 0, ms, low), jnp.where(yh == 0, low, ms)], axis=0)
        m1 = jnp.concatenate([m1[:128], jnp.maximum(m1[128:], ms)], axis=0).astype(BF).astype(F32)
        n1 = dot(weights(s1, m1), values, NN)
        ns = dot(weights(ss, jnp.where(yh == 0, m1[128:192], m1[192:])), suffix_values, NN)
        ns = jnp.concatenate([jnp.where(yh == 0, ns, 0.0), jnp.where(yh == 0, 0.0, ns)], axis=0)
        put(2, m1[:128], n1[:128])
        send(2)
        put(3, m1[128:], n1[128:] + ns)
        pl.when(i < 3)(lambda: send(3))
        return 0

    lax.fori_loop(0, 4, head, 0)
    pltpu.make_async_copy(sbuf.at[15], r1.at[x * 4 + y], rrecv).start()

    pltpu.make_async_copy(r1, r1, rrecv).wait()
    stats = [r1[i, 128:, :].astype(F32) for i in range(16)]
    top = functools.reduce(jnp.maximum, [s[0:1] for s in stats])
    ws = [jnp.exp2(s[0:1] - top) for s in stats]
    total = functools.reduce(jnp.add, [w * (s[1:2] + s[2:3]) for w, s in zip(ws, stats)])
    his = [w.astype(BF).astype(F32) for w in ws]
    spread = [
        jnp.concatenate([jnp.where(eye, w, 0.0).astype(BF) for w in part], axis=1)
        for part in (his, [w - h for w, h in zip(ws, his)])
    ]
    both = dot(jnp.concatenate(spread, axis=0), jnp.concatenate([r1[i, :128, :] for i in range(16)], axis=0), NN)
    flat = (both[:128] + both[128:]).astype(BF)
    stat = stat_tile(top, total)
    for d in range(8):
        s2[d, :16, :] = flat[d * 16 : d * 16 + 16, :]
        s2[d, 16:, :] = stat

    zt = 4 * c + y
    for o in range(1, 8):
        y_, c_ = (y + o // 2) % 4, (c + o % 2) % 2
        pltpu.make_async_remote_copy(
            src_ref=s2.at[y_ * 2 + c_], dst_ref=r2.at[z], send_sem=tsend.at[0], recv_sem=trecv,
            device_id=dev(x, y_, zt, c_), device_id_type=MESH,
        ).start()

    @pl.when(zt == z)
    def _():
        pltpu.make_async_copy(s2.at[y * 2 + c], r2.at[z], trecv).start()

    @pl.when(zt != z)
    def _():
        pltpu.make_async_remote_copy(
            src_ref=s2.at[y * 2 + c], dst_ref=r2.at[z], send_sem=tsend.at[1], recv_sem=trecv,
            device_id=dev(x, y, zt, c), device_id_type=MESH,
        ).start()

    pltpu.make_async_copy(r2, r2, trecv).wait()

    offset = y * 32 + c * 16
    pick = lax.broadcasted_iota(jnp.int32, (16, 128), 1) == lax.broadcasted_iota(jnp.int32, (16, 128), 0) + offset
    stats = [r2[i, 16:, :].astype(F32) for i in range(8)]
    m2 = functools.reduce(jnp.maximum, [s[0:1] for s in stats])
    ws = [jnp.exp2(s[0:1] - m2) for s in stats]
    total = functools.reduce(jnp.add, [w * (s[1:2] + s[2:3]) for w, s in zip(ws, stats)])
    acc = jnp.zeros((16, 128), F32)
    for i in range(8):
        column = jnp.sum(jnp.where(pick, ws[i], 0.0), axis=1, keepdims=True)
        acc = acc + column * r2[i, :16, :].astype(F32)
    column = jnp.sum(jnp.where(pick, total, 0.0), axis=1, keepdims=True)
    acc = acc / column
    for g in range(4):
        out_ref[:, g * 128 : (g + 1) * 128] = acc[g * 4 : g * 4 + 4, :].astype(BF)

    for i in range(5):
        exchanges[i].wait_send()
    pltpu.make_async_copy(s2.at[pl.ds(0, 7), pl.ds(0, 16)], s2.at[pl.ds(0, 7), pl.ds(0, 16)], zsend.at[0]).wait()

    @pl.when(hz != c)
    def _():
        pltpu.make_async_copy(q0, q0, zsend.at[1]).wait()

    most = q2.at[:, pl.ds(0, 480)]
    pltpu.make_async_copy(most, most, gsend).wait()
    most = sbuf.at[pl.ds(0, 15)]
    pltpu.make_async_copy(most, most, rsend).wait()
    most = s2.at[pl.ds(0, 7)]
    pltpu.make_async_copy(most, most, tsend.at[0]).wait()

    @pl.when(zt != z)
    def _():
        pltpu.make_async_copy(s2.at[0], s2.at[0], tsend.at[1]).wait()


def shards(queries, assignment, prefix_keys, prefix_values, suffix_keys, suffix_values, lengths):
    vmem, far = pl.BlockSpec(memory_space=pltpu.VMEM), pl.BlockSpec(memory_space=pl.ANY)
    dma = pltpu.SemaphoreType.DMA
    return pl.pallas_call(
        kernel,
        out_shape=jax.ShapeDtypeStruct(queries.shape, BF),
        in_specs=[far, far, far, far, far, far, far],
        out_specs=vmem,
        scratch_shapes=[
            pltpu.VMEM((1024, 512), BF),
            pltpu.VMEM((1024, 512), BF),
            pltpu.VMEM((8, 128, 512), BF),
            pltpu.VMEM((8, 128, 512), BF),
            pltpu.VMEM((16, 128), F32),
            pltpu.VMEM((16, 128), BF),
            pltpu.VMEM((4, 32, 128), BF),
            pltpu.VMEM((4, 512, 128), BF),
            pltpu.VMEM((512, 128), BF),
            pltpu.VMEM((512, 512), BF),
            pltpu.VMEM((8, 128), jnp.int32),
            pltpu.VMEM((8, 128), jnp.int32),
            pltpu.VMEM((64, 1024), F32),
            pltpu.VMEM((16, 144, 128), BF),
            pltpu.VMEM((16, 144, 128), BF),
            pltpu.VMEM((8, 32, 128), BF),
            pltpu.VMEM((8, 32, 128), BF),
            pltpu.VMEM((4, 512), BF),
            pltpu.SMEM((64,), jnp.int32),
            pltpu.SMEM((4,), jnp.int32),
            dma((3,)),
            dma((4,)),
            dma((5,)),
            dma((5,)),
            dma((2,)),
            dma((4,)),
            dma(()),
            dma((4,)),
            dma(()),
            dma(()),
            dma((2,)),
            dma(()),
        ],
        compiler_params=pltpu.CompilerParams(
            collective_id=0, has_side_effects=True, vmem_limit_bytes=48 * 1024 * 1024
        ),
        cost_estimate=pl.CostEstimate(flops=1_300_000_000, bytes_accessed=4_300_000, transcendentals=2_600_000),
    )(
        *(
            pltpu.with_memory_space_constraint(operand, pltpu.HBM)
            for operand in (
                queries, assignment, lengths, prefix_keys, prefix_values, suffix_keys, suffix_values
            )
        )
    )


def solution(mesh):
    in_specs = (
        P("rep", "tp"),
        P(),
        P(("rep", "tp"), None),
        P(("rep", "tp"), None),
        P("rep", "tp", None),
        P("rep", "tp", None),
        P("rep"),
    )
    out_specs = P("rep", "tp")
    return jax.shard_map(shards, mesh=mesh, in_specs=in_specs, out_specs=out_specs, check_vma=False)
```

```python
import functools
import math

import jax
import jax.numpy as jnp
from jax import lax
from jax.experimental import pallas as pl
from jax.experimental.pallas import tpu as pltpu
from jax.sharding import PartitionSpec as P

MESH = pl.DeviceIdType.MESH
HD = 128
HEADS_CORE = 4
C2 = math.log2(math.e) * HD ** (-0.5)
NEG = -(2.0**100)
BF = jnp.bfloat16
F32 = jnp.float32
NT = (((1,), (1,)), ((), ()))
NN = (((1,), (0,)), ((), ()))
AROUND = (
    (1, 0), (3, 0), (0, 1), (0, 3), (2, 0), (1, 1), (3, 1), (2, 1), (0, 2), (1, 2), (3, 2), (2, 2), (1, 3), (3, 3), (2, 3),
)


def dot(a, b, dims):
    return lax.dot_general(a, b, dims, preferred_element_type=F32)


def kernel(
    q_hbm, asg_hbm, len_hbm, pk, pv, sk, sv, out_ref,
    kbuf, vbuf, skbuf, svbuf, qf, q0, q1, q2, qs, perm, lens, lensall, bias, sbuf, r1, s2, r2,
    q_ref, asg_ref, len_ref, smallsem, ldsem, xsend, xrecv, zsend, zrecv, gsend, grecv, rsend, rrecv, tsend, trecv,
):
    rep, tp = lax.axis_index("rep"), lax.axis_index("tp")
    x, yh, c = rep // 4, (rep // 2) % 2, rep % 2
    z, yl = tp // 2, tp % 2
    y = yh * 2 + yl
    hz = z // 4

    def head_at(y_, i):
        return (y_ + 1 + i + c * (2 - 2 * i)) % 4

    def dev(x_, y_, z_, c_):
        return (x_ * 4 + (y_ // 2) * 2 + c_, z_ * 2 + y_ % 2)

    small = [
        pltpu.make_async_copy(src, dst, smallsem.at[i])
        for i, (src, dst) in enumerate(((q_hbm, q_ref), (asg_hbm, asg_ref), (len_hbm, len_ref)))
    ]
    for copy in small:
        copy.start()

    mine = pl.multiple_of(c * 512, 512)
    theirs = pl.multiple_of((1 - c) * 512, 512)
    rows2 = pl.multiple_of(c * 512, 512)
    pairs = ((pk, kbuf), (sk, skbuf), (pv, vbuf), (sv, svbuf))

    def local_dst(i):
        buf = pairs[i][1]
        return buf.at[pl.ds(rows2, 512)] if i % 2 == 0 else buf.at[pl.ds(c * 4, 4)]

    def src_of(i, cols):
        ref = pairs[i][0]
        return ref.at[:, pl.ds(cols, 512)] if i % 2 == 0 else ref.at[:, :, pl.ds(cols, 512)]

    loads = [pltpu.make_async_copy(src_of(i, mine), local_dst(i), ldsem.at[i]) for i in range(4)]
    barrier = pltpu.get_barrier_semaphore()

    def greet(x_, y_, z_, c_):
        pl.semaphore_signal(barrier, inc=1, device_id=dev(x_, y_, z_, c_), device_id_type=MESH)

    partner = dev(x, y, z, 1 - c)
    for k in range(4):
        for cs in range(2):
            zs = 4 * c + k

            @pl.when(jnp.logical_or(zs != z, cs != c))
            def _(zs=zs, cs=cs):
                greet(x, y, zs, cs)

    greet(x, y, z, 1 - c)
    for o in range(1, 16):
        greet((x + o // 4) % 4, (y + o % 4) % 4, z, c)
    for zs in range(8):

        @pl.when(jnp.logical_or(jnp.logical_or(zs != z, z % 4 != y), hz != c))
        def _(zs=zs):
            greet(x, z % 4, zs, hz)

    for copy in loads:
        copy.start()

    small[0].wait()
    q = q_ref[...].astype(F32)
    for g in range(4):
        qf[g * 4 : g * 4 + 4, :] = q[:, g * 128 : (g + 1) * 128]
    q0[...] = qf[...].astype(BF)

    n_z = jnp.where(hz == c, 7, 8)
    n_t = jnp.where(4 * c + y == z, 7, 8)
    pl.semaphore_wait(barrier, 16 + n_z + n_t)

    def ztile(ref_z):
        return q1.at[ref_z % 4, pl.ds(pl.multiple_of(c * 16, 16), 16)]

    for o in (4, 3, 5, 2, 6, 1, 7):
        z_ = (z + o) % 8
        pltpu.make_async_remote_copy(
            src_ref=q0, dst_ref=ztile(z), send_sem=zsend.at[0], recv_sem=zrecv.at[z % 4],
            device_id=dev(x, y, z_, hz), device_id_type=MESH,
        ).start()

    @pl.when(hz == c)
    def _():
        pltpu.make_async_copy(q0, ztile(z), zrecv.at[z % 4]).start()

    @pl.when(hz != c)
    def _():
        pltpu.make_async_remote_copy(
            src_ref=q0, dst_ref=ztile(z), send_sem=zsend.at[1], recv_sem=zrecv.at[z % 4],
            device_id=partner, device_id_type=MESH,
        ).start()

    exchanges = [
        pltpu.make_async_remote_copy(
            src_ref=src_of(i, theirs), dst_ref=local_dst(i), send_sem=xsend.at[i], recv_sem=xrecv.at[i],
            device_id=partner, device_id_type=MESH,
        )
        for i in range(4)
    ]
    exchanges.append(
        pltpu.make_async_remote_copy(
            src_ref=lens, dst_ref=lensall, send_sem=xsend.at[4], recv_sem=xrecv.at[4],
            device_id=partner, device_id_type=MESH,
        )
    )
    exchanges[0].start()

    small[1].wait()
    small[2].wait()
    own_len = jnp.zeros((8, 128), jnp.int32)
    sub8 = lax.broadcasted_iota(jnp.int32, (8, 128), 0)
    for s in range(4):
        own_len = jnp.where(sub8 % 4 == s, len_ref[s], own_len)
    lens[...] = own_len

    exchanges[4].start()

    lane = lax.broadcasted_iota(jnp.int32, (1, 128), 1)
    lane_row = ((lane // 64) * 2 + (lane // 16) % 2) * 4 + lane % 4
    lane_g = ((lane // 32) % 2) * 4 + (lane // 4) % 4
    sub = lax.broadcasted_iota(jnp.int32, (512, 128), 0)
    sub_row = (sub // 128) * 16 + ((sub // 64) % 2) * 8 + ((sub // 16) % 2) * 4 + sub % 4
    sub_g = ((sub // 32) % 2) * 4 + (sub // 4) % 4
    sub_code = sub_row * 8 + sub_g
    for xs in range(4):
        held = jnp.zeros((1, 128), jnp.int32)
        for r in range(16):
            held = jnp.where(lane_row == r, asg_ref[xs * 16 + r], held)
        code = held * 8 + lane_g
        perm[:, xs * 128 : (xs + 1) * 128] = jnp.where(sub_code == code, 1.0, 0.0).astype(BF)

    me_rows = pl.ds(pl.multiple_of((x * 4 + y) * 32, 32), 32)
    for k in range(4):
        pltpu.make_async_copy(q1.at[k], q1.at[k], zrecv.at[k]).wait()
    for i in range(4):
        k = head_at(y, i)
        pltpu.make_async_copy(q1.at[k], q2.at[k, me_rows], grecv.at[k]).start()
        for dx, dy in AROUND:
            y_ = (y + dy) % 4
            k = head_at(y_, i)
            pltpu.make_async_remote_copy(
                src_ref=q1.at[k], dst_ref=q2.at[k, me_rows], send_sem=gsend, recv_sem=grecv.at[k],
                device_id=dev((x + dx) % 4, y_, z, c), device_id_type=MESH,
            ).start()
        if i < 3:
            exchanges[(2, 1, 3)[i]].start()

    exchanges[4].wait_recv()
    rows = lax.broadcasted_iota(jnp.int32, (64, 128), 0)
    lanes = lax.broadcasted_iota(jnp.int32, (64, 128), 1)
    lens_own = jnp.concatenate([lens[...]] * 8, axis=0)
    lens_other = jnp.concatenate([lensall[...]] * 8, axis=0)
    row_c = (rows // 16) % 2
    live = jnp.where(row_c == c, lens_own, lens_other) - tp * 128
    row_slot = row_c * 4 + rows % 4
    for s in range(8):
        limit = jnp.where(row_slot == s, live, 0)
        bias[:, s * 128 : s * 128 + 128] = jnp.where(lanes < limit, 0.0, NEG)

    for i in range(4):
        loads[i].wait()
        exchanges[i].wait_recv()

    square = (128, 128)
    eye = lax.broadcasted_iota(jnp.int32, square, 0) == lax.broadcasted_iota(jnp.int32, square, 1)
    ones = jnp.ones((1024, 128), BF)
    stat_row = lax.broadcasted_iota(jnp.int32, (16, 128), 0)

    def as_row(column):
        return jnp.sum(jnp.where(eye, column, 0.0), axis=0, keepdims=True)

    def stat_tile(top, total):
        hi = total.astype(BF).astype(F32)
        return jnp.where(stat_row == 0, top, jnp.where(stat_row == 1, hi, total - hi)).astype(BF)

    def weights(scores, top):
        return jnp.exp2(scores - top).astype(BF)

    def largest(scores):
        return jnp.max(scores, axis=1, keepdims=True)

    def head(i, _):
        k = head_at(y, i)
        cols = pl.ds(pl.multiple_of(k * 128, 128), 128)
        pltpu.make_async_copy(q2.at[k], q2.at[k], grecv.at[k]).wait()
        qs[...] = dot(perm[...], q2[k], NN).astype(BF)
        chunks = [(x + a) % 4 for a in (1, 3, 2, 0)]
        parts = [qs[pl.ds(pl.multiple_of(j * 128, 128), 128), :] for j in chunks]
        keys = kbuf[:, cols]
        values = jnp.concatenate([vbuf[:, cols], ones], axis=1)
        suffix_keys = skbuf[:, :, cols].reshape(1024, 128)
        suffix_values = jnp.concatenate([svbuf[:, :, cols].reshape(1024, 128), ones], axis=1)

        s0 = dot(jnp.concatenate(parts[:2], axis=0), keys, NT) * C2
        s1 = dot(jnp.concatenate(parts[2:], axis=0), keys, NT) * C2
        own = pl.ds(pl.multiple_of(x * 128 + yh * 64, 64), 64)
        ss = dot(qs[own, :], suffix_keys, NT) * C2 + bias[...]

        def send(a):
            pltpu.make_async_remote_copy(
                src_ref=sbuf.at[i * 4 + a], dst_ref=r1.at[x * 4 + y], send_sem=rsend, recv_sem=rrecv,
                device_id=dev(chunks[a], k, z, c), device_id_type=MESH,
            ).start()

        def put(a, m, n):
            sbuf[i * 4 + a, :128, :] = n[:, :128].astype(BF)
            sbuf[i * 4 + a, 128:, :] = stat_tile(as_row(m), as_row(n[:, 128:]))

        m0 = largest(s0).astype(BF).astype(F32)
        n0 = dot(weights(s0, m0), values, NN)
        put(0, m0[:128], n0[:128])
        send(0)
        put(1, m0[128:], n0[128:])
        send(1)

        m1, ms = largest(s1), largest(ss)
        low = jnp.full((64, 1), NEG, F32)
        ms = jnp.concatenate([jnp.where(yh == 0, ms, low), jnp.where(yh == 0, low, ms)], axis=0)
        m1 = jnp.concatenate([m1[:128], jnp.maximum(m1[128:], ms)], axis=0).astype(BF).astype(F32)
        n1 = dot(weights(s1, m1), values, NN)
        ns = dot(weights(ss, jnp.where(yh == 0, m1[128:192], m1[192:])), suffix_values, NN)
        ns = jnp.concatenate([jnp.where(yh == 0, ns, 0.0), jnp.where(yh == 0, 0.0, ns)], axis=0)
        put(2, m1[:128], n1[:128])
        send(2)
        put(3, m1[128:], n1[128:] + ns)
        pl.when(i < 3)(lambda: send(3))
        return 0

    lax.fori_loop(0, 4, head, 0)
    pltpu.make_async_copy(sbuf.at[15], r1.at[x * 4 + y], rrecv).start()

    pltpu.make_async_copy(r1, r1, rrecv).wait()
    stats = [r1[i, 128:, :].astype(F32) for i in range(16)]
    top = functools.reduce(jnp.maximum, [s[0:1] for s in stats])
    ws = [jnp.exp2(s[0:1] - top) for s in stats]
    total = functools.reduce(jnp.add, [w * (s[1:2] + s[2:3]) for w, s in zip(ws, stats)])
    his = [w.astype(BF).astype(F32) for w in ws]
    spread = [
        jnp.concatenate([jnp.where(eye, w, 0.0).astype(BF) for w in part], axis=1)
        for part in (his, [w - h for w, h in zip(ws, his)])
    ]
    both = dot(jnp.concatenate(spread, axis=0), jnp.concatenate([r1[i, :128, :] for i in range(16)], axis=0), NN)
    flat = (both[:128] + both[128:]).astype(BF)
    stat = stat_tile(top, total)
    for d in range(8):
        s2[d, :16, :] = flat[d * 16 : d * 16 + 16, :]
        s2[d, 16:, :] = stat

    zt = 4 * c + y
    for o in range(1, 8):
        y_, c_ = (y + o // 2) % 4, (c + o % 2) % 2
        pltpu.make_async_remote_copy(
            src_ref=s2.at[y_ * 2 + c_], dst_ref=r2.at[z], send_sem=tsend.at[0], recv_sem=trecv,
            device_id=dev(x, y_, zt, c_), device_id_type=MESH,
        ).start()

    @pl.when(zt == z)
    def _():
        pltpu.make_async_copy(s2.at[y * 2 + c], r2.at[z], trecv).start()

    @pl.when(zt != z)
    def _():
        pltpu.make_async_remote_copy(
            src_ref=s2.at[y * 2 + c], dst_ref=r2.at[z], send_sem=tsend.at[1], recv_sem=trecv,
            device_id=dev(x, y, zt, c), device_id_type=MESH,
        ).start()

    pltpu.make_async_copy(r2, r2, trecv).wait()

    offset = y * 32 + c * 16
    pick = lax.broadcasted_iota(jnp.int32, (16, 128), 1) == lax.broadcasted_iota(jnp.int32, (16, 128), 0) + offset
    stats = [r2[i, 16:, :].astype(F32) for i in range(8)]
    m2 = functools.reduce(jnp.maximum, [s[0:1] for s in stats])
    ws = [jnp.exp2(s[0:1] - m2) for s in stats]
    total = functools.reduce(jnp.add, [w * (s[1:2] + s[2:3]) for w, s in zip(ws, stats)])
    acc = jnp.zeros((16, 128), F32)
    for i in range(8):
        column = jnp.sum(jnp.where(pick, ws[i], 0.0), axis=1, keepdims=True)
        acc = acc + column * r2[i, :16, :].astype(F32)
    column = jnp.sum(jnp.where(pick, total, 0.0), axis=1, keepdims=True)
    acc = acc / column
    for g in range(4):
        out_ref[:, g * 128 : (g + 1) * 128] = acc[g * 4 : g * 4 + 4, :].astype(BF)

    for i in range(5):
        exchanges[i].wait_send()
    pltpu.make_async_copy(s2.at[pl.ds(0, 7), pl.ds(0, 16)], s2.at[pl.ds(0, 7), pl.ds(0, 16)], zsend.at[0]).wait()

    @pl.when(hz != c)
    def _():
        pltpu.make_async_copy(q0, q0, zsend.at[1]).wait()

    most = q2.at[:, pl.ds(0, 480)]
    pltpu.make_async_copy(most, most, gsend).wait()
    most = sbuf.at[pl.ds(0, 15)]
    pltpu.make_async_copy(most, most, rsend).wait()
    most = s2.at[pl.ds(0, 7)]
    pltpu.make_async_copy(most, most, tsend.at[0]).wait()

    @pl.when(zt != z)
    def _():
        pltpu.make_async_copy(s2.at[0], s2.at[0], tsend.at[1]).wait()


def shards(queries, assignment, prefix_keys, prefix_values, suffix_keys, suffix_values, lengths):
    vmem, far = pl.BlockSpec(memory_space=pltpu.VMEM), pl.BlockSpec(memory_space=pl.ANY)
    dma = pltpu.SemaphoreType.DMA
    return pl.pallas_call(
        kernel,
        out_shape=jax.ShapeDtypeStruct(queries.shape, BF),
        in_specs=[far, far, far, far, far, far, far],
        out_specs=vmem,
        scratch_shapes=[
            pltpu.VMEM((1024, 512), BF),
            pltpu.VMEM((1024, 512), BF),
            pltpu.VMEM((8, 128, 512), BF),
            pltpu.VMEM((8, 128, 512), BF),
            pltpu.VMEM((16, 128), F32),
            pltpu.VMEM((16, 128), BF),
            pltpu.VMEM((4, 32, 128), BF),
            pltpu.VMEM((4, 512, 128), BF),
            pltpu.VMEM((512, 128), BF),
            pltpu.VMEM((512, 512), BF),
            pltpu.VMEM((8, 128), jnp.int32),
            pltpu.VMEM((8, 128), jnp.int32),
            pltpu.VMEM((64, 1024), F32),
            pltpu.VMEM((16, 144, 128), BF),
            pltpu.VMEM((16, 144, 128), BF),
            pltpu.VMEM((8, 32, 128), BF),
            pltpu.VMEM((8, 32, 128), BF),
            pltpu.VMEM((4, 512), BF),
            pltpu.SMEM((64,), jnp.int32),
            pltpu.SMEM((4,), jnp.int32),
            dma((3,)),
            dma((4,)),
            dma((5,)),
            dma((5,)),
            dma((2,)),
            dma((4,)),
            dma(()),
            dma((4,)),
            dma(()),
            dma(()),
            dma((2,)),
            dma(()),
        ],
        compiler_params=pltpu.CompilerParams(
            collective_id=0, has_side_effects=True, vmem_limit_bytes=48 * 1024 * 1024
        ),
        cost_estimate=pl.CostEstimate(flops=1_300_000_000, bytes_accessed=4_300_000, transcendentals=2_600_000),
    )(
        *(
            pltpu.with_memory_space_constraint(operand, pltpu.HBM)
            for operand in (
                queries, assignment, lengths, prefix_keys, prefix_values, suffix_keys, suffix_values
            )
        )
    )


def solution(mesh):
    in_specs = (
        P("rep", "tp"),
        P(),
        P(("rep", "tp"), None),
        P(("rep", "tp"), None),
        P("rep", "tp", None),
        P("rep", "tp", None),
        P("rep"),
    )
    out_specs = P("rep", "tp")
    return jax.shard_map(shards, mesh=mesh, in_specs=in_specs, out_specs=out_specs, check_vma=False)
```

```python
import functools
import math

import jax
import jax.numpy as jnp
from jax import lax
from jax.experimental import pallas as pl
from jax.experimental.pallas import tpu as pltpu
from jax.sharding import PartitionSpec as P

MESH = pl.DeviceIdType.MESH
HD = 128
HEADS_CORE = 4
C2 = math.log2(math.e) * HD ** (-0.5)
NEG = -(2.0**100)
BF = jnp.bfloat16
F32 = jnp.float32
NT = (((1,), (1,)), ((), ()))
NN = (((1,), (0,)), ((), ()))
AROUND = (
    (1, 0), (3, 0), (0, 1), (0, 3), (2, 0), (1, 1), (3, 1), (2, 1), (0, 2), (1, 2), (3, 2), (2, 2), (1, 3), (3, 3), (2, 3),
)


def rem(a, n):
    return lax.rem(a, jnp.int32(n))


def div(a, n):
    return lax.div(a, jnp.int32(n))


def dot(a, b, dims):
    return lax.dot_general(a, b, dims, preferred_element_type=F32)


def kernel(
    q_hbm, asg_hbm, len_hbm, pk, pv, sk, sv, out_ref,
    kbuf, vbuf, skbuf, svbuf, qf, q0, q1, q2, qs, perm, lens, lensall, bias, s0buf, sbuf, r1, s2, r2,
    q_ref, asg_ref, len_ref, smallsem, ldsem, xsend, xrecv, zsend, zrecv, gsend, grecv, rsend, rrecv, tsend, trecv,
):
    rep, tp = lax.axis_index("rep"), lax.axis_index("tp")
    x, yh, c = div(rep, 4), rem(div(rep, 2), 2), rem(rep, 2)
    z, yl = div(tp, 2), rem(tp, 2)
    y = yh * 2 + yl
    hz = div(z, 4)

    def head_at(y_, i):
        return rem(y_ + 1 + i + c * (2 - 2 * i), 4)

    def dev(x_, y_, z_, c_):
        return (x_ * 4 + div(y_, 2) * 2 + c_, z_ * 2 + rem(y_, 2))

    small = [
        pltpu.make_async_copy(src, dst, smallsem.at[i])
        for i, (src, dst) in enumerate(((q_hbm, q_ref), (asg_hbm, asg_ref), (len_hbm, len_ref)))
    ]
    for copy in small:
        copy.start()

    mine = pl.multiple_of(c * 512, 512)
    theirs = pl.multiple_of((1 - c) * 512, 512)
    rows2 = pl.multiple_of(c * 512, 512)
    pairs = ((pk, kbuf), (sk, skbuf), (pv, vbuf), (sv, svbuf))

    def local_dst(i):
        buf = pairs[i][1]
        return buf.at[pl.ds(rows2, 512)] if i % 2 == 0 else buf.at[pl.ds(c * 4, 4)]

    def src_of(i, cols):
        ref = pairs[i][0]
        return ref.at[:, pl.ds(cols, 512)] if i % 2 == 0 else ref.at[:, :, pl.ds(cols, 512)]

    loads = [pltpu.make_async_copy(src_of(i, mine), local_dst(i), ldsem.at[i]) for i in range(4)]
    barrier = pltpu.get_barrier_semaphore()

    def greet(x_, y_, z_, c_):
        pl.semaphore_signal(barrier, inc=1, device_id=dev(x_, y_, z_, c_), device_id_type=MESH)

    partner = dev(x, y, z, 1 - c)
    for k in range(4):
        for cs in range(2):
            zs = 4 * c + k

            @pl.when(jnp.logical_or(zs != z, cs != c))
            def _(zs=zs, cs=cs):
                greet(x, y, zs, cs)

    greet(x, y, z, 1 - c)
    for o in range(1, 16):
        greet(rem(x + o // 4, 4), rem(y + o % 4, 4), z, c)
    for zs in range(8):

        @pl.when(jnp.logical_or(jnp.logical_or(zs != z, rem(z, 4) != y), hz != c))
        def _(zs=zs):
            greet(x, rem(z, 4), zs, hz)

    for copy in loads:
        copy.start()

    small[0].wait()
    q = q_ref[...].astype(F32)
    for g in range(4):
        qf[g * 4 : g * 4 + 4, :] = q[:, g * 128 : (g + 1) * 128]
    q0[...] = qf[...].astype(BF)

    n_z = jnp.where(hz == c, 7, 8)
    n_t = jnp.where(4 * c + y == z, 7, 8)
    pl.semaphore_wait(barrier, 16 + n_z + n_t)

    def ztile(ref_z):
        return q1.at[rem(ref_z, 4), pl.ds(pl.multiple_of(c * 16, 16), 16)]

    for o in (4, 3, 5, 2, 6, 1, 7):
        z_ = rem(z + o, 8)
        pltpu.make_async_remote_copy(
            src_ref=q0, dst_ref=ztile(z), send_sem=zsend.at[0], recv_sem=zrecv.at[rem(z, 4)],
            device_id=dev(x, y, z_, hz), device_id_type=MESH,
        ).start()

    @pl.when(hz == c)
    def _():
        pltpu.make_async_copy(q0, ztile(z), zrecv.at[rem(z, 4)]).start()

    @pl.when(hz != c)
    def _():
        pltpu.make_async_remote_copy(
            src_ref=q0, dst_ref=ztile(z), send_sem=zsend.at[1], recv_sem=zrecv.at[rem(z, 4)],
            device_id=partner, device_id_type=MESH,
        ).start()

    exchanges = [
        pltpu.make_async_remote_copy(
            src_ref=src_of(i, theirs), dst_ref=local_dst(i), send_sem=xsend.at[i], recv_sem=xrecv.at[i],
            device_id=partner, device_id_type=MESH,
        )
        for i in range(4)
    ]
    exchanges.append(
        pltpu.make_async_remote_copy(
            src_ref=lens, dst_ref=lensall, send_sem=xsend.at[4], recv_sem=xrecv.at[4],
            device_id=partner, device_id_type=MESH,
        )
    )
    exchanges[0].start()

    small[1].wait()
    small[2].wait()
    own_len = jnp.zeros((8, 128), jnp.int32)
    sub8 = lax.broadcasted_iota(jnp.int32, (8, 128), 0)
    for s in range(4):
        own_len = jnp.where((sub8 & 3) == s, len_ref[s], own_len)
    lens[...] = own_len

    exchanges[4].start()

    lane = lax.broadcasted_iota(jnp.int32, (1, 128), 1)
    lane_row = ((lane >> 6) * 2 + ((lane >> 4) & 1)) * 4 + (lane & 3)
    lane_g = ((lane >> 5) & 1) * 4 + ((lane >> 2) & 3)
    sub = lax.broadcasted_iota(jnp.int32, (512, 128), 0)
    sub_row = (sub >> 6) * 8 + ((sub >> 4) & 1) * 4 + (sub & 3)
    sub_g = ((sub >> 5) & 1) * 4 + ((sub >> 2) & 3)
    sub_code = sub_row * 8 + sub_g
    for xs in range(4):
        held = jnp.zeros((1, 128), jnp.int32)
        for r in range(16):
            held = jnp.where(lane_row == r, asg_ref[xs * 16 + r], held)
        code = held * 8 + lane_g
        perm[:, xs * 128 : (xs + 1) * 128] = jnp.where(sub_code == code, 1.0, 0.0).astype(BF)

    me_rows = pl.ds(pl.multiple_of((x * 4 + y) * 32, 32), 32)
    for k in range(4):
        pltpu.make_async_copy(q1.at[k], q1.at[k], zrecv.at[k]).wait()
    for i in range(4):
        k = head_at(y, i)
        pltpu.make_async_copy(q1.at[k], q2.at[k, me_rows], grecv.at[k]).start()
        for dx, dy in AROUND:
            y_ = rem(y + dy, 4)
            k = head_at(y_, i)
            pltpu.make_async_remote_copy(
                src_ref=q1.at[k], dst_ref=q2.at[k, me_rows], send_sem=gsend, recv_sem=grecv.at[k],
                device_id=dev(rem(x + dx, 4), y_, z, c), device_id_type=MESH,
            ).start()
        if i < 3:
            exchanges[(2, 1, 3)[i]].start()

    exchanges[4].wait_recv()
    rows = lax.broadcasted_iota(jnp.int32, (64, 128), 0)
    lanes = lax.broadcasted_iota(jnp.int32, (64, 128), 1)
    lens_own = jnp.concatenate([lens[...]] * 8, axis=0)
    lens_other = jnp.concatenate([lensall[...]] * 8, axis=0)
    row_c = (rows >> 4) & 1
    live = jnp.where(row_c == c, lens_own, lens_other) - tp * 128
    row_slot = row_c * 4 + (rows & 3)
    for s in range(8):
        limit = jnp.where(row_slot == s, live, 0)
        bias[:, s * 128 : s * 128 + 128] = jnp.where(lanes < limit, 0.0, NEG)

    for i in range(4):
        loads[i].wait()
        exchanges[i].wait_recv()

    square = (128, 128)
    eye = lax.broadcasted_iota(jnp.int32, square, 0) == lax.broadcasted_iota(jnp.int32, square, 1)
    ones = jnp.ones((1024, 128), BF)
    stat_row = lax.broadcasted_iota(jnp.int32, (16, 128), 0)

    def as_row(column):
        return jnp.sum(jnp.where(eye, column, 0.0), axis=0, keepdims=True)

    def stat_tile(top, total):
        hi = total.astype(BF).astype(F32)
        return jnp.where(stat_row == 0, top, jnp.where(stat_row == 1, hi, total - hi)).astype(BF)

    def weights(scores, top):
        return jnp.exp2(scores - top).astype(BF)

    def largest(scores):
        return jnp.max(scores, axis=1, keepdims=True)

    def begin(i):
        k = head_at(y, i)
        pltpu.make_async_copy(q2.at[k], q2.at[k], grecv.at[k]).wait()
        qs[...] = dot(perm[...], q2[k], NN).astype(BF)
        s0buf[...] = dot(rows_of(0, 1), kbuf[:, columns(k)], NT) * C2

    def columns(k):
        return pl.ds(pl.multiple_of(k * 128, 128), 128)

    chunks = [rem(x + a, 4) for a in (1, 3, 2, 0)]

    def rows_of(*which):
        places = [pl.ds(pl.multiple_of(chunks[a] * 128, 128), 128) for a in which]
        return jnp.concatenate([qs[place, :] for place in places], axis=0)

    own = pl.ds(pl.multiple_of(x * 128 + yh * 64, 64), 64)
    low = jnp.full((64, 1), NEG, F32)

    def head(i, last):
        k = head_at(y, i)
        cols = columns(k)
        values = jnp.concatenate([vbuf[:, cols], ones], axis=1)
        suffix_keys = skbuf[:, :, cols].reshape(1024, 128)
        suffix_values = jnp.concatenate([svbuf[:, :, cols].reshape(1024, 128), ones], axis=1)

        def send(a):
            pltpu.make_async_remote_copy(
                src_ref=sbuf.at[i * 4 + a], dst_ref=r1.at[x * 4 + y], send_sem=rsend, recv_sem=rrecv,
                device_id=dev(chunks[a], k, z, c), device_id_type=MESH,
            ).start()

        def put(a, m, n):
            sbuf[i * 4 + a, :128, :] = n[:, :128].astype(BF)
            sbuf[i * 4 + a, 128:, :] = stat_tile(as_row(m), as_row(n[:, 128:]))

        s1 = dot(rows_of(2, 3), kbuf[:, cols], NT) * C2
        ss = dot(qs[own, :], suffix_keys, NT) * C2 + bias[...]
        s0 = s0buf[...]
        m0 = largest(s0).astype(BF).astype(F32)
        n0 = dot(weights(s0, m0), values, NN)
        put(0, m0[:128], n0[:128])
        send(0)
        put(1, m0[128:], n0[128:])
        send(1)
        if not last:
            begin(i + 1)

        m1, ms = largest(s1), largest(ss)
        ms = jnp.concatenate([jnp.where(yh == 0, ms, low), jnp.where(yh == 0, low, ms)], axis=0)
        m1 = jnp.concatenate([m1[:128], jnp.maximum(m1[128:], ms)], axis=0).astype(BF).astype(F32)
        n1 = dot(weights(s1, m1), values, NN)
        ns = dot(weights(ss, jnp.where(yh == 0, m1[128:192], m1[192:])), suffix_values, NN)
        ns = jnp.concatenate([jnp.where(yh == 0, ns, 0.0), jnp.where(yh == 0, 0.0, ns)], axis=0)
        put(2, m1[:128], n1[:128])
        send(2)
        put(3, m1[128:], n1[128:] + ns)
        if last:
            pltpu.make_async_copy(sbuf.at[15], r1.at[x * 4 + y], rrecv).start()
        else:
            send(3)
        return 0

    begin(0)
    lax.fori_loop(0, 3, lambda i, _: head(i, False), 0)
    head(3, True)

    pltpu.make_async_copy(r1, r1, rrecv).wait()
    stats = [r1[i, 128:, :].astype(F32) for i in range(16)]
    top = functools.reduce(jnp.maximum, [s[0:1] for s in stats])
    ws = [jnp.exp2(s[0:1] - top) for s in stats]
    total = functools.reduce(jnp.add, [w * (s[1:2] + s[2:3]) for w, s in zip(ws, stats)])
    his = [w.astype(BF).astype(F32) for w in ws]
    spread = [
        jnp.concatenate([jnp.where(eye, w, 0.0).astype(BF) for w in part], axis=1)
        for part in (his, [w - h for w, h in zip(ws, his)])
    ]
    both = dot(jnp.concatenate(spread, axis=0), jnp.concatenate([r1[i, :128, :] for i in range(16)], axis=0), NN)
    flat = (both[:128] + both[128:]).astype(BF)
    stat = stat_tile(top, total)
    for d in range(8):
        s2[d, :16, :] = flat[d * 16 : d * 16 + 16, :]
        s2[d, 16:, :] = stat

    zt = 4 * c + y
    for o in range(1, 8):
        y_, c_ = rem(y + o // 2, 4), rem(c + o % 2, 2)
        pltpu.make_async_remote_copy(
            src_ref=s2.at[y_ * 2 + c_], dst_ref=r2.at[z], send_sem=tsend.at[0], recv_sem=trecv,
            device_id=dev(x, y_, zt, c_), device_id_type=MESH,
        ).start()

    @pl.when(zt == z)
    def _():
        pltpu.make_async_copy(s2.at[y * 2 + c], r2.at[z], trecv).start()

    @pl.when(zt != z)
    def _():
        pltpu.make_async_remote_copy(
            src_ref=s2.at[y * 2 + c], dst_ref=r2.at[z], send_sem=tsend.at[1], recv_sem=trecv,
            device_id=dev(x, y, zt, c), device_id_type=MESH,
        ).start()

    pltpu.make_async_copy(r2, r2, trecv).wait()

    offset = y * 32 + c * 16
    pick = lax.broadcasted_iota(jnp.int32, (16, 128), 1) == lax.broadcasted_iota(jnp.int32, (16, 128), 0) + offset
    stats = [r2[i, 16:, :].astype(F32) for i in range(8)]
    m2 = functools.reduce(jnp.maximum, [s[0:1] for s in stats])
    ws = [jnp.exp2(s[0:1] - m2) for s in stats]
    total = functools.reduce(jnp.add, [w * (s[1:2] + s[2:3]) for w, s in zip(ws, stats)])
    acc = jnp.zeros((16, 128), F32)
    for i in range(8):
        column = jnp.sum(jnp.where(pick, ws[i], 0.0), axis=1, keepdims=True)
        acc = acc + column * r2[i, :16, :].astype(F32)
    column = jnp.sum(jnp.where(pick, total, 0.0), axis=1, keepdims=True)
    acc = acc / column
    for g in range(4):
        out_ref[:, g * 128 : (g + 1) * 128] = acc[g * 4 : g * 4 + 4, :].astype(BF)

    for i in range(5):
        exchanges[i].wait_send()
    pltpu.make_async_copy(s2.at[pl.ds(0, 7), pl.ds(0, 16)], s2.at[pl.ds(0, 7), pl.ds(0, 16)], zsend.at[0]).wait()

    @pl.when(hz != c)
    def _():
        pltpu.make_async_copy(q0, q0, zsend.at[1]).wait()

    most = q2.at[:, pl.ds(0, 480)]
    pltpu.make_async_copy(most, most, gsend).wait()
    most = sbuf.at[pl.ds(0, 15)]
    pltpu.make_async_copy(most, most, rsend).wait()
    most = s2.at[pl.ds(0, 7)]
    pltpu.make_async_copy(most, most, tsend.at[0]).wait()

    @pl.when(zt != z)
    def _():
        pltpu.make_async_copy(s2.at[0], s2.at[0], tsend.at[1]).wait()


def shards(queries, assignment, prefix_keys, prefix_values, suffix_keys, suffix_values, lengths):
    vmem, far = pl.BlockSpec(memory_space=pltpu.VMEM), pl.BlockSpec(memory_space=pl.ANY)
    dma = pltpu.SemaphoreType.DMA
    return pl.pallas_call(
        kernel,
        out_shape=jax.ShapeDtypeStruct(queries.shape, BF),
        in_specs=[far, far, far, far, far, far, far],
        out_specs=vmem,
        scratch_shapes=[
            pltpu.VMEM((1024, 512), BF),
            pltpu.VMEM((1024, 512), BF),
            pltpu.VMEM((8, 128, 512), BF),
            pltpu.VMEM((8, 128, 512), BF),
            pltpu.VMEM((16, 128), F32),
            pltpu.VMEM((16, 128), BF),
            pltpu.VMEM((4, 32, 128), BF),
            pltpu.VMEM((4, 512, 128), BF),
            pltpu.VMEM((512, 128), BF),
            pltpu.VMEM((512, 512), BF),
            pltpu.VMEM((8, 128), jnp.int32),
            pltpu.VMEM((8, 128), jnp.int32),
            pltpu.VMEM((64, 1024), F32),
            pltpu.VMEM((256, 1024), F32),
            pltpu.VMEM((16, 144, 128), BF),
            pltpu.VMEM((16, 144, 128), BF),
            pltpu.VMEM((8, 32, 128), BF),
            pltpu.VMEM((8, 32, 128), BF),
            pltpu.VMEM((4, 512), BF),
            pltpu.SMEM((64,), jnp.int32),
            pltpu.SMEM((4,), jnp.int32),
            dma((3,)),
            dma((4,)),
            dma((5,)),
            dma((5,)),
            dma((2,)),
            dma((4,)),
            dma(()),
            dma((4,)),
            dma(()),
            dma(()),
            dma((2,)),
            dma(()),
        ],
        compiler_params=pltpu.CompilerParams(
            collective_id=0, has_side_effects=True, vmem_limit_bytes=48 * 1024 * 1024
        ),
        cost_estimate=pl.CostEstimate(flops=1_300_000_000, bytes_accessed=4_300_000, transcendentals=2_600_000),
    )(
        *(
            pltpu.with_memory_space_constraint(operand, pltpu.HBM)
            for operand in (
                queries, assignment, lengths, prefix_keys, prefix_values, suffix_keys, suffix_values
            )
        )
    )


def solution(mesh):
    in_specs = (
        P("rep", "tp"),
        P(),
        P(("rep", "tp"), None),
        P(("rep", "tp"), None),
        P("rep", "tp", None),
        P("rep", "tp", None),
        P("rep"),
    )
    out_specs = P("rep", "tp")
    return jax.shard_map(shards, mesh=mesh, in_specs=in_specs, out_specs=out_specs, check_vma=False)
```

```python
import functools
import math

import jax
import jax.numpy as jnp
from jax import lax
from jax.experimental import pallas as pl
from jax.experimental.pallas import tpu as pltpu
from jax.sharding import PartitionSpec as P

MESH = pl.DeviceIdType.MESH
HD = 128
HEADS_CORE = 4
C2 = math.log2(math.e) * HD ** (-0.5)
NEG = -(2.0**100)
BF = jnp.bfloat16
F32 = jnp.float32
NT = (((1,), (1,)), ((), ()))
NN = (((1,), (0,)), ((), ()))
AROUND = (
    (1, 0), (3, 0), (0, 1), (0, 3), (2, 0), (1, 1), (3, 1), (2, 1), (0, 2), (1, 2), (3, 2), (2, 2), (1, 3), (3, 3), (2, 3),
)


def rem(a, n):
    return lax.rem(a, jnp.int32(n))


def div(a, n):
    return lax.div(a, jnp.int32(n))


def dot(a, b, dims):
    return lax.dot_general(a, b, dims, preferred_element_type=F32)


def kernel(
    q_hbm, asg_hbm, len_hbm, pk, pv, sk, sv, out_ref,
    kbuf, vbuf, skbuf, svbuf, qf, q0, q1, q2, qs, perm, lens, lensall, bias, s0buf, sbuf, r1, s2, r2,
    q_ref, asg_ref, len_ref, smallsem, ldsem, xsend, xrecv, zsend, zrecv, gsend, grecv, rsend, rrecv, tsend, trecv,
):
    rep, tp = lax.axis_index("rep"), lax.axis_index("tp")
    x, yh, c = div(rep, 4), rem(div(rep, 2), 2), rem(rep, 2)
    z, yl = div(tp, 2), rem(tp, 2)
    y = yh * 2 + yl
    hz = div(z, 4)

    def head_at(y_, i):
        return rem(y_ + 1 + i + c * (2 - 2 * i), 4)

    def dev(x_, y_, z_, c_):
        return (x_ * 4 + div(y_, 2) * 2 + c_, z_ * 2 + rem(y_, 2))

    small = [
        pltpu.make_async_copy(src, dst, smallsem.at[i])
        for i, (src, dst) in enumerate(((q_hbm, q_ref), (asg_hbm, asg_ref), (len_hbm, len_ref)))
    ]
    for copy in small:
        copy.start()

    mine = pl.multiple_of(c * 512, 512)
    theirs = pl.multiple_of((1 - c) * 512, 512)
    rows2 = pl.multiple_of(c * 512, 512)
    pairs = ((pk, kbuf), (sk, skbuf), (pv, vbuf), (sv, svbuf))

    def local_dst(i):
        buf = pairs[i][1]
        return buf.at[pl.ds(rows2, 512)] if i % 2 == 0 else buf.at[pl.ds(c * 4, 4)]

    def src_of(i, cols):
        ref = pairs[i][0]
        return ref.at[:, pl.ds(cols, 512)] if i % 2 == 0 else ref.at[:, :, pl.ds(cols, 512)]

    loads = [pltpu.make_async_copy(src_of(i, mine), local_dst(i), ldsem.at[i]) for i in range(4)]
    barrier = pltpu.get_barrier_semaphore()

    def greet(x_, y_, z_, c_):
        pl.semaphore_signal(barrier, inc=1, device_id=dev(x_, y_, z_, c_), device_id_type=MESH)

    partner = dev(x, y, z, 1 - c)
    for k in range(4):
        for cs in range(2):
            zs = 4 * c + k

            @pl.when(jnp.logical_or(zs != z, cs != c))
            def _(zs=zs, cs=cs):
                greet(x, y, zs, cs)

    greet(x, y, z, 1 - c)
    for o in range(1, 16):
        greet(rem(x + o // 4, 4), rem(y + o % 4, 4), z, c)
    for zs in range(8):

        @pl.when(jnp.logical_or(jnp.logical_or(zs != z, rem(z, 4) != y), hz != c))
        def _(zs=zs):
            greet(x, rem(z, 4), zs, hz)

    for copy in loads:
        copy.start()

    small[0].wait()
    q = q_ref[...].astype(F32)
    for g in range(4):
        qf[g * 4 : g * 4 + 4, :] = q[:, g * 128 : (g + 1) * 128]
    q0[...] = qf[...].astype(BF)

    n_z = jnp.where(hz == c, 7, 8)
    n_t = jnp.where(4 * c + y == z, 7, 8)
    pl.semaphore_wait(barrier, 16 + n_z + n_t)

    def ztile(ref_z):
        return q1.at[rem(ref_z, 4), pl.ds(pl.multiple_of(c * 16, 16), 16)]

    for o in (4, 3, 5, 2, 6, 1, 7):
        z_ = rem(z + o, 8)
        pltpu.make_async_remote_copy(
            src_ref=q0, dst_ref=ztile(z), send_sem=zsend.at[0], recv_sem=zrecv.at[rem(z, 4)],
            device_id=dev(x, y, z_, hz), device_id_type=MESH,
        ).start()

    @pl.when(hz == c)
    def _():
        pltpu.make_async_copy(q0, ztile(z), zrecv.at[rem(z, 4)]).start()

    @pl.when(hz != c)
    def _():
        pltpu.make_async_remote_copy(
            src_ref=q0, dst_ref=ztile(z), send_sem=zsend.at[1], recv_sem=zrecv.at[rem(z, 4)],
            device_id=partner, device_id_type=MESH,
        ).start()

    exchanges = [
        pltpu.make_async_remote_copy(
            src_ref=src_of(i, theirs), dst_ref=local_dst(i), send_sem=xsend.at[i], recv_sem=xrecv.at[i],
            device_id=partner, device_id_type=MESH,
        )
        for i in range(4)
    ]
    exchanges.append(
        pltpu.make_async_remote_copy(
            src_ref=lens, dst_ref=lensall, send_sem=xsend.at[4], recv_sem=xrecv.at[4],
            device_id=partner, device_id_type=MESH,
        )
    )
    exchanges[0].start()

    small[1].wait()
    small[2].wait()
    own_len = jnp.zeros((8, 128), jnp.int32)
    sub8 = lax.broadcasted_iota(jnp.int32, (8, 128), 0)
    for s in range(4):
        own_len = jnp.where((sub8 & 3) == s, len_ref[s], own_len)
    lens[...] = own_len

    exchanges[4].start()

    lane = lax.broadcasted_iota(jnp.int32, (1, 128), 1)
    lane_row = ((lane >> 6) * 2 + ((lane >> 4) & 1)) * 4 + (lane & 3)
    lane_g = ((lane >> 5) & 1) * 4 + ((lane >> 2) & 3)
    sub = lax.broadcasted_iota(jnp.int32, (512, 128), 0)
    sub_row = (sub >> 6) * 8 + ((sub >> 4) & 1) * 4 + (sub & 3)
    sub_g = ((sub >> 5) & 1) * 4 + ((sub >> 2) & 3)
    sub_code = sub_row * 8 + sub_g
    for xs in range(4):
        held = jnp.zeros((1, 128), jnp.int32)
        for r in range(16):
            held = jnp.where(lane_row == r, asg_ref[xs * 16 + r], held)
        code = held * 8 + lane_g
        perm[:, xs * 128 : (xs + 1) * 128] = jnp.where(sub_code == code, 1.0, 0.0).astype(BF)

    for k in range(4):
        pltpu.make_async_copy(q1.at[k], q1.at[k], zrecv.at[k]).wait()
    me_place = x * 4 + y
    for dx, dy in AROUND:
        pltpu.make_async_remote_copy(
            src_ref=q1, dst_ref=q2.at[me_place], send_sem=gsend, recv_sem=grecv,
            device_id=dev(rem(x + dx, 4), rem(y + dy, 4), z, c), device_id_type=MESH,
        ).start()
    pltpu.make_async_copy(q1, q2.at[me_place], grecv).start()
    for i in range(1, 4):
        exchanges[(2, 1, 3)[i - 1]].start()

    exchanges[4].wait_recv()
    rows = lax.broadcasted_iota(jnp.int32, (64, 128), 0)
    lanes = lax.broadcasted_iota(jnp.int32, (64, 128), 1)
    lens_own = jnp.concatenate([lens[...]] * 8, axis=0)
    lens_other = jnp.concatenate([lensall[...]] * 8, axis=0)
    row_c = (rows >> 4) & 1
    live = jnp.where(row_c == c, lens_own, lens_other) - tp * 128
    row_slot = row_c * 4 + (rows & 3)
    for s in range(8):
        limit = jnp.where(row_slot == s, live, 0)
        bias[:, s * 128 : s * 128 + 128] = jnp.where(lanes < limit, 0.0, NEG)

    for i in range(4):
        loads[i].wait()
        exchanges[i].wait_recv()

    square = (128, 128)
    eye = lax.broadcasted_iota(jnp.int32, square, 0) == lax.broadcasted_iota(jnp.int32, square, 1)
    ones = jnp.ones((1024, 128), BF)
    stat_row = lax.broadcasted_iota(jnp.int32, (16, 128), 0)

    def as_row(column):
        return jnp.sum(jnp.where(eye, column, 0.0), axis=0, keepdims=True)

    def stat_tile(top, total):
        hi = total.astype(BF).astype(F32)
        return jnp.where(stat_row == 0, top, jnp.where(stat_row == 1, hi, total - hi)).astype(BF)

    def weights(scores, top):
        return jnp.exp2(scores - top).astype(BF)

    def largest(scores):
        return jnp.max(scores, axis=1, keepdims=True)

    def begin(i):
        k = head_at(y, i)
        qs[...] = dot(perm[...], q2[:, k].reshape(512, 128), NN).astype(BF)
        s0buf[...] = dot(rows_of(0, 1), kbuf[:, columns(k)], NT) * C2

    def columns(k):
        return pl.ds(pl.multiple_of(k * 128, 128), 128)

    chunks = [rem(x + a, 4) for a in (1, 3, 2, 0)]

    def rows_of(*which):
        places = [pl.ds(pl.multiple_of(chunks[a] * 128, 128), 128) for a in which]
        return jnp.concatenate([qs[place, :] for place in places], axis=0)

    own = pl.ds(pl.multiple_of(x * 128 + yh * 64, 64), 64)
    low = jnp.full((64, 1), NEG, F32)

    def head(i, last):
        k = head_at(y, i)
        cols = columns(k)
        values = jnp.concatenate([vbuf[:, cols], ones], axis=1)
        suffix_keys = skbuf[:, :, cols].reshape(1024, 128)
        suffix_values = jnp.concatenate([svbuf[:, :, cols].reshape(1024, 128), ones], axis=1)

        def send(a):
            pltpu.make_async_remote_copy(
                src_ref=sbuf.at[i * 4 + a], dst_ref=r1.at[x * 4 + y], send_sem=rsend, recv_sem=rrecv,
                device_id=dev(chunks[a], k, z, c), device_id_type=MESH,
            ).start()

        def put(a, m, n):
            sbuf[i * 4 + a, :128, :] = n[:, :128].astype(BF)
            sbuf[i * 4 + a, 128:, :] = stat_tile(as_row(m), as_row(n[:, 128:]))

        s1 = dot(rows_of(2, 3), kbuf[:, cols], NT) * C2
        ss = dot(qs[own, :], suffix_keys, NT) * C2 + bias[...]
        s0 = s0buf[...]
        m0 = largest(s0).astype(BF).astype(F32)
        n0 = dot(weights(s0, m0), values, NN)
        put(0, m0[:128], n0[:128])
        send(0)
        put(1, m0[128:], n0[128:])
        send(1)
        if not last:
            begin(i + 1)

        m1, ms = largest(s1), largest(ss)
        ms = jnp.concatenate([jnp.where(yh == 0, ms, low), jnp.where(yh == 0, low, ms)], axis=0)
        m1 = jnp.concatenate([m1[:128], jnp.maximum(m1[128:], ms)], axis=0).astype(BF).astype(F32)
        n1 = dot(weights(s1, m1), values, NN)
        ns = dot(weights(ss, jnp.where(yh == 0, m1[128:192], m1[192:])), suffix_values, NN)
        ns = jnp.concatenate([jnp.where(yh == 0, ns, 0.0), jnp.where(yh == 0, 0.0, ns)], axis=0)
        put(2, m1[:128], n1[:128])
        send(2)
        put(3, m1[128:], n1[128:] + ns)
        if last:
            pltpu.make_async_copy(sbuf.at[15], r1.at[x * 4 + y], rrecv).start()
        else:
            send(3)
        return 0

    pltpu.make_async_copy(q2, q2, grecv).wait()
    begin(0)
    lax.fori_loop(0, 3, lambda i, _: head(i, False), 0)
    head(3, True)

    pltpu.make_async_copy(r1, r1, rrecv).wait()
    stats = [r1[i, 128:, :].astype(F32) for i in range(16)]
    top = functools.reduce(jnp.maximum, [s[0:1] for s in stats])
    ws = [jnp.exp2(s[0:1] - top) for s in stats]
    total = functools.reduce(jnp.add, [w * (s[1:2] + s[2:3]) for w, s in zip(ws, stats)])
    his = [w.astype(BF).astype(F32) for w in ws]
    spread = [
        jnp.concatenate([jnp.where(eye, w, 0.0).astype(BF) for w in part], axis=1)
        for part in (his, [w - h for w, h in zip(ws, his)])
    ]
    both = dot(jnp.concatenate(spread, axis=0), jnp.concatenate([r1[i, :128, :] for i in range(16)], axis=0), NN)
    flat = (both[:128] + both[128:]).astype(BF)
    stat = stat_tile(top, total)
    for d in range(8):
        s2[d, :16, :] = flat[d * 16 : d * 16 + 16, :]
        s2[d, 16:, :] = stat

    zt = 4 * c + y
    for o in range(1, 8):
        y_, c_ = rem(y + o // 2, 4), rem(c + o % 2, 2)
        pltpu.make_async_remote_copy(
            src_ref=s2.at[y_ * 2 + c_], dst_ref=r2.at[z], send_sem=tsend.at[0], recv_sem=trecv,
            device_id=dev(x, y_, zt, c_), device_id_type=MESH,
        ).start()

    @pl.when(zt == z)
    def _():
        pltpu.make_async_copy(s2.at[y * 2 + c], r2.at[z], trecv).start()

    @pl.when(zt != z)
    def _():
        pltpu.make_async_remote_copy(
            src_ref=s2.at[y * 2 + c], dst_ref=r2.at[z], send_sem=tsend.at[1], recv_sem=trecv,
            device_id=dev(x, y, zt, c), device_id_type=MESH,
        ).start()

    pltpu.make_async_copy(r2, r2, trecv).wait()

    offset = y * 32 + c * 16
    pick = lax.broadcasted_iota(jnp.int32, (16, 128), 1) == lax.broadcasted_iota(jnp.int32, (16, 128), 0) + offset
    stats = [r2[i, 16:, :].astype(F32) for i in range(8)]
    m2 = functools.reduce(jnp.maximum, [s[0:1] for s in stats])
    ws = [jnp.exp2(s[0:1] - m2) for s in stats]
    total = functools.reduce(jnp.add, [w * (s[1:2] + s[2:3]) for w, s in zip(ws, stats)])
    acc = jnp.zeros((16, 128), F32)
    for i in range(8):
        column = jnp.sum(jnp.where(pick, ws[i], 0.0), axis=1, keepdims=True)
        acc = acc + column * r2[i, :16, :].astype(F32)
    column = jnp.sum(jnp.where(pick, total, 0.0), axis=1, keepdims=True)
    acc = acc / column
    for g in range(4):
        out_ref[:, g * 128 : (g + 1) * 128] = acc[g * 4 : g * 4 + 4, :].astype(BF)

    for i in range(5):
        exchanges[i].wait_send()
    pltpu.make_async_copy(s2.at[pl.ds(0, 7), pl.ds(0, 16)], s2.at[pl.ds(0, 7), pl.ds(0, 16)], zsend.at[0]).wait()

    @pl.when(hz != c)
    def _():
        pltpu.make_async_copy(q0, q0, zsend.at[1]).wait()

    most = q2.at[pl.ds(0, 15)]
    pltpu.make_async_copy(most, most, gsend).wait()
    most = sbuf.at[pl.ds(0, 15)]
    pltpu.make_async_copy(most, most, rsend).wait()
    most = s2.at[pl.ds(0, 7)]
    pltpu.make_async_copy(most, most, tsend.at[0]).wait()

    @pl.when(zt != z)
    def _():
        pltpu.make_async_copy(s2.at[0], s2.at[0], tsend.at[1]).wait()


def shards(queries, assignment, prefix_keys, prefix_values, suffix_keys, suffix_values, lengths):
    vmem, far = pl.BlockSpec(memory_space=pltpu.VMEM), pl.BlockSpec(memory_space=pl.ANY)
    dma = pltpu.SemaphoreType.DMA
    return pl.pallas_call(
        kernel,
        out_shape=jax.ShapeDtypeStruct(queries.shape, BF),
        in_specs=[far, far, far, far, far, far, far],
        out_specs=vmem,
        scratch_shapes=[
            pltpu.VMEM((1024, 512), BF),
            pltpu.VMEM((1024, 512), BF),
            pltpu.VMEM((8, 128, 512), BF),
            pltpu.VMEM((8, 128, 512), BF),
            pltpu.VMEM((16, 128), F32),
            pltpu.VMEM((16, 128), BF),
            pltpu.VMEM((4, 32, 128), BF),
            pltpu.VMEM((16, 4, 32, 128), BF),
            pltpu.VMEM((512, 128), BF),
            pltpu.VMEM((512, 512), BF),
            pltpu.VMEM((8, 128), jnp.int32),
            pltpu.VMEM((8, 128), jnp.int32),
            pltpu.VMEM((64, 1024), F32),
            pltpu.VMEM((256, 1024), F32),
            pltpu.VMEM((16, 144, 128), BF),
            pltpu.VMEM((16, 144, 128), BF),
            pltpu.VMEM((8, 32, 128), BF),
            pltpu.VMEM((8, 32, 128), BF),
            pltpu.VMEM((4, 512), BF),
            pltpu.SMEM((64,), jnp.int32),
            pltpu.SMEM((4,), jnp.int32),
            dma((3,)),
            dma((4,)),
            dma((5,)),
            dma((5,)),
            dma((2,)),
            dma((4,)),
            dma(()),
            dma(()),
            dma(()),
            dma(()),
            dma((2,)),
            dma(()),
        ],
        compiler_params=pltpu.CompilerParams(
            collective_id=0, has_side_effects=True, vmem_limit_bytes=48 * 1024 * 1024
        ),
        cost_estimate=pl.CostEstimate(flops=1_300_000_000, bytes_accessed=4_300_000, transcendentals=2_600_000),
    )(
        *(
            pltpu.with_memory_space_constraint(operand, pltpu.HBM)
            for operand in (
                queries, assignment, lengths, prefix_keys, prefix_values, suffix_keys, suffix_values
            )
        )
    )


def solution(mesh):
    in_specs = (
        P("rep", "tp"),
        P(),
        P(("rep", "tp"), None),
        P(("rep", "tp"), None),
        P("rep", "tp", None),
        P("rep", "tp", None),
        P("rep"),
    )
    out_specs = P("rep", "tp")
    return jax.shard_map(shards, mesh=mesh, in_specs=in_specs, out_specs=out_specs, check_vma=False)
```

```python
import functools
import math

import jax
import jax.numpy as jnp
from jax import lax
from jax.experimental import pallas as pl
from jax.experimental.pallas import tpu as pltpu
from jax.sharding import PartitionSpec as P

MESH = pl.DeviceIdType.MESH
HD = 128
HEADS_CORE = 4
C2 = math.log2(math.e) * HD ** (-0.5)
NEG = -(2.0**100)
BF = jnp.bfloat16
F32 = jnp.float32
NT = (((1,), (1,)), ((), ()))
NN = (((1,), (0,)), ((), ()))
AROUND = (
    (1, 0), (3, 0), (0, 1), (0, 3), (1, 1), (3, 1), (0, 2), (1, 2), (3, 2), (1, 3), (3, 3),
)


def rem(a, n):
    return lax.rem(a, jnp.int32(n))


def div(a, n):
    return lax.div(a, jnp.int32(n))


def dot(a, b, dims):
    return lax.dot_general(a, b, dims, preferred_element_type=F32)


def kernel(
    q_hbm, asg_hbm, len_hbm, pk, pv, sk, sv, out_ref,
    kbuf, vbuf, skbuf, svbuf, qf, q0, q1, b1, q2, qs, perm, lens, lensall, bias, s0buf, sbuf, r1, s2, r2,
    q_ref, asg_ref, len_ref, smallsem, ldsem, xsend, xrecv, zsend, zrecv, bsend, brecv, fsend, gsend, grecv, rsend, rrecv, tsend, trecv,
):
    rep, tp = lax.axis_index("rep"), lax.axis_index("tp")
    x, yh, c = div(rep, 4), rem(div(rep, 2), 2), rem(rep, 2)
    z, yl = div(tp, 2), rem(tp, 2)
    y = yh * 2 + yl
    hz = div(z, 4)

    def head_at(y_, i):
        return rem(y_ + 1 + i + c * (2 - 2 * i), 4)

    def dev(x_, y_, z_, c_):
        return (x_ * 4 + div(y_, 2) * 2 + c_, z_ * 2 + rem(y_, 2))

    small = [
        pltpu.make_async_copy(src, dst, smallsem.at[i])
        for i, (src, dst) in enumerate(((q_hbm, q_ref), (asg_hbm, asg_ref), (len_hbm, len_ref)))
    ]
    for copy in small:
        copy.start()

    mine = pl.multiple_of(c * 512, 512)
    theirs = pl.multiple_of((1 - c) * 512, 512)
    rows2 = pl.multiple_of(c * 512, 512)
    pairs = ((pk, kbuf), (sk, skbuf), (pv, vbuf), (sv, svbuf))

    def local_dst(i):
        buf = pairs[i][1]
        return buf.at[pl.ds(rows2, 512)] if i % 2 == 0 else buf.at[pl.ds(c * 4, 4)]

    def src_of(i, cols):
        ref = pairs[i][0]
        return ref.at[:, pl.ds(cols, 512)] if i % 2 == 0 else ref.at[:, :, pl.ds(cols, 512)]

    loads = [pltpu.make_async_copy(src_of(i, mine), local_dst(i), ldsem.at[i]) for i in range(4)]
    barrier = pltpu.get_barrier_semaphore()

    def greet(x_, y_, z_, c_):
        pl.semaphore_signal(barrier, inc=1, device_id=dev(x_, y_, z_, c_), device_id_type=MESH)

    partner = dev(x, y, z, 1 - c)
    for k in range(4):
        for cs in range(2):
            zs = 4 * c + k

            @pl.when(jnp.logical_or(zs != z, cs != c))
            def _(zs=zs, cs=cs):
                greet(x, y, zs, cs)

    greet(x, y, z, 1 - c)
    for o in range(1, 16):
        greet(rem(x + o // 4, 4), rem(y + o % 4, 4), z, c)
    across = rem(x + 2, 4)

    @pl.when(hz == c)
    def _():
        for y_ in range(4):
            greet(across, y_, z, 1 - c)

    for zs in range(8):

        @pl.when(jnp.logical_or(jnp.logical_or(zs != z, rem(z, 4) != y), hz != c))
        def _(zs=zs):
            greet(x, rem(z, 4), zs, hz)

    for copy in loads:
        copy.start()

    small[0].wait()
    q = q_ref[...].astype(F32)
    for g in range(4):
        qf[g * 4 : g * 4 + 4, :] = q[:, g * 128 : (g + 1) * 128]
    q0[...] = qf[...].astype(BF)

    n_z = jnp.where(hz == c, 7, 8)
    n_t = jnp.where(4 * c + y == z, 7, 8)
    n_b = jnp.where(hz == c, 0, 4)
    pl.semaphore_wait(barrier, 16 + n_z + n_t + n_b)

    def ztile(ref_z):
        return q1.at[rem(ref_z, 4), pl.ds(pl.multiple_of(c * 16, 16), 16)]

    for o in (4, 3, 5, 2, 6, 1, 7):
        z_ = rem(z + o, 8)
        pltpu.make_async_remote_copy(
            src_ref=q0, dst_ref=ztile(z), send_sem=zsend.at[0], recv_sem=zrecv.at[rem(z, 4)],
            device_id=dev(x, y, z_, hz), device_id_type=MESH,
        ).start()

    @pl.when(hz == c)
    def _():
        pltpu.make_async_copy(q0, ztile(z), zrecv.at[rem(z, 4)]).start()

    @pl.when(hz != c)
    def _():
        pltpu.make_async_remote_copy(
            src_ref=q0, dst_ref=ztile(z), send_sem=zsend.at[1], recv_sem=zrecv.at[rem(z, 4)],
            device_id=partner, device_id_type=MESH,
        ).start()

    for dy in range(4):
        pltpu.make_async_remote_copy(
            src_ref=q0, dst_ref=b1.at[y, pl.ds(pl.multiple_of(c * 16, 16), 16)], send_sem=bsend, recv_sem=brecv,
            device_id=dev(across, rem(y + dy, 4), z, hz), device_id_type=MESH,
        ).start()

    exchanges = [
        pltpu.make_async_remote_copy(
            src_ref=src_of(i, theirs), dst_ref=local_dst(i), send_sem=xsend.at[i], recv_sem=xrecv.at[i],
            device_id=partner, device_id_type=MESH,
        )
        for i in range(4)
    ]
    exchanges.append(
        pltpu.make_async_remote_copy(
            src_ref=lens, dst_ref=lensall, send_sem=xsend.at[4], recv_sem=xrecv.at[4],
            device_id=partner, device_id_type=MESH,
        )
    )
    exchanges[0].start()

    small[1].wait()
    small[2].wait()
    own_len = jnp.zeros((8, 128), jnp.int32)
    sub8 = lax.broadcasted_iota(jnp.int32, (8, 128), 0)
    for s in range(4):
        own_len = jnp.where((sub8 & 3) == s, len_ref[s], own_len)
    lens[...] = own_len

    exchanges[4].start()

    lane = lax.broadcasted_iota(jnp.int32, (1, 128), 1)
    lane_row = ((lane >> 6) * 2 + ((lane >> 4) & 1)) * 4 + (lane & 3)
    lane_g = ((lane >> 5) & 1) * 4 + ((lane >> 2) & 3)
    sub = lax.broadcasted_iota(jnp.int32, (512, 128), 0)
    sub_row = (sub >> 6) * 8 + ((sub >> 4) & 1) * 4 + (sub & 3)
    sub_g = ((sub >> 5) & 1) * 4 + ((sub >> 2) & 3)
    sub_code = sub_row * 8 + sub_g
    for xs in range(4):
        held = jnp.zeros((1, 128), jnp.int32)
        for r in range(16):
            held = jnp.where(lane_row == r, asg_ref[xs * 16 + r], held)
        code = held * 8 + lane_g
        perm[:, xs * 128 : (xs + 1) * 128] = jnp.where(sub_code == code, 1.0, 0.0).astype(BF)

    for k in range(4):
        pltpu.make_async_copy(q1.at[k], q1.at[k], zrecv.at[k]).wait()
    for i in range(4):
        k = head_at(y, i)
        pltpu.make_async_copy(q1.at[k], q2.at[k, x, y], grecv.at[k]).start()
        for dx, dy in AROUND:
            y_ = rem(y + dy, 4)
            k = head_at(y_, i)
            pltpu.make_async_remote_copy(
                src_ref=q1.at[k], dst_ref=q2.at[k, x, y], send_sem=gsend.at[0 if dx else 1], recv_sem=grecv.at[k],
                device_id=dev(rem(x + dx, 4), y_, z, c), device_id_type=MESH,
            ).start()
        if i == 0:

            @pl.when(hz == c)
            def _():
                pltpu.make_async_copy(b1, b1, brecv).wait()
                k = rem(z, 4)
                for o in (4, 3, 5, 2, 6, 1, 7):
                    pltpu.make_async_remote_copy(
                        src_ref=b1, dst_ref=q2.at[k, across], send_sem=fsend, recv_sem=grecv.at[k],
                        device_id=dev(x, y, rem(z + o, 8), c), device_id_type=MESH,
                    ).start()
                pltpu.make_async_copy(b1, q2.at[k, across], grecv.at[k]).start()

        if i < 3:
            exchanges[(2, 1, 3)[i]].start()

    exchanges[4].wait_recv()
    rows = lax.broadcasted_iota(jnp.int32, (64, 128), 0)
    lanes = lax.broadcasted_iota(jnp.int32, (64, 128), 1)
    lens_own = jnp.concatenate([lens[...]] * 8, axis=0)
    lens_other = jnp.concatenate([lensall[...]] * 8, axis=0)
    row_c = (rows >> 4) & 1
    live = jnp.where(row_c == c, lens_own, lens_other) - tp * 128
    row_slot = row_c * 4 + (rows & 3)
    for s in range(8):
        limit = jnp.where(row_slot == s, live, 0)
        bias[:, s * 128 : s * 128 + 128] = jnp.where(lanes < limit, 0.0, NEG)

    for i in range(4):
        loads[i].wait()
        exchanges[i].wait_recv()

    square = (128, 128)
    eye = lax.broadcasted_iota(jnp.int32, square, 0) == lax.broadcasted_iota(jnp.int32, square, 1)
    ones = jnp.ones((1024, 128), BF)
    stat_row = lax.broadcasted_iota(jnp.int32, (16, 128), 0)

    def as_row(column):
        return jnp.sum(jnp.where(eye, column, 0.0), axis=0, keepdims=True)

    def stat_tile(top, total):
        hi = total.astype(BF).astype(F32)
        return jnp.where(stat_row == 0, top, jnp.where(stat_row == 1, hi, total - hi)).astype(BF)

    def weights(scores, top):
        return jnp.exp2(scores - top).astype(BF)

    def largest(scores):
        return jnp.max(scores, axis=1, keepdims=True)

    def begin(i):
        k = head_at(y, i)
        pltpu.make_async_copy(q2.at[k], q2.at[k], grecv.at[k]).wait()
        qs[...] = dot(perm[...], q2[k].reshape(512, 128), NN).astype(BF)
        s0buf[...] = dot(rows_of(0, 1), kbuf[:, columns(k)], NT) * C2

    def columns(k):
        return pl.ds(pl.multiple_of(k * 128, 128), 128)

    chunks = [rem(x + a, 4) for a in (1, 3, 2, 0)]

    def rows_of(*which):
        places = [pl.ds(pl.multiple_of(chunks[a] * 128, 128), 128) for a in which]
        return jnp.concatenate([qs[place, :] for place in places], axis=0)

    own = pl.ds(pl.multiple_of(x * 128 + yh * 64, 64), 64)
    low = jnp.full((64, 1), NEG, F32)

    def head(i, last):
        k = head_at(y, i)
        cols = columns(k)
        values = jnp.concatenate([vbuf[:, cols], ones], axis=1)
        suffix_keys = skbuf[:, :, cols].reshape(1024, 128)
        suffix_values = jnp.concatenate([svbuf[:, :, cols].reshape(1024, 128), ones], axis=1)

        def send(a):
            pltpu.make_async_remote_copy(
                src_ref=sbuf.at[i * 4 + a], dst_ref=r1.at[x * 4 + y], send_sem=rsend, recv_sem=rrecv,
                device_id=dev(chunks[a], k, z, c), device_id_type=MESH,
            ).start()

        def put(a, m, n):
            sbuf[i * 4 + a, :128, :] = n[:, :128].astype(BF)
            sbuf[i * 4 + a, 128:, :] = stat_tile(as_row(m), as_row(n[:, 128:]))

        s1 = dot(rows_of(2, 3), kbuf[:, cols], NT) * C2
        ss = dot(qs[own, :], suffix_keys, NT) * C2 + bias[...]
        s0 = s0buf[...]
        m0 = largest(s0).astype(BF).astype(F32)
        n0 = dot(weights(s0, m0), values, NN)
        put(0, m0[:128], n0[:128])
        send(0)
        put(1, m0[128:], n0[128:])
        send(1)
        if not last:
            begin(i + 1)

        m1, ms = largest(s1), largest(ss)
        ms = jnp.concatenate([jnp.where(yh == 0, ms, low), jnp.where(yh == 0, low, ms)], axis=0)
        m1 = jnp.concatenate([m1[:128], jnp.maximum(m1[128:], ms)], axis=0).astype(BF).astype(F32)
        n1 = dot(weights(s1, m1), values, NN)
        ns = dot(weights(ss, jnp.where(yh == 0, m1[128:192], m1[192:])), suffix_values, NN)
        ns = jnp.concatenate([jnp.where(yh == 0, ns, 0.0), jnp.where(yh == 0, 0.0, ns)], axis=0)
        put(2, m1[:128], n1[:128])
        send(2)
        put(3, m1[128:], n1[128:] + ns)
        if last:
            pltpu.make_async_copy(sbuf.at[15], r1.at[x * 4 + y], rrecv).start()
        else:
            send(3)
        return 0

    begin(0)
    lax.fori_loop(0, 3, lambda i, _: head(i, False), 0)
    head(3, True)

    pltpu.make_async_copy(r1, r1, rrecv).wait()
    stats = [r1[i, 128:, :].astype(F32) for i in range(16)]
    top = functools.reduce(jnp.maximum, [s[0:1] for s in stats])
    ws = [jnp.exp2(s[0:1] - top) for s in stats]
    total = functools.reduce(jnp.add, [w * (s[1:2] + s[2:3]) for w, s in zip(ws, stats)])
    his = [w.astype(BF).astype(F32) for w in ws]
    spread = [
        jnp.concatenate([jnp.where(eye, w, 0.0).astype(BF) for w in part], axis=1)
        for part in (his, [w - h for w, h in zip(ws, his)])
    ]
    both = dot(jnp.concatenate(spread, axis=0), jnp.concatenate([r1[i, :128, :] for i in range(16)], axis=0), NN)
    flat = (both[:128] + both[128:]).astype(BF)
    stat = stat_tile(top, total)
    for d in range(8):
        s2[d, :16, :] = flat[d * 16 : d * 16 + 16, :]
        s2[d, 16:, :] = stat

    zt = 4 * c + y
    for o in range(1, 8):
        y_, c_ = rem(y + o // 2, 4), rem(c + o % 2, 2)
        pltpu.make_async_remote_copy(
            src_ref=s2.at[y_ * 2 + c_], dst_ref=r2.at[z], send_sem=tsend.at[0], recv_sem=trecv,
            device_id=dev(x, y_, zt, c_), device_id_type=MESH,
        ).start()

    @pl.when(zt == z)
    def _():
        pltpu.make_async_copy(s2.at[y * 2 + c], r2.at[z], trecv).start()

    @pl.when(zt != z)
    def _():
        pltpu.make_async_remote_copy(
            src_ref=s2.at[y * 2 + c], dst_ref=r2.at[z], send_sem=tsend.at[1], recv_sem=trecv,
            device_id=dev(x, y, zt, c), device_id_type=MESH,
        ).start()

    pltpu.make_async_copy(r2, r2, trecv).wait()

    offset = y * 32 + c * 16
    pick = lax.broadcasted_iota(jnp.int32, (16, 128), 1) == lax.broadcasted_iota(jnp.int32, (16, 128), 0) + offset
    stats = [r2[i, 16:, :].astype(F32) for i in range(8)]
    m2 = functools.reduce(jnp.maximum, [s[0:1] for s in stats])
    ws = [jnp.exp2(s[0:1] - m2) for s in stats]
    total = functools.reduce(jnp.add, [w * (s[1:2] + s[2:3]) for w, s in zip(ws, stats)])
    acc = jnp.zeros((16, 128), F32)
    for i in range(8):
        column = jnp.sum(jnp.where(pick, ws[i], 0.0), axis=1, keepdims=True)
        acc = acc + column * r2[i, :16, :].astype(F32)
    column = jnp.sum(jnp.where(pick, total, 0.0), axis=1, keepdims=True)
    acc = acc / column
    for g in range(4):
        out_ref[:, g * 128 : (g + 1) * 128] = acc[g * 4 : g * 4 + 4, :].astype(BF)

    for i in range(5):
        exchanges[i].wait_send()
    pltpu.make_async_copy(s2.at[pl.ds(0, 7), pl.ds(0, 16)], s2.at[pl.ds(0, 7), pl.ds(0, 16)], zsend.at[0]).wait()

    @pl.when(hz != c)
    def _():
        pltpu.make_async_copy(q0, q0, zsend.at[1]).wait()

    most = q2.at[:, pl.ds(0, 1), pl.ds(0, 3)]
    pltpu.make_async_copy(q2.at[:, pl.ds(0, 2)], q2.at[:, pl.ds(0, 2)], gsend.at[0]).wait()
    pltpu.make_async_copy(most, most, gsend.at[1]).wait()
    pltpu.make_async_copy(q1.at[:, pl.ds(0, 16)], q1.at[:, pl.ds(0, 16)], bsend).wait()

    @pl.when(hz == c)
    def _():
        most = sbuf.at[pl.ds(0, 14), pl.ds(0, 64)]
        pltpu.make_async_copy(most, most, fsend).wait()

    most = sbuf.at[pl.ds(0, 15)]
    pltpu.make_async_copy(most, most, rsend).wait()
    most = s2.at[pl.ds(0, 7)]
    pltpu.make_async_copy(most, most, tsend.at[0]).wait()

    @pl.when(zt != z)
    def _():
        pltpu.make_async_copy(s2.at[0], s2.at[0], tsend.at[1]).wait()


def shards(queries, assignment, prefix_keys, prefix_values, suffix_keys, suffix_values, lengths):
    vmem, far = pl.BlockSpec(memory_space=pltpu.VMEM), pl.BlockSpec(memory_space=pl.ANY)
    dma = pltpu.SemaphoreType.DMA
    return pl.pallas_call(
        kernel,
        out_shape=jax.ShapeDtypeStruct(queries.shape, BF),
        in_specs=[far, far, far, far, far, far, far],
        out_specs=vmem,
        scratch_shapes=[
            pltpu.VMEM((1024, 512), BF),
            pltpu.VMEM((1024, 512), BF),
            pltpu.VMEM((8, 128, 512), BF),
            pltpu.VMEM((8, 128, 512), BF),
            pltpu.VMEM((16, 128), F32),
            pltpu.VMEM((16, 128), BF),
            pltpu.VMEM((4, 32, 128), BF),
            pltpu.VMEM((4, 32, 128), BF),
            pltpu.VMEM((4, 4, 4, 32, 128), BF),
            pltpu.VMEM((512, 128), BF),
            pltpu.VMEM((512, 512), BF),
            pltpu.VMEM((8, 128), jnp.int32),
            pltpu.VMEM((8, 128), jnp.int32),
            pltpu.VMEM((64, 1024), F32),
            pltpu.VMEM((256, 1024), F32),
            pltpu.VMEM((16, 144, 128), BF),
            pltpu.VMEM((16, 144, 128), BF),
            pltpu.VMEM((8, 32, 128), BF),
            pltpu.VMEM((8, 32, 128), BF),
            pltpu.VMEM((4, 512), BF),
            pltpu.SMEM((64,), jnp.int32),
            pltpu.SMEM((4,), jnp.int32),
            dma((3,)),
            dma((4,)),
            dma((5,)),
            dma((5,)),
            dma((2,)),
            dma((4,)),
            dma(()),
            dma(()),
            dma(()),
            dma((2,)),
            dma((4,)),
            dma(()),
            dma(()),
            dma((2,)),
            dma(()),
        ],
        compiler_params=pltpu.CompilerParams(
            collective_id=0, has_side_effects=True, vmem_limit_bytes=48 * 1024 * 1024
        ),
        cost_estimate=pl.CostEstimate(flops=1_300_000_000, bytes_accessed=4_300_000, transcendentals=2_600_000),
    )(
        *(
            pltpu.with_memory_space_constraint(operand, pltpu.HBM)
            for operand in (
                queries, assignment, lengths, prefix_keys, prefix_values, suffix_keys, suffix_values
            )
        )
    )


def solution(mesh):
    in_specs = (
        P("rep", "tp"),
        P(),
        P(("rep", "tp"), None),
        P(("rep", "tp"), None),
        P("rep", "tp", None),
        P("rep", "tp", None),
        P("rep"),
    )
    out_specs = P("rep", "tp")
    return jax.shard_map(shards, mesh=mesh, in_specs=in_specs, out_specs=out_specs, check_vma=False)
```

```python
import functools

import jax
import jax.numpy as jnp
from jax import lax
from jax.experimental import pallas as pl
from jax.experimental.pallas import tpu as pltpu
from jax.sharding import PartitionSpec as P

MESH = pl.DeviceIdType.MESH
HD = 128
HEADS_CORE = 4
SCALE = HD ** (-0.5)
NEG = -(2.0**100)
BF = jnp.bfloat16
F32 = jnp.float32
NT = (((1,), (1,)), ((), ()))
NN = (((1,), (0,)), ((), ()))
AROUND = (
    (1, 0), (3, 0), (0, 1), (0, 3), (2, 0), (1, 1), (3, 1), (2, 1), (0, 2), (1, 2), (3, 2), (2, 2), (1, 3), (3, 3), (2, 3),
)


def dot(a, b, dims):
    return lax.dot_general(a, b, dims, preferred_element_type=F32)


def kernel(
    q_hbm, asg_hbm, len_hbm, pk, pv, sk, sv, out_ref,
    kbuf, vbuf, skbuf, svbuf, qf, q0, q1, q2, qs, perm, lens, lensall, bias, sbuf, r1, s2, r2,
    q_ref, asg_ref, len_ref, smallsem, ldsem, xsend, xrecv, zsend, zrecv, gsend, grecv, rsend, rrecv, tsend, trecv,
):
    rep, tp = lax.axis_index("rep"), lax.axis_index("tp")
    x, yh, c = rep // 4, (rep // 2) % 2, rep % 2
    z, yl = tp // 2, tp % 2
    y = yh * 2 + yl
    hz = z // 4

    def head_at(y_, i):
        return (y_ + 1 + i + c * (2 - 2 * i)) % 4

    def dev(x_, y_, z_, c_):
        return (x_ * 4 + (y_ // 2) * 2 + c_, z_ * 2 + y_ % 2)

    small = [
        pltpu.make_async_copy(src, dst, smallsem.at[i])
        for i, (src, dst) in enumerate(((q_hbm, q_ref), (asg_hbm, asg_ref), (len_hbm, len_ref)))
    ]
    for copy in small:
        copy.start()

    mine = pl.multiple_of(c * 512, 512)
    theirs = pl.multiple_of((1 - c) * 512, 512)
    rows2 = pl.multiple_of(c * 512, 512)
    pairs = ((pk, kbuf), (sk, skbuf), (pv, vbuf), (sv, svbuf))

    def local_dst(i):
        buf = pairs[i][1]
        return buf.at[pl.ds(rows2, 512)] if i % 2 == 0 else buf.at[pl.ds(c * 4, 4)]

    def src_of(i, cols):
        ref = pairs[i][0]
        return ref.at[:, pl.ds(cols, 512)] if i % 2 == 0 else ref.at[:, :, pl.ds(cols, 512)]

    loads = [pltpu.make_async_copy(src_of(i, mine), local_dst(i), ldsem.at[i]) for i in range(4)]
    barrier = pltpu.get_barrier_semaphore()

    def greet(x_, y_, z_, c_):
        pl.semaphore_signal(barrier, inc=1, device_id=dev(x_, y_, z_, c_), device_id_type=MESH)

    partner = dev(x, y, z, 1 - c)
    for k in range(4):
        for cs in range(2):
            zs = 4 * c + k

            @pl.when(jnp.logical_or(zs != z, cs != c))
            def _(zs=zs, cs=cs):
                greet(x, y, zs, cs)

    greet(x, y, z, 1 - c)
    for o in range(1, 16):
        greet((x + o // 4) % 4, (y + o % 4) % 4, z, c)
    for zs in range(8):

        @pl.when(jnp.logical_or(jnp.logical_or(zs != z, z % 4 != y), hz != c))
        def _(zs=zs):
            greet(x, z % 4, zs, hz)

    for copy in loads:
        copy.start()

    small[0].wait()
    q = q_ref[...].astype(F32)
    for g in range(4):
        qf[g * 4 : g * 4 + 4, :] = q[:, g * 128 : (g + 1) * 128]
    q0[...] = qf[...].astype(BF)

    n_z = jnp.where(hz == c, 7, 8)
    n_t = jnp.where(4 * c + y == z, 7, 8)
    pl.semaphore_wait(barrier, 16 + n_z + n_t)

    def ztile(ref_z):
        return q1.at[ref_z % 4, pl.ds(pl.multiple_of(c * 16, 16), 16)]

    for o in (4, 3, 5, 2, 6, 1, 7):
        z_ = (z + o) % 8
        pltpu.make_async_remote_copy(
            src_ref=q0, dst_ref=ztile(z), send_sem=zsend.at[0], recv_sem=zrecv.at[z % 4],
            device_id=dev(x, y, z_, hz), device_id_type=MESH,
        ).start()

    @pl.when(hz == c)
    def _():
        pltpu.make_async_copy(q0, ztile(z), zrecv.at[z % 4]).start()

    @pl.when(hz != c)
    def _():
        pltpu.make_async_remote_copy(
            src_ref=q0, dst_ref=ztile(z), send_sem=zsend.at[1], recv_sem=zrecv.at[z % 4],
            device_id=partner, device_id_type=MESH,
        ).start()

    exchanges = [
        pltpu.make_async_remote_copy(
            src_ref=src_of(i, theirs), dst_ref=local_dst(i), send_sem=xsend.at[i], recv_sem=xrecv.at[i],
            device_id=partner, device_id_type=MESH,
        )
        for i in range(4)
    ]
    exchanges.append(
        pltpu.make_async_remote_copy(
            src_ref=lens, dst_ref=lensall, send_sem=xsend.at[4], recv_sem=xrecv.at[4],
            device_id=partner, device_id_type=MESH,
        )
    )
    exchanges[0].start()

    small[1].wait()
    small[2].wait()
    own_len = jnp.zeros((8, 128), jnp.int32)
    sub8 = lax.broadcasted_iota(jnp.int32, (8, 128), 0)
    for s in range(4):
        own_len = jnp.where((sub8 & 3) == s, len_ref[s], own_len)
    lens[...] = own_len

    exchanges[4].start()

    lane = lax.broadcasted_iota(jnp.int32, (1, 128), 1)
    lane_row = ((lane >> 6) * 2 + ((lane >> 4) & 1)) * 4 + (lane & 3)
    lane_g = ((lane >> 5) & 1) * 4 + ((lane >> 2) & 3)
    sub = lax.broadcasted_iota(jnp.int32, (512, 128), 0)
    sub_row = (sub >> 6) * 8 + ((sub >> 4) & 1) * 4 + (sub & 3)
    sub_g = ((sub >> 5) & 1) * 4 + ((sub >> 2) & 3)
    sub_code = sub_row * 8 + sub_g
    for xs in range(4):
        held = jnp.zeros((1, 128), jnp.int32)
        for r in range(16):
            held = jnp.where(lane_row == r, asg_ref[xs * 16 + r], held)
        code = held * 8 + lane_g
        perm[:, xs * 128 : (xs + 1) * 128] = jnp.where(sub_code == code, 1.0, 0.0).astype(BF)

    me_rows = pl.ds(pl.multiple_of((x * 4 + y) * 32, 32), 32)
    for k in range(4):
        pltpu.make_async_copy(q1.at[k], q1.at[k], zrecv.at[k]).wait()
    for i in range(4):
        k = head_at(y, i)
        pltpu.make_async_copy(q1.at[k], q2.at[k, me_rows], grecv.at[k]).start()
        for dx, dy in AROUND:
            y_ = (y + dy) % 4
            k = head_at(y_, i)
            pltpu.make_async_remote_copy(
                src_ref=q1.at[k], dst_ref=q2.at[k, me_rows], send_sem=gsend, recv_sem=grecv.at[k],
                device_id=dev((x + dx) % 4, y_, z, c), device_id_type=MESH,
            ).start()
        if i < 3:
            exchanges[(2, 1, 3)[i]].start()

    exchanges[4].wait_recv()
    rows = lax.broadcasted_iota(jnp.int32, (64, 128), 0)
    lanes = lax.broadcasted_iota(jnp.int32, (64, 128), 1)
    lens_own = jnp.concatenate([lens[...]] * 8, axis=0)
    lens_other = jnp.concatenate([lensall[...]] * 8, axis=0)
    row_c = (rows >> 4) & 1
    live = jnp.where(row_c == c, lens_own, lens_other) - tp * 128
    row_slot = row_c * 4 + (rows & 3)
    for s in range(8):
        limit = jnp.where(row_slot == s, live, 0)
        bias[:, s * 128 : s * 128 + 128] = jnp.where(lanes < limit, 0.0, NEG)

    for i in range(4):
        loads[i].wait()
        exchanges[i].wait_recv()

    square = (128, 128)
    eye = lax.broadcasted_iota(jnp.int32, square, 0) == lax.broadcasted_iota(jnp.int32, square, 1)
    ones = jnp.ones((1024, 128), BF)
    stat_row = lax.broadcasted_iota(jnp.int32, (16, 128), 0)

    def as_row(column):
        return jnp.sum(jnp.where(eye, column, 0.0), axis=0, keepdims=True)

    def stat_tile(top, total):
        hi = total.astype(BF).astype(F32)
        return jnp.where(stat_row == 0, top, jnp.where(stat_row == 1, hi, total - hi)).astype(BF)

    def weights(scores, top):
        return jnp.exp(scores - top).astype(BF)

    def largest(scores):
        return jnp.max(scores, axis=1, keepdims=True)

    def head(i, _):
        k = head_at(y, i)
        cols = pl.ds(pl.multiple_of(k * 128, 128), 128)
        pltpu.make_async_copy(q2.at[k], q2.at[k], grecv.at[k]).wait()
        qs[...] = dot(perm[...], q2[k], NN).astype(BF)
        chunks = [(x + a) % 4 for a in (1, 3, 2, 0)]
        parts = [qs[pl.ds(pl.multiple_of(j * 128, 128), 128), :] for j in chunks]
        keys = kbuf[:, cols]
        values = jnp.concatenate([vbuf[:, cols], ones], axis=1)
        suffix_keys = skbuf[:, :, cols].reshape(1024, 128)
        suffix_values = jnp.concatenate([svbuf[:, :, cols].reshape(1024, 128), ones], axis=1)

        s0 = dot(jnp.concatenate(parts[:2], axis=0), keys, NT) * SCALE
        s1 = dot(jnp.concatenate(parts[2:], axis=0), keys, NT) * SCALE
        own = pl.ds(pl.multiple_of(x * 128 + yh * 64, 64), 64)
        ss = dot(qs[own, :], suffix_keys, NT) * SCALE + bias[...]

        def send(a):
            pltpu.make_async_remote_copy(
                src_ref=sbuf.at[i * 4 + a], dst_ref=r1.at[x * 4 + y], send_sem=rsend, recv_sem=rrecv,
                device_id=dev(chunks[a], k, z, c), device_id_type=MESH,
            ).start()

        def put(a, m, n):
            sbuf[i * 4 + a, :128, :] = n[:, :128].astype(BF)
            sbuf[i * 4 + a, 128:, :] = stat_tile(as_row(m), as_row(n[:, 128:]))

        m0 = largest(s0).astype(BF).astype(F32)
        n0 = dot(weights(s0, m0), values, NN)
        put(0, m0[:128], n0[:128])
        send(0)
        put(1, m0[128:], n0[128:])
        send(1)

        m1, ms = largest(s1), largest(ss)
        low = jnp.full((64, 1), NEG, F32)
        ms = jnp.concatenate([jnp.where(yh == 0, ms, low), jnp.where(yh == 0, low, ms)], axis=0)
        m1 = jnp.concatenate([m1[:128], jnp.maximum(m1[128:], ms)], axis=0).astype(BF).astype(F32)
        n1 = dot(weights(s1, m1), values, NN)
        ns = dot(weights(ss, jnp.where(yh == 0, m1[128:192], m1[192:])), suffix_values, NN)
        ns = jnp.concatenate([jnp.where(yh == 0, ns, 0.0), jnp.where(yh == 0, 0.0, ns)], axis=0)
        put(2, m1[:128], n1[:128])
        send(2)
        put(3, m1[128:], n1[128:] + ns)
        pl.when(i < 3)(lambda: send(3))
        return 0

    lax.fori_loop(0, 4, head, 0)
    pltpu.make_async_copy(sbuf.at[15], r1.at[x * 4 + y], rrecv).start()

    pltpu.make_async_copy(r1, r1, rrecv).wait()
    stats = [r1[i, 128:, :].astype(F32) for i in range(16)]
    top = functools.reduce(jnp.maximum, [s[0:1] for s in stats])
    ws = [jnp.exp(s[0:1] - top) for s in stats]
    total = functools.reduce(jnp.add, [w * (s[1:2] + s[2:3]) for w, s in zip(ws, stats)])
    his = [w.astype(BF).astype(F32) for w in ws]
    spread = [
        jnp.concatenate([jnp.where(eye, w, 0.0).astype(BF) for w in part], axis=1)
        for part in (his, [w - h for w, h in zip(ws, his)])
    ]
    both = dot(jnp.concatenate(spread, axis=0), jnp.concatenate([r1[i, :128, :] for i in range(16)], axis=0), NN)
    flat = (both[:128] + both[128:]).astype(BF)
    stat = stat_tile(top, total)
    for d in range(8):
        s2[d, :16, :] = flat[d * 16 : d * 16 + 16, :]
        s2[d, 16:, :] = stat

    zt = 4 * c + y
    for o in range(1, 8):
        y_, c_ = (y + o // 2) % 4, (c + o % 2) % 2
        pltpu.make_async_remote_copy(
            src_ref=s2.at[y_ * 2 + c_], dst_ref=r2.at[z], send_sem=tsend.at[0], recv_sem=trecv,
            device_id=dev(x, y_, zt, c_), device_id_type=MESH,
        ).start()

    @pl.when(zt == z)
    def _():
        pltpu.make_async_copy(s2.at[y * 2 + c], r2.at[z], trecv).start()

    @pl.when(zt != z)
    def _():
        pltpu.make_async_remote_copy(
            src_ref=s2.at[y * 2 + c], dst_ref=r2.at[z], send_sem=tsend.at[1], recv_sem=trecv,
            device_id=dev(x, y, zt, c), device_id_type=MESH,
        ).start()

    pltpu.make_async_copy(r2, r2, trecv).wait()

    offset = y * 32 + c * 16
    pick = lax.broadcasted_iota(jnp.int32, (16, 128), 1) == lax.broadcasted_iota(jnp.int32, (16, 128), 0) + offset
    stats = [r2[i, 16:, :].astype(F32) for i in range(8)]
    m2 = functools.reduce(jnp.maximum, [s[0:1] for s in stats])
    ws = [jnp.exp(s[0:1] - m2) for s in stats]
    total = functools.reduce(jnp.add, [w * (s[1:2] + s[2:3]) for w, s in zip(ws, stats)])
    acc = jnp.zeros((16, 128), F32)
    for i in range(8):
        column = jnp.sum(jnp.where(pick, ws[i], 0.0), axis=1, keepdims=True)
        acc = acc + column * r2[i, :16, :].astype(F32)
    column = jnp.sum(jnp.where(pick, total, 0.0), axis=1, keepdims=True)
    acc = acc / column
    for g in range(4):
        out_ref[:, g * 128 : (g + 1) * 128] = acc[g * 4 : g * 4 + 4, :].astype(BF)

    for i in range(5):
        exchanges[i].wait_send()
    pltpu.make_async_copy(s2.at[pl.ds(0, 7), pl.ds(0, 16)], s2.at[pl.ds(0, 7), pl.ds(0, 16)], zsend.at[0]).wait()

    @pl.when(hz != c)
    def _():
        pltpu.make_async_copy(q0, q0, zsend.at[1]).wait()

    most = q2.at[:, pl.ds(0, 480)]
    pltpu.make_async_copy(most, most, gsend).wait()
    most = sbuf.at[pl.ds(0, 15)]
    pltpu.make_async_copy(most, most, rsend).wait()
    most = s2.at[pl.ds(0, 7)]
    pltpu.make_async_copy(most, most, tsend.at[0]).wait()

    @pl.when(zt != z)
    def _():
        pltpu.make_async_copy(s2.at[0], s2.at[0], tsend.at[1]).wait()


def shards(queries, assignment, prefix_keys, prefix_values, suffix_keys, suffix_values, lengths):
    vmem, far = pl.BlockSpec(memory_space=pltpu.VMEM), pl.BlockSpec(memory_space=pl.ANY)
    dma = pltpu.SemaphoreType.DMA
    return pl.pallas_call(
        kernel,
        out_shape=jax.ShapeDtypeStruct(queries.shape, BF),
        in_specs=[far, far, far, far, far, far, far],
        out_specs=vmem,
        scratch_shapes=[
            pltpu.VMEM((1024, 512), BF),
            pltpu.VMEM((1024, 512), BF),
            pltpu.VMEM((8, 128, 512), BF),
            pltpu.VMEM((8, 128, 512), BF),
            pltpu.VMEM((16, 128), F32),
            pltpu.VMEM((16, 128), BF),
            pltpu.VMEM((4, 32, 128), BF),
            pltpu.VMEM((4, 512, 128), BF),
            pltpu.VMEM((512, 128), BF),
            pltpu.VMEM((512, 512), BF),
            pltpu.VMEM((8, 128), jnp.int32),
            pltpu.VMEM((8, 128), jnp.int32),
            pltpu.VMEM((64, 1024), F32),
            pltpu.VMEM((16, 144, 128), BF),
            pltpu.VMEM((16, 144, 128), BF),
            pltpu.VMEM((8, 32, 128), BF),
            pltpu.VMEM((8, 32, 128), BF),
            pltpu.VMEM((4, 512), BF),
            pltpu.SMEM((64,), jnp.int32),
            pltpu.SMEM((4,), jnp.int32),
            dma((3,)),
            dma((4,)),
            dma((5,)),
            dma((5,)),
            dma((2,)),
            dma((4,)),
            dma(()),
            dma((4,)),
            dma(()),
            dma(()),
            dma((2,)),
            dma(()),
        ],
        compiler_params=pltpu.CompilerParams(
            collective_id=0, has_side_effects=True, vmem_limit_bytes=48 * 1024 * 1024
        ),
        cost_estimate=pl.CostEstimate(flops=1_300_000_000, bytes_accessed=4_300_000, transcendentals=2_600_000),
    )(
        *(
            pltpu.with_memory_space_constraint(operand, pltpu.HBM)
            for operand in (
                queries, assignment, lengths, prefix_keys, prefix_values, suffix_keys, suffix_values
            )
        )
    )


def solution(mesh):
    in_specs = (
        P("rep", "tp"),
        P(),
        P(("rep", "tp"), None),
        P(("rep", "tp"), None),
        P("rep", "tp", None),
        P("rep", "tp", None),
        P("rep"),
    )
    out_specs = P("rep", "tp")
    return jax.shard_map(shards, mesh=mesh, in_specs=in_specs, out_specs=out_specs, check_vma=False)
```

```python
import functools

import jax
import jax.numpy as jnp
from jax import lax
from jax.experimental import pallas as pl
from jax.experimental.pallas import tpu as pltpu
from jax.sharding import PartitionSpec as P

MESH = pl.DeviceIdType.MESH
HD = 128
HEADS_CORE = 4
SCALE = HD ** (-0.5)
NEG = -(2.0**100)
BF = jnp.bfloat16
F32 = jnp.float32
NT = (((1,), (1,)), ((), ()))
NN = (((1,), (0,)), ((), ()))
AROUND = (
    (1, 0), (3, 0), (0, 1), (0, 3), (2, 0), (1, 1), (3, 1), (2, 1), (0, 2), (1, 2), (3, 2), (2, 2), (1, 3), (3, 3), (2, 3),
)


def dot(a, b, dims):
    return lax.dot_general(a, b, dims, preferred_element_type=F32)


def kernel(
    q_hbm, asg_hbm, len_hbm, pk, pv, sk, sv, out_ref,
    kbuf, vbuf, skbuf, svbuf, qf, q0, q1, q2, qs, perm, lens, lensall, bias, sbuf, r1, s2, r2,
    q_ref, asg_ref, len_ref, smallsem, ldsem, xsend, xrecv, zsend, zrecv, gsend, grecv, rsend, rrecv, tsend, trecv,
):
    rep, tp = lax.axis_index("rep"), lax.axis_index("tp")
    x, yh, c = rep // 4, (rep // 2) % 2, rep % 2
    z, yl = tp // 2, tp % 2
    y = yh * 2 + yl
    hz = z // 4

    def head_at(y_, i):
        return (y_ + 1 + i + c * (2 - 2 * i)) % 4

    def dev(x_, y_, z_, c_):
        return (x_ * 4 + (y_ // 2) * 2 + c_, z_ * 2 + y_ % 2)

    small = [
        pltpu.make_async_copy(src, dst, smallsem.at[i])
        for i, (src, dst) in enumerate(((q_hbm, q_ref), (asg_hbm, asg_ref), (len_hbm, len_ref)))
    ]
    for copy in small:
        copy.start()

    mine = pl.multiple_of(c * 512, 512)
    theirs = pl.multiple_of((1 - c) * 512, 512)
    rows2 = pl.multiple_of(c * 512, 512)
    pairs = ((pk, kbuf), (sk, skbuf), (pv, vbuf), (sv, svbuf))

    def local_dst(i):
        buf = pairs[i][1]
        return buf.at[pl.ds(rows2, 512)] if i % 2 == 0 else buf.at[pl.ds(c * 4, 4)]

    def src_of(i, cols):
        ref = pairs[i][0]
        return ref.at[:, pl.ds(cols, 512)] if i % 2 == 0 else ref.at[:, :, pl.ds(cols, 512)]

    loads = [pltpu.make_async_copy(src_of(i, mine), local_dst(i), ldsem.at[i]) for i in range(4)]
    barrier = pltpu.get_barrier_semaphore()

    def greet(x_, y_, z_, c_):
        pl.semaphore_signal(barrier, inc=1, device_id=dev(x_, y_, z_, c_), device_id_type=MESH)

    partner = dev(x, y, z, 1 - c)
    for k in range(4):
        for cs in range(2):
            zs = 4 * c + k

            @pl.when(jnp.logical_or(zs != z, cs != c))
            def _(zs=zs, cs=cs):
                greet(x, y, zs, cs)

    greet(x, y, z, 1 - c)
    for o in range(1, 16):
        greet((x + o // 4) % 4, (y + o % 4) % 4, z, c)
    for zs in range(8):

        @pl.when(jnp.logical_or(jnp.logical_or(zs != z, z % 4 != y), hz != c))
        def _(zs=zs):
            greet(x, z % 4, zs, hz)

    small[0].wait()
    q = q_ref[...].astype(F32)
    for g in range(4):
        qf[g * 4 : g * 4 + 4, :] = q[:, g * 128 : (g + 1) * 128]
    q0[...] = qf[...].astype(BF)

    n_z = jnp.where(hz == c, 7, 8)
    n_t = jnp.where(4 * c + y == z, 7, 8)
    pl.semaphore_wait(barrier, 16 + n_z + n_t)

    def ztile(ref_z):
        return q1.at[ref_z % 4, pl.ds(pl.multiple_of(c * 16, 16), 16)]

    for o in (4, 3, 5, 2, 6, 1, 7):
        z_ = (z + o) % 8
        pltpu.make_async_remote_copy(
            src_ref=q0, dst_ref=ztile(z), send_sem=zsend.at[0], recv_sem=zrecv.at[z % 4],
            device_id=dev(x, y, z_, hz), device_id_type=MESH,
        ).start()

    @pl.when(hz == c)
    def _():
        pltpu.make_async_copy(q0, ztile(z), zrecv.at[z % 4]).start()

    @pl.when(hz != c)
    def _():
        pltpu.make_async_remote_copy(
            src_ref=q0, dst_ref=ztile(z), send_sem=zsend.at[1], recv_sem=zrecv.at[z % 4],
            device_id=partner, device_id_type=MESH,
        ).start()

    exchanges = [
        pltpu.make_async_remote_copy(
            src_ref=src_of(i, theirs), dst_ref=local_dst(i), send_sem=xsend.at[i], recv_sem=xrecv.at[i],
            device_id=partner, device_id_type=MESH,
        )
        for i in range(4)
    ]
    exchanges.append(
        pltpu.make_async_remote_copy(
            src_ref=lens, dst_ref=lensall, send_sem=xsend.at[4], recv_sem=xrecv.at[4],
            device_id=partner, device_id_type=MESH,
        )
    )
    exchanges[0].start()
    for copy in loads:
        copy.start()

    small[1].wait()
    small[2].wait()
    own_len = jnp.zeros((8, 128), jnp.int32)
    sub8 = lax.broadcasted_iota(jnp.int32, (8, 128), 0)
    for s in range(4):
        own_len = jnp.where((sub8 & 3) == s, len_ref[s], own_len)
    lens[...] = own_len

    exchanges[4].start()

    lane = lax.broadcasted_iota(jnp.int32, (1, 128), 1)
    lane_row = ((lane >> 6) * 2 + ((lane >> 4) & 1)) * 4 + (lane & 3)
    lane_g = ((lane >> 5) & 1) * 4 + ((lane >> 2) & 3)
    sub = lax.broadcasted_iota(jnp.int32, (512, 128), 0)
    sub_row = (sub >> 6) * 8 + ((sub >> 4) & 1) * 4 + (sub & 3)
    sub_g = ((sub >> 5) & 1) * 4 + ((sub >> 2) & 3)
    sub_code = sub_row * 8 + sub_g
    for xs in range(4):
        held = jnp.zeros((1, 128), jnp.int32)
        for r in range(16):
            held = jnp.where(lane_row == r, asg_ref[xs * 16 + r], held)
        code = held * 8 + lane_g
        perm[:, xs * 128 : (xs + 1) * 128] = jnp.where(sub_code == code, 1.0, 0.0).astype(BF)

    me_rows = pl.ds(pl.multiple_of((x * 4 + y) * 32, 32), 32)
    for k in range(4):
        pltpu.make_async_copy(q1.at[k], q1.at[k], zrecv.at[k]).wait()
    for i in range(4):
        k = head_at(y, i)
        pltpu.make_async_copy(q1.at[k], q2.at[k, me_rows], grecv.at[k]).start()
        for dx, dy in AROUND:
            y_ = (y + dy) % 4
            k = head_at(y_, i)
            pltpu.make_async_remote_copy(
                src_ref=q1.at[k], dst_ref=q2.at[k, me_rows], send_sem=gsend, recv_sem=grecv.at[k],
                device_id=dev((x + dx) % 4, y_, z, c), device_id_type=MESH,
            ).start()
        if i < 3:
            exchanges[(2, 1, 3)[i]].start()

    exchanges[4].wait_recv()
    rows = lax.broadcasted_iota(jnp.int32, (64, 128), 0)
    lanes = lax.broadcasted_iota(jnp.int32, (64, 128), 1)
    lens_own = jnp.concatenate([lens[...]] * 8, axis=0)
    lens_other = jnp.concatenate([lensall[...]] * 8, axis=0)
    row_c = (rows >> 4) & 1
    live = jnp.where(row_c == c, lens_own, lens_other) - tp * 128
    row_slot = row_c * 4 + (rows & 3)
    for s in range(8):
        limit = jnp.where(row_slot == s, live, 0)
        bias[:, s * 128 : s * 128 + 128] = jnp.where(lanes < limit, 0.0, NEG)

    for i in range(4):
        loads[i].wait()
        exchanges[i].wait_recv()

    square = (128, 128)
    eye = lax.broadcasted_iota(jnp.int32, square, 0) == lax.broadcasted_iota(jnp.int32, square, 1)
    ones = jnp.ones((1024, 128), BF)
    stat_row = lax.broadcasted_iota(jnp.int32, (16, 128), 0)

    def as_row(column):
        return jnp.sum(jnp.where(eye, column, 0.0), axis=0, keepdims=True)

    def stat_tile(top, total):
        hi = total.astype(BF).astype(F32)
        return jnp.where(stat_row == 0, top, jnp.where(stat_row == 1, hi, total - hi)).astype(BF)

    def weights(scores, top):
        return jnp.exp(scores - top).astype(BF)

    def largest(scores):
        return jnp.max(scores, axis=1, keepdims=True)

    def head(i, _):
        k = head_at(y, i)
        cols = pl.ds(pl.multiple_of(k * 128, 128), 128)
        pltpu.make_async_copy(q2.at[k], q2.at[k], grecv.at[k]).wait()
        qs[...] = dot(perm[...], q2[k], NN).astype(BF)
        chunks = [(x + a) % 4 for a in (1, 3, 2, 0)]
        parts = [qs[pl.ds(pl.multiple_of(j * 128, 128), 128), :] for j in chunks]
        keys = kbuf[:, cols]
        values = jnp.concatenate([vbuf[:, cols], ones], axis=1)
        suffix_keys = skbuf[:, :, cols].reshape(1024, 128)
        suffix_values = jnp.concatenate([svbuf[:, :, cols].reshape(1024, 128), ones], axis=1)

        s0 = dot(jnp.concatenate(parts[:2], axis=0), keys, NT) * SCALE
        s1 = dot(jnp.concatenate(parts[2:], axis=0), keys, NT) * SCALE
        own = pl.ds(pl.multiple_of(x * 128 + yh * 64, 64), 64)
        ss = dot(qs[own, :], suffix_keys, NT) * SCALE + bias[...]

        def send(a):
            pltpu.make_async_remote_copy(
                src_ref=sbuf.at[i * 4 + a], dst_ref=r1.at[i * 4 + x], send_sem=rsend, recv_sem=rrecv.at[i],
                device_id=dev(chunks[a], k, z, c), device_id_type=MESH,
            ).start()

        def put(a, m, n):
            sbuf[i * 4 + a, :128, :] = n[:, :128].astype(BF)
            sbuf[i * 4 + a, 128:, :] = stat_tile(as_row(m), as_row(n[:, 128:]))

        m0 = largest(s0).astype(BF).astype(F32)
        n0 = dot(weights(s0, m0), values, NN)
        put(0, m0[:128], n0[:128])
        send(0)
        put(1, m0[128:], n0[128:])
        send(1)

        m1, ms = largest(s1), largest(ss)
        low = jnp.full((64, 1), NEG, F32)
        ms = jnp.concatenate([jnp.where(yh == 0, ms, low), jnp.where(yh == 0, low, ms)], axis=0)
        m1 = jnp.concatenate([m1[:128], jnp.maximum(m1[128:], ms)], axis=0).astype(BF).astype(F32)
        n1 = dot(weights(s1, m1), values, NN)
        ns = dot(weights(ss, jnp.where(yh == 0, m1[128:192], m1[192:])), suffix_values, NN)
        ns = jnp.concatenate([jnp.where(yh == 0, ns, 0.0), jnp.where(yh == 0, 0.0, ns)], axis=0)
        put(2, m1[:128], n1[:128])
        send(2)
        put(3, m1[128:], n1[128:] + ns)
        pl.when(i < 3)(lambda: send(3))
        return 0

    lax.fori_loop(0, 4, head, 0)
    pltpu.make_async_copy(sbuf.at[15], r1.at[12 + x], rrecv.at[3]).start()

    def combine(pieces, top, total):
        stats = [r1[p, 128:, :].astype(F32) for p in pieces]
        tops = [s[0:1] for s in stats]
        new = functools.reduce(jnp.maximum, tops if top is None else [top] + tops)
        ws = [jnp.exp(t - new) for t in tops]
        sums = [w * (s[1:2] + s[2:3]) for w, s in zip(ws, stats)]
        old = None if top is None else jnp.exp(top - new)
        total = functools.reduce(jnp.add, sums if top is None else [old * total] + sums)
        his = [w.astype(BF).astype(F32) for w in ws]
        spread = [
            jnp.concatenate([jnp.where(eye, w, 0.0).astype(BF) for w in part], axis=1)
            for part in (his, [w - h for w, h in zip(ws, his)])
        ]
        parts = jnp.concatenate([r1[p, :128, :] for p in pieces], axis=0)
        both = dot(jnp.concatenate(spread, axis=0), parts, NN)
        return new, total, old, both[:128] + both[128:]

    for i in range(3):
        step = r1.at[pl.ds(i * 4, 4)]
        pltpu.make_async_copy(step, step, rrecv.at[i]).wait()
    top, total, _, early = combine(range(12), None, None)
    step = r1.at[pl.ds(12, 4)]
    pltpu.make_async_copy(step, step, rrecv.at[3]).wait()
    top, total, old, late = combine(range(12, 16), top, total)
    column = jnp.sum(jnp.where(eye, old, 0.0), axis=1, keepdims=True)
    flat = (column * early + late).astype(BF)
    stat = stat_tile(top, total)
    for d in range(8):
        s2[d, :16, :] = flat[d * 16 : d * 16 + 16, :]
        s2[d, 16:, :] = stat

    zt = 4 * c + y
    for o in range(1, 8):
        y_, c_ = (y + o // 2) % 4, (c + o % 2) % 2
        pltpu.make_async_remote_copy(
            src_ref=s2.at[y_ * 2 + c_], dst_ref=r2.at[z], send_sem=tsend.at[0], recv_sem=trecv,
            device_id=dev(x, y_, zt, c_), device_id_type=MESH,
        ).start()

    @pl.when(zt == z)
    def _():
        pltpu.make_async_copy(s2.at[y * 2 + c], r2.at[z], trecv).start()

    @pl.when(zt != z)
    def _():
        pltpu.make_async_remote_copy(
            src_ref=s2.at[y * 2 + c], dst_ref=r2.at[z], send_sem=tsend.at[1], recv_sem=trecv,
            device_id=dev(x, y, zt, c), device_id_type=MESH,
        ).start()

    pltpu.make_async_copy(r2, r2, trecv).wait()

    offset = y * 32 + c * 16
    pick = lax.broadcasted_iota(jnp.int32, (16, 128), 1) == lax.broadcasted_iota(jnp.int32, (16, 128), 0) + offset
    stats = [r2[i, 16:, :].astype(F32) for i in range(8)]
    m2 = functools.reduce(jnp.maximum, [s[0:1] for s in stats])
    ws = [jnp.exp(s[0:1] - m2) for s in stats]
    total = functools.reduce(jnp.add, [w * (s[1:2] + s[2:3]) for w, s in zip(ws, stats)])
    acc = jnp.zeros((16, 128), F32)
    for i in range(8):
        column = jnp.sum(jnp.where(pick, ws[i], 0.0), axis=1, keepdims=True)
        acc = acc + column * r2[i, :16, :].astype(F32)
    column = jnp.sum(jnp.where(pick, total, 0.0), axis=1, keepdims=True)
    acc = acc / column
    for g in range(4):
        out_ref[:, g * 128 : (g + 1) * 128] = acc[g * 4 : g * 4 + 4, :].astype(BF)

    for i in range(5):
        exchanges[i].wait_send()
    pltpu.make_async_copy(s2.at[pl.ds(0, 7), pl.ds(0, 16)], s2.at[pl.ds(0, 7), pl.ds(0, 16)], zsend.at[0]).wait()

    @pl.when(hz != c)
    def _():
        pltpu.make_async_copy(q0, q0, zsend.at[1]).wait()

    most = q2.at[:, pl.ds(0, 480)]
    pltpu.make_async_copy(most, most, gsend).wait()
    most = sbuf.at[pl.ds(0, 15)]
    pltpu.make_async_copy(most, most, rsend).wait()
    most = s2.at[pl.ds(0, 7)]
    pltpu.make_async_copy(most, most, tsend.at[0]).wait()

    @pl.when(zt != z)
    def _():
        pltpu.make_async_copy(s2.at[0], s2.at[0], tsend.at[1]).wait()


def shards(queries, assignment, prefix_keys, prefix_values, suffix_keys, suffix_values, lengths):
    vmem, far = pl.BlockSpec(memory_space=pltpu.VMEM), pl.BlockSpec(memory_space=pl.ANY)
    dma = pltpu.SemaphoreType.DMA
    return pl.pallas_call(
        kernel,
        out_shape=jax.ShapeDtypeStruct(queries.shape, BF),
        in_specs=[far, far, far, far, far, far, far],
        out_specs=vmem,
        scratch_shapes=[
            pltpu.VMEM((1024, 512), BF),
            pltpu.VMEM((1024, 512), BF),
            pltpu.VMEM((8, 128, 512), BF),
            pltpu.VMEM((8, 128, 512), BF),
            pltpu.VMEM((16, 128), F32),
            pltpu.VMEM((16, 128), BF),
            pltpu.VMEM((4, 32, 128), BF),
            pltpu.VMEM((4, 512, 128), BF),
            pltpu.VMEM((512, 128), BF),
            pltpu.VMEM((512, 512), BF),
            pltpu.VMEM((8, 128), jnp.int32),
            pltpu.VMEM((8, 128), jnp.int32),
            pltpu.VMEM((64, 1024), F32),
            pltpu.VMEM((16, 144, 128), BF),
            pltpu.VMEM((16, 144, 128), BF),
            pltpu.VMEM((8, 32, 128), BF),
            pltpu.VMEM((8, 32, 128), BF),
            pltpu.VMEM((4, 512), BF),
            pltpu.SMEM((64,), jnp.int32),
            pltpu.SMEM((4,), jnp.int32),
            dma((3,)),
            dma((4,)),
            dma((5,)),
            dma((5,)),
            dma((2,)),
            dma((4,)),
            dma(()),
            dma((4,)),
            dma(()),
            dma((4,)),
            dma((2,)),
            dma(()),
        ],
        compiler_params=pltpu.CompilerParams(
            collective_id=0, has_side_effects=True, vmem_limit_bytes=48 * 1024 * 1024
        ),
        cost_estimate=pl.CostEstimate(flops=1_300_000_000, bytes_accessed=4_300_000, transcendentals=2_600_000),
    )(
        *(
            pltpu.with_memory_space_constraint(operand, pltpu.HBM)
            for operand in (
                queries, assignment, lengths, prefix_keys, prefix_values, suffix_keys, suffix_values
            )
        )
    )


def solution(mesh):
    in_specs = (
        P("rep", "tp"),
        P(),
        P(("rep", "tp"), None),
        P(("rep", "tp"), None),
        P("rep", "tp", None),
        P("rep", "tp", None),
        P("rep"),
    )
    out_specs = P("rep", "tp")
    return jax.shard_map(shards, mesh=mesh, in_specs=in_specs, out_specs=out_specs, check_vma=False)
```

```python
import functools
import math

import jax
import jax.numpy as jnp
from jax import lax
from jax.experimental import pallas as pl
from jax.experimental.pallas import tpu as pltpu
from jax.sharding import PartitionSpec as P

MESH = pl.DeviceIdType.MESH
HD = 128
HEADS_CORE = 4
C2 = math.log2(math.e) * HD ** (-0.5)
NEG = -(2.0**100)
BF = jnp.bfloat16
F32 = jnp.float32
NT = (((1,), (1,)), ((), ()))
NN = (((1,), (0,)), ((), ()))
AROUND = (
    (1, 0), (3, 0), (0, 1), (0, 3), (1, 1), (3, 1), (0, 2), (1, 2), (3, 2), (1, 3), (3, 3), (2, 0), (2, 1), (2, 3), (2, 2),
)


def rem(a, n):
    return lax.rem(a, jnp.int32(n))


def div(a, n):
    return lax.div(a, jnp.int32(n))


def dot(a, b, dims):
    return lax.dot_general(a, b, dims, preferred_element_type=F32)


def kernel(
    q_hbm, asg_hbm, len_hbm, pk, pv, sk, sv, out_ref,
    kbuf, vbuf, skbuf, svbuf, qf, q0, q1, b1, q2, qs, perm, lens, lensall, bias, s0buf, sbuf, r1, s2, r2,
    q_ref, asg_ref, len_ref, smallsem, ldsem, xsend, xrecv, zsend, zrecv, bsend, brecv, fsend, gsend, grecv, rsend, rrecv, tsend, trecv,
):
    rep, tp = lax.axis_index("rep"), lax.axis_index("tp")
    x, yh, c = div(rep, 4), rem(div(rep, 2), 2), rem(rep, 2)
    z, yl = div(tp, 2), rem(tp, 2)
    y = yh * 2 + yl
    hz = div(z, 4)

    def head_at(y_, i):
        return rem(y_ + 1 + i + c * (2 - 2 * i), 4)

    def late(y_, k, c_):
        return rem((k - y_) * (1 - 2 * c_) + 7, 4) >= 2

    def dev(x_, y_, z_, c_):
        return (x_ * 4 + div(y_, 2) * 2 + c_, z_ * 2 + rem(y_, 2))

    small = [
        pltpu.make_async_copy(src, dst, smallsem.at[i])
        for i, (src, dst) in enumerate(((q_hbm, q_ref), (asg_hbm, asg_ref), (len_hbm, len_ref)))
    ]
    for copy in small:
        copy.start()

    mine = pl.multiple_of(c * 512, 512)
    theirs = pl.multiple_of((1 - c) * 512, 512)
    rows2 = pl.multiple_of(c * 512, 512)
    pairs = ((pk, kbuf), (sk, skbuf), (pv, vbuf), (sv, svbuf))

    def local_dst(i):
        buf = pairs[i][1]
        return buf.at[pl.ds(rows2, 512)] if i % 2 == 0 else buf.at[pl.ds(c * 4, 4)]

    def src_of(i, cols):
        ref = pairs[i][0]
        return ref.at[:, pl.ds(cols, 512)] if i % 2 == 0 else ref.at[:, :, pl.ds(cols, 512)]

    loads = [pltpu.make_async_copy(src_of(i, mine), local_dst(i), ldsem.at[i]) for i in range(4)]
    barrier = pltpu.get_barrier_semaphore()

    def greet(x_, y_, z_, c_):
        pl.semaphore_signal(barrier, inc=1, device_id=dev(x_, y_, z_, c_), device_id_type=MESH)

    partner = dev(x, y, z, 1 - c)
    for k in range(4):
        for cs in range(2):
            zs = 4 * c + k

            @pl.when(jnp.logical_or(zs != z, cs != c))
            def _(zs=zs, cs=cs):
                greet(x, y, zs, cs)

    greet(x, y, z, 1 - c)
    for o in range(1, 16):
        greet(rem(x + o // 4, 4), rem(y + o % 4, 4), z, c)
    across = rem(x + 2, 4)

    @pl.when(hz == c)
    def _():
        for y_ in range(4):
            greet(across, y_, z, 1 - c)

    for zs in range(8):

        @pl.when(jnp.logical_or(jnp.logical_or(zs != z, rem(z, 4) != y), hz != c))
        def _(zs=zs):
            greet(x, rem(z, 4), zs, hz)

    for copy in loads:
        copy.start()

    small[0].wait()
    q = q_ref[...].astype(F32)
    for g in range(4):
        qf[g * 4 : g * 4 + 4, :] = q[:, g * 128 : (g + 1) * 128]
    q0[...] = qf[...].astype(BF)

    n_z = jnp.where(hz == c, 7, 8)
    n_t = jnp.where(4 * c + y == z, 7, 8)
    n_b = jnp.where(hz == c, 0, 4)
    pl.semaphore_wait(barrier, 16 + n_z + n_t + n_b)

    def ztile(ref_z):
        return q1.at[rem(ref_z, 4), pl.ds(pl.multiple_of(c * 16, 16), 16)]

    for o in (4, 3, 5, 2, 6, 1, 7):
        z_ = rem(z + o, 8)
        pltpu.make_async_remote_copy(
            src_ref=q0, dst_ref=ztile(z), send_sem=zsend.at[0], recv_sem=zrecv.at[rem(z, 4)],
            device_id=dev(x, y, z_, hz), device_id_type=MESH,
        ).start()

    @pl.when(hz == c)
    def _():
        pltpu.make_async_copy(q0, ztile(z), zrecv.at[rem(z, 4)]).start()

    @pl.when(hz != c)
    def _():
        pltpu.make_async_remote_copy(
            src_ref=q0, dst_ref=ztile(z), send_sem=zsend.at[1], recv_sem=zrecv.at[rem(z, 4)],
            device_id=partner, device_id_type=MESH,
        ).start()

    for dy in range(4):
        y_ = rem(y + dy, 4)

        @pl.when(late(y_, rem(z, 4), hz))
        def _(y_=y_):
            pltpu.make_async_remote_copy(
                src_ref=q0, dst_ref=b1.at[y, pl.ds(pl.multiple_of(c * 16, 16), 16)], send_sem=bsend, recv_sem=brecv,
                device_id=dev(across, y_, z, hz), device_id_type=MESH,
            ).start()

    passes = jnp.logical_and(hz == c, late(y, rem(z, 4), c))

    exchanges = [
        pltpu.make_async_remote_copy(
            src_ref=src_of(i, theirs), dst_ref=local_dst(i), send_sem=xsend.at[i], recv_sem=xrecv.at[i],
            device_id=partner, device_id_type=MESH,
        )
        for i in range(4)
    ]
    exchanges.append(
        pltpu.make_async_remote_copy(
            src_ref=lens, dst_ref=lensall, send_sem=xsend.at[4], recv_sem=xrecv.at[4],
            device_id=partner, device_id_type=MESH,
        )
    )
    exchanges[0].start()

    small[1].wait()
    small[2].wait()
    own_len = jnp.zeros((8, 128), jnp.int32)
    sub8 = lax.broadcasted_iota(jnp.int32, (8, 128), 0)
    for s in range(4):
        own_len = jnp.where((sub8 & 3) == s, len_ref[s], own_len)
    lens[...] = own_len

    exchanges[4].start()

    lane = lax.broadcasted_iota(jnp.int32, (1, 128), 1)
    lane_row = ((lane >> 6) * 2 + ((lane >> 4) & 1)) * 4 + (lane & 3)
    lane_g = ((lane >> 5) & 1) * 4 + ((lane >> 2) & 3)
    sub = lax.broadcasted_iota(jnp.int32, (512, 128), 0)
    sub_row = (sub >> 6) * 8 + ((sub >> 4) & 1) * 4 + (sub & 3)
    sub_g = ((sub >> 5) & 1) * 4 + ((sub >> 2) & 3)
    sub_code = sub_row * 8 + sub_g
    for xs in range(4):
        held = jnp.zeros((1, 128), jnp.int32)
        for r in range(16):
            held = jnp.where(lane_row == r, asg_ref[xs * 16 + r], held)
        code = held * 8 + lane_g
        perm[:, xs * 128 : (xs + 1) * 128] = jnp.where(sub_code == code, 1.0, 0.0).astype(BF)

    for k in range(4):
        pltpu.make_async_copy(q1.at[k], q1.at[k], zrecv.at[k]).wait()
    for i in range(4):
        k = head_at(y, i)
        pltpu.make_async_copy(q1.at[k], q2.at[k, x, y], grecv.at[k]).start()
        for dx, dy in AROUND[: 15 if i < 2 else 11]:
            y_ = rem(y + dy, 4)
            k = head_at(y_, i)
            pltpu.make_async_remote_copy(
                src_ref=q1.at[k], dst_ref=q2.at[k, x, y], send_sem=gsend.at[(1, 0, 2, 0)[dx]], recv_sem=grecv.at[k],
                device_id=dev(rem(x + dx, 4), y_, z, c), device_id_type=MESH,
            ).start()
        if i == 1:

            @pl.when(passes)
            def _():
                pltpu.make_async_copy(b1, b1, brecv).wait()
                k = rem(z, 4)
                for o in (4, 3, 5, 2, 6, 1, 7):
                    pltpu.make_async_remote_copy(
                        src_ref=b1, dst_ref=q2.at[k, across], send_sem=fsend, recv_sem=grecv.at[k],
                        device_id=dev(x, y, rem(z + o, 8), c), device_id_type=MESH,
                    ).start()
                pltpu.make_async_copy(b1, q2.at[k, across], grecv.at[k]).start()

        if i < 3:
            exchanges[(2, 1, 3)[i]].start()

    exchanges[4].wait_recv()
    rows = lax.broadcasted_iota(jnp.int32, (64, 128), 0)
    lanes = lax.broadcasted_iota(jnp.int32, (64, 128), 1)
    lens_own = jnp.concatenate([lens[...]] * 8, axis=0)
    lens_other = jnp.concatenate([lensall[...]] * 8, axis=0)
    row_c = (rows >> 4) & 1
    live = jnp.where(row_c == c, lens_own, lens_other) - tp * 128
    row_slot = row_c * 4 + (rows & 3)
    for s in range(8):
        limit = jnp.where(row_slot == s, live, 0)
        bias[:, s * 128 : s * 128 + 128] = jnp.where(lanes < limit, 0.0, NEG)

    for i in range(4):
        loads[i].wait()
        exchanges[i].wait_recv()

    square = (128, 128)
    eye = lax.broadcasted_iota(jnp.int32, square, 0) == lax.broadcasted_iota(jnp.int32, square, 1)
    ones = jnp.ones((1024, 128), BF)
    stat_row = lax.broadcasted_iota(jnp.int32, (16, 128), 0)

    def as_row(column):
        return jnp.sum(jnp.where(eye, column, 0.0), axis=0, keepdims=True)

    def stat_tile(top, total):
        hi = total.astype(BF).astype(F32)
        return jnp.where(stat_row == 0, top, jnp.where(stat_row == 1, hi, total - hi)).astype(BF)

    def weights(scores, top):
        return jnp.exp2(scores - top).astype(BF)

    def largest(scores):
        return jnp.max(scores, axis=1, keepdims=True)

    def begin(i):
        k = head_at(y, i)
        pltpu.make_async_copy(q2.at[k], q2.at[k], grecv.at[k]).wait()
        qs[...] = dot(perm[...], q2[k].reshape(512, 128), NN).astype(BF)
        s0buf[...] = dot(rows_of(0, 1), kbuf[:, columns(k)], NT) * C2

    def columns(k):
        return pl.ds(pl.multiple_of(k * 128, 128), 128)

    chunks = [rem(x + a, 4) for a in (1, 3, 2, 0)]

    def rows_of(*which):
        places = [pl.ds(pl.multiple_of(chunks[a] * 128, 128), 128) for a in which]
        return jnp.concatenate([qs[place, :] for place in places], axis=0)

    own = pl.ds(pl.multiple_of(x * 128 + yh * 64, 64), 64)
    low = jnp.full((64, 1), NEG, F32)

    def head(i, last):
        k = head_at(y, i)
        cols = columns(k)
        values = jnp.concatenate([vbuf[:, cols], ones], axis=1)
        suffix_keys = skbuf[:, :, cols].reshape(1024, 128)
        suffix_values = jnp.concatenate([svbuf[:, :, cols].reshape(1024, 128), ones], axis=1)

        def send(a):
            pltpu.make_async_remote_copy(
                src_ref=sbuf.at[i * 4 + a], dst_ref=r1.at[x * 4 + y], send_sem=rsend, recv_sem=rrecv,
                device_id=dev(chunks[a], k, z, c), device_id_type=MESH,
            ).start()

        def put(a, m, n):
            sbuf[i * 4 + a, :128, :] = n[:, :128].astype(BF)
            sbuf[i * 4 + a, 128:, :] = stat_tile(as_row(m), as_row(n[:, 128:]))

        s1 = dot(rows_of(2, 3), kbuf[:, cols], NT) * C2
        ss = dot(qs[own, :], suffix_keys, NT) * C2 + bias[...]
        s0 = s0buf[...]
        m0 = largest(s0).astype(BF).astype(F32)
        n0 = dot(weights(s0, m0), values, NN)
        put(0, m0[:128], n0[:128])
        send(0)
        put(1, m0[128:], n0[128:])
        send(1)
        if not last:
            begin(i + 1)

        m1, ms = largest(s1), largest(ss)
        ms = jnp.concatenate([jnp.where(yh == 0, ms, low), jnp.where(yh == 0, low, ms)], axis=0)
        m1 = jnp.concatenate([m1[:128], jnp.maximum(m1[128:], ms)], axis=0).astype(BF).astype(F32)
        n1 = dot(weights(s1, m1), values, NN)
        ns = dot(weights(ss, jnp.where(yh == 0, m1[128:192], m1[192:])), suffix_values, NN)
        ns = jnp.concatenate([jnp.where(yh == 0, ns, 0.0), jnp.where(yh == 0, 0.0, ns)], axis=0)
        put(2, m1[:128], n1[:128])
        send(2)
        put(3, m1[128:], n1[128:] + ns)
        if last:
            pltpu.make_async_copy(sbuf.at[15], r1.at[x * 4 + y], rrecv).start()
        else:
            send(3)
        return 0

    begin(0)
    lax.fori_loop(0, 3, lambda i, _: head(i, False), 0)
    head(3, True)

    pltpu.make_async_copy(r1, r1, rrecv).wait()
    stats = [r1[i, 128:, :].astype(F32) for i in range(16)]
    top = functools.reduce(jnp.maximum, [s[0:1] for s in stats])
    ws = [jnp.exp2(s[0:1] - top) for s in stats]
    total = functools.reduce(jnp.add, [w * (s[1:2] + s[2:3]) for w, s in zip(ws, stats)])
    his = [w.astype(BF).astype(F32) for w in ws]
    spread = [
        jnp.concatenate([jnp.where(eye, w, 0.0).astype(BF) for w in part], axis=1)
        for part in (his, [w - h for w, h in zip(ws, his)])
    ]
    both = dot(jnp.concatenate(spread, axis=0), jnp.concatenate([r1[i, :128, :] for i in range(16)], axis=0), NN)
    flat = (both[:128] + both[128:]).astype(BF)
    stat = stat_tile(top, total)
    for d in range(8):
        s2[d, :16, :] = flat[d * 16 : d * 16 + 16, :]
        s2[d, 16:, :] = stat

    zt = 4 * c + y
    for o in range(1, 8):
        y_, c_ = rem(y + o // 2, 4), rem(c + o % 2, 2)
        pltpu.make_async_remote_copy(
            src_ref=s2.at[y_ * 2 + c_], dst_ref=r2.at[z], send_sem=tsend.at[0], recv_sem=trecv,
            device_id=dev(x, y_, zt, c_), device_id_type=MESH,
        ).start()

    @pl.when(zt == z)
    def _():
        pltpu.make_async_copy(s2.at[y * 2 + c], r2.at[z], trecv).start()

    @pl.when(zt != z)
    def _():
        pltpu.make_async_remote_copy(
            src_ref=s2.at[y * 2 + c], dst_ref=r2.at[z], send_sem=tsend.at[1], recv_sem=trecv,
            device_id=dev(x, y, zt, c), device_id_type=MESH,
        ).start()

    pltpu.make_async_copy(r2, r2, trecv).wait()

    offset = y * 32 + c * 16
    pick = lax.broadcasted_iota(jnp.int32, (16, 128), 1) == lax.broadcasted_iota(jnp.int32, (16, 128), 0) + offset
    stats = [r2[i, 16:, :].astype(F32) for i in range(8)]
    m2 = functools.reduce(jnp.maximum, [s[0:1] for s in stats])
    ws = [jnp.exp2(s[0:1] - m2) for s in stats]
    total = functools.reduce(jnp.add, [w * (s[1:2] + s[2:3]) for w, s in zip(ws, stats)])
    acc = jnp.zeros((16, 128), F32)
    for i in range(8):
        column = jnp.sum(jnp.where(pick, ws[i], 0.0), axis=1, keepdims=True)
        acc = acc + column * r2[i, :16, :].astype(F32)
    column = jnp.sum(jnp.where(pick, total, 0.0), axis=1, keepdims=True)
    acc = acc / column
    for g in range(4):
        out_ref[:, g * 128 : (g + 1) * 128] = acc[g * 4 : g * 4 + 4, :].astype(BF)

    for i in range(5):
        exchanges[i].wait_send()
    pltpu.make_async_copy(s2.at[pl.ds(0, 7), pl.ds(0, 16)], s2.at[pl.ds(0, 7), pl.ds(0, 16)], zsend.at[0]).wait()

    @pl.when(hz != c)
    def _():
        pltpu.make_async_copy(q0, q0, zsend.at[1]).wait()

    most = q2.at[:, pl.ds(0, 1), pl.ds(0, 3)]
    pltpu.make_async_copy(q2.at[:, pl.ds(0, 2)], q2.at[:, pl.ds(0, 2)], gsend.at[0]).wait()
    pltpu.make_async_copy(most, most, gsend.at[1]).wait()
    most = q2.at[pl.ds(0, 2), pl.ds(0, 1)]
    pltpu.make_async_copy(most, most, gsend.at[2]).wait()
    most = q1.at[pl.ds(0, 2), pl.ds(0, 16)]
    pltpu.make_async_copy(most, most, bsend).wait()

    @pl.when(passes)
    def _():
        most = sbuf.at[pl.ds(0, 14), pl.ds(0, 64)]
        pltpu.make_async_copy(most, most, fsend).wait()

    most = sbuf.at[pl.ds(0, 15)]
    pltpu.make_async_copy(most, most, rsend).wait()
    most = s2.at[pl.ds(0, 7)]
    pltpu.make_async_copy(most, most, tsend.at[0]).wait()

    @pl.when(zt != z)
    def _():
        pltpu.make_async_copy(s2.at[0], s2.at[0], tsend.at[1]).wait()


def shards(queries, assignment, prefix_keys, prefix_values, suffix_keys, suffix_values, lengths):
    vmem, far = pl.BlockSpec(memory_space=pltpu.VMEM), pl.BlockSpec(memory_space=pl.ANY)
    dma = pltpu.SemaphoreType.DMA
    return pl.pallas_call(
        kernel,
        out_shape=jax.ShapeDtypeStruct(queries.shape, BF),
        in_specs=[far, far, far, far, far, far, far],
        out_specs=vmem,
        scratch_shapes=[
            pltpu.VMEM((1024, 512), BF),
            pltpu.VMEM((1024, 512), BF),
            pltpu.VMEM((8, 128, 512), BF),
            pltpu.VMEM((8, 128, 512), BF),
            pltpu.VMEM((16, 128), F32),
            pltpu.VMEM((16, 128), BF),
            pltpu.VMEM((4, 32, 128), BF),
            pltpu.VMEM((4, 32, 128), BF),
            pltpu.VMEM((4, 4, 4, 32, 128), BF),
            pltpu.VMEM((512, 128), BF),
            pltpu.VMEM((512, 512), BF),
            pltpu.VMEM((8, 128), jnp.int32),
            pltpu.VMEM((8, 128), jnp.int32),
            pltpu.VMEM((64, 1024), F32),
            pltpu.VMEM((256, 1024), F32),
            pltpu.VMEM((16, 144, 128), BF),
            pltpu.VMEM((16, 144, 128), BF),
            pltpu.VMEM((8, 32, 128), BF),
            pltpu.VMEM((8, 32, 128), BF),
            pltpu.VMEM((4, 512), BF),
            pltpu.SMEM((64,), jnp.int32),
            pltpu.SMEM((4,), jnp.int32),
            dma((3,)),
            dma((4,)),
            dma((5,)),
            dma((5,)),
            dma((2,)),
            dma((4,)),
            dma(()),
            dma(()),
            dma(()),
            dma((3,)),
            dma((4,)),
            dma(()),
            dma(()),
            dma((2,)),
            dma(()),
        ],
        compiler_params=pltpu.CompilerParams(
            collective_id=0, has_side_effects=True, vmem_limit_bytes=48 * 1024 * 1024
        ),
        cost_estimate=pl.CostEstimate(flops=1_300_000_000, bytes_accessed=4_300_000, transcendentals=2_600_000),
    )(
        *(
            pltpu.with_memory_space_constraint(operand, pltpu.HBM)
            for operand in (
                queries, assignment, lengths, prefix_keys, prefix_values, suffix_keys, suffix_values
            )
        )
    )


def solution(mesh):
    in_specs = (
        P("rep", "tp"),
        P(),
        P(("rep", "tp"), None),
        P(("rep", "tp"), None),
        P("rep", "tp", None),
        P("rep", "tp", None),
        P("rep"),
    )
    out_specs = P("rep", "tp")
    return jax.shard_map(shards, mesh=mesh, in_specs=in_specs, out_specs=out_specs, check_vma=False)
```

```python
import functools

import jax
import jax.numpy as jnp
from jax import lax
from jax.experimental import pallas as pl
from jax.experimental.pallas import tpu as pltpu
from jax.sharding import PartitionSpec as P

MESH = pl.DeviceIdType.MESH
HD = 128
HEADS_CORE = 4
SCALE = HD ** (-0.5)
NEG = -(2.0**100)
BF = jnp.bfloat16
F32 = jnp.float32
NT = (((1,), (1,)), ((), ()))
NN = (((1,), (0,)), ((), ()))
AROUND = (
    (1, 0), (3, 0), (0, 1), (0, 3), (2, 0), (1, 1), (3, 1), (2, 1), (0, 2), (1, 2), (3, 2), (2, 2), (1, 3), (3, 3), (2, 3),
)


def dot(a, b, dims):
    return lax.dot_general(a, b, dims, preferred_element_type=F32)


def kernel(
    q_hbm, asg_hbm, len_hbm, pk, pv, sk, sv, out_ref,
    kbuf, vbuf, skbuf, svbuf, qf, q0, q1, q2, qs, perm, lens, lensall, bias, sbuf, r1, s2, r2,
    q_ref, asg_ref, len_ref, smallsem, ldsem, xsend, xrecv, zsend, zrecv, gsend, grecv, rsend, rrecv, tsend, trecv,
):
    rep, tp = lax.axis_index("rep"), lax.axis_index("tp")
    x, yh, c = rep // 4, (rep // 2) % 2, rep % 2
    z, yl = tp // 2, tp % 2
    y = yh * 2 + yl
    hz = z // 4

    def head_at(y_, i):
        return (y_ + 1 + i + c * (2 - 2 * i)) % 4

    def dev(x_, y_, z_, c_):
        return (x_ * 4 + (y_ // 2) * 2 + c_, z_ * 2 + y_ % 2)

    small = [
        pltpu.make_async_copy(src, dst, smallsem.at[i])
        for i, (src, dst) in enumerate(((q_hbm, q_ref), (asg_hbm, asg_ref), (len_hbm, len_ref)))
    ]
    for copy in small:
        copy.start()

    mine = pl.multiple_of(c * 512, 512)
    theirs = pl.multiple_of((1 - c) * 512, 512)
    rows2 = pl.multiple_of(c * 512, 512)
    pairs = ((pk, kbuf), (sk, skbuf), (pv, vbuf), (sv, svbuf))

    def local_dst(i):
        buf = pairs[i][1]
        return buf.at[pl.ds(rows2, 512)] if i % 2 == 0 else buf.at[pl.ds(c * 4, 4)]

    def src_of(i, cols):
        ref = pairs[i][0]
        return ref.at[:, pl.ds(cols, 512)] if i % 2 == 0 else ref.at[:, :, pl.ds(cols, 512)]

    loads = [pltpu.make_async_copy(src_of(i, mine), local_dst(i), ldsem.at[i]) for i in range(4)]
    barrier = pltpu.get_barrier_semaphore()

    def greet(x_, y_, z_, c_):
        pl.semaphore_signal(barrier, inc=1, device_id=dev(x_, y_, z_, c_), device_id_type=MESH)

    partner = dev(x, y, z, 1 - c)
    for k in range(4):
        for cs in range(2):
            zs = 4 * c + k

            @pl.when(jnp.logical_or(zs != z, cs != c))
            def _(zs=zs, cs=cs):
                greet(x, y, zs, cs)

    greet(x, y, z, 1 - c)
    for o in range(1, 16):
        greet((x + o // 4) % 4, (y + o % 4) % 4, z, c)
    for zs in range(8):

        @pl.when(jnp.logical_or(jnp.logical_or(zs != z, z % 4 != y), hz != c))
        def _(zs=zs):
            greet(x, z % 4, zs, hz)

    for copy in loads:
        copy.start()

    small[0].wait()
    q = q_ref[...].astype(F32)
    for g in range(4):
        qf[g * 4 : g * 4 + 4, :] = q[:, g * 128 : (g + 1) * 128]
    q0[...] = qf[...].astype(BF)

    n_z = jnp.where(hz == c, 7, 8)
    n_t = jnp.where(4 * c + y == z, 7, 8)
    pl.semaphore_wait(barrier, 16 + n_z + n_t)

    def ztile(ref_z):
        return q1.at[ref_z % 4, pl.ds(pl.multiple_of(c * 16, 16), 16)]

    for o in (4, 3, 5, 2, 6, 1, 7):
        z_ = (z + o) % 8
        pltpu.make_async_remote_copy(
            src_ref=q0, dst_ref=ztile(z), send_sem=zsend.at[0], recv_sem=zrecv.at[z % 4],
            device_id=dev(x, y, z_, hz), device_id_type=MESH,
        ).start()

    @pl.when(hz == c)
    def _():
        pltpu.make_async_copy(q0, ztile(z), zrecv.at[z % 4]).start()

    @pl.when(hz != c)
    def _():
        pltpu.make_async_remote_copy(
            src_ref=q0, dst_ref=ztile(z), send_sem=zsend.at[1], recv_sem=zrecv.at[z % 4],
            device_id=partner, device_id_type=MESH,
        ).start()

    exchanges = [
        pltpu.make_async_remote_copy(
            src_ref=src_of(i, theirs), dst_ref=local_dst(i), send_sem=xsend.at[i], recv_sem=xrecv.at[i],
            device_id=partner, device_id_type=MESH,
        )
        for i in range(4)
    ]
    exchanges.append(
        pltpu.make_async_remote_copy(
            src_ref=lens, dst_ref=lensall, send_sem=xsend.at[4], recv_sem=xrecv.at[4],
            device_id=partner, device_id_type=MESH,
        )
    )
    exchanges[0].start()

    small[1].wait()
    small[2].wait()
    own_len = jnp.zeros((8, 128), jnp.int32)
    sub8 = lax.broadcasted_iota(jnp.int32, (8, 128), 0)
    for s in range(4):
        own_len = jnp.where((sub8 & 3) == s, len_ref[s], own_len)
    lens[...] = own_len

    exchanges[4].start()

    lane = lax.broadcasted_iota(jnp.int32, (1, 128), 1)
    lane_row = ((lane >> 6) * 2 + ((lane >> 4) & 1)) * 4 + (lane & 3)
    lane_g = ((lane >> 5) & 1) * 4 + ((lane >> 2) & 3)
    sub = lax.broadcasted_iota(jnp.int32, (512, 128), 0)
    sub_row = (sub >> 6) * 8 + ((sub >> 4) & 1) * 4 + (sub & 3)
    sub_g = ((sub >> 5) & 1) * 4 + ((sub >> 2) & 3)
    sub_code = sub_row * 8 + sub_g
    for xs in range(4):
        held = jnp.zeros((1, 128), jnp.int32)
        for r in range(16):
            held = jnp.where(lane_row == r, asg_ref[xs * 16 + r], held)
        code = held * 8 + lane_g
        perm[:, xs * 128 : (xs + 1) * 128] = jnp.where(sub_code == code, 1.0, 0.0).astype(BF)

    me_rows = pl.ds(pl.multiple_of((x * 4 + y) * 32, 32), 32)
    for k in range(4):
        pltpu.make_async_copy(q1.at[k], q1.at[k], zrecv.at[k]).wait()
    for i in range(4):
        k = head_at(y, i)
        pltpu.make_async_copy(q1.at[k], q2.at[k, me_rows], grecv.at[k]).start()
        for dx, dy in AROUND:
            y_ = (y + dy) % 4
            k = head_at(y_, i)
            pltpu.make_async_remote_copy(
                src_ref=q1.at[k], dst_ref=q2.at[k, me_rows], send_sem=gsend, recv_sem=grecv.at[k],
                device_id=dev((x + dx) % 4, y_, z, c), device_id_type=MESH,
            ).start()
        if i < 3:
            exchanges[(2, 1, 3)[i]].start()

    exchanges[4].wait_recv()
    rows = lax.broadcasted_iota(jnp.int32, (64, 128), 0)
    lanes = lax.broadcasted_iota(jnp.int32, (64, 128), 1)
    lens_own = jnp.concatenate([lens[...]] * 8, axis=0)
    lens_other = jnp.concatenate([lensall[...]] * 8, axis=0)
    row_c = (rows >> 4) & 1
    live = jnp.where(row_c == c, lens_own, lens_other) - tp * 128
    row_slot = row_c * 4 + (rows & 3)
    for s in range(8):
        limit = jnp.where(row_slot == s, live, 0)
        bias[:, s * 128 : s * 128 + 128] = jnp.where(lanes < limit, 0.0, NEG)

    for i in range(4):
        loads[i].wait()
        exchanges[i].wait_recv()

    square = (128, 128)
    eye = lax.broadcasted_iota(jnp.int32, square, 0) == lax.broadcasted_iota(jnp.int32, square, 1)
    ones = jnp.ones((1024, 128), BF)
    stat_row = lax.broadcasted_iota(jnp.int32, (16, 128), 0)

    def as_row(column):
        return jnp.sum(jnp.where(eye, column, 0.0), axis=0, keepdims=True)

    def stat_tile(top, total):
        hi = total.astype(BF).astype(F32)
        return jnp.where(stat_row == 0, top, jnp.where(stat_row == 1, hi, total - hi)).astype(BF)

    def weights(scores, top):
        return jnp.exp(scores - top).astype(BF)

    def largest(scores):
        return jnp.max(scores, axis=1, keepdims=True)

    def head(i, _):
        k = head_at(y, i)
        cols = pl.ds(pl.multiple_of(k * 128, 128), 128)
        pltpu.make_async_copy(q2.at[k], q2.at[k], grecv.at[k]).wait()
        qs[...] = dot(perm[...], q2[k], NN).astype(BF)
        chunks = [(x + a) % 4 for a in (1, 3, 2, 0)]
        parts = [qs[pl.ds(pl.multiple_of(j * 128, 128), 128), :] for j in chunks]
        keys = kbuf[:, cols]
        values = jnp.concatenate([vbuf[:, cols], ones], axis=1)
        suffix_keys = skbuf[:, :, cols].reshape(1024, 128)
        suffix_values = jnp.concatenate([svbuf[:, :, cols].reshape(1024, 128), ones], axis=1)

        scores = dot(jnp.concatenate(parts, axis=0), keys, NT) * SCALE
        own = pl.ds(pl.multiple_of(x * 128 + yh * 64, 64), 64)
        ss = dot(qs[own, :], suffix_keys, NT) * SCALE + bias[...]

        def send(a):
            pltpu.make_async_remote_copy(
                src_ref=sbuf.at[i * 4 + a], dst_ref=r1.at[x * 4 + y], send_sem=rsend, recv_sem=rrecv,
                device_id=dev(chunks[a], k, z, c), device_id_type=MESH,
            ).start()

        def put(a, m, n):
            sbuf[i * 4 + a, :128, :] = n[:, :128].astype(BF)
            sbuf[i * 4 + a, 128:, :] = stat_tile(as_row(m), as_row(n[:, 128:]))

        m, ms = largest(scores), largest(ss)
        low = jnp.full((64, 1), NEG, F32)
        ms = jnp.concatenate([jnp.where(yh == 0, ms, low), jnp.where(yh == 0, low, ms)], axis=0)
        m = jnp.concatenate([m[:384], jnp.maximum(m[384:], ms)], axis=0).astype(BF).astype(F32)
        n = dot(weights(scores, m), values, NN)
        for a in range(3):
            put(a, m[a * 128 : a * 128 + 128], n[a * 128 : a * 128 + 128])
            send(a)
        ns = dot(weights(ss, jnp.where(yh == 0, m[384:448], m[448:])), suffix_values, NN)
        ns = jnp.concatenate([jnp.where(yh == 0, ns, 0.0), jnp.where(yh == 0, 0.0, ns)], axis=0)
        put(3, m[384:], n[384:] + ns)
        pl.when(i < 3)(lambda: send(3))
        return 0

    lax.fori_loop(0, 4, head, 0)
    pltpu.make_async_copy(sbuf.at[15], r1.at[x * 4 + y], rrecv).start()

    pltpu.make_async_copy(r1, r1, rrecv).wait()
    stats = [r1[i, 128:, :].astype(F32) for i in range(16)]
    top = functools.reduce(jnp.maximum, [s[0:1] for s in stats])
    ws = [jnp.exp(s[0:1] - top) for s in stats]
    total = functools.reduce(jnp.add, [w * (s[1:2] + s[2:3]) for w, s in zip(ws, stats)])
    his = [w.astype(BF).astype(F32) for w in ws]
    spread = [
        jnp.concatenate([jnp.where(eye, w, 0.0).astype(BF) for w in part], axis=1)
        for part in (his, [w - h for w, h in zip(ws, his)])
    ]
    both = dot(jnp.concatenate(spread, axis=0), jnp.concatenate([r1[i, :128, :] for i in range(16)], axis=0), NN)
    flat = (both[:128] + both[128:]).astype(BF)
    stat = stat_tile(top, total)
    for d in range(8):
        s2[d, :16, :] = flat[d * 16 : d * 16 + 16, :]
        s2[d, 16:, :] = stat

    zt = 4 * c + y
    for o in range(1, 8):
        y_, c_ = (y + o // 2) % 4, (c + o % 2) % 2
        pltpu.make_async_remote_copy(
            src_ref=s2.at[y_ * 2 + c_], dst_ref=r2.at[z], send_sem=tsend.at[0], recv_sem=trecv,
            device_id=dev(x, y_, zt, c_), device_id_type=MESH,
        ).start()

    @pl.when(zt == z)
    def _():
        pltpu.make_async_copy(s2.at[y * 2 + c], r2.at[z], trecv).start()

    @pl.when(zt != z)
    def _():
        pltpu.make_async_remote_copy(
            src_ref=s2.at[y * 2 + c], dst_ref=r2.at[z], send_sem=tsend.at[1], recv_sem=trecv,
            device_id=dev(x, y, zt, c), device_id_type=MESH,
        ).start()

    pltpu.make_async_copy(r2, r2, trecv).wait()

    offset = y * 32 + c * 16
    pick = lax.broadcasted_iota(jnp.int32, (16, 128), 1) == lax.broadcasted_iota(jnp.int32, (16, 128), 0) + offset
    stats = [r2[i, 16:, :].astype(F32) for i in range(8)]
    m2 = functools.reduce(jnp.maximum, [s[0:1] for s in stats])
    ws = [jnp.exp(s[0:1] - m2) for s in stats]
    total = functools.reduce(jnp.add, [w * (s[1:2] + s[2:3]) for w, s in zip(ws, stats)])
    acc = jnp.zeros((16, 128), F32)
    for i in range(8):
        column = jnp.sum(jnp.where(pick, ws[i], 0.0), axis=1, keepdims=True)
        acc = acc + column * r2[i, :16, :].astype(F32)
    column = jnp.sum(jnp.where(pick, total, 0.0), axis=1, keepdims=True)
    acc = acc / column
    for g in range(4):
        out_ref[:, g * 128 : (g + 1) * 128] = acc[g * 4 : g * 4 + 4, :].astype(BF)

    for i in range(5):
        exchanges[i].wait_send()
    pltpu.make_async_copy(s2.at[pl.ds(0, 7), pl.ds(0, 16)], s2.at[pl.ds(0, 7), pl.ds(0, 16)], zsend.at[0]).wait()

    @pl.when(hz != c)
    def _():
        pltpu.make_async_copy(q0, q0, zsend.at[1]).wait()

    most = q2.at[:, pl.ds(0, 480)]
    pltpu.make_async_copy(most, most, gsend).wait()
    most = sbuf.at[pl.ds(0, 15)]
    pltpu.make_async_copy(most, most, rsend).wait()
    most = s2.at[pl.ds(0, 7)]
    pltpu.make_async_copy(most, most, tsend.at[0]).wait()

    @pl.when(zt != z)
    def _():
        pltpu.make_async_copy(s2.at[0], s2.at[0], tsend.at[1]).wait()


def shards(queries, assignment, prefix_keys, prefix_values, suffix_keys, suffix_values, lengths):
    vmem, far = pl.BlockSpec(memory_space=pltpu.VMEM), pl.BlockSpec(memory_space=pl.ANY)
    dma = pltpu.SemaphoreType.DMA
    return pl.pallas_call(
        kernel,
        out_shape=jax.ShapeDtypeStruct(queries.shape, BF),
        in_specs=[far, far, far, far, far, far, far],
        out_specs=vmem,
        scratch_shapes=[
            pltpu.VMEM((1024, 512), BF),
            pltpu.VMEM((1024, 512), BF),
            pltpu.VMEM((8, 128, 512), BF),
            pltpu.VMEM((8, 128, 512), BF),
            pltpu.VMEM((16, 128), F32),
            pltpu.VMEM((16, 128), BF),
            pltpu.VMEM((4, 32, 128), BF),
            pltpu.VMEM((4, 512, 128), BF),
            pltpu.VMEM((512, 128), BF),
            pltpu.VMEM((512, 512), BF),
            pltpu.VMEM((8, 128), jnp.int32),
            pltpu.VMEM((8, 128), jnp.int32),
            pltpu.VMEM((64, 1024), F32),
            pltpu.VMEM((16, 144, 128), BF),
            pltpu.VMEM((16, 144, 128), BF),
            pltpu.VMEM((8, 32, 128), BF),
            pltpu.VMEM((8, 32, 128), BF),
            pltpu.VMEM((4, 512), BF),
            pltpu.SMEM((64,), jnp.int32),
            pltpu.SMEM((4,), jnp.int32),
            dma((3,)),
            dma((4,)),
            dma((5,)),
            dma((5,)),
            dma((2,)),
            dma((4,)),
            dma(()),
            dma((4,)),
            dma(()),
            dma(()),
            dma((2,)),
            dma(()),
        ],
        compiler_params=pltpu.CompilerParams(
            collective_id=0, has_side_effects=True, vmem_limit_bytes=48 * 1024 * 1024
        ),
        cost_estimate=pl.CostEstimate(flops=1_300_000_000, bytes_accessed=4_300_000, transcendentals=2_600_000),
    )(
        *(
            pltpu.with_memory_space_constraint(operand, pltpu.HBM)
            for operand in (
                queries, assignment, lengths, prefix_keys, prefix_values, suffix_keys, suffix_values
            )
        )
    )


def solution(mesh):
    in_specs = (
        P("rep", "tp"),
        P(),
        P(("rep", "tp"), None),
        P(("rep", "tp"), None),
        P("rep", "tp", None),
        P("rep", "tp", None),
        P("rep"),
    )
    out_specs = P("rep", "tp")
    return jax.shard_map(shards, mesh=mesh, in_specs=in_specs, out_specs=out_specs, check_vma=False)
```

```python
import functools

import jax
import jax.numpy as jnp
from jax import lax
from jax.experimental import pallas as pl
from jax.experimental.pallas import tpu as pltpu
from jax.sharding import PartitionSpec as P

MESH = pl.DeviceIdType.MESH
HD = 128
HEADS_CORE = 4
SCALE = HD ** (-0.5)
NEG = -(2.0**100)
BF = jnp.bfloat16
F32 = jnp.float32
NT = (((1,), (1,)), ((), ()))
NN = (((1,), (0,)), ((), ()))
AROUND = (
    (1, 0), (3, 0), (0, 1), (0, 3), (2, 0), (1, 1), (3, 1), (2, 1), (0, 2), (1, 2), (3, 2), (2, 2), (1, 3), (3, 3), (2, 3),
)


def dot(a, b, dims):
    return lax.dot_general(a, b, dims, preferred_element_type=F32)


def kernel(
    q_hbm, asg_hbm, len_hbm, pk, pv, sk, sv, out_ref,
    kbuf, vbuf, skbuf, svbuf, qf, q0, q1, q2, qs, perm, lens, lensall, bias, sbuf, r1, s2, r2,
    q_ref, asg_ref, len_ref, smallsem, ldsem, xsend, xrecv, zsend, zrecv, gsend, grecv, rsend, rrecv, tsend, trecv,
):
    rep, tp = lax.axis_index("rep"), lax.axis_index("tp")
    x, yh, c = rep // 4, (rep // 2) % 2, rep % 2
    z, yl = tp // 2, tp % 2
    y = yh * 2 + yl
    hz = z // 4

    def head_at(y_, i):
        return (y_ + 1 + i + c * (2 - 2 * i)) % 4

    def dev(x_, y_, z_, c_):
        return (x_ * 4 + (y_ // 2) * 2 + c_, z_ * 2 + y_ % 2)

    small = [
        pltpu.make_async_copy(src, dst, smallsem.at[i])
        for i, (src, dst) in enumerate(((q_hbm, q_ref), (asg_hbm, asg_ref), (len_hbm, len_ref)))
    ]
    for copy in small:
        copy.start()

    mine = pl.multiple_of(c * 512, 512)
    theirs = pl.multiple_of((1 - c) * 512, 512)
    rows2 = pl.multiple_of(c * 512, 512)
    pairs = ((pk, kbuf), (sk, skbuf), (pv, vbuf), (sv, svbuf))

    def local_dst(i):
        buf = pairs[i][1]
        return buf.at[pl.ds(rows2, 512)] if i % 2 == 0 else buf.at[pl.ds(c * 4, 4)]

    def src_of(i, cols):
        ref = pairs[i][0]
        return ref.at[:, pl.ds(cols, 512)] if i % 2 == 0 else ref.at[:, :, pl.ds(cols, 512)]

    loads = [pltpu.make_async_copy(src_of(i, mine), local_dst(i), ldsem.at[i]) for i in range(4)]
    barrier = pltpu.get_barrier_semaphore()

    def greet(x_, y_, z_, c_):
        pl.semaphore_signal(barrier, inc=1, device_id=dev(x_, y_, z_, c_), device_id_type=MESH)

    partner = dev(x, y, z, 1 - c)
    for k in range(4):
        for cs in range(2):
            zs = 4 * c + k

            @pl.when(jnp.logical_or(zs != z, cs != c))
            def _(zs=zs, cs=cs):
                greet(x, y, zs, cs)

    greet(x, y, z, 1 - c)
    for o in range(1, 16):
        greet((x + o // 4) % 4, (y + o % 4) % 4, z, c)
    for zs in range(8):

        @pl.when(jnp.logical_or(jnp.logical_or(zs != z, z % 4 != y), hz != c))
        def _(zs=zs):
            greet(x, z % 4, zs, hz)

    small[0].wait()
    q = q_ref[...].astype(F32)
    for g in range(4):
        qf[g * 4 : g * 4 + 4, :] = q[:, g * 128 : (g + 1) * 128]
    q0[...] = qf[...].astype(BF)

    n_z = jnp.where(hz == c, 7, 8)
    n_t = jnp.where(4 * c + y == z, 7, 8)
    pl.semaphore_wait(barrier, 16 + n_z + n_t)

    def ztile(ref_z):
        return q1.at[ref_z % 4, pl.ds(pl.multiple_of(c * 16, 16), 16)]

    for o in (4, 3, 5, 2, 6, 1, 7):
        z_ = (z + o) % 8
        pltpu.make_async_remote_copy(
            src_ref=q0, dst_ref=ztile(z), send_sem=zsend.at[0], recv_sem=zrecv.at[z % 4],
            device_id=dev(x, y, z_, hz), device_id_type=MESH,
        ).start()

    @pl.when(hz == c)
    def _():
        pltpu.make_async_copy(q0, ztile(z), zrecv.at[z % 4]).start()

    @pl.when(hz != c)
    def _():
        pltpu.make_async_remote_copy(
            src_ref=q0, dst_ref=ztile(z), send_sem=zsend.at[1], recv_sem=zrecv.at[z % 4],
            device_id=partner, device_id_type=MESH,
        ).start()

    exchanges = [
        pltpu.make_async_remote_copy(
            src_ref=src_of(i, theirs), dst_ref=local_dst(i), send_sem=xsend.at[i], recv_sem=xrecv.at[i],
            device_id=partner, device_id_type=MESH,
        )
        for i in range(4)
    ]
    exchanges.append(
        pltpu.make_async_remote_copy(
            src_ref=lens, dst_ref=lensall, send_sem=xsend.at[4], recv_sem=xrecv.at[4],
            device_id=partner, device_id_type=MESH,
        )
    )
    exchanges[0].start()
    for copy in loads:
        copy.start()

    small[1].wait()
    small[2].wait()
    own_len = jnp.zeros((8, 128), jnp.int32)
    sub8 = lax.broadcasted_iota(jnp.int32, (8, 128), 0)
    for s in range(4):
        own_len = jnp.where((sub8 & 3) == s, len_ref[s], own_len)
    lens[...] = own_len

    exchanges[4].start()

    lane = lax.broadcasted_iota(jnp.int32, (1, 128), 1)
    lane_row = ((lane >> 6) * 2 + ((lane >> 4) & 1)) * 4 + (lane & 3)
    lane_g = ((lane >> 5) & 1) * 4 + ((lane >> 2) & 3)
    sub = lax.broadcasted_iota(jnp.int32, (512, 128), 0)
    sub_row = (sub >> 6) * 8 + ((sub >> 4) & 1) * 4 + (sub & 3)
    sub_g = ((sub >> 5) & 1) * 4 + ((sub >> 2) & 3)
    sub_code = sub_row * 8 + sub_g
    for xs in range(4):
        held = jnp.zeros((1, 128), jnp.int32)
        for r in range(16):
            held = jnp.where(lane_row == r, asg_ref[xs * 16 + r], held)
        code = held * 8 + lane_g
        perm[:, xs * 128 : (xs + 1) * 128] = jnp.where(sub_code == code, 1.0, 0.0).astype(BF)

    me_rows = pl.ds(pl.multiple_of((x * 4 + y) * 32, 32), 32)
    for k in range(4):
        pltpu.make_async_copy(q1.at[k], q1.at[k], zrecv.at[k]).wait()
    for i in range(4):
        k = head_at(y, i)
        pltpu.make_async_copy(q1.at[k], q2.at[k, me_rows], grecv.at[k]).start()
        for dx, dy in AROUND:
            y_ = (y + dy) % 4
            k = head_at(y_, i)
            pltpu.make_async_remote_copy(
                src_ref=q1.at[k], dst_ref=q2.at[k, me_rows], send_sem=gsend, recv_sem=grecv.at[k],
                device_id=dev((x + dx) % 4, y_, z, c), device_id_type=MESH,
            ).start()
        if i < 3:
            exchanges[(2, 1, 3)[i]].start()

    exchanges[4].wait_recv()
    rows = lax.broadcasted_iota(jnp.int32, (64, 128), 0)
    lanes = lax.broadcasted_iota(jnp.int32, (64, 128), 1)
    lens_own = jnp.concatenate([lens[...]] * 8, axis=0)
    lens_other = jnp.concatenate([lensall[...]] * 8, axis=0)
    row_c = (rows >> 4) & 1
    live = jnp.where(row_c == c, lens_own, lens_other) - tp * 128
    row_slot = row_c * 4 + (rows & 3)
    for s in range(8):
        limit = jnp.where(row_slot == s, live, 0)
        bias[:, s * 128 : s * 128 + 128] = jnp.where(lanes < limit, 0.0, NEG)

    for i in range(4):
        loads[i].wait()
        exchanges[i].wait_recv()

    square = (128, 128)
    eye = lax.broadcasted_iota(jnp.int32, square, 0) == lax.broadcasted_iota(jnp.int32, square, 1)
    ones = jnp.ones((1024, 128), BF)
    stat_row = lax.broadcasted_iota(jnp.int32, (16, 128), 0)

    def as_row(column):
        return jnp.sum(jnp.where(eye, column, 0.0), axis=0, keepdims=True)

    def stat_tile(top, total):
        hi = total.astype(BF).astype(F32)
        return jnp.where(stat_row == 0, top, jnp.where(stat_row == 1, hi, total - hi)).astype(BF)

    def weights(scores, top):
        return jnp.exp(scores - top).astype(BF)

    def largest(scores):
        return jnp.max(scores, axis=1, keepdims=True)

    def head(i, _):
        k = head_at(y, i)
        cols = pl.ds(pl.multiple_of(k * 128, 128), 128)
        pltpu.make_async_copy(q2.at[k], q2.at[k], grecv.at[k]).wait()
        qs[...] = dot(perm[...], q2[k], NN).astype(BF)
        chunks = [(x + a) % 4 for a in (1, 3, 2, 0)]
        parts = [qs[pl.ds(pl.multiple_of(j * 128, 128), 128), :] for j in chunks]
        keys = kbuf[:, cols]
        values = jnp.concatenate([vbuf[:, cols], ones], axis=1)
        suffix_keys = skbuf[:, :, cols].reshape(1024, 128)
        suffix_values = jnp.concatenate([svbuf[:, :, cols].reshape(1024, 128), ones], axis=1)

        s0 = dot(jnp.concatenate(parts[:2], axis=0), keys, NT) * SCALE
        s1 = dot(parts[2], keys, NT) * SCALE
        s3 = dot(parts[3], keys, NT) * SCALE
        own = pl.ds(pl.multiple_of(x * 128 + yh * 64, 64), 64)
        ss = dot(qs[own, :], suffix_keys, NT) * SCALE + bias[...]

        def send(a):
            pltpu.make_async_remote_copy(
                src_ref=sbuf.at[i * 4 + a], dst_ref=r1.at[i * 4 + x], send_sem=rsend, recv_sem=rrecv.at[i],
                device_id=dev(chunks[a], k, z, c), device_id_type=MESH,
            ).start()

        def put(a, m, n):
            sbuf[i * 4 + a, :128, :] = n[:, :128].astype(BF)
            sbuf[i * 4 + a, 128:, :] = stat_tile(as_row(m), as_row(n[:, 128:]))

        m0 = largest(s0).astype(BF).astype(F32)
        n0 = dot(weights(s0, m0), values, NN)
        put(0, m0[:128], n0[:128])
        send(0)
        put(1, m0[128:], n0[128:])
        send(1)

        m1 = largest(s1).astype(BF).astype(F32)
        put(2, m1, dot(weights(s1, m1), values, NN))
        send(2)

        m2, ms = largest(s3), largest(ss)
        low = jnp.full((64, 1), NEG, F32)
        ms = jnp.concatenate([jnp.where(yh == 0, ms, low), jnp.where(yh == 0, low, ms)], axis=0)
        m2 = jnp.maximum(m2, ms).astype(BF).astype(F32)
        n2 = dot(weights(s3, m2), values, NN)
        ns = dot(weights(ss, jnp.where(yh == 0, m2[:64], m2[64:])), suffix_values, NN)
        ns = jnp.concatenate([jnp.where(yh == 0, ns, 0.0), jnp.where(yh == 0, 0.0, ns)], axis=0)
        put(3, m2, n2 + ns)
        pl.when(i < 3)(lambda: send(3))
        return 0

    lax.fori_loop(0, 4, head, 0)
    pltpu.make_async_copy(sbuf.at[15], r1.at[12 + x], rrecv.at[3]).start()

    def combine(pieces, top, total):
        stats = [r1[p, 128:, :].astype(F32) for p in pieces]
        tops = [s[0:1] for s in stats]
        new = functools.reduce(jnp.maximum, tops if top is None else [top] + tops)
        ws = [jnp.exp(t - new) for t in tops]
        sums = [w * (s[1:2] + s[2:3]) for w, s in zip(ws, stats)]
        old = None if top is None else jnp.exp(top - new)
        total = functools.reduce(jnp.add, sums if top is None else [old * total] + sums)
        his = [w.astype(BF).astype(F32) for w in ws]
        spread = [
            jnp.concatenate([jnp.where(eye, w, 0.0).astype(BF) for w in part], axis=1)
            for part in (his, [w - h for w, h in zip(ws, his)])
        ]
        parts = jnp.concatenate([r1[p, :128, :] for p in pieces], axis=0)
        both = dot(jnp.concatenate(spread, axis=0), parts, NN)
        return new, total, old, both[:128] + both[128:]

    for i in range(3):
        step = r1.at[pl.ds(i * 4, 4)]
        pltpu.make_async_copy(step, step, rrecv.at[i]).wait()
    top, total, _, early = combine(range(12), None, None)
    step = r1.at[pl.ds(12, 4)]
    pltpu.make_async_copy(step, step, rrecv.at[3]).wait()
    top, total, old, late = combine(range(12, 16), top, total)
    column = jnp.sum(jnp.where(eye, old, 0.0), axis=1, keepdims=True)
    flat = (column * early + late).astype(BF)
    stat = stat_tile(top, total)
    for d in range(8):
        s2[d, :16, :] = flat[d * 16 : d * 16 + 16, :]
        s2[d, 16:, :] = stat

    zt = 4 * c + y
    for o in range(1, 8):
        y_, c_ = (y + o // 2) % 4, (c + o % 2) % 2
        pltpu.make_async_remote_copy(
            src_ref=s2.at[y_ * 2 + c_], dst_ref=r2.at[z], send_sem=tsend.at[0], recv_sem=trecv,
            device_id=dev(x, y_, zt, c_), device_id_type=MESH,
        ).start()

    @pl.when(zt == z)
    def _():
        pltpu.make_async_copy(s2.at[y * 2 + c], r2.at[z], trecv).start()

    @pl.when(zt != z)
    def _():
        pltpu.make_async_remote_copy(
            src_ref=s2.at[y * 2 + c], dst_ref=r2.at[z], send_sem=tsend.at[1], recv_sem=trecv,
            device_id=dev(x, y, zt, c), device_id_type=MESH,
        ).start()

    pltpu.make_async_copy(r2, r2, trecv).wait()

    offset = y * 32 + c * 16
    pick = lax.broadcasted_iota(jnp.int32, (16, 128), 1) == lax.broadcasted_iota(jnp.int32, (16, 128), 0) + offset
    stats = [r2[i, 16:, :].astype(F32) for i in range(8)]
    m2 = functools.reduce(jnp.maximum, [s[0:1] for s in stats])
    ws = [jnp.exp(s[0:1] - m2) for s in stats]
    total = functools.reduce(jnp.add, [w * (s[1:2] + s[2:3]) for w, s in zip(ws, stats)])
    acc = jnp.zeros((16, 128), F32)
    for i in range(8):
        column = jnp.sum(jnp.where(pick, ws[i], 0.0), axis=1, keepdims=True)
        acc = acc + column * r2[i, :16, :].astype(F32)
    column = jnp.sum(jnp.where(pick, total, 0.0), axis=1, keepdims=True)
    acc = acc / column
    for g in range(4):
        out_ref[:, g * 128 : (g + 1) * 128] = acc[g * 4 : g * 4 + 4, :].astype(BF)

    for i in range(5):
        exchanges[i].wait_send()
    pltpu.make_async_copy(s2.at[pl.ds(0, 7), pl.ds(0, 16)], s2.at[pl.ds(0, 7), pl.ds(0, 16)], zsend.at[0]).wait()

    @pl.when(hz != c)
    def _():
        pltpu.make_async_copy(q0, q0, zsend.at[1]).wait()

    most = q2.at[:, pl.ds(0, 480)]
    pltpu.make_async_copy(most, most, gsend).wait()
    most = sbuf.at[pl.ds(0, 15)]
    pltpu.make_async_copy(most, most, rsend).wait()
    most = s2.at[pl.ds(0, 7)]
    pltpu.make_async_copy(most, most, tsend.at[0]).wait()

    @pl.when(zt != z)
    def _():
        pltpu.make_async_copy(s2.at[0], s2.at[0], tsend.at[1]).wait()


def shards(queries, assignment, prefix_keys, prefix_values, suffix_keys, suffix_values, lengths):
    vmem, far = pl.BlockSpec(memory_space=pltpu.VMEM), pl.BlockSpec(memory_space=pl.ANY)
    dma = pltpu.SemaphoreType.DMA
    return pl.pallas_call(
        kernel,
        out_shape=jax.ShapeDtypeStruct(queries.shape, BF),
        in_specs=[far, far, far, far, far, far, far],
        out_specs=vmem,
        scratch_shapes=[
            pltpu.VMEM((1024, 512), BF),
            pltpu.VMEM((1024, 512), BF),
            pltpu.VMEM((8, 128, 512), BF),
            pltpu.VMEM((8, 128, 512), BF),
            pltpu.VMEM((16, 128), F32),
            pltpu.VMEM((16, 128), BF),
            pltpu.VMEM((4, 32, 128), BF),
            pltpu.VMEM((4, 512, 128), BF),
            pltpu.VMEM((512, 128), BF),
            pltpu.VMEM((512, 512), BF),
            pltpu.VMEM((8, 128), jnp.int32),
            pltpu.VMEM((8, 128), jnp.int32),
            pltpu.VMEM((64, 1024), F32),
            pltpu.VMEM((16, 144, 128), BF),
            pltpu.VMEM((16, 144, 128), BF),
            pltpu.VMEM((8, 32, 128), BF),
            pltpu.VMEM((8, 32, 128), BF),
            pltpu.VMEM((4, 512), BF),
            pltpu.SMEM((64,), jnp.int32),
            pltpu.SMEM((4,), jnp.int32),
            dma((3,)),
            dma((4,)),
            dma((5,)),
            dma((5,)),
            dma((2,)),
            dma((4,)),
            dma(()),
            dma((4,)),
            dma(()),
            dma((4,)),
            dma((2,)),
            dma(()),
        ],
        compiler_params=pltpu.CompilerParams(
            collective_id=0, has_side_effects=True, vmem_limit_bytes=48 * 1024 * 1024
        ),
        cost_estimate=pl.CostEstimate(flops=1_300_000_000, bytes_accessed=4_300_000, transcendentals=2_600_000),
    )(
        *(
            pltpu.with_memory_space_constraint(operand, pltpu.HBM)
            for operand in (
                queries, assignment, lengths, prefix_keys, prefix_values, suffix_keys, suffix_values
            )
        )
    )


def solution(mesh):
    in_specs = (
        P("rep", "tp"),
        P(),
        P(("rep", "tp"), None),
        P(("rep", "tp"), None),
        P("rep", "tp", None),
        P("rep", "tp", None),
        P("rep"),
    )
    out_specs = P("rep", "tp")
    return jax.shard_map(shards, mesh=mesh, in_specs=in_specs, out_specs=out_specs, check_vma=False)
```

```python
import functools

import jax
import jax.numpy as jnp
from jax import lax
from jax.experimental import pallas as pl
from jax.experimental.pallas import tpu as pltpu
from jax.sharding import PartitionSpec as P

MESH = pl.DeviceIdType.MESH
HD = 128
HEADS_CORE = 4
SCALE = HD ** (-0.5)
NEG = -(2.0**100)
BF = jnp.bfloat16
F32 = jnp.float32
NT = (((1,), (1,)), ((), ()))
NN = (((1,), (0,)), ((), ()))
AROUND = (
    (1, 0), (3, 0), (0, 1), (0, 3), (2, 0), (1, 1), (3, 1), (2, 1), (0, 2), (1, 2), (3, 2), (2, 2), (1, 3), (3, 3), (2, 3),
)


def dot(a, b, dims):
    return lax.dot_general(a, b, dims, preferred_element_type=F32)


def kernel(
    q_hbm, asg_hbm, len_hbm, pk, pv, sk, sv, out_ref,
    kbuf, vbuf, skbuf, svbuf, qf, q0, q1, q2, qs, perm, lens, lensall, bias, sbuf, r1, s2, r2,
    q_ref, asg_ref, len_ref, smallsem, ldsem, xsend, xrecv, zsend, zrecv, gsend, grecv, rsend, rrecv, tsend, trecv,
):
    rep, tp = lax.axis_index("rep"), lax.axis_index("tp")
    x, yh, c = rep // 4, (rep // 2) % 2, rep % 2
    z, yl = tp // 2, tp % 2
    y = yh * 2 + yl
    hz = z // 4

    def head_at(y_, i):
        return (y_ + 1 + i + c * (2 - 2 * i)) % 4

    def dev(x_, y_, z_, c_):
        return (x_ * 4 + (y_ // 2) * 2 + c_, z_ * 2 + y_ % 2)

    small = [
        pltpu.make_async_copy(src, dst, smallsem.at[i])
        for i, (src, dst) in enumerate(((q_hbm, q_ref), (asg_hbm, asg_ref), (len_hbm, len_ref)))
    ]
    for copy in small:
        copy.start()

    mine = pl.multiple_of(c * 512, 512)
    theirs = pl.multiple_of((1 - c) * 512, 512)
    rows2 = pl.multiple_of(c * 512, 512)
    pairs = ((pk, kbuf), (sk, skbuf), (pv, vbuf), (sv, svbuf))

    def local_dst(i):
        buf = pairs[i][1]
        return buf.at[pl.ds(rows2, 512)] if i % 2 == 0 else buf.at[pl.ds(c * 4, 4)]

    def src_of(i, cols):
        ref = pairs[i][0]
        return ref.at[:, pl.ds(cols, 512)] if i % 2 == 0 else ref.at[:, :, pl.ds(cols, 512)]

    loads = [pltpu.make_async_copy(src_of(i, mine), local_dst(i), ldsem.at[i]) for i in range(4)]
    barrier = pltpu.get_barrier_semaphore()

    def greet(x_, y_, z_, c_):
        pl.semaphore_signal(barrier, inc=1, device_id=dev(x_, y_, z_, c_), device_id_type=MESH)

    partner = dev(x, y, z, 1 - c)
    for k in range(4):
        for cs in range(2):
            zs = 4 * c + k

            @pl.when(jnp.logical_or(zs != z, cs != c))
            def _(zs=zs, cs=cs):
                greet(x, y, zs, cs)

    greet(x, y, z, 1 - c)
    for o in range(1, 16):
        greet((x + o // 4) % 4, (y + o % 4) % 4, z, c)
    for zs in range(8):

        @pl.when(jnp.logical_or(jnp.logical_or(zs != z, z % 4 != y), hz != c))
        def _(zs=zs):
            greet(x, z % 4, zs, hz)

    for copy in loads:
        copy.start()

    small[0].wait()
    q = q_ref[...].astype(F32)
    for g in range(4):
        qf[g * 4 : g * 4 + 4, :] = q[:, g * 128 : (g + 1) * 128]
    q0[...] = qf[...].astype(BF)

    n_z = jnp.where(hz == c, 7, 8)
    n_t = jnp.where(4 * c + y == z, 7, 8)
    pl.semaphore_wait(barrier, 16 + n_z + n_t)

    def ztile(ref_z):
        return q1.at[ref_z % 4, pl.ds(pl.multiple_of(c * 16, 16), 16)]

    for o in (4, 3, 5, 2, 6, 1, 7):
        z_ = (z + o) % 8
        pltpu.make_async_remote_copy(
            src_ref=q0, dst_ref=ztile(z), send_sem=zsend.at[0], recv_sem=zrecv.at[z % 4],
            device_id=dev(x, y, z_, hz), device_id_type=MESH,
        ).start()

    @pl.when(hz == c)
    def _():
        pltpu.make_async_copy(q0, ztile(z), zrecv.at[z % 4]).start()

    @pl.when(hz != c)
    def _():
        pltpu.make_async_remote_copy(
            src_ref=q0, dst_ref=ztile(z), send_sem=zsend.at[1], recv_sem=zrecv.at[z % 4],
            device_id=partner, device_id_type=MESH,
        ).start()

    exchanges = [
        pltpu.make_async_remote_copy(
            src_ref=src_of(i, theirs), dst_ref=local_dst(i), send_sem=xsend.at[i], recv_sem=xrecv.at[i],
            device_id=partner, device_id_type=MESH,
        )
        for i in range(4)
    ]
    exchanges.append(
        pltpu.make_async_remote_copy(
            src_ref=lens, dst_ref=lensall, send_sem=xsend.at[4], recv_sem=xrecv.at[4],
            device_id=partner, device_id_type=MESH,
        )
    )
    exchanges[0].start()

    small[1].wait()
    small[2].wait()
    own_len = jnp.zeros((8, 128), jnp.int32)
    sub8 = lax.broadcasted_iota(jnp.int32, (8, 128), 0)
    for s in range(4):
        own_len = jnp.where((sub8 & 3) == s, len_ref[s], own_len)
    lens[...] = own_len

    exchanges[4].start()

    lane = lax.broadcasted_iota(jnp.int32, (1, 128), 1)
    lane_row = ((lane >> 6) * 2 + ((lane >> 4) & 1)) * 4 + (lane & 3)
    lane_g = ((lane >> 5) & 1) * 4 + ((lane >> 2) & 3)
    sub = lax.broadcasted_iota(jnp.int32, (512, 128), 0)
    sub_row = (sub >> 6) * 8 + ((sub >> 4) & 1) * 4 + (sub & 3)
    sub_g = ((sub >> 5) & 1) * 4 + ((sub >> 2) & 3)
    sub_code = sub_row * 8 + sub_g
    for xs in range(4):
        held = jnp.zeros((1, 128), jnp.int32)
        for r in range(16):
            held = jnp.where(lane_row == r, asg_ref[xs * 16 + r], held)
        code = held * 8 + lane_g
        perm[:, xs * 128 : (xs + 1) * 128] = jnp.where(sub_code == code, 1.0, 0.0).astype(BF)

    @pl.when(c == 1)
    def _():
        exchanges[0].wait_recv()

    me_rows = pl.ds(pl.multiple_of((x * 4 + y) * 32, 32), 32)
    for k in range(4):
        pltpu.make_async_copy(q1.at[k], q1.at[k], zrecv.at[k]).wait()
    for i in range(4):
        k = head_at(y, i)
        pltpu.make_async_copy(q1.at[k], q2.at[k, me_rows], grecv.at[k]).start()
        for dx, dy in AROUND:
            y_ = (y + dy) % 4
            k = head_at(y_, i)
            pltpu.make_async_remote_copy(
                src_ref=q1.at[k], dst_ref=q2.at[k, me_rows], send_sem=gsend, recv_sem=grecv.at[k],
                device_id=dev((x + dx) % 4, y_, z, c), device_id_type=MESH,
            ).start()
        if i < 3:
            exchanges[(2, 1, 3)[i]].start()

    exchanges[4].wait_recv()
    rows = lax.broadcasted_iota(jnp.int32, (64, 128), 0)
    lanes = lax.broadcasted_iota(jnp.int32, (64, 128), 1)
    lens_own = jnp.concatenate([lens[...]] * 8, axis=0)
    lens_other = jnp.concatenate([lensall[...]] * 8, axis=0)
    row_c = (rows >> 4) & 1
    live = jnp.where(row_c == c, lens_own, lens_other) - tp * 128
    row_slot = row_c * 4 + (rows & 3)
    for s in range(8):
        limit = jnp.where(row_slot == s, live, 0)
        bias[:, s * 128 : s * 128 + 128] = jnp.where(lanes < limit, 0.0, NEG)

    @pl.when(c == 0)
    def _():
        exchanges[0].wait_recv()

    for i in range(4):
        loads[i].wait()
        if i > 0:
            exchanges[i].wait_recv()

    square = (128, 128)
    eye = lax.broadcasted_iota(jnp.int32, square, 0) == lax.broadcasted_iota(jnp.int32, square, 1)
    ones = jnp.ones((1024, 128), BF)
    stat_row = lax.broadcasted_iota(jnp.int32, (16, 128), 0)

    def as_row(column):
        return jnp.sum(jnp.where(eye, column, 0.0), axis=0, keepdims=True)

    def stat_tile(top, total):
        hi = total.astype(BF).astype(F32)
        return jnp.where(stat_row == 0, top, jnp.where(stat_row == 1, hi, total - hi)).astype(BF)

    def weights(scores, top):
        return jnp.exp(scores - top).astype(BF)

    def largest(scores):
        return jnp.max(scores, axis=1, keepdims=True)

    def head(i, _):
        k = head_at(y, i)
        cols = pl.ds(pl.multiple_of(k * 128, 128), 128)
        pltpu.make_async_copy(q2.at[k], q2.at[k], grecv.at[k]).wait()
        qs[...] = dot(perm[...], q2[k], NN).astype(BF)
        chunks = [(x + a) % 4 for a in (1, 3, 2, 0)]
        parts = [qs[pl.ds(pl.multiple_of(j * 128, 128), 128), :] for j in chunks]
        keys = kbuf[:, cols]
        values = jnp.concatenate([vbuf[:, cols], ones], axis=1)
        suffix_keys = skbuf[:, :, cols].reshape(1024, 128)
        suffix_values = jnp.concatenate([svbuf[:, :, cols].reshape(1024, 128), ones], axis=1)

        s0 = dot(jnp.concatenate(parts[:2], axis=0), keys, NT) * SCALE
        s1 = dot(jnp.concatenate(parts[2:], axis=0), keys, NT) * SCALE
        own = pl.ds(pl.multiple_of(x * 128 + yh * 64, 64), 64)
        ss = dot(qs[own, :], suffix_keys, NT) * SCALE + bias[...]

        def send(a):
            pltpu.make_async_remote_copy(
                src_ref=sbuf.at[i * 4 + a], dst_ref=r1.at[x * 4 + y], send_sem=rsend, recv_sem=rrecv,
                device_id=dev(chunks[a], k, z, c), device_id_type=MESH,
            ).start()

        def put(a, m, n):
            sbuf[i * 4 + a, :128, :] = n[:, :128].astype(BF)
            sbuf[i * 4 + a, 128:, :] = stat_tile(as_row(m), as_row(n[:, 128:]))

        m0 = largest(s0).astype(BF).astype(F32)
        n0 = dot(weights(s0, m0), values, NN)
        put(0, m0[:128], n0[:128])
        send(0)
        put(1, m0[128:], n0[128:])
        send(1)

        m1, ms = largest(s1), largest(ss)
        low = jnp.full((64, 1), NEG, F32)
        ms = jnp.concatenate([jnp.where(yh == 0, ms, low), jnp.where(yh == 0, low, ms)], axis=0)
        m1 = jnp.concatenate([m1[:128], jnp.maximum(m1[128:], ms)], axis=0).astype(BF).astype(F32)
        n1 = dot(weights(s1, m1), values, NN)
        ns = dot(weights(ss, jnp.where(yh == 0, m1[128:192], m1[192:])), suffix_values, NN)
        ns = jnp.concatenate([jnp.where(yh == 0, ns, 0.0), jnp.where(yh == 0, 0.0, ns)], axis=0)
        put(2, m1[:128], n1[:128])
        send(2)
        put(3, m1[128:], n1[128:] + ns)
        pl.when(i < 3)(lambda: send(3))
        return 0

    lax.fori_loop(0, 4, head, 0)
    pltpu.make_async_copy(sbuf.at[15], r1.at[x * 4 + y], rrecv).start()

    pltpu.make_async_copy(r1, r1, rrecv).wait()
    stats = [r1[i, 128:, :].astype(F32) for i in range(16)]
    top = functools.reduce(jnp.maximum, [s[0:1] for s in stats])
    ws = [jnp.exp(s[0:1] - top) for s in stats]
    total = functools.reduce(jnp.add, [w * (s[1:2] + s[2:3]) for w, s in zip(ws, stats)])
    his = [w.astype(BF).astype(F32) for w in ws]
    spread = [
        jnp.concatenate([jnp.where(eye, w, 0.0).astype(BF) for w in part], axis=1)
        for part in (his, [w - h for w, h in zip(ws, his)])
    ]
    both = dot(jnp.concatenate(spread, axis=0), jnp.concatenate([r1[i, :128, :] for i in range(16)], axis=0), NN)
    flat = (both[:128] + both[128:]).astype(BF)
    stat = stat_tile(top, total)
    for d in range(8):
        s2[d, :16, :] = flat[d * 16 : d * 16 + 16, :]
        s2[d, 16:, :] = stat

    zt = 4 * c + y
    for o in range(1, 8):
        y_, c_ = (y + o // 2) % 4, (c + o % 2) % 2
        pltpu.make_async_remote_copy(
            src_ref=s2.at[y_ * 2 + c_], dst_ref=r2.at[z], send_sem=tsend.at[0], recv_sem=trecv,
            device_id=dev(x, y_, zt, c_), device_id_type=MESH,
        ).start()

    @pl.when(zt == z)
    def _():
        pltpu.make_async_copy(s2.at[y * 2 + c], r2.at[z], trecv).start()

    @pl.when(zt != z)
    def _():
        pltpu.make_async_remote_copy(
            src_ref=s2.at[y * 2 + c], dst_ref=r2.at[z], send_sem=tsend.at[1], recv_sem=trecv,
            device_id=dev(x, y, zt, c), device_id_type=MESH,
        ).start()

    pltpu.make_async_copy(r2, r2, trecv).wait()

    offset = y * 32 + c * 16
    pick = lax.broadcasted_iota(jnp.int32, (16, 128), 1) == lax.broadcasted_iota(jnp.int32, (16, 128), 0) + offset
    stats = [r2[i, 16:, :].astype(F32) for i in range(8)]
    m2 = functools.reduce(jnp.maximum, [s[0:1] for s in stats])
    ws = [jnp.exp(s[0:1] - m2) for s in stats]
    total = functools.reduce(jnp.add, [w * (s[1:2] + s[2:3]) for w, s in zip(ws, stats)])
    acc = jnp.zeros((16, 128), F32)
    for i in range(8):
        column = jnp.sum(jnp.where(pick, ws[i], 0.0), axis=1, keepdims=True)
        acc = acc + column * r2[i, :16, :].astype(F32)
    column = jnp.sum(jnp.where(pick, total, 0.0), axis=1, keepdims=True)
    acc = acc / column
    for g in range(4):
        out_ref[:, g * 128 : (g + 1) * 128] = acc[g * 4 : g * 4 + 4, :].astype(BF)

    for i in range(5):
        exchanges[i].wait_send()
    pltpu.make_async_copy(s2.at[pl.ds(0, 7), pl.ds(0, 16)], s2.at[pl.ds(0, 7), pl.ds(0, 16)], zsend.at[0]).wait()

    @pl.when(hz != c)
    def _():
        pltpu.make_async_copy(q0, q0, zsend.at[1]).wait()

    most = q2.at[:, pl.ds(0, 480)]
    pltpu.make_async_copy(most, most, gsend).wait()
    most = sbuf.at[pl.ds(0, 15)]
    pltpu.make_async_copy(most, most, rsend).wait()
    most = s2.at[pl.ds(0, 7)]
    pltpu.make_async_copy(most, most, tsend.at[0]).wait()

    @pl.when(zt != z)
    def _():
        pltpu.make_async_copy(s2.at[0], s2.at[0], tsend.at[1]).wait()


def shards(queries, assignment, prefix_keys, prefix_values, suffix_keys, suffix_values, lengths):
    vmem, far = pl.BlockSpec(memory_space=pltpu.VMEM), pl.BlockSpec(memory_space=pl.ANY)
    dma = pltpu.SemaphoreType.DMA
    return pl.pallas_call(
        kernel,
        out_shape=jax.ShapeDtypeStruct(queries.shape, BF),
        in_specs=[far, far, far, far, far, far, far],
        out_specs=vmem,
        scratch_shapes=[
            pltpu.VMEM((1024, 512), BF),
            pltpu.VMEM((1024, 512), BF),
            pltpu.VMEM((8, 128, 512), BF),
            pltpu.VMEM((8, 128, 512), BF),
            pltpu.VMEM((16, 128), F32),
            pltpu.VMEM((16, 128), BF),
            pltpu.VMEM((4, 32, 128), BF),
            pltpu.VMEM((4, 512, 128), BF),
            pltpu.VMEM((512, 128), BF),
            pltpu.VMEM((512, 512), BF),
            pltpu.VMEM((8, 128), jnp.int32),
            pltpu.VMEM((8, 128), jnp.int32),
            pltpu.VMEM((64, 1024), F32),
            pltpu.VMEM((16, 144, 128), BF),
            pltpu.VMEM((16, 144, 128), BF),
            pltpu.VMEM((8, 32, 128), BF),
            pltpu.VMEM((8, 32, 128), BF),
            pltpu.VMEM((4, 512), BF),
            pltpu.SMEM((64,), jnp.int32),
            pltpu.SMEM((4,), jnp.int32),
            dma((3,)),
            dma((4,)),
            dma((5,)),
            dma((5,)),
            dma((2,)),
            dma((4,)),
            dma(()),
            dma((4,)),
            dma(()),
            dma(()),
            dma((2,)),
            dma(()),
        ],
        compiler_params=pltpu.CompilerParams(
            collective_id=0, has_side_effects=True, vmem_limit_bytes=48 * 1024 * 1024
        ),
        cost_estimate=pl.CostEstimate(flops=1_300_000_000, bytes_accessed=4_300_000, transcendentals=2_600_000),
    )(
        *(
            pltpu.with_memory_space_constraint(operand, pltpu.HBM)
            for operand in (
                queries, assignment, lengths, prefix_keys, prefix_values, suffix_keys, suffix_values
            )
        )
    )


def solution(mesh):
    in_specs = (
        P("rep", "tp"),
        P(),
        P(("rep", "tp"), None),
        P(("rep", "tp"), None),
        P("rep", "tp", None),
        P("rep", "tp", None),
        P("rep"),
    )
    out_specs = P("rep", "tp")
    return jax.shard_map(shards, mesh=mesh, in_specs=in_specs, out_specs=out_specs, check_vma=False)
```

```python
import functools

import jax
import jax.numpy as jnp
from jax import lax
from jax.experimental import pallas as pl
from jax.experimental.pallas import tpu as pltpu
from jax.sharding import PartitionSpec as P

MESH = pl.DeviceIdType.MESH
HD = 128
HEADS_CORE = 4
SCALE = HD ** (-0.5)
NEG = -(2.0**100)
BF = jnp.bfloat16
F32 = jnp.float32
NT = (((1,), (1,)), ((), ()))
NN = (((1,), (0,)), ((), ()))
AROUND = (
    (1, 0), (3, 0), (0, 1), (0, 3), (2, 0), (1, 1), (3, 1), (2, 1), (0, 2), (1, 2), (3, 2), (2, 2), (1, 3), (3, 3), (2, 3),
)


def dot(a, b, dims):
    return lax.dot_general(a, b, dims, preferred_element_type=F32)


def kernel(
    q_hbm, asg_hbm, len_hbm, pk, pv, sk, sv, out_ref,
    kbuf, vbuf, skbuf, svbuf, qf, q0, q1, q2, qs, perm, lens, lensall, bias, sbuf, r1, s2, r2,
    q_ref, asg_ref, len_ref, smallsem, ldsem, xsend, xrecv, zsend, zrecv, gsend, grecv, rsend, rrecv, tsend, trecv,
):
    rep, tp = lax.axis_index("rep"), lax.axis_index("tp")
    x, yh, c = rep // 4, (rep // 2) % 2, rep % 2
    z, yl = tp // 2, tp % 2
    y = yh * 2 + yl
    hz = z // 4

    def head_at(y_, i):
        return (c * (y_ + 3 - i) + (1 - c) * i) % 4

    def dev(x_, y_, z_, c_):
        return (x_ * 4 + (y_ // 2) * 2 + c_, z_ * 2 + y_ % 2)

    small = [
        pltpu.make_async_copy(src, dst, smallsem.at[i])
        for i, (src, dst) in enumerate(((q_hbm, q_ref), (asg_hbm, asg_ref), (len_hbm, len_ref)))
    ]
    for copy in small:
        copy.start()

    mine = pl.multiple_of(c * 512, 512)
    theirs = pl.multiple_of((1 - c) * 512, 512)
    rows2 = pl.multiple_of(c * 512, 512)
    pairs = ((pk, kbuf), (sk, skbuf), (pv, vbuf), (sv, svbuf))

    def local_dst(i):
        buf = pairs[i][1]
        return buf.at[pl.ds(rows2, 512)] if i % 2 == 0 else buf.at[pl.ds(c * 4, 4)]

    def src_of(i, cols):
        ref = pairs[i][0]
        return ref.at[:, pl.ds(cols, 512)] if i % 2 == 0 else ref.at[:, :, pl.ds(cols, 512)]

    loads = [pltpu.make_async_copy(src_of(i, mine), local_dst(i), ldsem.at[i]) for i in range(4)]
    barrier = pltpu.get_barrier_semaphore()

    def greet(x_, y_, z_, c_):
        pl.semaphore_signal(barrier, inc=1, device_id=dev(x_, y_, z_, c_), device_id_type=MESH)

    partner = dev(x, y, z, 1 - c)
    for k in range(4):
        for cs in range(2):
            zs = 4 * c + k

            @pl.when(jnp.logical_or(zs != z, cs != c))
            def _(zs=zs, cs=cs):
                greet(x, y, zs, cs)

    greet(x, y, z, 1 - c)
    for o in range(1, 16):
        greet((x + o // 4) % 4, (y + o % 4) % 4, z, c)
    for zs in range(8):

        @pl.when(jnp.logical_or(jnp.logical_or(zs != z, z % 4 != y), hz != c))
        def _(zs=zs):
            greet(x, z % 4, zs, hz)

    for copy in loads:
        copy.start()

    small[0].wait()
    q = q_ref[...].astype(F32)
    for g in range(4):
        qf[g * 4 : g * 4 + 4, :] = q[:, g * 128 : (g + 1) * 128]
    q0[...] = qf[...].astype(BF)

    n_z = jnp.where(hz == c, 7, 8)
    n_t = jnp.where(4 * c + y == z, 7, 8)
    pl.semaphore_wait(barrier, 16 + n_z + n_t)

    def ztile(ref_z):
        return q1.at[ref_z % 4, pl.ds(pl.multiple_of(c * 16, 16), 16)]

    for o in (4, 3, 5, 2, 6, 1, 7):
        z_ = (z + o) % 8
        pltpu.make_async_remote_copy(
            src_ref=q0, dst_ref=ztile(z), send_sem=zsend.at[0], recv_sem=zrecv.at[z % 4],
            device_id=dev(x, y, z_, hz), device_id_type=MESH,
        ).start()

    @pl.when(hz == c)
    def _():
        pltpu.make_async_copy(q0, ztile(z), zrecv.at[z % 4]).start()

    @pl.when(hz != c)
    def _():
        pltpu.make_async_remote_copy(
            src_ref=q0, dst_ref=ztile(z), send_sem=zsend.at[1], recv_sem=zrecv.at[z % 4],
            device_id=partner, device_id_type=MESH,
        ).start()

    exchanges = [
        pltpu.make_async_remote_copy(
            src_ref=src_of(i, theirs), dst_ref=local_dst(i), send_sem=xsend.at[i], recv_sem=xrecv.at[i],
            device_id=partner, device_id_type=MESH,
        )
        for i in range(4)
    ]
    exchanges.append(
        pltpu.make_async_remote_copy(
            src_ref=lens, dst_ref=lensall, send_sem=xsend.at[4], recv_sem=xrecv.at[4],
            device_id=partner, device_id_type=MESH,
        )
    )
    exchanges[0].start()

    small[1].wait()
    small[2].wait()
    own_len = jnp.zeros((8, 128), jnp.int32)
    sub8 = lax.broadcasted_iota(jnp.int32, (8, 128), 0)
    for s in range(4):
        own_len = jnp.where((sub8 & 3) == s, len_ref[s], own_len)
    lens[...] = own_len

    exchanges[4].start()

    lane = lax.broadcasted_iota(jnp.int32, (1, 128), 1)
    lane_row = ((lane >> 6) * 2 + ((lane >> 4) & 1)) * 4 + (lane & 3)
    lane_g = ((lane >> 5) & 1) * 4 + ((lane >> 2) & 3)
    sub = lax.broadcasted_iota(jnp.int32, (512, 128), 0)
    sub_row = (sub >> 6) * 8 + ((sub >> 4) & 1) * 4 + (sub & 3)
    sub_g = ((sub >> 5) & 1) * 4 + ((sub >> 2) & 3)
    sub_code = sub_row * 8 + sub_g
    for xs in range(4):
        held = jnp.zeros((1, 128), jnp.int32)
        for r in range(16):
            held = jnp.where(lane_row == r, asg_ref[xs * 16 + r], held)
        code = held * 8 + lane_g
        perm[:, xs * 128 : (xs + 1) * 128] = jnp.where(sub_code == code, 1.0, 0.0).astype(BF)

    @pl.when(c == 1)
    def _():
        exchanges[0].wait_recv()

    me_rows = pl.ds(pl.multiple_of((x * 4 + y) * 32, 32), 32)
    for k in range(4):
        pltpu.make_async_copy(q1.at[k], q1.at[k], zrecv.at[k]).wait()
    for i in range(4):
        k = head_at(y, i)
        pltpu.make_async_copy(q1.at[k], q2.at[k, me_rows], grecv.at[k]).start()
        for dx, dy in AROUND:
            y_ = (y + dy) % 4
            k = head_at(y_, i)
            pltpu.make_async_remote_copy(
                src_ref=q1.at[k], dst_ref=q2.at[k, me_rows], send_sem=gsend, recv_sem=grecv.at[k],
                device_id=dev((x + dx) % 4, y_, z, c), device_id_type=MESH,
            ).start()
        if i < 3:
            exchanges[(2, 1, 3)[i]].start()

    exchanges[4].wait_recv()
    rows = lax.broadcasted_iota(jnp.int32, (64, 128), 0)
    lanes = lax.broadcasted_iota(jnp.int32, (64, 128), 1)
    lens_own = jnp.concatenate([lens[...]] * 8, axis=0)
    lens_other = jnp.concatenate([lensall[...]] * 8, axis=0)
    row_c = (rows >> 4) & 1
    live = jnp.where(row_c == c, lens_own, lens_other) - tp * 128
    row_slot = row_c * 4 + (rows & 3)
    for s in range(8):
        limit = jnp.where(row_slot == s, live, 0)
        bias[:, s * 128 : s * 128 + 128] = jnp.where(lanes < limit, 0.0, NEG)

    @pl.when(c == 0)
    def _():
        exchanges[0].wait_recv()

    for i in range(4):
        loads[i].wait()
        if i > 0:
            exchanges[i].wait_recv()

    square = (128, 128)
    eye = lax.broadcasted_iota(jnp.int32, square, 0) == lax.broadcasted_iota(jnp.int32, square, 1)
    ones = jnp.ones((1024, 128), BF)
    stat_row = lax.broadcasted_iota(jnp.int32, (16, 128), 0)

    def as_row(column):
        return jnp.sum(jnp.where(eye, column, 0.0), axis=0, keepdims=True)

    def stat_tile(top, total):
        hi = total.astype(BF).astype(F32)
        return jnp.where(stat_row == 0, top, jnp.where(stat_row == 1, hi, total - hi)).astype(BF)

    def weights(scores, top):
        return jnp.exp(scores - top).astype(BF)

    def largest(scores):
        return jnp.max(scores, axis=1, keepdims=True)

    def head(i, _):
        k = head_at(y, i)
        cols = pl.ds(pl.multiple_of(k * 128, 128), 128)
        pltpu.make_async_copy(q2.at[k], q2.at[k], grecv.at[k]).wait()
        qs[...] = dot(perm[...], q2[k], NN).astype(BF)
        chunks = [(x + a) % 4 for a in (1, 3, 2, 0)]
        parts = [qs[pl.ds(pl.multiple_of(j * 128, 128), 128), :] for j in chunks]
        keys = kbuf[:, cols]
        values = jnp.concatenate([vbuf[:, cols], ones], axis=1)
        suffix_keys = skbuf[:, :, cols].reshape(1024, 128)
        suffix_values = jnp.concatenate([svbuf[:, :, cols].reshape(1024, 128), ones], axis=1)

        s0 = dot(jnp.concatenate(parts[:2], axis=0), keys, NT) * SCALE
        s1 = dot(jnp.concatenate(parts[2:], axis=0), keys, NT) * SCALE
        own = pl.ds(pl.multiple_of(x * 128 + yh * 64, 64), 64)
        ss = dot(qs[own, :], suffix_keys, NT) * SCALE + bias[...]

        def send(a):
            pltpu.make_async_remote_copy(
                src_ref=sbuf.at[i * 4 + a], dst_ref=r1.at[x * 4 + y], send_sem=rsend, recv_sem=rrecv,
                device_id=dev(chunks[a], k, z, c), device_id_type=MESH,
            ).start()

        def put(a, m, n):
            sbuf[i * 4 + a, :128, :] = n[:, :128].astype(BF)
            sbuf[i * 4 + a, 128:, :] = stat_tile(as_row(m), as_row(n[:, 128:]))

        m0 = largest(s0).astype(BF).astype(F32)
        n0 = dot(weights(s0, m0), values, NN)
        put(0, m0[:128], n0[:128])
        send(0)
        put(1, m0[128:], n0[128:])
        send(1)

        m1, ms = largest(s1), largest(ss)
        low = jnp.full((64, 1), NEG, F32)
        ms = jnp.concatenate([jnp.where(yh == 0, ms, low), jnp.where(yh == 0, low, ms)], axis=0)
        m1 = jnp.concatenate([m1[:128], jnp.maximum(m1[128:], ms)], axis=0).astype(BF).astype(F32)
        n1 = dot(weights(s1, m1), values, NN)
        ns = dot(weights(ss, jnp.where(yh == 0, m1[128:192], m1[192:])), suffix_values, NN)
        ns = jnp.concatenate([jnp.where(yh == 0, ns, 0.0), jnp.where(yh == 0, 0.0, ns)], axis=0)
        put(2, m1[:128], n1[:128])
        send(2)
        put(3, m1[128:], n1[128:] + ns)
        pl.when(k != y)(lambda: send(3))

        @pl.when(k == y)
        def _():
            pltpu.make_async_copy(sbuf.at[i * 4 + 3], r1.at[x * 4 + y], rrecv).start()

        return 0

    lax.fori_loop(0, 4, head, 0)

    pltpu.make_async_copy(r1, r1, rrecv).wait()
    stats = [r1[i, 128:, :].astype(F32) for i in range(16)]
    top = functools.reduce(jnp.maximum, [s[0:1] for s in stats])
    ws = [jnp.exp(s[0:1] - top) for s in stats]
    total = functools.reduce(jnp.add, [w * (s[1:2] + s[2:3]) for w, s in zip(ws, stats)])
    his = [w.astype(BF).astype(F32) for w in ws]
    spread = [
        jnp.concatenate([jnp.where(eye, w, 0.0).astype(BF) for w in part], axis=1)
        for part in (his, [w - h for w, h in zip(ws, his)])
    ]
    both = dot(jnp.concatenate(spread, axis=0), jnp.concatenate([r1[i, :128, :] for i in range(16)], axis=0), NN)
    flat = (both[:128] + both[128:]).astype(BF)
    stat = stat_tile(top, total)
    for d in range(8):
        s2[d, :16, :] = flat[d * 16 : d * 16 + 16, :]
        s2[d, 16:, :] = stat

    zt = 4 * c + y
    for o in range(1, 8):
        y_, c_ = (y + o // 2) % 4, (c + o % 2) % 2
        pltpu.make_async_remote_copy(
            src_ref=s2.at[y_ * 2 + c_], dst_ref=r2.at[z], send_sem=tsend.at[0], recv_sem=trecv,
            device_id=dev(x, y_, zt, c_), device_id_type=MESH,
        ).start()

    @pl.when(zt == z)
    def _():
        pltpu.make_async_copy(s2.at[y * 2 + c], r2.at[z], trecv).start()

    @pl.when(zt != z)
    def _():
        pltpu.make_async_remote_copy(
            src_ref=s2.at[y * 2 + c], dst_ref=r2.at[z], send_sem=tsend.at[1], recv_sem=trecv,
            device_id=dev(x, y, zt, c), device_id_type=MESH,
        ).start()

    pltpu.make_async_copy(r2, r2, trecv).wait()

    offset = y * 32 + c * 16
    pick = lax.broadcasted_iota(jnp.int32, (16, 128), 1) == lax.broadcasted_iota(jnp.int32, (16, 128), 0) + offset
    stats = [r2[i, 16:, :].astype(F32) for i in range(8)]
    m2 = functools.reduce(jnp.maximum, [s[0:1] for s in stats])
    ws = [jnp.exp(s[0:1] - m2) for s in stats]
    total = functools.reduce(jnp.add, [w * (s[1:2] + s[2:3]) for w, s in zip(ws, stats)])
    acc = jnp.zeros((16, 128), F32)
    for i in range(8):
        column = jnp.sum(jnp.where(pick, ws[i], 0.0), axis=1, keepdims=True)
        acc = acc + column * r2[i, :16, :].astype(F32)
    column = jnp.sum(jnp.where(pick, total, 0.0), axis=1, keepdims=True)
    acc = acc / column
    for g in range(4):
        out_ref[:, g * 128 : (g + 1) * 128] = acc[g * 4 : g * 4 + 4, :].astype(BF)

    for i in range(5):
        exchanges[i].wait_send()
    pltpu.make_async_copy(s2.at[pl.ds(0, 7), pl.ds(0, 16)], s2.at[pl.ds(0, 7), pl.ds(0, 16)], zsend.at[0]).wait()

    @pl.when(hz != c)
    def _():
        pltpu.make_async_copy(q0, q0, zsend.at[1]).wait()

    most = q2.at[:, pl.ds(0, 480)]
    pltpu.make_async_copy(most, most, gsend).wait()
    most = sbuf.at[pl.ds(0, 15)]
    pltpu.make_async_copy(most, most, rsend).wait()
    most = s2.at[pl.ds(0, 7)]
    pltpu.make_async_copy(most, most, tsend.at[0]).wait()

    @pl.when(zt != z)
    def _():
        pltpu.make_async_copy(s2.at[0], s2.at[0], tsend.at[1]).wait()


def shards(queries, assignment, prefix_keys, prefix_values, suffix_keys, suffix_values, lengths):
    vmem, far = pl.BlockSpec(memory_space=pltpu.VMEM), pl.BlockSpec(memory_space=pl.ANY)
    dma = pltpu.SemaphoreType.DMA
    return pl.pallas_call(
        kernel,
        out_shape=jax.ShapeDtypeStruct(queries.shape, BF),
        in_specs=[far, far, far, far, far, far, far],
        out_specs=vmem,
        scratch_shapes=[
            pltpu.VMEM((1024, 512), BF),
            pltpu.VMEM((1024, 512), BF),
            pltpu.VMEM((8, 128, 512), BF),
            pltpu.VMEM((8, 128, 512), BF),
            pltpu.VMEM((16, 128), F32),
            pltpu.VMEM((16, 128), BF),
            pltpu.VMEM((4, 32, 128), BF),
            pltpu.VMEM((4, 512, 128), BF),
            pltpu.VMEM((512, 128), BF),
            pltpu.VMEM((512, 512), BF),
            pltpu.VMEM((8, 128), jnp.int32),
            pltpu.VMEM((8, 128), jnp.int32),
            pltpu.VMEM((64, 1024), F32),
            pltpu.VMEM((16, 144, 128), BF),
            pltpu.VMEM((16, 144, 128), BF),
            pltpu.VMEM((8, 32, 128), BF),
            pltpu.VMEM((8, 32, 128), BF),
            pltpu.VMEM((4, 512), BF),
            pltpu.SMEM((64,), jnp.int32),
            pltpu.SMEM((4,), jnp.int32),
            dma((3,)),
            dma((4,)),
            dma((5,)),
            dma((5,)),
            dma((2,)),
            dma((4,)),
            dma(()),
            dma((4,)),
            dma(()),
            dma(()),
            dma((2,)),
            dma(()),
        ],
        compiler_params=pltpu.CompilerParams(
            collective_id=0, has_side_effects=True, vmem_limit_bytes=48 * 1024 * 1024
        ),
        cost_estimate=pl.CostEstimate(flops=1_300_000_000, bytes_accessed=4_300_000, transcendentals=2_600_000),
    )(
        *(
            pltpu.with_memory_space_constraint(operand, pltpu.HBM)
            for operand in (
                queries, assignment, lengths, prefix_keys, prefix_values, suffix_keys, suffix_values
            )
        )
    )


def solution(mesh):
    in_specs = (
        P("rep", "tp"),
        P(),
        P(("rep", "tp"), None),
        P(("rep", "tp"), None),
        P("rep", "tp", None),
        P("rep", "tp", None),
        P("rep"),
    )
    out_specs = P("rep", "tp")
    return jax.shard_map(shards, mesh=mesh, in_specs=in_specs, out_specs=out_specs, check_vma=False)
```

```python
import functools

import jax
import jax.numpy as jnp
from jax import lax
from jax.experimental import pallas as pl
from jax.experimental.pallas import tpu as pltpu
from jax.sharding import PartitionSpec as P

MESH = pl.DeviceIdType.MESH
HD = 128
HEADS_CORE = 4
SCALE = HD ** (-0.5)
NEG = -(2.0**100)
BF = jnp.bfloat16
F32 = jnp.float32
NT = (((1,), (1,)), ((), ()))
NN = (((1,), (0,)), ((), ()))
AROUND = (
    (1, 0), (3, 0), (0, 1), (0, 3), (2, 0), (1, 1), (3, 1), (2, 1), (0, 2), (1, 2), (3, 2), (2, 2), (1, 3), (3, 3), (2, 3),
)


def dot(a, b, dims):
    return lax.dot_general(a, b, dims, preferred_element_type=F32)


def kernel(
    q_hbm, asg_hbm, len_hbm, pk, pv, sk, sv, out_ref,
    kbuf, vbuf, skbuf, svbuf, qf, q0, q1, q2, qs, perm, lens, lensall, bias, sbuf, r1, s2, r2,
    q_ref, asg_ref, len_ref, smallsem, ldsem, xsend, xrecv, zsend, zrecv, gsend, grecv, rsend, rrecv, tsend, trecv,
):
    rep, tp = lax.axis_index("rep"), lax.axis_index("tp")
    x, yh, c = rep // 4, (rep // 2) % 2, rep % 2
    z, yl = tp // 2, tp % 2
    y = yh * 2 + yl
    hz = z // 4

    def head_at(y_, i):
        return (y_ + 1 + i + c * (2 - 2 * i)) % 4

    def dev(x_, y_, z_, c_):
        return (x_ * 4 + (y_ // 2) * 2 + c_, z_ * 2 + y_ % 2)

    small = [
        pltpu.make_async_copy(src, dst, smallsem.at[i])
        for i, (src, dst) in enumerate(((q_hbm, q_ref), (asg_hbm, asg_ref), (len_hbm, len_ref)))
    ]
    for copy in small:
        copy.start()

    mine = pl.multiple_of(c * 512, 512)
    theirs = pl.multiple_of((1 - c) * 512, 512)
    rows2 = pl.multiple_of(c * 512, 512)
    pairs = ((pk, kbuf), (sk, skbuf), (pv, vbuf), (sv, svbuf))

    def local_dst(i):
        buf = pairs[i][1]
        return buf.at[pl.ds(rows2, 512)] if i % 2 == 0 else buf.at[pl.ds(c * 4, 4)]

    def src_of(i, cols):
        ref = pairs[i][0]
        return ref.at[:, pl.ds(cols, 512)] if i % 2 == 0 else ref.at[:, :, pl.ds(cols, 512)]

    loads = [pltpu.make_async_copy(src_of(i, mine), local_dst(i), ldsem.at[i]) for i in range(4)]
    barrier = pltpu.get_barrier_semaphore()

    def greet(x_, y_, z_, c_):
        pl.semaphore_signal(barrier, inc=1, device_id=dev(x_, y_, z_, c_), device_id_type=MESH)

    partner = dev(x, y, z, 1 - c)
    for k in range(4):
        for cs in range(2):
            zs = 4 * c + k

            @pl.when(jnp.logical_or(zs != z, cs != c))
            def _(zs=zs, cs=cs):
                greet(x, y, zs, cs)

    greet(x, y, z, 1 - c)
    for o in range(1, 16):
        greet((x + o // 4) % 4, (y + o % 4) % 4, z, c)
    for zs in range(8):

        @pl.when(jnp.logical_or(jnp.logical_or(zs != z, z % 4 != y), hz != c))
        def _(zs=zs):
            greet(x, z % 4, zs, hz)

    small[0].wait()
    q = q_ref[...].astype(F32)
    for g in range(4):
        qf[g * 4 : g * 4 + 4, :] = q[:, g * 128 : (g + 1) * 128]
    q0[...] = qf[...].astype(BF)

    n_z = jnp.where(hz == c, 7, 8)
    n_t = jnp.where(4 * c + y == z, 7, 8)
    pl.semaphore_wait(barrier, 16 + n_z + n_t)

    def ztile(ref_z):
        return q1.at[ref_z % 4, pl.ds(pl.multiple_of(c * 16, 16), 16)]

    for o in (4, 3, 5, 2, 6, 1, 7):
        z_ = (z + o) % 8
        pltpu.make_async_remote_copy(
            src_ref=q0, dst_ref=ztile(z), send_sem=zsend.at[0], recv_sem=zrecv.at[z % 4],
            device_id=dev(x, y, z_, hz), device_id_type=MESH,
        ).start()

    @pl.when(hz == c)
    def _():
        pltpu.make_async_copy(q0, ztile(z), zrecv.at[z % 4]).start()

    @pl.when(hz != c)
    def _():
        pltpu.make_async_remote_copy(
            src_ref=q0, dst_ref=ztile(z), send_sem=zsend.at[1], recv_sem=zrecv.at[z % 4],
            device_id=partner, device_id_type=MESH,
        ).start()

    exchanges = [
        pltpu.make_async_remote_copy(
            src_ref=src_of(i, theirs), dst_ref=local_dst(i), send_sem=xsend.at[i], recv_sem=xrecv.at[i],
            device_id=partner, device_id_type=MESH,
        )
        for i in range(4)
    ]
    exchanges.append(
        pltpu.make_async_remote_copy(
            src_ref=lens, dst_ref=lensall, send_sem=xsend.at[4], recv_sem=xrecv.at[4],
            device_id=partner, device_id_type=MESH,
        )
    )
    exchanges[0].start()
    for copy in loads:
        copy.start()

    small[1].wait()
    small[2].wait()
    own_len = jnp.zeros((8, 128), jnp.int32)
    sub8 = lax.broadcasted_iota(jnp.int32, (8, 128), 0)
    for s in range(4):
        own_len = jnp.where((sub8 & 3) == s, len_ref[s], own_len)
    lens[...] = own_len

    exchanges[4].start()

    lane = lax.broadcasted_iota(jnp.int32, (1, 128), 1)
    lane_row = ((lane >> 6) * 2 + ((lane >> 4) & 1)) * 4 + (lane & 3)
    lane_g = ((lane >> 5) & 1) * 4 + ((lane >> 2) & 3)
    sub = lax.broadcasted_iota(jnp.int32, (512, 128), 0)
    sub_row = (sub >> 6) * 8 + ((sub >> 4) & 1) * 4 + (sub & 3)
    sub_g = ((sub >> 5) & 1) * 4 + ((sub >> 2) & 3)
    sub_code = sub_row * 8 + sub_g
    for xs in range(4):
        held = jnp.zeros((1, 128), jnp.int32)
        for r in range(16):
            held = jnp.where(lane_row == r, asg_ref[xs * 16 + r], held)
        code = held * 8 + lane_g
        perm[:, xs * 128 : (xs + 1) * 128] = jnp.where(sub_code == code, 1.0, 0.0).astype(BF)

    me_rows = pl.ds(pl.multiple_of((x * 4 + y) * 32, 32), 32)
    for k in range(4):
        pltpu.make_async_copy(q1.at[k], q1.at[k], zrecv.at[k]).wait()
    for i in range(4):
        k = head_at(y, i)
        pltpu.make_async_copy(q1.at[k], q2.at[k, me_rows], grecv.at[k]).start()
        for dx, dy in AROUND:
            y_ = (y + dy) % 4
            k = head_at(y_, i)
            pltpu.make_async_remote_copy(
                src_ref=q1.at[k], dst_ref=q2.at[k, me_rows], send_sem=gsend, recv_sem=grecv.at[k],
                device_id=dev((x + dx) % 4, y_, z, c), device_id_type=MESH,
            ).start()
        if i < 3:
            exchanges[(2, 1, 3)[i]].start()

    exchanges[4].wait_recv()
    rows = lax.broadcasted_iota(jnp.int32, (64, 128), 0)
    lanes = lax.broadcasted_iota(jnp.int32, (64, 128), 1)
    lens_own = jnp.concatenate([lens[...]] * 8, axis=0)
    lens_other = jnp.concatenate([lensall[...]] * 8, axis=0)
    row_c = (rows >> 4) & 1
    live = jnp.where(row_c == c, lens_own, lens_other) - tp * 128
    row_slot = row_c * 4 + (rows & 3)
    for s in range(8):
        limit = jnp.where(row_slot == s, live, 0)
        bias[:, s * 128 : s * 128 + 128] = jnp.where(lanes < limit, 0.0, NEG)

    for i in range(4):
        loads[i].wait()
        exchanges[i].wait_recv()

    square = (128, 128)
    eye = lax.broadcasted_iota(jnp.int32, square, 0) == lax.broadcasted_iota(jnp.int32, square, 1)
    ones = jnp.ones((1024, 128), BF)
    stat_row = lax.broadcasted_iota(jnp.int32, (16, 128), 0)

    def as_row(column):
        return jnp.sum(jnp.where(eye, column, 0.0), axis=0, keepdims=True)

    def stat_tile(top, total):
        hi = total.astype(BF).astype(F32)
        return jnp.where(stat_row == 0, top, jnp.where(stat_row == 1, hi, total - hi)).astype(BF)

    def weights(scores, top):
        return jnp.exp(scores - top).astype(BF)

    def largest(scores):
        return jnp.max(scores, axis=1, keepdims=True)

    def head(i, _):
        k = head_at(y, i)
        cols = pl.ds(pl.multiple_of(k * 128, 128), 128)
        pltpu.make_async_copy(q2.at[k], q2.at[k], grecv.at[k]).wait()
        qs[...] = dot(perm[...], q2[k], NN).astype(BF)
        chunks = [(x + a) % 4 for a in (1, 3, 2, 0)]
        parts = [qs[pl.ds(pl.multiple_of(j * 128, 128), 128), :] for j in chunks]
        keys = kbuf[:, cols]
        values = jnp.concatenate([vbuf[:, cols], ones], axis=1)
        suffix_keys = skbuf[:, :, cols].reshape(1024, 128)
        suffix_values = jnp.concatenate([svbuf[:, :, cols].reshape(1024, 128), ones], axis=1)

        s0 = dot(jnp.concatenate(parts[:2], axis=0), keys, NT) * SCALE
        s1 = dot(jnp.concatenate(parts[2:], axis=0), keys, NT) * SCALE
        own = pl.ds(pl.multiple_of(x * 128 + yh * 64, 64), 64)
        ss = dot(qs[own, :], suffix_keys, NT) * SCALE + bias[...]

        def send(a):
            pltpu.make_async_remote_copy(
                src_ref=sbuf.at[i * 4 + a], dst_ref=r1.at[x * 4 + y], send_sem=rsend, recv_sem=rrecv,
                device_id=dev(chunks[a], k, z, c), device_id_type=MESH,
            ).start()

        def put(a, m, n):
            sbuf[i * 4 + a, :128, :] = n[:, :128].astype(BF)
            sbuf[i * 4 + a, 128:, :] = stat_tile(as_row(m), as_row(n[:, 128:]))

        m0 = largest(s0).astype(BF).astype(F32)
        n0 = dot(weights(s0, m0), values, NN)
        put(0, m0[:128], n0[:128])
        send(0)
        put(1, m0[128:], n0[128:])
        send(1)

        m1, ms = largest(s1), largest(ss)
        low = jnp.full((64, 1), NEG, F32)
        ms = jnp.concatenate([jnp.where(yh == 0, ms, low), jnp.where(yh == 0, low, ms)], axis=0)
        m1 = jnp.concatenate([m1[:128], jnp.maximum(m1[128:], ms)], axis=0).astype(BF).astype(F32)
        n1 = dot(weights(s1, m1), values, NN)
        ns = dot(weights(ss, jnp.where(yh == 0, m1[128:192], m1[192:])), suffix_values, NN)
        ns = jnp.concatenate([jnp.where(yh == 0, ns, 0.0), jnp.where(yh == 0, 0.0, ns)], axis=0)
        put(2, m1[:128], n1[:128])
        send(2)
        put(3, m1[128:], n1[128:] + ns)
        pl.when(i < 3)(lambda: send(3))
        return 0

    lax.fori_loop(0, 4, head, 0)
    pltpu.make_async_copy(sbuf.at[15], r1.at[x * 4 + y], rrecv).start()

    pltpu.make_async_copy(r1, r1, rrecv).wait()
    stats = [r1[i, 128:, :].astype(F32) for i in range(16)]
    top = functools.reduce(jnp.maximum, [s[0:1] for s in stats])
    ws = [jnp.exp(s[0:1] - top) for s in stats]
    total = functools.reduce(jnp.add, [w * (s[1:2] + s[2:3]) for w, s in zip(ws, stats)])
    his = [w.astype(BF).astype(F32) for w in ws]
    spread = [
        jnp.concatenate([jnp.where(eye, w, 0.0).astype(BF) for w in part], axis=1)
        for part in (his, [w - h for w, h in zip(ws, his)])
    ]
    both = dot(jnp.concatenate(spread, axis=0), jnp.concatenate([r1[i, :128, :] for i in range(16)], axis=0), NN)
    flat = (both[:128] + both[128:]).astype(BF)
    stat = stat_tile(top, total)
    for d in range(8):
        s2[d, :16, :] = flat[d * 16 : d * 16 + 16, :]
        s2[d, 16:, :] = stat

    zt = 4 * c + y
    for o in range(1, 8):
        y_, c_ = (y + o // 2) % 4, (c + o % 2) % 2
        pltpu.make_async_remote_copy(
            src_ref=s2.at[y_ * 2 + c_], dst_ref=r2.at[z], send_sem=tsend.at[0], recv_sem=trecv,
            device_id=dev(x, y_, zt, c_), device_id_type=MESH,
        ).start()

    @pl.when(zt == z)
    def _():
        pltpu.make_async_copy(s2.at[y * 2 + c], r2.at[z], trecv).start()

    @pl.when(zt != z)
    def _():
        pltpu.make_async_remote_copy(
            src_ref=s2.at[y * 2 + c], dst_ref=r2.at[z], send_sem=tsend.at[1], recv_sem=trecv,
            device_id=dev(x, y, zt, c), device_id_type=MESH,
        ).start()

    pltpu.make_async_copy(r2, r2, trecv).wait()

    offset = y * 32 + c * 16
    pick = lax.broadcasted_iota(jnp.int32, (16, 128), 1) == lax.broadcasted_iota(jnp.int32, (16, 128), 0) + offset
    stats = [r2[i, 16:, :].astype(F32) for i in range(8)]
    m2 = functools.reduce(jnp.maximum, [s[0:1] for s in stats])
    ws = [jnp.exp(s[0:1] - m2) for s in stats]
    total = functools.reduce(jnp.add, [w * (s[1:2] + s[2:3]) for w, s in zip(ws, stats)])
    acc = jnp.zeros((16, 128), F32)
    for i in range(8):
        column = jnp.sum(jnp.where(pick, ws[i], 0.0), axis=1, keepdims=True)
        acc = acc + column * r2[i, :16, :].astype(F32)
    column = jnp.sum(jnp.where(pick, total, 0.0), axis=1, keepdims=True)
    acc = acc / column
    for g in range(4):
        out_ref[:, g * 128 : (g + 1) * 128] = acc[g * 4 : g * 4 + 4, :].astype(BF)

    for i in range(5):
        exchanges[i].wait_send()
    pltpu.make_async_copy(s2.at[pl.ds(0, 7), pl.ds(0, 16)], s2.at[pl.ds(0, 7), pl.ds(0, 16)], zsend.at[0]).wait()

    @pl.when(hz != c)
    def _():
        pltpu.make_async_copy(q0, q0, zsend.at[1]).wait()

    most = q2.at[:, pl.ds(0, 480)]
    pltpu.make_async_copy(most, most, gsend).wait()
    most = sbuf.at[pl.ds(0, 15)]
    pltpu.make_async_copy(most, most, rsend).wait()
    most = s2.at[pl.ds(0, 7)]
    pltpu.make_async_copy(most, most, tsend.at[0]).wait()

    @pl.when(zt != z)
    def _():
        pltpu.make_async_copy(s2.at[0], s2.at[0], tsend.at[1]).wait()


def shards(queries, assignment, prefix_keys, prefix_values, suffix_keys, suffix_values, lengths):
    vmem, far = pl.BlockSpec(memory_space=pltpu.VMEM), pl.BlockSpec(memory_space=pl.ANY)
    dma = pltpu.SemaphoreType.DMA
    return pl.pallas_call(
        kernel,
        out_shape=jax.ShapeDtypeStruct(queries.shape, BF),
        in_specs=[far, far, far, far, far, far, far],
        out_specs=vmem,
        scratch_shapes=[
            pltpu.VMEM((1024, 512), BF),
            pltpu.VMEM((1024, 512), BF),
            pltpu.VMEM((8, 128, 512), BF),
            pltpu.VMEM((8, 128, 512), BF),
            pltpu.VMEM((16, 128), F32),
            pltpu.VMEM((16, 128), BF),
            pltpu.VMEM((4, 32, 128), BF),
            pltpu.VMEM((4, 512, 128), BF),
            pltpu.VMEM((512, 128), BF),
            pltpu.VMEM((512, 512), BF),
            pltpu.VMEM((8, 128), jnp.int32),
            pltpu.VMEM((8, 128), jnp.int32),
            pltpu.VMEM((64, 1024), F32),
            pltpu.VMEM((16, 144, 128), BF),
            pltpu.VMEM((16, 144, 128), BF),
            pltpu.VMEM((8, 32, 128), BF),
            pltpu.VMEM((8, 32, 128), BF),
            pltpu.VMEM((4, 512), BF),
            pltpu.SMEM((64,), jnp.int32),
            pltpu.SMEM((4,), jnp.int32),
            dma((3,)),
            dma((4,)),
            dma((5,)),
            dma((5,)),
            dma((2,)),
            dma((4,)),
            dma(()),
            dma((4,)),
            dma(()),
            dma(()),
            dma((2,)),
            dma(()),
        ],
        compiler_params=pltpu.CompilerParams(
            collective_id=0, has_side_effects=True, vmem_limit_bytes=48 * 1024 * 1024
        ),
        cost_estimate=pl.CostEstimate(flops=1_300_000_000, bytes_accessed=4_300_000, transcendentals=2_600_000),
    )(
        *(
            pltpu.with_memory_space_constraint(operand, pltpu.HBM)
            for operand in (
                queries, assignment, lengths, prefix_keys, prefix_values, suffix_keys, suffix_values
            )
        )
    )


def solution(mesh):
    in_specs = (
        P("rep", "tp"),
        P(),
        P(("rep", "tp"), None),
        P(("rep", "tp"), None),
        P("rep", "tp", None),
        P("rep", "tp", None),
        P("rep"),
    )
    out_specs = P("rep", "tp")
    return jax.shard_map(shards, mesh=mesh, in_specs=in_specs, out_specs=out_specs, check_vma=False)
```
